32 devices in a mesh: row: 8 (over z, y), col: 4 (over x, core).
Axes of the slice: x: 2, y: 2, z: 4, core: 2. Of those that a mesh axis runs over, the one named last changes fastest.
Arguments:
- probes: bfloat16 [32768, 64], P(('row', 'col')), may hold values from -2 to 2
- points: bfloat16 [3, 32768], P(None, ('row', 'col')), may hold values from 0 to 1
- skeleton: bfloat16 [3, 14336], P(None, ('row', 'col')), may hold values from 0 to 1
- leaf_basis: bfloat16 [32768, 64], P(('row', 'col')), may hold values from -0.375 to 0.375
- transfer: bfloat16 [12288, 64], P(('row', 'col')), may hold values from -0.75 to 0.75
- near_list: int32 [8, 4, 2, 64], P('row', 'col'), may hold values from 0 to 31, as said below
- near_count: int32 [8, 4], P('row', 'col'), may hold values from 8 to 64, as said below
- far_list: int32 [8, 4, 2, 128], P('row', 'col'), may hold values from 0 to 55, as said below
- far_count: int32 [8, 4], P('row', 'col'), may hold values from 16 to 128, as said below
Outputs:
- sample: bfloat16 [32768, 64], P(('row', 'col'))
The draws below stay inside these ranges and needn't reach their ends.
Inputs may be any that keep to these rules, and one draw needn't show every extreme that they name: `near_list`: row entries index the 16 row leaves of the device's row, column entries the 32 column leaves of its column; only the first near_count slots are used. `near_count`: used slots of one device: 64 on some device in every draw, else 64/2, /4 or /8. `far_list`: row entries index the 28 row clusters, column entries the 56 column clusters; both clusters of a slot lie on the same level; only the first far_count slots are used. `far_count`: used slots of one device: 128 on some device in every draw, else 128/2, /4 or /8.
All inputs are finite; a program needn't handle non-finite values.
Results may differ from the reference program's by a relative error of at most 0.02.
Values may be sent and summed in bfloat16 or wider, within the bound.
No kernel may reach another device: no remote copies, remote signals or barrier semaphores. Data moves between devices by JAX's collectives and lax.ppermute only.
A program may use at most 64 MiB of HBM per device.

```python
import math
import jax
import jax.numpy as jnp
from jax import lax

LEAF = 256
RANK = 64
SAMPLES = 64
NEAR_MOST = 64
FAR_MOST = 128
NPTS = 32768
CLUSTERS = 224
N_ROW = 8
N_COL = 4
DEVICES = 32


def live_counts(key, most):
    first, second = jax.random.split(key)
    shifts = jax.random.randint(first, (N_ROW * N_COL,), 0, 4)
    counts = jnp.right_shift(jnp.full((N_ROW * N_COL,), most, jnp.int32), shifts)
    chosen = jax.random.randint(second, (), 0, N_ROW * N_COL)
    counts = counts.at[chosen].set(most)
    return counts.reshape(N_ROW, N_COL)


def draw_near_count(key, part):
    key = jax.random.fold_in(key, 11)
    return live_counts(key, NEAR_MOST)


def draw_far_count(key, part):
    key = jax.random.fold_in(key, 13)
    return live_counts(key, FAR_MOST)


def draw_near_list(key, part):
    key = jax.random.fold_in(key, 17)
    first, second = jax.random.split(key)
    shape = (N_ROW, N_COL, 1, NEAR_MOST)
    targets = jax.random.randint(first, shape, 0, 4 * N_COL)
    sources = jax.random.randint(second, shape, 0, 4 * N_ROW)
    return jnp.concatenate([targets, sources], axis=2).astype(jnp.int32)


def draw_far_list(key, part):
    key = jax.random.fold_in(key, 19)
    keys = jax.random.split(key, 5)
    shape = (N_ROW, N_COL, 1, FAR_MOST)
    level = jax.random.randint(keys[0], shape, 0, 3)
    offset = jnp.where(level == 0, 0, jnp.where(level == 1, 4, 6))
    span = jnp.right_shift(jnp.full(shape, 4, jnp.int32), level)
    target_dev = jax.random.randint(keys[1], shape, 0, N_COL)
    target_local = jax.random.randint(keys[2], shape, 0, 4) % span
    source_dev = jax.random.randint(keys[3], shape, 0, N_ROW)
    source_local = jax.random.randint(keys[4], shape, 0, 4) % span
    targets = target_dev * 7 + offset + target_local
    sources = source_dev * 7 + offset + source_local
    return jnp.concatenate([targets, sources], axis=2).astype(jnp.int32)


def steps_of(key, shape, shards, least, high):
    def one(dim, blocks):
        steps = jax.random.uniform(jax.random.fold_in(jax.random.fold_in(key, 6), dim), (blocks,), jnp.float32, least / len(shards), high / len(shards))
        return jnp.repeat(jnp.exp(steps), shape[dim] // blocks).reshape((-1,) + (1,) * (len(shape) - dim - 1))

    factor_of = one(*shards[0])
    for cut in shards[1:]:
        factor_of = factor_of * one(*cut)
    return factor_of


def bell_draw(own_key, dims, deviation, bound, cuts=(), held_as=jnp.bfloat16):
    loudness = steps_of(own_key, dims, cuts, -0.22, 0.18) if cuts else 1.0
    array = jax.random.normal(own_key, dims, jnp.float32) * deviation * loudness
    return jnp.minimum(jnp.maximum(array, -bound), bound).astype(held_as)


def setup_inputs(seed: int = 0) -> dict:
    key_of = jax.random.split(jax.random.key(seed), 10)
    probes = bell_draw(key_of[0], (NPTS, SAMPLES), 0.25, 2.0, ((0, 32),))
    points = jnp.clip(1.0 * jax.random.uniform(key_of[1], (3, NPTS), jnp.float32) ** steps_of(key_of[1], (3, NPTS), ((1, 32),), -0.2, 0.2), 0.0, 1.0).astype(jnp.bfloat16)
    skeleton = jnp.clip(1.0 * jax.random.uniform(key_of[2], (3, CLUSTERS * RANK), jnp.float32) ** steps_of(key_of[2], (3, CLUSTERS * RANK), ((1, 32),), -0.2, 0.2), 0.0, 1.0).astype(jnp.bfloat16)
    leaf_basis = bell_draw(key_of[3], (NPTS, RANK), LEAF ** -0.5, 0.375, ((0, 32),))
    transfer = bell_draw(key_of[4], (6 * DEVICES * RANK, RANK), RANK ** -0.5, 0.75, ((0, 32),))
    near_list = draw_near_list(jax.random.fold_in(key_of[9], 71), 0)
    near_count = draw_near_count(jax.random.fold_in(key_of[9], 71), 0)
    far_list = draw_far_list(jax.random.fold_in(key_of[9], 71), 0)
    far_count = draw_far_count(jax.random.fold_in(key_of[9], 71), 0)
    return dict(probes=probes, points=points, skeleton=skeleton, leaf_basis=leaf_basis, transfer=transfer, near_list=near_list, near_count=near_count, far_list=far_list, far_count=far_count)


length_scale = 0.15
root_three = math.sqrt(3.0)

def rounded(values):
    return lax.optimization_barrier(values.astype(jnp.bfloat16)).astype(jnp.float32)

def matern(first, second):
    first = first.astype(jnp.float32)
    second = second.astype(jnp.float32)
    dist = jnp.zeros(first.shape[1:] + second.shape[-1:], jnp.float32)
    for axis in range(3):
        gap = first[axis][..., :, None] - second[axis][..., None, :]
        dist = dist + gap * gap
    scaled = root_three * jnp.sqrt(dist) / length_scale
    return (1.0 + scaled) * jnp.exp(-scaled)

def upward(probe_rows, basis_rows, move_rows):
    leaf = jnp.einsum('klr,kls->krs', basis_rows.reshape(4, LEAF, RANK).astype(jnp.float32), probe_rows.reshape(4, LEAF, SAMPLES).astype(jnp.float32))
    leaf = leaf.astype(jnp.bfloat16)
    moves = move_rows.reshape(6, RANK, RANK).astype(jnp.float32)
    middle = jnp.einsum('kap,kas->kps', moves[0:4], leaf.astype(jnp.float32))
    middle = middle.reshape(2, 2, RANK, SAMPLES).sum(axis=1).astype(jnp.bfloat16)
    upper = jnp.einsum('kap,kas->kps', moves[4:6], middle.astype(jnp.float32))
    upper = upper.sum(axis=0, keepdims=True).astype(jnp.bfloat16)
    return jnp.concatenate([leaf, middle, upper], axis=0)

def near_terms(row_points, col_points, col_probes, pairs, live, groups):
    row_leaves = row_points.reshape(3, -1, LEAF)
    col_leaves = col_points.reshape(3, -1, LEAF)
    col_values = col_probes.reshape(-1, LEAF, SAMPLES)
    totals = jnp.zeros((row_leaves.shape[1], LEAF, SAMPLES), jnp.float32)

    def step(group, totals):
        slots = lax.dynamic_slice_in_dim(pairs, group * 4, 4, 1)
        alive = group * 4 + jnp.arange(4, dtype=jnp.int32) < live
        targets = slots[0]
        sources = slots[1]
        kernel = rounded(matern(row_leaves[:, targets], col_leaves[:, sources]))
        values = col_values[sources].astype(jnp.float32)
        term = jnp.einsum('gab,gbs->gas', kernel, values)
        term = jnp.where(alive[:, None, None], term, 0.0)
        return totals.at[targets].add(term)
    totals = lax.fori_loop(0, groups, step, totals)
    return totals.reshape(-1, SAMPLES)

def far_terms(row_skel, col_skel, col_coeffs, pairs, live, groups):
    row_sets = row_skel.reshape(3, -1, RANK)
    col_sets = col_skel.reshape(3, -1, RANK)
    totals = jnp.zeros((row_sets.shape[1], RANK, SAMPLES), jnp.float32)

    def step(group, totals):
        slots = lax.dynamic_slice_in_dim(pairs, group * 16, 16, 1)
        alive = group * 16 + jnp.arange(16, dtype=jnp.int32) < live
        targets = slots[0]
        sources = slots[1]
        kernel = rounded(matern(row_sets[:, targets], col_sets[:, sources]))
        values = col_coeffs[sources].astype(jnp.float32)
        term = jnp.einsum('gab,gbs->gas', kernel, values)
        term = jnp.where(alive[:, None, None], term, 0.0)
        return totals.at[targets].add(term)
    return lax.fori_loop(0, groups, step, totals)

def descend(far_total, moves):
    moves = moves.astype(jnp.float32)
    upper = far_total[:, 6]
    middle = far_total[:, 4:6] + jnp.einsum('dkab,dbs->dkas', moves[:, 4:6], upper, precision=lax.Precision.HIGHEST)
    spread = jnp.repeat(middle, 2, axis=1)
    return far_total[:, 0:4] + jnp.einsum('dkab,dkbs->dkas', moves[:, 0:4], spread, precision=lax.Precision.HIGHEST)

def reference(probes, points, skeleton, leaf_basis, transfer, near_list, near_count, far_list, far_count):
    probes_dev = probes.reshape(N_ROW, N_COL, 4 * LEAF, SAMPLES)
    basis_dev = leaf_basis.reshape(N_ROW, N_COL, 4 * LEAF, RANK)
    moves_dev = transfer.reshape(N_ROW, N_COL, 6 * RANK, RANK)
    coeffs = jax.vmap(jax.vmap(upward))(probes_dev, basis_dev, moves_dev)
    points_dev = points.reshape(3, N_ROW, N_COL, 4 * LEAF)
    skel_dev = skeleton.reshape(3, N_ROW, N_COL, 7 * RANK)
    column_side = (jnp.moveaxis(probes_dev, 1, 0).reshape(N_COL, N_ROW * 4 * LEAF, SAMPLES), jnp.moveaxis(points_dev, 2, 0).reshape(N_COL, 3, N_ROW * 4 * LEAF), jnp.moveaxis(skel_dev, 2, 0).reshape(N_COL, 3, N_ROW * 7 * RANK), jnp.moveaxis(coeffs, 1, 0).reshape(N_COL, N_ROW * 7, RANK, SAMPLES))

    def one_row(inputs):
        row_points, row_skel, near_pairs, near_live, far_pairs, far_live, basis_rows, move_rows = inputs

        def one_device(carry, items):
            near_total, far_total = carry
            col_probes, col_points, col_skel, col_coeffs, n_pairs, n_live, f_pairs, f_live = items
            near_part = near_terms(row_points, col_points, col_probes, n_pairs, n_live, (n_live + 3) // 4)
            far_part = far_terms(row_skel, col_skel, col_coeffs, f_pairs, f_live, (f_live + 15) // 16)
            return ((near_total + rounded(near_part), far_total + far_part), None)
        start = (jnp.zeros((N_COL * 4 * LEAF, SAMPLES), jnp.float32), jnp.zeros((N_COL * 7, RANK, SAMPLES), jnp.float32))
        (near_total, far_total), unused = lax.scan(one_device, start, column_side + (near_pairs, near_live, far_pairs, far_live))
        leaf_far = descend(far_total.reshape(N_COL, 7, RANK, SAMPLES), move_rows.reshape(N_COL, 6, RANK, RANK))
        expanded = jnp.einsum('dklr,dkrs->dkls', basis_rows.reshape(N_COL, 4, LEAF, RANK).astype(jnp.float32), leaf_far, precision=lax.Precision.HIGHEST)
        return (near_total.reshape(N_COL, 4, LEAF, SAMPLES) + expanded).astype(jnp.bfloat16)
    rows = lax.map(one_row, (jnp.moveaxis(points_dev, 1, 0).reshape(N_ROW, 3, N_COL * 4 * LEAF), jnp.moveaxis(skel_dev, 1, 0).reshape(N_ROW, 3, N_COL * 7 * RANK), near_list, near_count, far_list, far_count, basis_dev, moves_dev))
    return rows.reshape(N_ROW * N_COL * 4 * LEAF, SAMPLES)
```

```python
import functools
import math

import jax
import jax.numpy as jnp
from jax import lax
from jax.experimental import pallas as pl
from jax.experimental.pallas import tpu as pltpu
from jax.sharding import PartitionSpec as P

LEAF = 256
RANK = 64
SAMPLES = 64
OWN = 4 * LEAF
CLUSTERS = 7
WIDE = 8 * RANK
NEAR_GROUP = 8
FAR_GROUP = 16
F32 = jnp.float32
BF16 = jnp.bfloat16
LOG2E = 1.0 / math.log(2.0)
SCALE = 3.0 / 0.15**2 * LOG2E**2

VMEM = pl.BlockSpec(memory_space=pltpu.VMEM)
NN = (((1,), (0,)), ((), ()))
NT = (((1,), (1,)), ((), ()))
TN = (((0,), (0,)), ((), ()))


def dot(a, b, dims=NN):
    return lax.dot_general(a, b, dims, preferred_element_type=F32)


def dot_wide(a, b):
    high = a.astype(BF16)
    low = (a - high.astype(F32)).astype(BF16)
    return dot(high, b) + dot(low, b)


def split(x):
    high = x.astype(BF16).astype(F32)
    rest = x - high
    middle = rest.astype(BF16).astype(F32)
    return high, middle, (rest - middle).astype(BF16).astype(F32)


def features(points, is_row):
    coords = points.astype(F32)
    axes = [coords[d : d + 1] for d in range(3)]
    norm = SCALE * (axes[0] * axes[0] + axes[1] * axes[1] + axes[2] * axes[2])
    ones = jnp.ones_like(norm)
    if is_row:
        rows = [piece for x in axes for piece in split(-2.0 * SCALE * x)]
        rows += list(split(norm)) + [ones] * 3
    else:
        rows = [x for x in axes for _ in range(3)]
        rows += [ones] * 3 + list(split(norm))
    rows.append(jnp.zeros_like(norm))
    return jnp.concatenate(rows, axis=0).astype(BF16)


def matern_of(square):
    square = jnp.maximum(square, 1e-12)
    t = square * lax.rsqrt(square)
    e = jnp.exp2(-t)
    return (e + (math.log(2.0) * t) * e).astype(BF16)


def upward_kernel(probes, basis, moves, out):
    leaves = []
    for l in range(4):
        part = slice(l * LEAF, (l + 1) * LEAF)
        leaves.append(dot(probes[:, part], basis[:, part], NT))
    pairs = [jnp.concatenate(leaves[2 * j : 2 * j + 2], axis=1).astype(BF16) for j in range(2)]
    middle = [dot(pairs[j], moves[:, j * 128 : (j + 1) * 128], NT) for j in range(2)]
    middle = jnp.concatenate(middle, axis=1).astype(BF16)
    top = dot(middle, moves[:, 256:384], NT)
    out[:, 0:128] = pairs[0]
    out[:, 128:256] = pairs[1]
    out[:, 256:384] = middle
    out[:, 384:512] = jnp.concatenate([top, jnp.zeros_like(top)], axis=1).astype(BF16)


def far_place(index, me):
    device = lax.shift_right_logical(index * 9363, 16)
    return (device ^ me) * CLUSTERS + (index - device * CLUSTERS)


def near_place(index, me):
    return (lax.shift_right_logical(index, 2) ^ me) * 4 + (index & 3)


def values_kernel(
    n_row, n_col, near_list, near_count, far_list, far_count, *refs
):
    row_refs, refs = refs[:n_col], refs[n_col:]
    col_refs, refs = refs[:n_row], refs[n_row:]
    near_out, far_out, near_row, near_col, far_row, far_col = refs
    my_row = lax.axis_index("row")
    my_col = lax.axis_index("col")
    group = pl.program_id(0)

    @pl.when(group == 0)
    def _():
        for refs, near, far, is_row in (
            (row_refs, near_row, far_row, True),
            (col_refs, near_col, far_col, False),
        ):
            for i, ref in enumerate(refs):
                made = features(ref[...], is_row)
                for l in range(4):
                    near[4 * i + l] = made[:, l * LEAF : (l + 1) * LEAF]
                for l in range(CLUSTERS):
                    far[CLUSTERS * i + l] = made[:, OWN + l * RANK : OWN + (l + 1) * RANK]

    def near_step(i, _):
        slot = group * NEAR_GROUP + i
        a = near_place(near_list[0, slot], my_col)
        b = near_place(near_list[1, slot], my_row)
        for half in range(2):
            rows = slice(half * 128, (half + 1) * 128)
            near_out[i, rows] = matern_of(dot(near_col[b][:, rows], near_row[a], TN))
        return 0

    lax.fori_loop(0, jnp.clip(near_count[0, 0] - group * NEAR_GROUP, 0, NEAR_GROUP), near_step, 0)

    def far_step(i, _):
        slot = group * FAR_GROUP + i
        a = far_place(far_list[0, slot], my_col)
        b = far_place(far_list[1, slot], my_row)
        far_out[i] = matern_of(dot(far_col[b], far_row[a], TN))
        return 0

    lax.fori_loop(0, jnp.clip(far_count[0, 0] - group * FAR_GROUP, 0, FAR_GROUP), far_step, 0)


def apply_kernel(
    n_row, n_col, near_list, near_count, far_list, far_count, near_values, far_values, *refs
):
    probe_refs, refs = refs[:n_row], refs[n_row:]
    coeff_refs, refs = refs[:n_row], refs[n_row:]
    outs, refs = refs[:n_col], refs[n_col:]
    probes, coeffs, near_total, far_total = refs
    my_row = lax.axis_index("row")
    my_col = lax.axis_index("col")
    group = pl.program_id(0)

    @pl.when(group == 0)
    def _():
        near_total[...] = jnp.zeros_like(near_total)
        far_total[...] = jnp.zeros_like(far_total)
        for i in range(n_row):
            for l in range(4):
                probes[4 * i + l] = probe_refs[i][:, l * LEAF : (l + 1) * LEAF]
            for l in range(CLUSTERS):
                coeffs[CLUSTERS * i + l] = coeff_refs[i][:, l * RANK : (l + 1) * RANK]

    def near_step(i, _):
        slot = group * NEAR_GROUP + i
        a = near_place(near_list[0, slot], my_col)
        b = near_place(near_list[1, slot], my_row)
        near_total[a] += dot(probes[b], near_values[i])
        return 0

    lax.fori_loop(0, jnp.clip(near_count[0, 0] - group * NEAR_GROUP, 0, NEAR_GROUP), near_step, 0)

    def far_step(i, _):
        slot = group * FAR_GROUP + i
        a = far_place(far_list[0, slot], my_col)
        b = far_place(far_list[1, slot], my_row)
        far_total[a] += dot(coeffs[b], far_values[i])
        return 0

    lax.fori_loop(0, jnp.clip(far_count[0, 0] - group * FAR_GROUP, 0, FAR_GROUP), far_step, 0)

    @pl.when(group == pl.num_programs(0) - 1)
    def _():
        for i in range(n_col):
            for l in range(4):
                outs[i][:, l * LEAF : (l + 1) * LEAF] = near_total[4 * i + l].astype(BF16)
            parts = [far_total[CLUSTERS * i + l] for l in range(CLUSTERS)]
            parts.append(jnp.zeros_like(parts[0]))
            for j in range(4):
                pair = jnp.concatenate(parts[2 * j : 2 * j + 2], axis=1)
                outs[i][:, OWN + j * 128 : OWN + (j + 1) * 128] = pair.astype(BF16)


def final_kernel(n_col, basis, moves, *refs):
    parts, out = refs[:n_col], refs[n_col]
    far = sum(part[:, OWN:].astype(F32) for part in parts)
    middle = far[:, 256:384] + dot_wide(far[:, 384:448], moves[:, 256:384])
    for j in range(2):
        pair = far[:, j * 128 : (j + 1) * 128] + dot_wide(
            middle[:, j * RANK : (j + 1) * RANK], moves[:, j * 128 : (j + 1) * 128]
        )
        for k in range(2):
            l = 2 * j + k
            part = slice(l * LEAF, (l + 1) * LEAF)
            near = sum(ref[:, part].astype(F32) for ref in parts)
            expanded = dot_wide(pair[:, k * RANK : (k + 1) * RANK], basis[:, part])
            out[:, part] = (near + expanded).astype(BF16)


def exchange(x, axis, offset):
    size = lax.axis_size(axis)
    return lax.ppermute(x, axis, [(i, i ^ offset) for i in range(size)])


def local(
    probes, points, skeleton, leaf_basis, transfer, near_list, near_count, far_list, far_count
):
    n_row = lax.axis_size("row")
    n_col = lax.axis_size("col")
    n_y = n_row // min(n_row, 4)
    probes, basis, moves = probes.T, leaf_basis.T, transfer.T
    coords = jnp.concatenate([points, skeleton], axis=1)
    row_coords = [coords] + [exchange(coords, "col", k) for k in range(1, n_col)]
    col_coords = [coords] + [exchange(coords, "row", k) for k in range(1, n_row)]

    def gather(x):
        blocks = [None] * n_row
        for z in range(0, n_row, n_y):
            blocks[z] = x if z == 0 else exchange(x, "row", z)
            for y in range(1, n_y):
                blocks[z + y] = exchange(blocks[z], "row", y)
        return blocks

    col_probes = gather(probes)
    coeffs = pl.pallas_call(
        upward_kernel,
        out_shape=jax.ShapeDtypeStruct((SAMPLES, WIDE), BF16),
        in_specs=[VMEM] * 3,
        out_specs=VMEM,
        name="upward",
    )(probes, basis, moves)
    col_coeffs = gather(coeffs)

    lists = (near_list[0, 0], near_count, far_list[0, 0], far_count)
    near_most, far_most = near_list.shape[-1], far_list.shape[-1]
    steps = near_most // NEAR_GROUP
    assert far_most == steps * FAR_GROUP

    def near_block(g, near_list, near_count, far_list, far_count):
        return (jnp.minimum(g, lax.shift_right_logical(near_count[0, 0] - 1, 3)), 0, 0)

    def far_block(g, near_list, near_count, far_list, far_count):
        return (jnp.minimum(g, lax.shift_right_logical(far_count[0, 0] - 1, 4)), 0, 0)

    near_spec = pl.BlockSpec((NEAR_GROUP, LEAF, LEAF), near_block)
    far_spec = pl.BlockSpec((FAR_GROUP, RANK, RANK), far_block)
    evaluations = near_most * LEAF * LEAF + far_most * RANK * RANK
    near_values, far_values = pl.pallas_call(
        functools.partial(values_kernel, n_row, n_col),
        out_shape=[
            jax.ShapeDtypeStruct((near_most, LEAF, LEAF), BF16),
            jax.ShapeDtypeStruct((far_most, RANK, RANK), BF16),
        ],
        grid_spec=pltpu.PrefetchScalarGridSpec(
            num_scalar_prefetch=4,
            grid=(steps,),
            in_specs=[VMEM] * (n_row + n_col),
            out_specs=[near_spec, far_spec],
            scratch_shapes=[
                pltpu.VMEM((4 * n_col, 16, LEAF), BF16),
                pltpu.VMEM((4 * n_row, 16, LEAF), BF16),
                pltpu.VMEM((CLUSTERS * n_col, 16, RANK), BF16),
                pltpu.VMEM((CLUSTERS * n_row, 16, RANK), BF16),
            ],
        ),
        compiler_params=pltpu.CompilerParams(vmem_limit_bytes=32 << 20),
        cost_estimate=pl.CostEstimate(
            flops=evaluations * 40, bytes_accessed=evaluations * 2, transcendentals=evaluations * 2
        ),
        name="values",
    )(*lists, *row_coords, *col_coords)

    partials = pl.pallas_call(
        functools.partial(apply_kernel, n_row, n_col),
        out_shape=[jax.ShapeDtypeStruct((SAMPLES, OWN + WIDE), BF16)] * n_col,
        grid_spec=pltpu.PrefetchScalarGridSpec(
            num_scalar_prefetch=4,
            grid=(steps,),
            in_specs=[near_spec, far_spec] + [VMEM] * (2 * n_row),
            out_specs=[VMEM] * n_col,
            scratch_shapes=[
                pltpu.VMEM((4 * n_row, SAMPLES, LEAF), BF16),
                pltpu.VMEM((CLUSTERS * n_row, SAMPLES, RANK), BF16),
                pltpu.VMEM((4 * n_col, SAMPLES, LEAF), F32),
                pltpu.VMEM((CLUSTERS * n_col, SAMPLES, RANK), F32),
            ],
        ),
        compiler_params=pltpu.CompilerParams(vmem_limit_bytes=48 << 20),
        cost_estimate=pl.CostEstimate(
            flops=evaluations * 2 * SAMPLES, bytes_accessed=evaluations * 2, transcendentals=0
        ),
        name="apply",
    )(*lists, near_values, far_values, *col_probes, *col_coeffs)

    arrived = [partials[0]] + [exchange(partials[k], "col", k) for k in range(1, n_col)]
    sample = pl.pallas_call(
        functools.partial(final_kernel, n_col),
        out_shape=jax.ShapeDtypeStruct((SAMPLES, OWN), BF16),
        in_specs=[VMEM] * (2 + n_col),
        out_specs=VMEM,
        name="final",
    )(basis, moves, *arrived)
    return sample.T


def solution(mesh):
    placed = (
        P(("row", "col"), None),
        P(None, ("row", "col")),
        P(None, ("row", "col")),
        P(("row", "col"), None),
        P(("row", "col"), None),
        P("row", "col", None, None),
        P("row", "col"),
        P("row", "col", None, None),
        P("row", "col"),
    )
    return jax.shard_map(
        local, mesh=mesh, in_specs=placed, out_specs=P(("row", "col"), None), check_vma=False
    )
```

```python
import functools
import math

import jax
import jax.numpy as jnp
import numpy as np
from jax import lax
from jax.experimental import pallas as pl
from jax.experimental.pallas import tpu as pltpu
from jax.sharding import PartitionSpec as P

LEAF = 256
RANK = 64
SAMPLES = 64
OWN = 4 * LEAF
CLUSTERS = 7
LANES = 128
F32 = jnp.float32
BF16 = jnp.bfloat16
FAR_ROW = OWN // LANES * SAMPLES
COORD_ROW = FAR_ROW + CLUSTERS * SAMPLES // 2
COORD_ROWS = 48
PACKED_ROWS = COORD_ROW + COORD_ROWS
SKELETON_ROW = 24
FEATURES = 16
STAGES = 3
NEAR_UNROLL = 4
FAR_UNROLL = 8
LN2 = math.log(2.0)
SCALE = 3.0 / 0.15**2 / LN2**2

VMEM = pl.BlockSpec(memory_space=pltpu.VMEM)
SMEM = pl.BlockSpec(memory_space=pltpu.SMEM)
NN = (((1,), (0,)), ((), ()))
NT = (((1,), (1,)), ((), ()))


def dot(a, b, dims=NN):
    return lax.dot_general(a, b, dims, preferred_element_type=F32)


def dot_wide(a, b):
    high = a.astype(BF16)
    low = (a - high.astype(F32)).astype(BF16)
    return dot(high, b) + dot(low, b)


def split(x):
    high = x.astype(BF16).astype(F32)
    rest = x - high
    middle = rest.astype(BF16).astype(F32)
    return [high, middle, (rest - middle).astype(BF16).astype(F32)]


def feature_rows(axes, is_row):
    norm = SCALE * (axes[0] * axes[0] + axes[1] * axes[1] + axes[2] * axes[2])
    ones = jnp.ones_like(norm)
    if is_row:
        rows = [piece for x in axes for piece in split(-2.0 * SCALE * x)]
        rows += split(norm) + [ones] * 3
    else:
        rows = [x for x in axes for _ in range(3)] + [ones] * 3 + split(norm)
    return rows + [jnp.zeros_like(norm)]


def features(coords, is_row):
    sets = []
    for first, chunks in ((0, 8), (SKELETON_ROW, 4)):
        axes = [coords[first + chunks * d : first + chunks * (d + 1)] for d in range(3)]
        rows = feature_rows(axes, is_row)
        sets.append(
            [jnp.concatenate([row[j : j + 1] for row in rows], axis=0) for j in range(chunks)]
        )
    return sets


def matern_of(square):
    square = jnp.maximum(square, 1e-12)
    t = square * lax.rsqrt(square)
    e = jnp.exp2(-t)
    return (e + (LN2 * t) * e).astype(BF16)


def pack_kernel(probes, basis, moves, points, skeleton, packed, coords):
    leaves = []
    for l in range(4):
        part = slice(l * LEAF, (l + 1) * LEAF)
        leaves.append(dot(probes[:, part], basis[:, part], NT))
    pairs = [jnp.concatenate(leaves[2 * j : 2 * j + 2], axis=1).astype(BF16) for j in range(2)]
    middle = [dot(pairs[j], moves[:, j * 128 : (j + 1) * 128], NT) for j in range(2)]
    middle = jnp.concatenate(middle, axis=1).astype(BF16)
    top = dot(middle, moves[:, 256:384], NT)
    top = jnp.concatenate([top[:32], top[32:]], axis=1).astype(BF16)
    for j in range(8):
        packed[j * SAMPLES : (j + 1) * SAMPLES] = probes[:, j * LANES : (j + 1) * LANES]
    packed[FAR_ROW : FAR_ROW + 64] = pairs[0]
    packed[FAR_ROW + 64 : FAR_ROW + 128] = pairs[1]
    packed[FAR_ROW + 128 : FAR_ROW + 192] = middle
    packed[FAR_ROW + 192 : FAR_ROW + 224] = top
    near = points[...].astype(F32)
    far = skeleton[...].astype(F32)
    far = jnp.concatenate([far, jnp.zeros((3, 64), F32)], axis=1)
    rows = [near[d : d + 1, j * LANES : (j + 1) * LANES] for d in range(3) for j in range(8)]
    rows += [far[d : d + 1, j * LANES : (j + 1) * LANES] for d in range(3) for j in range(4)]
    rows.append(jnp.zeros((COORD_ROWS - len(rows), LANES), F32))
    made = jnp.concatenate(rows, axis=0).astype(BF16)
    packed[COORD_ROW:] = made
    coords[...] = made


class Plan:
    def __init__(self, near_most, far_most):
        self.near = near_most + NEAR_UNROLL
        self.far = far_most + FAR_UNROLL
        self.stage = 2 * (self.near + self.far)
        self.counts = STAGES * self.stage
        self.size = self.counts + 2 * STAGES


def plan_kernel(
    n_row, n_col, plan, near_list, near_count, far_list, far_count, table, *refs
):
    coord_refs, (out, near_row, far_low, far_high) = refs[:n_col], refs[n_col:]
    my_row = lax.axis_index("row")
    my_col = lax.axis_index("col")
    for k in range(2 * STAGES):
        out[plan.counts + k] = 0

    def add(kind, capacity, first, device, row, column):
        info = table[device]
        stage = lax.shift_right_logical(info, 8)
        counter = plan.counts + 2 * stage + kind
        place = stage * plan.stage + first + out[counter]
        out[place] = row
        out[place + capacity] = (info & 255) * (4, CLUSTERS)[kind] + column
        out[counter] = out[counter] + 1

    def near_step(i, _):
        a, b = near_list[0, i], near_list[1, i]
        row = (lax.shift_right_logical(a, 2) ^ my_col) * 4 + (a & 3)
        add(0, plan.near, 0, lax.shift_right_logical(b, 2) ^ my_row, row, b & 3)
        return 0

    lax.fori_loop(0, near_count[0, 0], near_step, 0)

    def far_step(i, _):
        a, b = far_list[0, i], far_list[1, i]
        a_device = lax.shift_right_logical(a * 9363, 16)
        b_device = lax.shift_right_logical(b * 9363, 16)
        row = (a_device ^ my_col) * CLUSTERS + (a - a_device * CLUSTERS)
        add(1, plan.far, 2 * plan.near, b_device ^ my_row, row, b - b_device * CLUSTERS)
        return 0

    lax.fori_loop(0, far_count[0, 0], far_step, 0)
    for stage in range(STAGES):
        for kind, capacity, first, dummy, unroll in (
            (0, plan.near, 0, 4 * n_col, NEAR_UNROLL),
            (1, plan.far, 2 * plan.near, CLUSTERS * n_col, FAR_UNROLL),
        ):
            place = stage * plan.stage + first + out[plan.counts + 2 * stage + kind]
            for u in range(unroll - 1):
                out[place + u] = dummy
                out[place + capacity + u] = 0

    for i in range(n_col):
        near, far = features(coord_refs[i][...].astype(F32), True)
        for l in range(4):
            pair = jnp.concatenate(near[2 * l : 2 * l + 2], axis=1)
            near_row[4 * i + l] = pair.astype(BF16)
        for l in range(CLUSTERS):
            chunk = far[l // 2]
            half = chunk[:, (l % 2) * 64 : (l % 2) * 64 + 64]
            empty = jnp.zeros_like(half)
            far_low[CLUSTERS * i + l] = jnp.concatenate([half, empty], axis=1).astype(BF16)
            far_high[CLUSTERS * i + l] = jnp.concatenate([empty, half], axis=1).astype(BF16)
    near_row[4 * n_col] = jnp.zeros(near_row.shape[1:], BF16)
    far_low[CLUSTERS * n_col] = jnp.zeros(far_low.shape[1:], BF16)
    far_high[CLUSTERS * n_col] = jnp.zeros(far_high.shape[1:], BF16)


def stage_kernel(n_col, n_blocks, plan, stage, lists, near_row, far_low, far_high, *refs):
    blocks, refs = refs[:n_blocks], refs[n_blocks:]
    if stage > 0:
        refs = refs[3:]
    last = stage == STAGES - 1
    totals, refs = refs[:3], refs[3:]
    if last:
        outs, refs = refs[:n_col], refs[n_col:]
    probes, near_col, coeffs, far_col = refs
    near_total, far_even, far_odd = totals
    if stage == 0:
        for total in totals:
            total[...] = jnp.zeros_like(total)

    for i, block in enumerate(blocks):
        near, far = features(block[COORD_ROW:].astype(F32), False)
        for l in range(4):
            for h in range(2):
                j = 2 * l + h
                half = slice(h * LANES, (h + 1) * LANES)
                probes[4 * i + l, :, half] = block[j * SAMPLES : (j + 1) * SAMPLES]
                near_col[4 * i + l, half] = near[j].T.astype(BF16)
        for j in range(4):
            tall = far[j].T.astype(BF16)
            far_col[CLUSTERS * i + 2 * j] = tall[:64]
            if j < 3:
                far_col[CLUSTERS * i + 2 * j + 1] = tall[64:]
                pair = block[FAR_ROW + 64 * j : FAR_ROW + 64 * (j + 1)]
                coeffs[CLUSTERS * i + 2 * j] = pair[:, :64]
                coeffs[CLUSTERS * i + 2 * j + 1] = pair[:, 64:]
            else:
                top = block[FAR_ROW + 192 : FAR_ROW + 224]
                coeffs[CLUSTERS * i + 6, :32] = top[:, :64]
                coeffs[CLUSTERS * i + 6, 32:] = top[:, 64:]

    def near_step(g, _):
        place = stage * plan.stage + g * NEAR_UNROLL
        terms = []
        for u in range(NEAR_UNROLL):
            a, b = lists[place + u], lists[place + plan.near + u]
            halves = [
                matern_of(dot(near_col[b, h * LANES : (h + 1) * LANES], near_row[a]))
                for h in range(2)
            ]
            terms.append((a, dot(probes[b], jnp.concatenate(halves, axis=0))))
        for a, term in terms:
            near_total[a] += term
        return 0

    count = lists[plan.counts + 2 * stage]
    lax.fori_loop(0, (count + NEAR_UNROLL - 1) // NEAR_UNROLL, near_step, 0)

    def far_step(g, _):
        place = stage * plan.stage + 2 * plan.near + g * FAR_UNROLL
        terms = []
        for u in range(0, FAR_UNROLL, 2):
            a0, a1 = lists[place + u], lists[place + u + 1]
            b0, b1 = lists[place + plan.far + u], lists[place + plan.far + u + 1]
            square = dot(far_col[b0], far_low[a0]) + dot(far_col[b1], far_high[a1])
            left = jnp.concatenate([coeffs[b0], coeffs[b1]], axis=0)
            terms.append((a0, a1, dot(left, matern_of(square))))
        for a0, a1, term in terms:
            far_even[a0] += term[:64]
            far_odd[a1] += term[64:]
        return 0

    count = lists[plan.counts + 2 * stage + 1]
    lax.fori_loop(0, (count + FAR_UNROLL - 1) // FAR_UNROLL, far_step, 0)

    if last:
        for i in range(n_col):
            for j in range(8):
                half = slice(j % 2 * LANES, (j % 2 + 1) * LANES)
                part = near_total[4 * i + j // 2, :, half]
                outs[i][j * SAMPLES : (j + 1) * SAMPLES] = part.astype(BF16)
            parts = []
            for l in range(CLUSTERS):
                even, odd = far_even[CLUSTERS * i + l], far_odd[CLUSTERS * i + l]
                parts.append(even[:, :64] + odd[:, 64:])
            for j in range(3):
                pair = jnp.concatenate(parts[2 * j : 2 * j + 2], axis=1)
                outs[i][FAR_ROW + 64 * j : FAR_ROW + 64 * (j + 1)] = pair.astype(BF16)
            pair = jnp.concatenate([parts[6][:32], parts[6][32:]], axis=1)
            outs[i][FAR_ROW + 192 : FAR_ROW + 224] = pair.astype(BF16)


def final_kernel(n_col, basis, moves, *refs):
    parts, out = refs[:n_col], refs[n_col]

    def total(first, rows):
        return sum(part[first : first + rows].astype(F32) for part in parts)

    top = total(FAR_ROW + 192, 32)
    top = jnp.concatenate([top[:, :64], top[:, 64:]], axis=0)
    middle = total(FAR_ROW + 128, 64) + dot_wide(top, moves[:, 256:384])
    for j in range(2):
        pair = total(FAR_ROW + 64 * j, 64) + dot_wide(
            middle[:, j * RANK : (j + 1) * RANK], moves[:, j * 128 : (j + 1) * 128]
        )
        for k in range(2):
            l = 2 * j + k
            expanded = dot_wide(
                pair[:, k * RANK : (k + 1) * RANK], basis[:, l * LEAF : (l + 1) * LEAF]
            )
            for h in range(2):
                place = (2 * l + h) * LANES
                near = total((2 * l + h) * SAMPLES, SAMPLES)
                made = near + expanded[:, h * LANES : (h + 1) * LANES]
                out[:, place : place + LANES] = made.astype(BF16)


def exchange(x, axis, offset):
    size = lax.axis_size(axis)
    return lax.ppermute(x, axis, [(i, i ^ offset) for i in range(size)])


def stages_of(n_row, n_y):
    stages = [[], [], []]
    for j in range(n_row):
        z, y = j // n_y, j % n_y
        if j in (0, 1) or (z == 1 and y == 0):
            stages[0].append(j)
        elif y == 0 or (z == 1 and y == 1):
            stages[1].append(j)
        else:
            stages[2].append(j)
    return stages


def local(
    probes, points, skeleton, leaf_basis, transfer, near_list, near_count, far_list, far_count
):
    n_row = lax.axis_size("row")
    n_col = lax.axis_size("col")
    n_y = n_row // min(n_row, 4)
    probes, basis, moves = probes.T, leaf_basis.T, transfer.T
    packed, coords = pl.pallas_call(
        pack_kernel,
        out_shape=[
            jax.ShapeDtypeStruct((PACKED_ROWS, LANES), BF16),
            jax.ShapeDtypeStruct((COORD_ROWS, LANES), BF16),
        ],
        in_specs=[VMEM] * 5,
        out_specs=[VMEM] * 2,
        name="pack",
    )(probes, basis, moves, points, skeleton)

    blocks = [packed] + [None] * (n_row - 1)
    for y in range(1, n_y):
        blocks[y] = exchange(packed, "row", y)
    for z in range(n_y, n_row, n_y):
        blocks[z] = exchange(packed, "row", z)
    row_coords = [coords] + [exchange(coords, "col", k) for k in range(1, n_col)]
    for z in range(n_y, n_row, n_y):
        for y in range(1, n_y):
            blocks[z + y] = exchange(blocks[z], "row", y)

    plan = Plan(near_list.shape[-1], far_list.shape[-1])
    stages = stages_of(n_row, n_y)
    table = np.zeros((n_row,), np.int32)
    for s, members in enumerate(stages):
        for i, j in enumerate(members):
            table[j] = s * 256 + i
    near_rows, far_rows = 4 * n_col + 1, CLUSTERS * n_col + 1
    lists, *row_features = pl.pallas_call(
        functools.partial(plan_kernel, n_row, n_col, plan),
        out_shape=[
            jax.ShapeDtypeStruct((plan.size,), jnp.int32),
            jax.ShapeDtypeStruct((near_rows, FEATURES, LEAF), BF16),
            jax.ShapeDtypeStruct((far_rows, FEATURES, LANES), BF16),
            jax.ShapeDtypeStruct((far_rows, FEATURES, LANES), BF16),
        ],
        in_specs=[SMEM] * 5 + [VMEM] * n_col,
        out_specs=[SMEM] + [VMEM] * 3,
        name="plan",
    )(near_list[0, 0], near_count, far_list[0, 0], far_count, jnp.asarray(table), *row_coords)

    sums = [
        jax.ShapeDtypeStruct((near_rows, SAMPLES, LEAF), F32),
        jax.ShapeDtypeStruct((far_rows, SAMPLES, LANES), F32),
        jax.ShapeDtypeStruct((far_rows, SAMPLES, LANES), F32),
    ]
    totals = []
    for s, members in enumerate(stages):
        n = len(members)
        last = s == STAGES - 1
        n_in = 4 + n
        n_out = n_col if last else 0
        totals = pl.pallas_call(
            functools.partial(stage_kernel, n_col, n, plan, s),
            out_shape=sums + [jax.ShapeDtypeStruct((COORD_ROW, LANES), BF16)] * n_out,
            in_specs=[SMEM] + [VMEM] * (n_in - 1 + len(totals)),
            out_specs=[VMEM] * (3 + n_out),
            scratch_shapes=[
                pltpu.VMEM((4 * n, SAMPLES, LEAF), BF16),
                pltpu.VMEM((4 * n, LEAF, FEATURES), BF16),
                pltpu.VMEM((CLUSTERS * n, SAMPLES, RANK), BF16),
                pltpu.VMEM((CLUSTERS * n, RANK, FEATURES), BF16),
            ],
            input_output_aliases={n_in + k: k for k in range(len(totals))},
            compiler_params=pltpu.CompilerParams(vmem_limit_bytes=40 << 20),
            cost_estimate=pl.CostEstimate(
                flops=1 << 30, bytes_accessed=1 << 22, transcendentals=1 << 21
            ),
            name=f"stage{s}",
        )(lists, *row_features, *[blocks[j] for j in members], *totals)

    parts = totals[3:]
    arrived = [parts[0]] + [exchange(parts[k], "col", k) for k in range(1, n_col)]
    sample = pl.pallas_call(
        functools.partial(final_kernel, n_col),
        out_shape=jax.ShapeDtypeStruct((SAMPLES, OWN), BF16),
        in_specs=[VMEM] * (2 + n_col),
        out_specs=VMEM,
        name="final",
    )(basis, moves, *arrived)
    return sample.T


def solution(mesh):
    placed = (
        P(("row", "col"), None),
        P(None, ("row", "col")),
        P(None, ("row", "col")),
        P(("row", "col"), None),
        P(("row", "col"), None),
        P("row", "col", None, None),
        P("row", "col"),
        P("row", "col", None, None),
        P("row", "col"),
    )
    return jax.shard_map(
        local, mesh=mesh, in_specs=placed, out_specs=P(("row", "col"), None), check_vma=False
    )
```

```python
import functools
import math

import jax
import jax.numpy as jnp
import numpy as np
from jax import lax
from jax.experimental import pallas as pl
from jax.experimental.pallas import tpu as pltpu
from jax.sharding import PartitionSpec as P

LEAF = 256
RANK = 64
SAMPLES = 64
OWN = 4 * LEAF
CLUSTERS = 7
LANES = 128
F32 = jnp.float32
BF16 = jnp.bfloat16
FAR_ROW = OWN // LANES * SAMPLES
COORD_ROW = FAR_ROW + CLUSTERS * SAMPLES // 2
COORD_ROWS = 96
PACKED_ROWS = COORD_ROW + COORD_ROWS
FEATURES = 16
STAGES = 3
NEAR_UNROLL = 4
FAR_UNROLL = 8
RATE = math.sqrt(3.0) / 0.15

VMEM = pl.BlockSpec(memory_space=pltpu.VMEM)
SMEM = pl.BlockSpec(memory_space=pltpu.SMEM)
NN = (((1,), (0,)), ((), ()))
NT = (((1,), (1,)), ((), ()))


def dot(a, b, dims=NN):
    return lax.dot_general(a, b, dims, preferred_element_type=F32)


def dot_wide(a, b):
    high = a.astype(BF16)
    low = (a - high.astype(F32)).astype(BF16)
    return dot(high, b) + dot(low, b)


def lanes(a, b):
    return jnp.concatenate([a, b], axis=1)


def rows(*parts):
    return jnp.concatenate(parts, axis=0)


def features(points):
    norm = points * points
    norm = norm[0:1] + norm[1:2] + norm[2:3]
    high = norm.astype(BF16).astype(F32)
    rest = norm - high
    middle = rest.astype(BF16).astype(F32)
    ones = jnp.ones_like(norm)
    return rows(points, high, middle, rest - middle, ones, ones)


def row_side(made):
    ones = made[6:7]
    return rows(-2.0 * made[0:3], ones, ones, ones, made[3:4], made[4:5])


def matern_of(square):
    square = jnp.maximum(square, 1e-14)
    dist = square * lax.rsqrt(square)
    e = jnp.exp2(dist * (-RATE / math.log(2.0)))
    return ((1.0 + RATE * dist) * e).astype(BF16)


def pack_kernel(probes, basis, moves, points, skeleton, packed, coords):
    leaves = []
    for l in range(4):
        part = slice(l * LEAF, (l + 1) * LEAF)
        leaves.append(dot(basis[:, part], probes[:, part], NT).astype(BF16))
    middle = [
        dot(moves[:, j * 128 : (j + 1) * 128], rows(*leaves[2 * j : 2 * j + 2])).astype(BF16)
        for j in range(2)
    ]
    top = dot(moves[:, 256:384], rows(*middle)).astype(BF16)
    for j in range(8):
        packed[j * SAMPLES : (j + 1) * SAMPLES] = probes[:, j * LANES : (j + 1) * LANES]
    packed[FAR_ROW : FAR_ROW + 64] = lanes(leaves[0], leaves[1])
    packed[FAR_ROW + 64 : FAR_ROW + 128] = lanes(leaves[2], leaves[3])
    packed[FAR_ROW + 128 : FAR_ROW + 192] = lanes(middle[0], middle[1])
    packed[FAR_ROW + 192 : FAR_ROW + 224] = lanes(top[:32], top[32:])
    near = features(points[...].astype(F32))
    far = features(lanes(skeleton[...].astype(F32), jnp.zeros((3, 64), F32)))
    chunks = [near[:, j * LANES : (j + 1) * LANES] for j in range(8)]
    chunks += [far[:, j * LANES : (j + 1) * LANES] for j in range(4)]
    made = rows(*chunks).astype(BF16)
    packed[COORD_ROW:] = made
    coords[...] = made


class Plan:
    def __init__(self, near_most, far_most):
        self.near = near_most + NEAR_UNROLL
        self.far = far_most + FAR_UNROLL
        self.stage = 2 * (self.near + self.far)
        self.counts = STAGES * self.stage
        self.size = self.counts + 2 * STAGES


def plan_kernel(n_row, n_col, plan, near_list, near_count, far_list, far_count, table, out):
    my_row = lax.axis_index("row")
    my_col = lax.axis_index("col")
    for k in range(2 * STAGES):
        out[plan.counts + k] = 0

    def add(kind, capacity, first, device, row, column):
        info = table[device]
        stage = lax.shift_right_logical(info, 8)
        counter = plan.counts + 2 * stage + kind
        place = stage * plan.stage + first + out[counter]
        out[place] = row
        out[place + capacity] = (info & 255) * (4, CLUSTERS)[kind] + column
        out[counter] = out[counter] + 1

    def near_step(i, _):
        a, b = near_list[0, i], near_list[1, i]
        row = (lax.shift_right_logical(a, 2) ^ my_col) * 4 + (a & 3)
        add(0, plan.near, 0, lax.shift_right_logical(b, 2) ^ my_row, row, b & 3)
        return 0

    lax.fori_loop(0, near_count[0, 0], near_step, 0)

    def far_step(i, _):
        a, b = far_list[0, i], far_list[1, i]
        a_device = lax.shift_right_logical(a * 9363, 16)
        b_device = lax.shift_right_logical(b * 9363, 16)
        row = (a_device ^ my_col) * CLUSTERS + (a - a_device * CLUSTERS)
        add(1, plan.far, 2 * plan.near, b_device ^ my_row, row, b - b_device * CLUSTERS)
        return 0

    lax.fori_loop(0, far_count[0, 0], far_step, 0)
    for stage in range(STAGES):
        for kind, capacity, first, dummy, unroll in (
            (0, plan.near, 0, 4 * n_col, NEAR_UNROLL),
            (1, plan.far, 2 * plan.near, CLUSTERS * n_col, FAR_UNROLL),
        ):
            place = stage * plan.stage + first + out[plan.counts + 2 * stage + kind]
            for u in range(unroll - 1):
                out[place + u] = dummy
                out[place + capacity + u] = 0


def row_kernel(n_col, coords, near_row, far_row):
    me = lax.axis_index("col")
    empty = jnp.zeros((8, LANES), F32)
    for i in range(n_col):
        first = pl.multiple_of((me ^ i) * COORD_ROWS, 16)
        slabs = [coords[pl.ds(first + 16 * s, 16)].astype(F32) for s in range(6)]
        for l in range(4):
            even, odd = row_side(slabs[l][:8]), row_side(slabs[l][8:])
            near_row[4 * i + l, 0, :LANES] = rows(even, empty).T.astype(BF16)
            near_row[4 * i + l, 0, LANES:] = rows(odd, empty).T.astype(BF16)
            near_row[4 * i + l, 1, :LANES] = rows(empty, even).T.astype(BF16)
            near_row[4 * i + l, 1, LANES:] = rows(empty, odd).T.astype(BF16)
        for c in range(4):
            slab = slabs[4 + c // 2]
            made = row_side(slab[8 * (c % 2) : 8 * (c % 2) + 8])
            tall = rows(made, empty).T.astype(BF16)
            far_row[CLUSTERS * i + 2 * c] = tall[:64]
            if c < 3:
                far_row[CLUSTERS * i + 2 * c + 1] = tall[64:]
    near_row[4 * n_col] = jnp.zeros(near_row.shape[1:], BF16)
    far_row[CLUSTERS * n_col] = jnp.zeros(far_row.shape[1:], BF16)


def stage_kernel(n_col, n_blocks, plan, stage, lists, near_row, far_row, *refs):
    blocks, refs = refs[:n_blocks], refs[n_blocks:]
    if stage > 0:
        refs = refs[3:]
    last = stage == STAGES - 1
    totals, refs = refs[:3], refs[3:]
    if last:
        outs, refs = refs[:n_col], refs[n_col:]
    probes, near_col, coeff_low, coeff_high, far_low, far_high = refs
    near_total, far_even, far_odd = totals
    if stage == 0:
        for total in totals:
            total[...] = jnp.zeros_like(total)

    for i, block in enumerate(blocks):
        for l in range(4):
            for h in range(2):
                j = 2 * l + h
                half = slice(h * LANES, (h + 1) * LANES)
                probes[4 * i + l, :, half] = block[j * SAMPLES : (j + 1) * SAMPLES]
            near_col[4 * i + l] = block[COORD_ROW + 16 * l : COORD_ROW + 16 * (l + 1)]
        slabs = [block[COORD_ROW + 64 + 16 * p : COORD_ROW + 80 + 16 * p] for p in range(2)]
        for k in range(CLUSTERS):
            c, half = k // 2, slice(k % 2 * 64, k % 2 * 64 + 64)
            if k < 6:
                own = block[FAR_ROW + 64 * c : FAR_ROW + 64 * (c + 1)][:, half]
            else:
                own = block[FAR_ROW + 192 : FAR_ROW + 224]
                own = rows(own[:, :64], own[:, 64:])
            empty = jnp.zeros_like(own)
            coeff_low[CLUSTERS * i + k] = lanes(own, empty)
            coeff_high[CLUSTERS * i + k] = lanes(empty, own)
            made = slabs[c // 2].astype(F32)[8 * (c % 2) : 8 * (c % 2) + 8, half]
            empty = jnp.zeros_like(made)
            blank = jnp.zeros((8, LANES), F32)
            far_low[CLUSTERS * i + k] = rows(lanes(made, empty), blank).astype(BF16)
            far_high[CLUSTERS * i + k] = rows(lanes(empty, made), blank).astype(BF16)

    def near_step(g, _):
        place = stage * plan.stage + g * NEAR_UNROLL
        terms = []
        for u in range(NEAR_UNROLL):
            a, b = lists[place + u], lists[place + plan.near + u]
            parts = []
            for q in range(2):
                part = slice(q * LANES, (q + 1) * LANES)
                halves = [matern_of(dot(near_row[a, h, part], near_col[b])) for h in range(2)]
                parts.append(dot(probes[b], lanes(*halves), NT))
            terms.append((a, parts))
        for a, parts in terms:
            for q in range(2):
                near_total[a, :, q * LANES : (q + 1) * LANES] += parts[q]
        return 0

    count = lists[plan.counts + 2 * stage]
    lax.fori_loop(0, (count + NEAR_UNROLL - 1) // NEAR_UNROLL, near_step, 0)

    def far_step(g, _):
        place = stage * plan.stage + 2 * plan.near + g * FAR_UNROLL
        terms = []
        for u in range(0, FAR_UNROLL, 2):
            a0, a1 = lists[place + u], lists[place + u + 1]
            b0, b1 = lists[place + plan.far + u], lists[place + plan.far + u + 1]
            square = dot(far_row[a0], far_low[b0]) + dot(far_row[a1], far_high[b1])
            both = rows(coeff_low[b0], coeff_high[b1])
            terms.append((a0, a1, dot(matern_of(square), both)))
        for a0, a1, term in terms:
            far_even[a0] += term
            far_odd[a1] += term
        return 0

    count = lists[plan.counts + 2 * stage + 1]
    lax.fori_loop(0, (count + FAR_UNROLL - 1) // FAR_UNROLL, far_step, 0)

    if last:
        for i in range(n_col):
            for j in range(8):
                half = slice(j % 2 * LANES, (j % 2 + 1) * LANES)
                part = near_total[4 * i + j // 2, :, half]
                outs[i][j * SAMPLES : (j + 1) * SAMPLES] = part.astype(BF16)
            parts = []
            for l in range(CLUSTERS):
                even, odd = far_even[CLUSTERS * i + l], far_odd[CLUSTERS * i + l]
                parts.append(even[:, :64] + odd[:, 64:])
            for j in range(3):
                pair = lanes(*parts[2 * j : 2 * j + 2])
                outs[i][FAR_ROW + 64 * j : FAR_ROW + 64 * (j + 1)] = pair.astype(BF16)
            pair = lanes(parts[6][:32], parts[6][32:])
            outs[i][FAR_ROW + 192 : FAR_ROW + 224] = pair.astype(BF16)


def final_kernel(n_col, basis, moves, *refs):
    parts, out = refs[:n_col], refs[n_col]

    def total(first, count):
        return sum(part[first : first + count].astype(F32) for part in parts)

    def turned(first):
        tall = total(first, 64).T
        return lanes(tall[:64], tall[64:])

    top = total(FAR_ROW + 192, 32)
    top = rows(top[:, :64], top[:, 64:]).T
    middle = turned(FAR_ROW + 128) + dot_wide(top, moves[:, 256:384])
    for j in range(2):
        pair = turned(FAR_ROW + 64 * j) + dot_wide(
            middle[:, j * RANK : (j + 1) * RANK], moves[:, j * 128 : (j + 1) * 128]
        )
        for k in range(2):
            l = 2 * j + k
            expanded = dot_wide(
                pair[:, k * RANK : (k + 1) * RANK], basis[:, l * LEAF : (l + 1) * LEAF]
            )
            for h in range(2):
                place = (2 * l + h) * LANES
                near = total((2 * l + h) * SAMPLES, SAMPLES)
                made = near + expanded[:, h * LANES : (h + 1) * LANES]
                out[:, place : place + LANES] = made.astype(BF16)


def exchange(x, axis, offset):
    size = lax.axis_size(axis)
    return lax.ppermute(x, axis, [(i, i ^ offset) for i in range(size)])


def stages_of(n_row, n_y):
    stages = [[], [], []]
    for j in range(n_row):
        z, y = j // n_y, j % n_y
        if j in (0, 1) or (z == 1 and y == 0):
            stages[0].append(j)
        elif y == 0 or (z == 1 and y == 1):
            stages[1].append(j)
        else:
            stages[2].append(j)
    return stages


def local(
    probes, points, skeleton, leaf_basis, transfer, near_list, near_count, far_list, far_count
):
    n_row = lax.axis_size("row")
    n_col = lax.axis_size("col")
    n_y = n_row // min(n_row, 4)
    probes, basis, moves = probes.T, leaf_basis.T, transfer.T
    packed, coords = pl.pallas_call(
        pack_kernel,
        out_shape=[
            jax.ShapeDtypeStruct((PACKED_ROWS, LANES), BF16),
            jax.ShapeDtypeStruct((COORD_ROWS, LANES), BF16),
        ],
        in_specs=[VMEM] * 5,
        out_specs=[VMEM] * 2,
        name="pack",
    )(probes, basis, moves, points, skeleton)

    blocks = [packed] + [None] * (n_row - 1)
    for y in range(1, n_y):
        blocks[y] = exchange(packed, "row", y)
    for z in range(n_y, n_row, n_y):
        blocks[z] = exchange(packed, "row", z)
    row_coords = lax.all_gather(coords, "col", axis=0, tiled=True)
    for z in range(n_y, n_row, n_y):
        for y in range(1, n_y):
            blocks[z + y] = exchange(blocks[z], "row", y)

    plan = Plan(near_list.shape[-1], far_list.shape[-1])
    stages = stages_of(n_row, n_y)
    table = np.zeros((n_row,), np.int32)
    for s, members in enumerate(stages):
        for i, j in enumerate(members):
            table[j] = s * 256 + i
    near_rows, far_rows = 4 * n_col + 1, CLUSTERS * n_col + 1
    lists = pl.pallas_call(
        functools.partial(plan_kernel, n_row, n_col, plan),
        out_shape=jax.ShapeDtypeStruct((plan.size,), jnp.int32),
        in_specs=[SMEM] * 5,
        out_specs=SMEM,
        compiler_params=pltpu.CompilerParams(vmem_limit_bytes=8 << 20),
        cost_estimate=pl.CostEstimate(flops=1 << 28, bytes_accessed=1 << 20, transcendentals=0),
        name="plan",
    )(near_list[0, 0], near_count, far_list[0, 0], far_count, jnp.asarray(table))
    row_features = pl.pallas_call(
        functools.partial(row_kernel, n_col),
        out_shape=[
            jax.ShapeDtypeStruct((near_rows, 2, LEAF, FEATURES), BF16),
            jax.ShapeDtypeStruct((far_rows, RANK, FEATURES), BF16),
        ],
        in_specs=[VMEM],
        out_specs=[VMEM] * 2,
        compiler_params=pltpu.CompilerParams(vmem_limit_bytes=16 << 20),
        name="row_side",
    )(row_coords)

    sums = [
        jax.ShapeDtypeStruct((near_rows, SAMPLES, LEAF), F32),
        jax.ShapeDtypeStruct((far_rows, RANK, LANES), F32),
        jax.ShapeDtypeStruct((far_rows, RANK, LANES), F32),
    ]
    totals = []
    for s, members in enumerate(stages):
        n = len(members)
        last = s == STAGES - 1
        n_in = 3 + n
        n_out = n_col if last else 0
        totals = pl.pallas_call(
            functools.partial(stage_kernel, n_col, n, plan, s),
            out_shape=sums + [jax.ShapeDtypeStruct((COORD_ROW, LANES), BF16)] * n_out,
            in_specs=[SMEM] + [VMEM] * (n_in - 1 + len(totals)),
            out_specs=[VMEM] * (3 + n_out),
            scratch_shapes=[
                pltpu.VMEM((4 * n, SAMPLES, LEAF), BF16),
                pltpu.VMEM((4 * n, FEATURES, LANES), BF16),
                pltpu.VMEM((CLUSTERS * n, RANK, LANES), BF16),
                pltpu.VMEM((CLUSTERS * n, RANK, LANES), BF16),
                pltpu.VMEM((CLUSTERS * n, FEATURES, LANES), BF16),
                pltpu.VMEM((CLUSTERS * n, FEATURES, LANES), BF16),
            ],
            input_output_aliases={n_in + k: k for k in range(len(totals))},
            compiler_params=pltpu.CompilerParams(vmem_limit_bytes=40 << 20),
            cost_estimate=pl.CostEstimate(
                flops=1 << 30, bytes_accessed=1 << 22, transcendentals=1 << 21
            ),
            name=f"stage{s}",
        )(lists, *row_features, *[blocks[j] for j in members], *totals)

    parts = totals[3:]
    arrived = [parts[0]] + [exchange(parts[k], "col", k) for k in range(1, n_col)]
    sample = pl.pallas_call(
        functools.partial(final_kernel, n_col),
        out_shape=jax.ShapeDtypeStruct((SAMPLES, OWN), BF16),
        in_specs=[VMEM] * (2 + n_col),
        out_specs=VMEM,
        compiler_params=pltpu.CompilerParams(vmem_limit_bytes=16 << 20),
        name="final",
    )(basis, moves, *arrived)
    return sample.T


def solution(mesh):
    placed = (
        P(("row", "col"), None),
        P(None, ("row", "col")),
        P(None, ("row", "col")),
        P(("row", "col"), None),
        P(("row", "col"), None),
        P("row", "col", None, None),
        P("row", "col"),
        P("row", "col", None, None),
        P("row", "col"),
    )
    return jax.shard_map(
        local, mesh=mesh, in_specs=placed, out_specs=P(("row", "col"), None), check_vma=False
    )
```

```python
import functools
import math

import jax
import jax.numpy as jnp
import numpy as np
from jax import lax
from jax.experimental import pallas as pl
from jax.experimental.pallas import tpu as pltpu
from jax.sharding import PartitionSpec as P

LEAF = 256
RANK = 64
SAMPLES = 64
OWN = 4 * LEAF
CLUSTERS = 7
LANES = 128
F32 = jnp.float32
BF16 = jnp.bfloat16
FAR_ROW = OWN // LANES * SAMPLES
COORD_ROW = FAR_ROW + CLUSTERS * SAMPLES // 2
COORD_ROWS = 96
PACKED_ROWS = COORD_ROW + COORD_ROWS
FEATURES = 16
CLASSES = 3
NEAR_UNROLL = 4
FAR_UNROLL = 16
RATE = math.sqrt(3.0) / 0.15

VMEM = pl.BlockSpec(memory_space=pltpu.VMEM)
SMEM = pl.BlockSpec(memory_space=pltpu.SMEM)
NN = (((1,), (0,)), ((), ()))
NT = (((1,), (1,)), ((), ()))


def dot(a, b, dims=NN):
    return lax.dot_general(a, b, dims, preferred_element_type=F32)


def dot_wide(a, b):
    high = a.astype(BF16)
    low = (a - high.astype(F32)).astype(BF16)
    return dot(high, b) + dot(low, b)


def lanes(a, b):
    return jnp.concatenate([a, b], axis=1)


def rows(*parts):
    return jnp.concatenate(parts, axis=0)


def features(points):
    norm = points * points
    norm = norm[0:1] + norm[1:2] + norm[2:3]
    high = norm.astype(BF16).astype(F32)
    rest = norm - high
    middle = rest.astype(BF16).astype(F32)
    ones = jnp.ones_like(norm)
    return rows(points, high, middle, rest - middle, ones, ones)


def row_side(made):
    ones = made[6:7]
    return rows(-2.0 * made[0:3], ones, ones, ones, made[3:4], made[4:5])


def matern_of(square):
    square = jnp.maximum(square, 1e-14)
    dist = square * lax.rsqrt(square)
    e = jnp.exp2(dist * (-RATE / math.log(2.0)))
    return ((1.0 + RATE * dist) * e).astype(BF16)


def pack_kernel(probes, basis, moves, points, skeleton, packed, coords):
    leaves = []
    for l in range(4):
        part = slice(l * LEAF, (l + 1) * LEAF)
        leaves.append(dot(basis[:, part], probes[:, part], NT).astype(BF16))
    middle = [
        dot(moves[:, j * 128 : (j + 1) * 128], rows(*leaves[2 * j : 2 * j + 2])).astype(BF16)
        for j in range(2)
    ]
    top = dot(moves[:, 256:384], rows(*middle)).astype(BF16)
    for j in range(8):
        packed[j * SAMPLES : (j + 1) * SAMPLES] = probes[:, j * LANES : (j + 1) * LANES]
    packed[FAR_ROW : FAR_ROW + 64] = lanes(leaves[0], leaves[1])
    packed[FAR_ROW + 64 : FAR_ROW + 128] = lanes(leaves[2], leaves[3])
    packed[FAR_ROW + 128 : FAR_ROW + 192] = lanes(middle[0], middle[1])
    packed[FAR_ROW + 192 : FAR_ROW + 224] = lanes(top[:32], top[32:])
    near = features(points[...].astype(F32))
    far = features(lanes(skeleton[...].astype(F32), jnp.zeros((3, 64), F32)))
    chunks = [near[:, j * LANES : (j + 1) * LANES] for j in range(8)]
    chunks += [far[:, j * LANES : (j + 1) * LANES] for j in range(4)]
    made = rows(*chunks).astype(BF16)
    packed[COORD_ROW:] = made
    coords[...] = made


class Plan:
    def __init__(self, near_most, far_most):
        self.near = near_most + NEAR_UNROLL
        self.far = far_most + FAR_UNROLL
        self.stride = 2 * (self.near + self.far)
        self.counts = CLASSES * self.stride
        self.size = self.counts + 2 * CLASSES


def plan_kernel(n_col, late_mask, plan, near_list, near_count, far_list, far_count, out):
    my_row = lax.axis_index("row")
    my_col = lax.axis_index("col")
    for k in range(2 * CLASSES):
        out[plan.counts + k] = 0

    def add(kind, capacity, first, row_device, row, col_device, column):
        per_device = (4, CLUSTERS)[kind]
        target = row_device ^ my_col
        source = col_device ^ my_row
        remote = target >= 2
        group = jnp.where(remote, lax.shift_right_logical(late_mask, source) & 1, 2)
        counter = plan.counts + 2 * group + kind
        place = group * plan.stride + first + out[counter]
        out[place] = (target - jnp.where(remote, 2, 0)) * per_device + row
        out[place + capacity] = source * per_device + column
        out[counter] = out[counter] + 1

    def near_step(i, _):
        a, b = near_list[0, i], near_list[1, i]
        a_device, b_device = lax.shift_right_logical(a, 2), lax.shift_right_logical(b, 2)
        add(0, plan.near, 0, a_device, a & 3, b_device, b & 3)
        return 0

    lax.fori_loop(0, near_count[0, 0], near_step, 0)

    def far_step(i, _):
        a, b = far_list[0, i], far_list[1, i]
        a_device = lax.shift_right_logical(a * 9363, 16)
        b_device = lax.shift_right_logical(b * 9363, 16)
        row, column = a - a_device * CLUSTERS, b - b_device * CLUSTERS
        add(1, plan.far, 2 * plan.near, a_device, row, b_device, column)
        return 0

    lax.fori_loop(0, far_count[0, 0], far_step, 0)
    for group in range(CLASSES):
        targets = 2 if group == 2 else n_col - 2
        for kind, capacity, first, dummy, unroll in (
            (0, plan.near, 0, 4 * targets, NEAR_UNROLL),
            (1, plan.far, 2 * plan.near, CLUSTERS * targets, FAR_UNROLL),
        ):
            place = group * plan.stride + first + out[plan.counts + 2 * group + kind]
            for u in range(unroll - 1):
                out[place + u] = dummy
                out[place + capacity + u] = 0


def row_kernel(n_col, coords, near_row, far_row):
    me = lax.axis_index("col")
    empty = jnp.zeros((8, LANES), F32)
    for i in range(n_col):
        first = pl.multiple_of((me ^ i) * COORD_ROWS, 16)
        slabs = [coords[pl.ds(first + 16 * s, 16)].astype(F32) for s in range(6)]
        near, far = (4 * i, CLUSTERS * i) if i < 2 else (4 * i + 1, CLUSTERS * i + 1)
        for l in range(4):
            for h in range(2):
                made = row_side(slabs[l][8 * h : 8 * h + 8])
                near_row[near + l, h * LANES : (h + 1) * LANES] = rows(made, empty).T.astype(BF16)
        for c in range(4):
            slab = slabs[4 + c // 2]
            made = row_side(slab[8 * (c % 2) : 8 * (c % 2) + 8])
            tall = rows(made, empty).T.astype(BF16)
            far_row[far + 2 * c] = tall[:64]
            if c < 3:
                far_row[far + 2 * c + 1] = tall[64:]
    for blank in (8, 4 * n_col + 1):
        near_row[blank] = jnp.zeros(near_row.shape[1:], BF16)
    for blank in (2 * CLUSTERS, CLUSTERS * n_col + 1):
        far_row[blank] = jnp.zeros(far_row.shape[1:], BF16)


def prepare(i, block, probes, near_col, coeff_low, coeff_high, far_low, far_high):
    for l in range(4):
        for h in range(2):
            j = 2 * l + h
            half = slice(h * LANES, (h + 1) * LANES)
            probes[4 * i + l, :, half] = block[j * SAMPLES : (j + 1) * SAMPLES]
        slab = block[COORD_ROW + 16 * l : COORD_ROW + 16 * (l + 1)]
        near_col[4 * i + l, :, :LANES] = slab
        near_col[4 * i + l, :, LANES:] = rows(slab[8:], slab[:8])
    slabs = [block[COORD_ROW + 64 + 16 * p : COORD_ROW + 80 + 16 * p] for p in range(2)]
    for k in range(CLUSTERS):
        c, half = k // 2, slice(k % 2 * 64, k % 2 * 64 + 64)
        if k < 6:
            own = block[FAR_ROW + 64 * c : FAR_ROW + 64 * (c + 1)][:, half]
        else:
            own = block[FAR_ROW + 192 : FAR_ROW + 224]
            own = rows(own[:, :64], own[:, 64:])
        empty = jnp.zeros_like(own)
        coeff_low[CLUSTERS * i + k] = lanes(own, empty)
        coeff_high[CLUSTERS * i + k] = lanes(empty, own)
        made = slabs[c // 2].astype(F32)[8 * (c % 2) : 8 * (c % 2) + 8, half]
        empty = jnp.zeros_like(made)
        blank = jnp.zeros((8, LANES), F32)
        far_low[CLUSTERS * i + k] = rows(lanes(made, empty), blank).astype(BF16)
        far_high[CLUSTERS * i + k] = rows(lanes(empty, made), blank).astype(BF16)


def work(plan, group, lists, near_row, far_row, prepared, totals):
    probes, near_col, coeff_low, coeff_high, far_low, far_high = prepared
    near_total, far_even, far_odd = totals
    near_first, far_first = (0, 0) if group == 2 else (9, 2 * CLUSTERS + 1)

    def near_step(g, _):
        place = group * plan.stride + g * NEAR_UNROLL
        terms = []
        for u in range(NEAR_UNROLL):
            a, b = lists[place + u], lists[place + plan.near + u]
            parts = []
            for q in range(2):
                part = slice(q * LANES, (q + 1) * LANES)
                parts.append(matern_of(dot(near_row[near_first + a, part], near_col[b])))
            terms.append((a, dot(probes[b], rows(*parts), NT)))
        for a, term in terms:
            near_total[a] += term
        return 0

    count = lists[plan.counts + 2 * group]
    lax.fori_loop(0, (count + NEAR_UNROLL - 1) // NEAR_UNROLL, near_step, 0)

    def far_step(g, _):
        place = group * plan.stride + 2 * plan.near + g * FAR_UNROLL
        terms = []
        for u in range(0, FAR_UNROLL, 2):
            a0, a1 = lists[place + u], lists[place + u + 1]
            b0, b1 = lists[place + plan.far + u], lists[place + plan.far + u + 1]
            square = dot(far_row[far_first + a0], far_low[b0])
            square += dot(far_row[far_first + a1], far_high[b1])
            both = rows(coeff_low[b0], coeff_high[b1])
            terms.append((a0, a1, dot(matern_of(square), both)))
        for a0, a1, term in terms:
            far_even[a0] += term
            far_odd[a1] += term
        return 0

    count = lists[plan.counts + 2 * group + 1]
    lax.fori_loop(0, (count + FAR_UNROLL - 1) // FAR_UNROLL, far_step, 0)


def write_parts(outs, near_total, far_even, far_odd):
    for i, out in enumerate(outs):
        for j in range(8):
            half = slice(j % 2 * LANES, (j % 2 + 1) * LANES)
            part = near_total[4 * i + j // 2, :, half]
            out[j * SAMPLES : (j + 1) * SAMPLES] = part.astype(BF16)
        parts = []
        for l in range(CLUSTERS):
            even, odd = far_even[CLUSTERS * i + l], far_odd[CLUSTERS * i + l]
            parts.append(even[:, :64] + odd[:, 64:])
        for j in range(3):
            pair = lanes(*parts[2 * j : 2 * j + 2])
            out[FAR_ROW + 64 * j : FAR_ROW + 64 * (j + 1)] = pair.astype(BF16)
        pair = lanes(parts[6][:32], parts[6][32:])
        out[FAR_ROW + 192 : FAR_ROW + 224] = pair.astype(BF16)


def clear(totals):
    for total in totals:
        total[...] = jnp.zeros_like(total)


def early_kernel(plan, members, lists, near_row, far_row, *refs):
    blocks, refs = refs[: len(members)], refs[len(members) :]
    prepared, totals = refs[:6], refs[6:]
    clear(totals)
    for i, block in zip(members, blocks):
        prepare(i, block, *prepared)
    work(plan, 0, lists, near_row, far_row, prepared, totals)


def late_kernel(plan, members, lists, near_row, far_row, *refs):
    blocks, refs = refs[: len(members)], refs[len(members) + 9 :]
    prepared, totals, outs = refs[:6], refs[6:9], refs[9:]
    for i, block in zip(members, blocks):
        prepare(i, block, *prepared)
    work(plan, 1, lists, near_row, far_row, prepared, totals)
    write_parts(outs, *totals)


def here_kernel(plan, lists, near_row, far_row, *refs):
    prepared, outs, totals = refs[:6], refs[6:8], refs[8:]
    clear(totals)
    work(plan, 2, lists, near_row, far_row, prepared, totals)
    write_parts(outs, *totals)


def final_kernel(n_col, basis, moves, *refs):
    parts, out = refs[:n_col], refs[n_col]

    def total(first, count):
        return sum(part[first : first + count].astype(F32) for part in parts)

    def turned(first):
        tall = total(first, 64).T
        return lanes(tall[:64], tall[64:])

    top = total(FAR_ROW + 192, 32)
    top = rows(top[:, :64], top[:, 64:]).T
    middle = turned(FAR_ROW + 128) + dot_wide(top, moves[:, 256:384])
    for j in range(2):
        pair = turned(FAR_ROW + 64 * j) + dot_wide(
            middle[:, j * RANK : (j + 1) * RANK], moves[:, j * 128 : (j + 1) * 128]
        )
        for k in range(2):
            l = 2 * j + k
            expanded = dot_wide(
                pair[:, k * RANK : (k + 1) * RANK], basis[:, l * LEAF : (l + 1) * LEAF]
            )
            for h in range(2):
                place = (2 * l + h) * LANES
                near = total((2 * l + h) * SAMPLES, SAMPLES)
                made = near + expanded[:, h * LANES : (h + 1) * LANES]
                out[:, place : place + LANES] = made.astype(BF16)


def exchange(x, axis, offset):
    size = lax.axis_size(axis)
    return lax.ppermute(x, axis, [(i, i ^ offset) for i in range(size)])


def local(
    probes, points, skeleton, leaf_basis, transfer, near_list, near_count, far_list, far_count
):
    n_row = lax.axis_size("row")
    n_col = lax.axis_size("col")
    n_y = n_row // min(n_row, 4)
    probes, basis, moves = probes.T, leaf_basis.T, transfer.T
    packed, coords = pl.pallas_call(
        pack_kernel,
        out_shape=[
            jax.ShapeDtypeStruct((PACKED_ROWS, LANES), BF16),
            jax.ShapeDtypeStruct((COORD_ROWS, LANES), BF16),
        ],
        in_specs=[VMEM] * 5,
        out_specs=[VMEM] * 2,
        name="pack",
    )(probes, basis, moves, points, skeleton)

    blocks = [packed] + [None] * (n_row - 1)
    for y in range(1, n_y):
        blocks[y] = exchange(packed, "row", y)
    for z in range(n_y, n_row, n_y):
        blocks[z] = exchange(packed, "row", z)
    row_coords = lax.all_gather(coords, "col", axis=0, tiled=True)
    for z in range(n_y, n_row, n_y):
        for y in range(1, n_y):
            blocks[z + y] = exchange(blocks[z], "row", y)

    plan = Plan(near_list.shape[-1], far_list.shape[-1])
    early = [j for j in range(n_row) if j % n_y == 0 or j < n_y]
    late = [j for j in range(n_row) if j not in early]
    late_mask = sum(1 << j for j in late)
    lists = pl.pallas_call(
        functools.partial(plan_kernel, n_col, np.uint32(late_mask).astype(np.int32), plan),
        out_shape=jax.ShapeDtypeStruct((plan.size,), jnp.int32),
        in_specs=[SMEM] * 4,
        out_specs=SMEM,
        compiler_params=pltpu.CompilerParams(vmem_limit_bytes=8 << 20),
        cost_estimate=pl.CostEstimate(flops=1 << 32, bytes_accessed=1 << 12, transcendentals=0),
        name="plan",
    )(near_list[0, 0], near_count, far_list[0, 0], far_count)
    row_features = pl.pallas_call(
        functools.partial(row_kernel, n_col),
        out_shape=[
            jax.ShapeDtypeStruct((4 * n_col + 2, LEAF, FEATURES), BF16),
            jax.ShapeDtypeStruct((CLUSTERS * n_col + 2, RANK, FEATURES), BF16),
        ],
        in_specs=[VMEM],
        out_specs=[VMEM] * 2,
        compiler_params=pltpu.CompilerParams(vmem_limit_bytes=16 << 20),
        name="row_side",
    )(row_coords)

    def sums(targets):
        near = (4 * targets + 1, SAMPLES, LEAF)
        far = (CLUSTERS * targets + 1, RANK, LANES)
        return [near, far, far]

    part = jax.ShapeDtypeStruct((COORD_ROW, LANES), BF16)
    held = [
        jax.ShapeDtypeStruct(shape, BF16)
        for shape in [
            (4 * n_row, SAMPLES, LEAF),
            (4 * n_row, FEATURES, LEAF),
            (CLUSTERS * n_row, RANK, LANES),
            (CLUSTERS * n_row, RANK, LANES),
            (CLUSTERS * n_row, FEATURES, LANES),
            (CLUSTERS * n_row, FEATURES, LANES),
        ]
    ]
    held += [jax.ShapeDtypeStruct(shape, F32) for shape in sums(n_col - 2)]
    params = pltpu.CompilerParams(vmem_limit_bytes=32 << 20)
    cost = pl.CostEstimate(flops=1 << 33, bytes_accessed=1 << 20, transcendentals=0)
    handed = pl.pallas_call(
        functools.partial(early_kernel, plan, early),
        out_shape=held,
        in_specs=[SMEM] + [VMEM] * (2 + len(early)),
        out_specs=[VMEM] * len(held),
        compiler_params=params,
        cost_estimate=cost,
        name="far_targets_early",
    )(lists, *row_features, *[blocks[j] for j in early])
    first = 3 + len(late)
    handed = pl.pallas_call(
        functools.partial(late_kernel, plan, late),
        out_shape=held + [part] * (n_col - 2),
        in_specs=[SMEM] + [VMEM] * (first - 1 + len(held)),
        out_specs=[VMEM] * (len(held) + n_col - 2),
        input_output_aliases={first + k: k for k in range(len(held))},
        compiler_params=params,
        cost_estimate=cost,
        name="far_targets_late",
    )(lists, *row_features, *[blocks[j] for j in late], *handed)
    prepared, parts = handed[:6], handed[len(held) :]
    arrived = [exchange(parts[k - 2], "col", k) for k in range(2, n_col)]
    here = pl.pallas_call(
        functools.partial(here_kernel, plan),
        out_shape=[part] * 2,
        in_specs=[SMEM] + [VMEM] * (2 + len(prepared)),
        out_specs=[VMEM] * 2,
        scratch_shapes=[pltpu.VMEM(shape, F32) for shape in sums(2)],
        compiler_params=params,
        cost_estimate=cost,
        name="near_targets",
    )(lists, *row_features, *prepared)
    arrived += [here[0], exchange(here[1], "col", 1)]
    sample = pl.pallas_call(
        functools.partial(final_kernel, n_col),
        out_shape=jax.ShapeDtypeStruct((SAMPLES, OWN), BF16),
        in_specs=[VMEM] * (2 + n_col),
        out_specs=VMEM,
        compiler_params=pltpu.CompilerParams(vmem_limit_bytes=16 << 20),
        name="final",
    )(basis, moves, *arrived)
    return sample.T


def solution(mesh):
    placed = (
        P(("row", "col"), None),
        P(None, ("row", "col")),
        P(None, ("row", "col")),
        P(("row", "col"), None),
        P(("row", "col"), None),
        P("row", "col", None, None),
        P("row", "col"),
        P("row", "col", None, None),
        P("row", "col"),
    )
    return jax.shard_map(
        local, mesh=mesh, in_specs=placed, out_specs=P(("row", "col"), None), check_vma=False
    )
```

```python
import functools
import math

import jax
import jax.numpy as jnp
import numpy as np
from jax import lax
from jax.experimental import pallas as pl
from jax.experimental.pallas import tpu as pltpu
from jax.sharding import PartitionSpec as P

LEAF = 256
RANK = 64
SAMPLES = 64
OWN = 4 * LEAF
CLUSTERS = 7
LANES = 128
F32 = jnp.float32
BF16 = jnp.bfloat16
FAR_ROW = OWN // LANES * SAMPLES
COORD_ROW = FAR_ROW + CLUSTERS * SAMPLES // 2
COORD_ROWS = 96
PACKED_ROWS = COORD_ROW + COORD_ROWS
FEATURES = 16
CLASSES = 3
NEAR_UNROLL = 4
FAR_UNROLL = 16
RATE = math.sqrt(3.0) / 0.15

VMEM = pl.BlockSpec(memory_space=pltpu.VMEM)
SMEM = pl.BlockSpec(memory_space=pltpu.SMEM)
NN = (((1,), (0,)), ((), ()))
NT = (((1,), (1,)), ((), ()))


def dot(a, b, dims=NN):
    return lax.dot_general(a, b, dims, preferred_element_type=F32)


def dot_wide(a, b):
    high = a.astype(BF16)
    low = (a - high.astype(F32)).astype(BF16)
    return dot(high, b) + dot(low, b)


def lanes(a, b):
    return jnp.concatenate([a, b], axis=1)


def rows(*parts):
    return jnp.concatenate(parts, axis=0)


def features(points):
    norm = points * points
    norm = norm[0:1] + norm[1:2] + norm[2:3]
    high = norm.astype(BF16).astype(F32)
    rest = norm - high
    middle = rest.astype(BF16).astype(F32)
    ones = jnp.ones_like(norm)
    return rows(points, high, middle, rest - middle, ones, ones)


def row_side(made):
    ones = made[6:7]
    return rows(-2.0 * made[0:3], ones, ones, ones, made[3:4], made[4:5])


def matern_of(square):
    square = jnp.maximum(square, 1e-14)
    dist = square * lax.rsqrt(square)
    e = jnp.exp2(dist * (-RATE / math.log(2.0)))
    return ((1.0 + RATE * dist) * e).astype(BF16)


def pack_kernel(probes, basis, moves, points, skeleton, packed):
    leaves = []
    for l in range(4):
        part = slice(l * LEAF, (l + 1) * LEAF)
        leaves.append(dot(basis[:, part], probes[:, part], NT).astype(BF16))
    middle = [
        dot(moves[:, j * 128 : (j + 1) * 128], rows(*leaves[2 * j : 2 * j + 2])).astype(BF16)
        for j in range(2)
    ]
    top = dot(moves[:, 256:384], rows(*middle)).astype(BF16)
    for j in range(8):
        packed[j * SAMPLES : (j + 1) * SAMPLES] = probes[:, j * LANES : (j + 1) * LANES]
    packed[FAR_ROW : FAR_ROW + 64] = lanes(leaves[0], leaves[1])
    packed[FAR_ROW + 64 : FAR_ROW + 128] = lanes(leaves[2], leaves[3])
    packed[FAR_ROW + 128 : FAR_ROW + 192] = lanes(middle[0], middle[1])
    packed[FAR_ROW + 192 : FAR_ROW + 224] = lanes(top[:32], top[32:])
    near = features(points[...].astype(F32))
    far = features(lanes(skeleton[...].astype(F32), jnp.zeros((3, 64), F32)))
    chunks = [near[:, j * LANES : (j + 1) * LANES] for j in range(8)]
    chunks += [far[:, j * LANES : (j + 1) * LANES] for j in range(4)]
    packed[COORD_ROW:] = rows(*chunks).astype(BF16)


class Plan:
    def __init__(self, near_most, far_most):
        self.near = near_most + NEAR_UNROLL
        self.far = far_most + FAR_UNROLL
        self.stride = 2 * (self.near + self.far)
        self.counts = CLASSES * self.stride
        self.size = self.counts + 2 * CLASSES


def plan_kernel(n_col, late_mask, plan, *refs):
    sources, packed, out, again, coords = refs[:4], refs[4], refs[5], refs[6], refs[7]
    lists, sems = refs[8:12], refs[12]
    copies = [pltpu.make_async_copy(s, d, sems.at[k]) for k, (s, d) in enumerate(zip(sources, lists))]
    for copy in copies:
        copy.start()
    again[...] = packed[...]
    coords[...] = packed[COORD_ROW:]
    for copy in copies:
        copy.wait()
    near_list, near_count, far_list, far_count = lists
    my_row = lax.axis_index("row")
    my_col = lax.axis_index("col")
    for k in range(2 * CLASSES):
        out[plan.counts + k] = 0

    def add(kind, capacity, first, row_device, row, col_device, column):
        per_device = (4, CLUSTERS)[kind]
        target = row_device ^ my_col
        source = col_device ^ my_row
        remote = target >= 2
        group = jnp.where(remote, lax.shift_right_logical(late_mask, source) & 1, 2)
        counter = plan.counts + 2 * group + kind
        place = group * plan.stride + first + out[counter]
        out[place] = (target - jnp.where(remote, 2, 0)) * per_device + row
        out[place + capacity] = source * per_device + column
        out[counter] = out[counter] + 1

    def near_step(i, _):
        a, b = near_list[0, i], near_list[1, i]
        a_device, b_device = lax.shift_right_logical(a, 2), lax.shift_right_logical(b, 2)
        add(0, plan.near, 0, a_device, a & 3, b_device, b & 3)
        return 0

    lax.fori_loop(0, near_count[0, 0], near_step, 0)

    def far_step(i, _):
        a, b = far_list[0, i], far_list[1, i]
        a_device = lax.shift_right_logical(a * 9363, 16)
        b_device = lax.shift_right_logical(b * 9363, 16)
        row, column = a - a_device * CLUSTERS, b - b_device * CLUSTERS
        add(1, plan.far, 2 * plan.near, a_device, row, b_device, column)
        return 0

    lax.fori_loop(0, far_count[0, 0], far_step, 0)
    for group in range(CLASSES):
        targets = 2 if group == 2 else n_col - 2
        for kind, capacity, first, dummy, unroll in (
            (0, plan.near, 0, 4 * targets, NEAR_UNROLL),
            (1, plan.far, 2 * plan.near, CLUSTERS * targets, FAR_UNROLL),
        ):
            place = group * plan.stride + first + out[plan.counts + 2 * group + kind]
            for u in range(unroll - 1):
                out[place + u] = dummy
                out[place + capacity + u] = 0


def row_kernel(n_col, coords, near_row, far_row):
    me = lax.axis_index("col")
    empty = jnp.zeros((8, LANES), F32)
    for i in range(n_col):
        first = pl.multiple_of((me ^ i) * COORD_ROWS, 16)
        slabs = [coords[pl.ds(first + 16 * s, 16)].astype(F32) for s in range(6)]
        near, far = (4 * i, CLUSTERS * i) if i < 2 else (4 * i + 1, CLUSTERS * i + 1)
        for l in range(4):
            for h in range(2):
                made = row_side(slabs[l][8 * h : 8 * h + 8])
                near_row[near + l, h * LANES : (h + 1) * LANES] = rows(made, empty).T.astype(BF16)
        for c in range(4):
            slab = slabs[4 + c // 2]
            made = row_side(slab[8 * (c % 2) : 8 * (c % 2) + 8])
            tall = rows(made, empty).T.astype(BF16)
            far_row[far + 2 * c] = tall[:64]
            if c < 3:
                far_row[far + 2 * c + 1] = tall[64:]
    for blank in (8, 4 * n_col + 1):
        near_row[blank] = jnp.zeros(near_row.shape[1:], BF16)
    for blank in (2 * CLUSTERS, CLUSTERS * n_col + 1):
        far_row[blank] = jnp.zeros(far_row.shape[1:], BF16)


def prepare(i, block, probes, near_col, coeff_low, coeff_high, far_low, far_high):
    for l in range(4):
        for h in range(2):
            j = 2 * l + h
            half = slice(h * LANES, (h + 1) * LANES)
            probes[4 * i + l, :, half] = block[j * SAMPLES : (j + 1) * SAMPLES]
        slab = block[COORD_ROW + 16 * l : COORD_ROW + 16 * (l + 1)]
        near_col[4 * i + l, :, :LANES] = slab
        near_col[4 * i + l, :, LANES:] = rows(slab[8:], slab[:8])
    slabs = [block[COORD_ROW + 64 + 16 * p : COORD_ROW + 80 + 16 * p] for p in range(2)]
    for k in range(CLUSTERS):
        c, half = k // 2, slice(k % 2 * 64, k % 2 * 64 + 64)
        if k < 6:
            own = block[FAR_ROW + 64 * c : FAR_ROW + 64 * (c + 1)][:, half]
        else:
            own = block[FAR_ROW + 192 : FAR_ROW + 224]
            own = rows(own[:, :64], own[:, 64:])
        empty = jnp.zeros_like(own)
        coeff_low[CLUSTERS * i + k] = lanes(own, empty)
        coeff_high[CLUSTERS * i + k] = lanes(empty, own)
        made = slabs[c // 2].astype(F32)[8 * (c % 2) : 8 * (c % 2) + 8, half]
        empty = jnp.zeros_like(made)
        blank = jnp.zeros((8, LANES), F32)
        far_low[CLUSTERS * i + k] = rows(lanes(made, empty), blank).astype(BF16)
        far_high[CLUSTERS * i + k] = rows(lanes(empty, made), blank).astype(BF16)


def work(plan, group, lists, near_row, far_row, prepared, totals):
    probes, near_col, coeff_low, coeff_high, far_low, far_high = prepared
    near_total, far_even, far_odd = totals
    near_first, far_first = (0, 0) if group == 2 else (9, 2 * CLUSTERS + 1)

    def near_step(g, _):
        place = group * plan.stride + g * NEAR_UNROLL
        terms = []
        for u in range(NEAR_UNROLL):
            a, b = lists[place + u], lists[place + plan.near + u]
            parts = []
            for q in range(2):
                part = slice(q * LANES, (q + 1) * LANES)
                parts.append(matern_of(dot(near_row[near_first + a, part], near_col[b])))
            terms.append((a, dot(probes[b], rows(*parts), NT)))
        for a, term in terms:
            near_total[a] += term
        return 0

    count = lists[plan.counts + 2 * group]
    lax.fori_loop(0, (count + NEAR_UNROLL - 1) // NEAR_UNROLL, near_step, 0)

    def far_step(g, _):
        place = group * plan.stride + 2 * plan.near + g * FAR_UNROLL
        terms = []
        for u in range(0, FAR_UNROLL, 2):
            a0, a1 = lists[place + u], lists[place + u + 1]
            b0, b1 = lists[place + plan.far + u], lists[place + plan.far + u + 1]
            square = dot(far_row[far_first + a0], far_low[b0])
            square += dot(far_row[far_first + a1], far_high[b1])
            both = rows(coeff_low[b0], coeff_high[b1])
            terms.append((a0, a1, dot(matern_of(square), both)))
        for a0, a1, term in terms:
            far_even[a0] += term
            far_odd[a1] += term
        return 0

    count = lists[plan.counts + 2 * group + 1]
    lax.fori_loop(0, (count + FAR_UNROLL - 1) // FAR_UNROLL, far_step, 0)


def write_parts(outs, near_total, far_even, far_odd):
    for i, out in enumerate(outs):
        for j in range(8):
            half = slice(j % 2 * LANES, (j % 2 + 1) * LANES)
            part = near_total[4 * i + j // 2, :, half]
            out[j * SAMPLES : (j + 1) * SAMPLES] = part.astype(BF16)
        parts = []
        for l in range(CLUSTERS):
            even, odd = far_even[CLUSTERS * i + l], far_odd[CLUSTERS * i + l]
            parts.append(even[:, :64] + odd[:, 64:])
        for j in range(3):
            pair = lanes(*parts[2 * j : 2 * j + 2])
            out[FAR_ROW + 64 * j : FAR_ROW + 64 * (j + 1)] = pair.astype(BF16)
        pair = lanes(parts[6][:32], parts[6][32:])
        out[FAR_ROW + 192 : FAR_ROW + 224] = pair.astype(BF16)


def clear(totals):
    for total in totals:
        total[...] = jnp.zeros_like(total)


def early_kernel(plan, members, lists, near_row, far_row, *refs):
    blocks, refs = refs[: len(members)], refs[len(members) :]
    prepared, totals = refs[:6], refs[6:]
    clear(totals)
    for i, block in zip(members, blocks):
        prepare(i, block, *prepared)
    work(plan, 0, lists, near_row, far_row, prepared, totals)


def late_kernel(plan, members, lists, near_row, far_row, *refs):
    blocks, refs = refs[: len(members)], refs[len(members) + 9 :]
    prepared, totals, outs = refs[:6], refs[6:9], refs[9:]
    for i, block in zip(members, blocks):
        prepare(i, block, *prepared)
    work(plan, 1, lists, near_row, far_row, prepared, totals)
    write_parts(outs, *totals)


def here_kernel(plan, lists, near_row, far_row, *refs):
    prepared, outs, totals = refs[:6], refs[6:8], refs[8:]
    clear(totals)
    work(plan, 2, lists, near_row, far_row, prepared, totals)
    write_parts(outs, *totals)


def final_kernel(n_col, basis, moves, *refs):
    parts, out = refs[:n_col], refs[n_col]

    def total(first, count):
        return sum(part[first : first + count].astype(F32) for part in parts)

    def turned(first):
        tall = total(first, 64).T
        return lanes(tall[:64], tall[64:])

    top = total(FAR_ROW + 192, 32)
    top = rows(top[:, :64], top[:, 64:]).T
    middle = turned(FAR_ROW + 128) + dot_wide(top, moves[:, 256:384])
    for j in range(2):
        pair = turned(FAR_ROW + 64 * j) + dot_wide(
            middle[:, j * RANK : (j + 1) * RANK], moves[:, j * 128 : (j + 1) * 128]
        )
        for k in range(2):
            l = 2 * j + k
            expanded = dot_wide(
                pair[:, k * RANK : (k + 1) * RANK], basis[:, l * LEAF : (l + 1) * LEAF]
            )
            for h in range(2):
                place = (2 * l + h) * LANES
                near = total((2 * l + h) * SAMPLES, SAMPLES)
                made = near + expanded[:, h * LANES : (h + 1) * LANES]
                out[:, place : place + LANES] = made.astype(BF16)


def exchange(x, axis, offset):
    size = lax.axis_size(axis)
    return lax.ppermute(x, axis, [(i, i ^ offset) for i in range(size)])


def local(
    probes, points, skeleton, leaf_basis, transfer, near_list, near_count, far_list, far_count
):
    n_row = lax.axis_size("row")
    n_col = lax.axis_size("col")
    n_y = n_row // min(n_row, 4)
    probes, basis, moves = probes.T, leaf_basis.T, transfer.T
    packed = pl.pallas_call(
        pack_kernel,
        out_shape=jax.ShapeDtypeStruct((PACKED_ROWS, LANES), BF16),
        in_specs=[VMEM] * 5,
        out_specs=VMEM,
        name="pack",
    )(probes, basis, moves, points, skeleton)

    plan = Plan(near_list.shape[-1], far_list.shape[-1])
    early = [j for j in range(n_row) if j % n_y == 0 or j < n_y]
    late = [j for j in range(n_row) if j not in early]
    late_mask = sum(1 << j for j in late)
    sources = (near_list[0, 0], near_count, far_list[0, 0], far_count)
    lists, again, coords = pl.pallas_call(
        functools.partial(plan_kernel, n_col, np.uint32(late_mask).astype(np.int32), plan),
        out_shape=[
            jax.ShapeDtypeStruct((plan.size,), jnp.int32),
            jax.ShapeDtypeStruct((PACKED_ROWS, LANES), BF16),
            jax.ShapeDtypeStruct((COORD_ROWS, LANES), BF16),
        ],
        in_specs=[pl.BlockSpec(memory_space=pl.ANY)] * 4 + [VMEM],
        out_specs=[SMEM] + [VMEM] * 2,
        scratch_shapes=[pltpu.SMEM(source.shape, jnp.int32) for source in sources]
        + [pltpu.SemaphoreType.DMA((4,))],
        cost_estimate=pl.CostEstimate(flops=1 << 32, bytes_accessed=1 << 12, transcendentals=0),
        name="plan",
    )(*sources, packed)

    blocks = [packed] + [None] * (n_row - 1)
    for z in range(n_y, n_row, n_y):
        blocks[z] = exchange(packed if z < n_row - n_y else again, "row", z)
    for z in range(0, n_row, n_y):
        for y in range(1, n_y):
            blocks[z + y] = exchange(blocks[z], "row", y)
    row_coords = lax.all_gather(coords, "col", axis=0, tiled=True)

    row_features = pl.pallas_call(
        functools.partial(row_kernel, n_col),
        out_shape=[
            jax.ShapeDtypeStruct((4 * n_col + 2, LEAF, FEATURES), BF16),
            jax.ShapeDtypeStruct((CLUSTERS * n_col + 2, RANK, FEATURES), BF16),
        ],
        in_specs=[VMEM],
        out_specs=[VMEM] * 2,
        compiler_params=pltpu.CompilerParams(vmem_limit_bytes=16 << 20),
        name="row_side",
    )(row_coords)

    def sums(targets):
        near = (4 * targets + 1, SAMPLES, LEAF)
        far = (CLUSTERS * targets + 1, RANK, LANES)
        return [near, far, far]

    part = jax.ShapeDtypeStruct((COORD_ROW, LANES), BF16)
    held = [
        jax.ShapeDtypeStruct(shape, BF16)
        for shape in [
            (4 * n_row, SAMPLES, LEAF),
            (4 * n_row, FEATURES, LEAF),
            (CLUSTERS * n_row, RANK, LANES),
            (CLUSTERS * n_row, RANK, LANES),
            (CLUSTERS * n_row, FEATURES, LANES),
            (CLUSTERS * n_row, FEATURES, LANES),
        ]
    ]
    held += [jax.ShapeDtypeStruct(shape, F32) for shape in sums(n_col - 2)]
    params = pltpu.CompilerParams(vmem_limit_bytes=32 << 20)
    cost = pl.CostEstimate(flops=1 << 33, bytes_accessed=1 << 20, transcendentals=0)
    handed = pl.pallas_call(
        functools.partial(early_kernel, plan, early),
        out_shape=held,
        in_specs=[SMEM] + [VMEM] * (2 + len(early)),
        out_specs=[VMEM] * len(held),
        compiler_params=params,
        cost_estimate=cost,
        name="far_targets_early",
    )(lists, *row_features, *[blocks[j] for j in early])
    first = 3 + len(late)
    handed = pl.pallas_call(
        functools.partial(late_kernel, plan, late),
        out_shape=held + [part] * (n_col - 2),
        in_specs=[SMEM] + [VMEM] * (first - 1 + len(held)),
        out_specs=[VMEM] * (len(held) + n_col - 2),
        input_output_aliases={first + k: k for k in range(len(held))},
        compiler_params=params,
        cost_estimate=cost,
        name="far_targets_late",
    )(lists, *row_features, *[blocks[j] for j in late], *handed)
    prepared, parts = handed[:6], handed[len(held) :]
    arrived = [exchange(parts[k - 2], "col", k) for k in range(2, n_col)]
    here = pl.pallas_call(
        functools.partial(here_kernel, plan),
        out_shape=[part] * 2,
        in_specs=[SMEM] + [VMEM] * (2 + len(prepared)),
        out_specs=[VMEM] * 2,
        scratch_shapes=[pltpu.VMEM(shape, F32) for shape in sums(2)],
        compiler_params=params,
        cost_estimate=cost,
        name="near_targets",
    )(lists, *row_features, *prepared)
    arrived += [here[0], exchange(here[1], "col", 1)]
    sample = pl.pallas_call(
        functools.partial(final_kernel, n_col),
        out_shape=jax.ShapeDtypeStruct((SAMPLES, OWN), BF16),
        in_specs=[VMEM] * (2 + n_col),
        out_specs=VMEM,
        compiler_params=pltpu.CompilerParams(vmem_limit_bytes=16 << 20),
        name="final",
    )(basis, moves, *arrived)
    return sample.T


def solution(mesh):
    placed = (
        P(("row", "col"), None),
        P(None, ("row", "col")),
        P(None, ("row", "col")),
        P(("row", "col"), None),
        P(("row", "col"), None),
        P("row", "col", None, None),
        P("row", "col"),
        P("row", "col", None, None),
        P("row", "col"),
    )
    return jax.shard_map(
        local, mesh=mesh, in_specs=placed, out_specs=P(("row", "col"), None), check_vma=False
    )
```

```python
import functools
import math

import jax
import jax.numpy as jnp
import numpy as np
from jax import lax
from jax.experimental import pallas as pl
from jax.experimental.pallas import tpu as pltpu
from jax.sharding import PartitionSpec as P

LEAF = 256
RANK = 64
SAMPLES = 64
OWN = 4 * LEAF
CLUSTERS = 7
LANES = 128
F32 = jnp.float32
BF16 = jnp.bfloat16
FAR_ROW = OWN // LANES * SAMPLES
COORD_ROW = FAR_ROW + CLUSTERS * SAMPLES // 2
COORD_ROWS = 96
PACKED_ROWS = COORD_ROW + COORD_ROWS
FEATURES = 16
CLASSES = 3
NEAR_UNROLL = 4
FAR_UNROLL = 16
RATE = math.sqrt(3.0) / 0.15

VMEM = pl.BlockSpec(memory_space=pltpu.VMEM)
SMEM = pl.BlockSpec(memory_space=pltpu.SMEM)
NN = (((1,), (0,)), ((), ()))
NT = (((1,), (1,)), ((), ()))


def dot(a, b, dims=NN):
    return lax.dot_general(a, b, dims, preferred_element_type=F32)


def dot_wide(a, b):
    high = a.astype(BF16)
    low = (a - high.astype(F32)).astype(BF16)
    return dot(high, b) + dot(low, b)


def lanes(a, b):
    return jnp.concatenate([a, b], axis=1)


def rows(*parts):
    return jnp.concatenate(parts, axis=0)


def features(points):
    norm = points * points
    norm = norm[0:1] + norm[1:2] + norm[2:3]
    high = norm.astype(BF16).astype(F32)
    rest = norm - high
    middle = rest.astype(BF16).astype(F32)
    ones = jnp.ones_like(norm)
    return rows(points, high, middle, rest - middle, ones, ones)


def row_side(made):
    ones = made[6:7]
    return rows(-2.0 * made[0:3], ones, ones, ones, made[3:4], made[4:5])


def matern_of(square):
    square = jnp.maximum(square, 1e-14)
    dist = square * lax.rsqrt(square)
    e = jnp.exp2(dist * (-RATE / math.log(2.0)))
    return ((1.0 + RATE * dist) * e).astype(BF16)


def pack_kernel(probes, basis, moves, points, skeleton, packed, coords):
    near = features(points[...].astype(F32))
    far = features(lanes(skeleton[...].astype(F32), jnp.zeros((3, 64), F32)))
    chunks = [near[:, j * LANES : (j + 1) * LANES] for j in range(8)]
    chunks += [far[:, j * LANES : (j + 1) * LANES] for j in range(4)]
    made = rows(*chunks).astype(BF16)
    packed[COORD_ROW:] = made
    coords[...] = made
    leaves = []
    for l in range(4):
        part = slice(l * LEAF, (l + 1) * LEAF)
        leaves.append(dot(basis[:, part], probes[:, part], NT).astype(BF16))
    middle = [
        dot(moves[:, j * 128 : (j + 1) * 128], rows(*leaves[2 * j : 2 * j + 2])).astype(BF16)
        for j in range(2)
    ]
    top = dot(moves[:, 256:384], rows(*middle)).astype(BF16)
    for j in range(8):
        packed[j * SAMPLES : (j + 1) * SAMPLES] = probes[:, j * LANES : (j + 1) * LANES]
    packed[FAR_ROW : FAR_ROW + 64] = lanes(leaves[0], leaves[1])
    packed[FAR_ROW + 64 : FAR_ROW + 128] = lanes(leaves[2], leaves[3])
    packed[FAR_ROW + 128 : FAR_ROW + 192] = lanes(middle[0], middle[1])
    packed[FAR_ROW + 192 : FAR_ROW + 224] = lanes(top[:32], top[32:])


class Plan:
    def __init__(self, near_most, far_most):
        self.near = near_most + NEAR_UNROLL
        self.far = far_most + FAR_UNROLL
        self.far_first = -(-CLASSES * self.near // LANES) * LANES
        self.size = self.far_first + -(-CLASSES * self.far // LANES) * LANES


def iota(shape, axis):
    return lax.broadcasted_iota(jnp.int32, shape, axis)


def sort_slots(a_device, a_rest, b_device, b_rest, count, per_device, late_mask, n_col, most, width):
    slots = a_device.shape[1]
    target = a_device ^ lax.axis_index("col")
    source = b_device ^ lax.axis_index("row")
    remote = target >= 2
    is_late = lax.shift_right_logical(jnp.full_like(source, late_mask), source) & 1
    alive = iota((1, slots), 1) < count
    group = jnp.where(alive, jnp.where(remote, is_late, 2), 7)
    row = (target - jnp.where(remote, 2, 0)) * per_device + a_rest
    column = source * per_device + b_rest
    member = jnp.where(iota((8, slots), 0) == group, 1.0, 0.0)
    before = jnp.where(iota((slots, slots), 0) < iota((slots, slots), 1), 1.0, 0.0)
    ahead = dot(member.astype(BF16), before.astype(BF16))
    ahead = jnp.sum(member * ahead, axis=0, keepdims=True).astype(jnp.int32)
    place = jnp.where(alive, group * most + ahead, -1)
    chosen = jnp.where(iota((width, slots), 0) == place, 1.0, 0.0).astype(BF16)
    ones = jnp.ones((6, slots), F32)
    values = rows(row.astype(F32), column.astype(F32), ones).astype(BF16)
    found = dot(values, chosen, NT)
    here = iota((1, width), 1) >= 2 * most
    blank = jnp.where(here, 2.0 * per_device, (n_col - 2.0) * per_device)
    made = rows(found[0:1] + blank * (1.0 - found[2:3]), found[1:2])
    return made.astype(jnp.int32), jnp.sum(member, axis=1, keepdims=True).astype(jnp.int32)


def plan_kernel(n_col, late_mask, plan, slots, packed, mate, _, out, counts, again, both):
    again[...] = packed[...]
    both[:COORD_ROWS] = packed[COORD_ROW:]
    both[COORD_ROWS:] = mate[...]
    near_most, far_most = plan.near - NEAR_UNROLL, plan.far - FAR_UNROLL
    a, b = slots[0:1, :near_most], slots[1:2, :near_most]
    near, near_counts = sort_slots(
        lax.shift_right_logical(a, 2), a & 3, lax.shift_right_logical(b, 2), b & 3,
        slots[4:5, 0:1], 4, late_mask, n_col, plan.near, plan.far_first,
    )
    a, b = slots[2:3, :far_most], slots[3:4, :far_most]
    a_device = lax.shift_right_logical(a * 9363, 16)
    b_device = lax.shift_right_logical(b * 9363, 16)
    far, far_counts = sort_slots(
        a_device, a - a_device * CLUSTERS, b_device, b - b_device * CLUSTERS,
        slots[5:6, 0:1], CLUSTERS, late_mask, n_col, plan.far, plan.size - plan.far_first,
    )
    out[:, : plan.far_first] = near
    out[:, plan.far_first :] = far
    counts[...] = jnp.where(iota((8, LANES), 1) == 0, near_counts, far_counts)


def row_kernel(n_col, *refs):
    chips, near_row, far_row = refs[:-2], refs[-2], refs[-1]
    empty = jnp.zeros((8, LANES), F32)
    for i in range(n_col):
        first = i % 2 * COORD_ROWS
        slabs = [chips[i // 2][first + 16 * s : first + 16 * s + 16].astype(F32) for s in range(6)]
        near, far = (4 * i, CLUSTERS * i) if i < 2 else (4 * i + 1, CLUSTERS * i + 1)
        for l in range(4):
            for h in range(2):
                made = row_side(slabs[l][8 * h : 8 * h + 8])
                near_row[near + l, h * LANES : (h + 1) * LANES] = rows(made, empty).T.astype(BF16)
        for c in range(4):
            slab = slabs[4 + c // 2]
            made = row_side(slab[8 * (c % 2) : 8 * (c % 2) + 8])
            tall = rows(made, empty).T.astype(BF16)
            far_row[far + 2 * c] = tall[:64]
            if c < 3:
                far_row[far + 2 * c + 1] = tall[64:]
    for blank in (8, 4 * n_col + 1):
        near_row[blank] = jnp.zeros(near_row.shape[1:], BF16)
    for blank in (2 * CLUSTERS, CLUSTERS * n_col + 1):
        far_row[blank] = jnp.zeros(far_row.shape[1:], BF16)


def prepare(i, block, probes, near_col, coeff_low, coeff_high, far_low, far_high):
    for l in range(4):
        for h in range(2):
            j = 2 * l + h
            half = slice(h * LANES, (h + 1) * LANES)
            probes[4 * i + l, :, half] = block[j * SAMPLES : (j + 1) * SAMPLES]
        slab = block[COORD_ROW + 16 * l : COORD_ROW + 16 * (l + 1)]
        near_col[4 * i + l, :, :LANES] = slab
        near_col[4 * i + l, :, LANES:] = rows(slab[8:], slab[:8])
    slabs = [block[COORD_ROW + 64 + 16 * p : COORD_ROW + 80 + 16 * p] for p in range(2)]
    for k in range(CLUSTERS):
        c, half = k // 2, slice(k % 2 * 64, k % 2 * 64 + 64)
        if k < 6:
            own = block[FAR_ROW + 64 * c : FAR_ROW + 64 * (c + 1)][:, half]
        else:
            own = block[FAR_ROW + 192 : FAR_ROW + 224]
            own = rows(own[:, :64], own[:, 64:])
        empty = jnp.zeros_like(own)
        coeff_low[CLUSTERS * i + k] = lanes(own, empty)
        coeff_high[CLUSTERS * i + k] = lanes(empty, own)
        made = slabs[c // 2].astype(F32)[8 * (c % 2) : 8 * (c % 2) + 8, half]
        empty = jnp.zeros_like(made)
        blank = jnp.zeros((8, LANES), F32)
        far_low[CLUSTERS * i + k] = rows(lanes(made, empty), blank).astype(BF16)
        far_high[CLUSTERS * i + k] = rows(lanes(empty, made), blank).astype(BF16)


def work(plan, group, lists, counts, near_row, far_row, prepared, totals):
    probes, near_col, coeff_low, coeff_high, far_low, far_high = prepared
    near_total, far_even, far_odd = totals
    near_first, far_first = (0, 0) if group == 2 else (9, 2 * CLUSTERS + 1)

    def near_step(g, _):
        place = group * plan.near + g * NEAR_UNROLL
        terms = []
        for u in range(NEAR_UNROLL):
            a, b = lists[0, place + u], lists[1, place + u]
            parts = []
            for q in range(2):
                part = slice(q * LANES, (q + 1) * LANES)
                parts.append(matern_of(dot(near_row[near_first + a, part], near_col[b])))
            terms.append((a, dot(probes[b], rows(*parts), NT)))
        for a, term in terms:
            near_total[a] += term
        return 0

    count = counts[group, 0]
    lax.fori_loop(0, (count + NEAR_UNROLL - 1) // NEAR_UNROLL, near_step, 0)

    def far_step(g, _):
        place = plan.far_first + group * plan.far + g * FAR_UNROLL
        terms = []
        for u in range(0, FAR_UNROLL, 2):
            a0, a1 = lists[0, place + u], lists[0, place + u + 1]
            b0, b1 = lists[1, place + u], lists[1, place + u + 1]
            square = dot(far_row[far_first + a0], far_low[b0])
            square += dot(far_row[far_first + a1], far_high[b1])
            both = rows(coeff_low[b0], coeff_high[b1])
            terms.append((a0, a1, dot(matern_of(square), both)))
        for a0, a1, term in terms:
            far_even[a0] += term
            far_odd[a1] += term
        return 0

    count = counts[group, 1]
    lax.fori_loop(0, (count + FAR_UNROLL - 1) // FAR_UNROLL, far_step, 0)


def write_parts(outs, near_total, far_even, far_odd):
    for i, out in enumerate(outs):
        for j in range(8):
            half = slice(j % 2 * LANES, (j % 2 + 1) * LANES)
            part = near_total[4 * i + j // 2, :, half]
            out[j * SAMPLES : (j + 1) * SAMPLES] = part.astype(BF16)
        parts = []
        for l in range(CLUSTERS):
            even, odd = far_even[CLUSTERS * i + l], far_odd[CLUSTERS * i + l]
            parts.append(even[:, :64] + odd[:, 64:])
        for j in range(3):
            pair = lanes(*parts[2 * j : 2 * j + 2])
            out[FAR_ROW + 64 * j : FAR_ROW + 64 * (j + 1)] = pair.astype(BF16)
        pair = lanes(parts[6][:32], parts[6][32:])
        out[FAR_ROW + 192 : FAR_ROW + 224] = pair.astype(BF16)


def clear(totals):
    for total in totals:
        total[...] = jnp.zeros_like(total)


def early_kernel(plan, members, lists, counts, near_row, far_row, *refs):
    blocks, refs = refs[: len(members)], refs[len(members) :]
    prepared, totals = refs[:6], refs[6:]
    clear(totals)
    for i, block in zip(members, blocks):
        prepare(i, block, *prepared)
    work(plan, 0, lists, counts, near_row, far_row, prepared, totals)


def late_kernel(plan, members, lists, counts, near_row, far_row, *refs):
    blocks, refs = refs[: len(members)], refs[len(members) + 9 :]
    prepared, totals, outs = refs[:6], refs[6:9], refs[9:]
    for i, block in zip(members, blocks):
        prepare(i, block, *prepared)
    work(plan, 1, lists, counts, near_row, far_row, prepared, totals)
    write_parts(outs, *totals)


def here_kernel(plan, lists, counts, near_row, far_row, *refs):
    prepared, outs, totals = refs[:6], refs[6:8], refs[8:]
    clear(totals)
    work(plan, 2, lists, counts, near_row, far_row, prepared, totals)
    write_parts(outs, *totals)


def final_kernel(n_col, basis, moves, *refs):
    parts, out = refs[:n_col], refs[n_col]

    def total(first, count):
        return sum(part[first : first + count].astype(F32) for part in parts)

    def turned(first):
        tall = total(first, 64).T
        return lanes(tall[:64], tall[64:])

    top = total(FAR_ROW + 192, 32)
    top = rows(top[:, :64], top[:, 64:]).T
    middle = turned(FAR_ROW + 128) + dot_wide(top, moves[:, 256:384])
    for j in range(2):
        pair = turned(FAR_ROW + 64 * j) + dot_wide(
            middle[:, j * RANK : (j + 1) * RANK], moves[:, j * 128 : (j + 1) * 128]
        )
        for k in range(2):
            l = 2 * j + k
            expanded = dot_wide(
                pair[:, k * RANK : (k + 1) * RANK], basis[:, l * LEAF : (l + 1) * LEAF]
            )
            for h in range(2):
                place = (2 * l + h) * LANES
                near = total((2 * l + h) * SAMPLES, SAMPLES)
                made = near + expanded[:, h * LANES : (h + 1) * LANES]
                out[:, place : place + LANES] = made.astype(BF16)


def exchange(x, axis, offset):
    size = lax.axis_size(axis)
    return lax.ppermute(x, axis, [(i, i ^ offset) for i in range(size)])


def local(
    probes, points, skeleton, leaf_basis, transfer, near_list, near_count, far_list, far_count
):
    n_row = lax.axis_size("row")
    n_col = lax.axis_size("col")
    n_y = n_row // min(n_row, 4)
    probes, basis, moves = probes.T, leaf_basis.T, transfer.T
    inputs = (probes, basis, moves, points, skeleton)
    small = pltpu.CompilerParams(vmem_limit_bytes=8 << 20)
    packed, coords = pl.pallas_call(
        pack_kernel,
        out_shape=[
            jax.ShapeDtypeStruct((PACKED_ROWS, LANES), BF16),
            jax.ShapeDtypeStruct((COORD_ROWS, LANES), BF16),
        ],
        in_specs=[VMEM] * 5,
        out_specs=[VMEM] * 2,
        name="pack",
    )(*inputs)

    plan = Plan(near_list.shape[-1], far_list.shape[-1])
    early = [j for j in range(n_row) if j % n_y == 0 or j < n_y]
    late = [j for j in range(n_row) if j not in early]
    late_mask = sum(1 << j for j in late)
    width = max(LANES, near_list.shape[-1], far_list.shape[-1])

    def placed(x, row):
        return jnp.pad(x, ((row, 8 - row - x.shape[0]), (0, width - x.shape[1])))

    slots = placed(near_list[0, 0], 0) + placed(far_list[0, 0], 2)
    slots = slots + placed(near_count, 4) + placed(far_count, 5)
    own_y = exchange(packed, "row", 1)
    lists, counts, again, both = pl.pallas_call(
        functools.partial(plan_kernel, n_col, np.uint32(late_mask).astype(np.int32), plan),
        out_shape=[
            jax.ShapeDtypeStruct((2, plan.size), jnp.int32),
            jax.ShapeDtypeStruct((8, LANES), jnp.int32),
            jax.ShapeDtypeStruct((PACKED_ROWS, LANES), BF16),
            jax.ShapeDtypeStruct((2 * COORD_ROWS, LANES), BF16),
        ],
        in_specs=[VMEM] * 3 + [pl.BlockSpec(memory_space=pl.ANY)],
        out_specs=[VMEM] * 4,
        compiler_params=small,
        cost_estimate=pl.CostEstimate(flops=1 << 30, bytes_accessed=1 << 12, transcendentals=0),
        name="plan",
    )(slots, packed, exchange(coords, "col", 1), own_y)

    blocks = [packed] + [None] * (n_row - 1)
    for z in range(n_y, n_row, n_y):
        blocks[z] = exchange(packed if z < n_row - n_y else again, "row", z)
    for z in range(0, n_row, n_y):
        for y in range(1, n_y):
            blocks[z + y] = own_y if z + y == 1 else exchange(blocks[z], "row", y)
    row_coords = [both] + [exchange(both, "col", k) for k in range(2, n_col, 2)]

    row_features = pl.pallas_call(
        functools.partial(row_kernel, n_col),
        out_shape=[
            jax.ShapeDtypeStruct((4 * n_col + 2, LEAF, FEATURES), BF16),
            jax.ShapeDtypeStruct((CLUSTERS * n_col + 2, RANK, FEATURES), BF16),
        ],
        in_specs=[VMEM] * (n_col // 2),
        out_specs=[VMEM] * 2,
        compiler_params=small,
        name="row_side",
    )(*row_coords)

    def sums(targets):
        near = (4 * targets + 1, SAMPLES, LEAF)
        far = (CLUSTERS * targets + 1, RANK, LANES)
        return [near, far, far]

    part = jax.ShapeDtypeStruct((COORD_ROW, LANES), BF16)
    held = [
        jax.ShapeDtypeStruct(shape, BF16)
        for shape in [
            (4 * n_row, SAMPLES, LEAF),
            (4 * n_row, FEATURES, LEAF),
            (CLUSTERS * n_row, RANK, LANES),
            (CLUSTERS * n_row, RANK, LANES),
            (CLUSTERS * n_row, FEATURES, LANES),
            (CLUSTERS * n_row, FEATURES, LANES),
        ]
    ]
    held += [jax.ShapeDtypeStruct(shape, F32) for shape in sums(n_col - 2)]
    params = pltpu.CompilerParams(vmem_limit_bytes=32 << 20)
    cost = pl.CostEstimate(flops=1 << 33, bytes_accessed=1 << 20, transcendentals=0)
    handed = pl.pallas_call(
        functools.partial(early_kernel, plan, early),
        out_shape=held,
        in_specs=[SMEM] * 2 + [VMEM] * (2 + len(early)),
        out_specs=[VMEM] * len(held),
        compiler_params=params,
        cost_estimate=cost,
        name="far_targets_early",
    )(lists, counts, *row_features, *[blocks[j] for j in early])
    first = 4 + len(late)
    handed = pl.pallas_call(
        functools.partial(late_kernel, plan, late),
        out_shape=held + [part] * (n_col - 2),
        in_specs=[SMEM] * 2 + [VMEM] * (first - 2 + len(held)),
        out_specs=[VMEM] * (len(held) + n_col - 2),
        input_output_aliases={first + k: k for k in range(len(held))},
        compiler_params=params,
        cost_estimate=cost,
        name="far_targets_late",
    )(lists, counts, *row_features, *[blocks[j] for j in late], *handed)
    prepared, parts = handed[:6], handed[len(held) :]
    arrived = [exchange(parts[k - 2], "col", k) for k in range(2, n_col)]
    here = pl.pallas_call(
        functools.partial(here_kernel, plan),
        out_shape=[part] * 2,
        in_specs=[SMEM] * 2 + [VMEM] * (2 + len(prepared)),
        out_specs=[VMEM] * 2,
        scratch_shapes=[pltpu.VMEM(shape, F32) for shape in sums(2)],
        compiler_params=params,
        cost_estimate=cost,
        name="near_targets",
    )(lists, counts, *row_features, *prepared)
    arrived += [here[0], exchange(here[1], "col", 1)]
    sample = pl.pallas_call(
        functools.partial(final_kernel, n_col),
        out_shape=jax.ShapeDtypeStruct((SAMPLES, OWN), BF16),
        in_specs=[VMEM] * (2 + n_col),
        out_specs=VMEM,
        compiler_params=pltpu.CompilerParams(vmem_limit_bytes=16 << 20),
        name="final",
    )(basis, moves, *arrived)
    return sample.T


def solution(mesh):
    placed = (
        P(("row", "col"), None),
        P(None, ("row", "col")),
        P(None, ("row", "col")),
        P(("row", "col"), None),
        P(("row", "col"), None),
        P("row", "col", None, None),
        P("row", "col"),
        P("row", "col", None, None),
        P("row", "col"),
    )
    return jax.shard_map(
        local, mesh=mesh, in_specs=placed, out_specs=P(("row", "col"), None), check_vma=False
    )
```

```python
import functools
import math

import jax
import jax.numpy as jnp
import numpy as np
from jax import lax
from jax.experimental import pallas as pl
from jax.experimental.pallas import tpu as pltpu
from jax.sharding import PartitionSpec as P

LEAF = 256
RANK = 64
SAMPLES = 64
OWN = 4 * LEAF
CLUSTERS = 7
LANES = 128
F32 = jnp.float32
BF16 = jnp.bfloat16
FAR_ROW = OWN // LANES * SAMPLES
COORD_ROW = FAR_ROW + CLUSTERS * SAMPLES // 2
COORD_ROWS = 96
PACKED_ROWS = COORD_ROW + COORD_ROWS
FEATURES = 16
CLASSES = 3
NEAR_UNROLL = 4
FAR_UNROLL = 16
RATE = math.sqrt(3.0) / 0.15

VMEM = pl.BlockSpec(memory_space=pltpu.VMEM)
SMEM = pl.BlockSpec(memory_space=pltpu.SMEM)
NN = (((1,), (0,)), ((), ()))
NT = (((1,), (1,)), ((), ()))


def dot(a, b, dims=NN):
    return lax.dot_general(a, b, dims, preferred_element_type=F32)


def dot_wide(a, b):
    high = a.astype(BF16)
    low = (a - high.astype(F32)).astype(BF16)
    return dot(high, b) + dot(low, b)


def lanes(a, b):
    return jnp.concatenate([a, b], axis=1)


def rows(*parts):
    return jnp.concatenate(parts, axis=0)


def features(points):
    norm = points * points
    norm = norm[0:1] + norm[1:2] + norm[2:3]
    high = norm.astype(BF16).astype(F32)
    rest = norm - high
    middle = rest.astype(BF16).astype(F32)
    ones = jnp.ones_like(norm)
    return rows(points, high, middle, rest - middle, ones, ones)


def row_side(made):
    ones = made[6:7]
    return rows(-2.0 * made[0:3], ones, ones, ones, made[3:4], made[4:5])


def matern_of(square):
    square = jnp.maximum(square, 1e-14)
    dist = square * lax.rsqrt(square)
    e = jnp.exp2(dist * (-RATE / math.log(2.0)))
    return ((1.0 + RATE * dist) * e).astype(BF16)


def pack_kernel(probes, basis, moves, points, skeleton, packed, coords):
    near = features(points[...].astype(F32))
    far = features(lanes(skeleton[...].astype(F32), jnp.zeros((3, 64), F32)))
    chunks = [near[:, j * LANES : (j + 1) * LANES] for j in range(8)]
    chunks += [far[:, j * LANES : (j + 1) * LANES] for j in range(4)]
    made = rows(*chunks).astype(BF16)
    packed[COORD_ROW:] = made
    coords[...] = made
    leaves = []
    for l in range(4):
        part = slice(l * LEAF, (l + 1) * LEAF)
        leaves.append(dot(basis[:, part], probes[:, part], NT).astype(BF16))
    middle = [
        dot(moves[:, j * 128 : (j + 1) * 128], rows(*leaves[2 * j : 2 * j + 2])).astype(BF16)
        for j in range(2)
    ]
    top = dot(moves[:, 256:384], rows(*middle)).astype(BF16)
    for j in range(8):
        packed[j * SAMPLES : (j + 1) * SAMPLES] = probes[:, j * LANES : (j + 1) * LANES]
    packed[FAR_ROW : FAR_ROW + 64] = lanes(leaves[0], leaves[1])
    packed[FAR_ROW + 64 : FAR_ROW + 128] = lanes(leaves[2], leaves[3])
    packed[FAR_ROW + 128 : FAR_ROW + 192] = lanes(middle[0], middle[1])
    packed[FAR_ROW + 192 : FAR_ROW + 224] = lanes(top[:32], top[32:])


class Plan:
    def __init__(self, near_most, far_most):
        self.near = near_most + NEAR_UNROLL
        self.far = far_most + FAR_UNROLL
        self.far_first = -(-CLASSES * self.near // LANES) * LANES
        self.size = self.far_first + -(-CLASSES * self.far // LANES) * LANES


def iota(shape, axis):
    return lax.broadcasted_iota(jnp.int32, shape, axis)


def is_inner(n_y):
    z = lax.axis_index("row") // n_y
    return (z == 1) | (z == 2)


def pick_kernel(n_y, inner, outer, out):
    @pl.when(is_inner(n_y))
    def _():
        out[...] = inner[...]

    @pl.when(jnp.logical_not(is_inner(n_y)))
    def _():
        out[...] = outer[...]


def sort_slots(
    a_device, a_rest, b_device, b_rest, count, per_device, late_mask, n_col, n_y, most, width
):
    slots = a_device.shape[1]
    target = a_device ^ lax.axis_index("col")
    source = b_device ^ lax.axis_index("row")
    source = jnp.where(is_inner(n_y) & (source >= 2 * n_y), source ^ n_y, source)
    remote = target >= 2
    is_late = lax.shift_right_logical(jnp.full_like(source, late_mask), source) & 1
    alive = iota((1, slots), 1) < count
    group = jnp.where(alive, jnp.where(remote, is_late, 2), 7)
    row = (target - jnp.where(remote, 2, 0)) * per_device + a_rest
    column = source * per_device + b_rest
    member = jnp.where(iota((8, slots), 0) == group, 1.0, 0.0)
    before = jnp.where(iota((slots, slots), 0) < iota((slots, slots), 1), 1.0, 0.0)
    ahead = dot(member.astype(BF16), before.astype(BF16))
    ahead = jnp.sum(member * ahead, axis=0, keepdims=True).astype(jnp.int32)
    place = jnp.where(alive, group * most + ahead, -1)
    chosen = jnp.where(iota((width, slots), 0) == place, 1.0, 0.0).astype(BF16)
    ones = jnp.ones((6, slots), F32)
    values = rows(row.astype(F32), column.astype(F32), ones).astype(BF16)
    found = dot(values, chosen, NT)
    here = iota((1, width), 1) >= 2 * most
    blank = jnp.where(here, 2.0 * per_device, (n_col - 2.0) * per_device)
    made = rows(found[0:1] + blank * (1.0 - found[2:3]), found[1:2])
    return made.astype(jnp.int32), jnp.sum(member, axis=1, keepdims=True).astype(jnp.int32)


def plan_kernel(n_col, n_y, late_mask, plan, slots, coords, mate, out, counts, both):
    both[:COORD_ROWS] = coords[...]
    both[COORD_ROWS:] = mate[...]
    near_most, far_most = plan.near - NEAR_UNROLL, plan.far - FAR_UNROLL
    a, b = slots[0:1, :near_most], slots[1:2, :near_most]
    near, near_counts = sort_slots(
        lax.shift_right_logical(a, 2), a & 3, lax.shift_right_logical(b, 2), b & 3,
        slots[4:5, 0:1], 4, late_mask, n_col, n_y, plan.near, plan.far_first,
    )
    a, b = slots[2:3, :far_most], slots[3:4, :far_most]
    a_device = lax.shift_right_logical(a * 9363, 16)
    b_device = lax.shift_right_logical(b * 9363, 16)
    far, far_counts = sort_slots(
        a_device, a - a_device * CLUSTERS, b_device, b - b_device * CLUSTERS,
        slots[5:6, 0:1], CLUSTERS, late_mask, n_col, n_y, plan.far, plan.size - plan.far_first,
    )
    out[:, : plan.far_first] = near
    out[:, plan.far_first :] = far
    counts[...] = jnp.where(iota((8, LANES), 1) == 0, near_counts, far_counts)


def row_kernel(n_col, *refs):
    chips, near_row, far_row = refs[:-2], refs[-2], refs[-1]
    empty = jnp.zeros((8, LANES), F32)
    for i in range(n_col):
        first = i % 2 * COORD_ROWS
        slabs = [chips[i // 2][first + 16 * s : first + 16 * s + 16].astype(F32) for s in range(6)]
        near, far = (4 * i, CLUSTERS * i) if i < 2 else (4 * i + 1, CLUSTERS * i + 1)
        for l in range(4):
            for h in range(2):
                made = row_side(slabs[l][8 * h : 8 * h + 8])
                near_row[near + l, h * LANES : (h + 1) * LANES] = rows(made, empty).T.astype(BF16)
        for c in range(4):
            slab = slabs[4 + c // 2]
            made = row_side(slab[8 * (c % 2) : 8 * (c % 2) + 8])
            tall = rows(made, empty).T.astype(BF16)
            far_row[far + 2 * c] = tall[:64]
            if c < 3:
                far_row[far + 2 * c + 1] = tall[64:]
    for blank in (8, 4 * n_col + 1):
        near_row[blank] = jnp.zeros(near_row.shape[1:], BF16)
    for blank in (2 * CLUSTERS, CLUSTERS * n_col + 1):
        far_row[blank] = jnp.zeros(far_row.shape[1:], BF16)


def prepare(i, block, probes, near_col, coeff_low, coeff_high, far_low, far_high):
    for l in range(4):
        for h in range(2):
            j = 2 * l + h
            half = slice(h * LANES, (h + 1) * LANES)
            probes[4 * i + l, :, half] = block[j * SAMPLES : (j + 1) * SAMPLES]
        slab = block[COORD_ROW + 16 * l : COORD_ROW + 16 * (l + 1)]
        near_col[4 * i + l, :, :LANES] = slab
        near_col[4 * i + l, :, LANES:] = rows(slab[8:], slab[:8])
    slabs = [block[COORD_ROW + 64 + 16 * p : COORD_ROW + 80 + 16 * p] for p in range(2)]
    for k in range(CLUSTERS):
        c, half = k // 2, slice(k % 2 * 64, k % 2 * 64 + 64)
        if k < 6:
            own = block[FAR_ROW + 64 * c : FAR_ROW + 64 * (c + 1)][:, half]
        else:
            own = block[FAR_ROW + 192 : FAR_ROW + 224]
            own = rows(own[:, :64], own[:, 64:])
        empty = jnp.zeros_like(own)
        coeff_low[CLUSTERS * i + k] = lanes(own, empty)
        coeff_high[CLUSTERS * i + k] = lanes(empty, own)
        made = slabs[c // 2].astype(F32)[8 * (c % 2) : 8 * (c % 2) + 8, half]
        empty = jnp.zeros_like(made)
        blank = jnp.zeros((8, LANES), F32)
        far_low[CLUSTERS * i + k] = rows(lanes(made, empty), blank).astype(BF16)
        far_high[CLUSTERS * i + k] = rows(lanes(empty, made), blank).astype(BF16)


def work(plan, group, lists, counts, near_row, far_row, prepared, totals):
    probes, near_col, coeff_low, coeff_high, far_low, far_high = prepared
    near_total, far_even, far_odd = totals
    near_first, far_first = (0, 0) if group == 2 else (9, 2 * CLUSTERS + 1)

    def near_step(g, _):
        place = group * plan.near + g * NEAR_UNROLL
        terms = []
        for u in range(NEAR_UNROLL):
            a, b = lists[0, place + u], lists[1, place + u]
            parts = []
            for q in range(2):
                part = slice(q * LANES, (q + 1) * LANES)
                parts.append(matern_of(dot(near_row[near_first + a, part], near_col[b])))
            terms.append((a, dot(probes[b], rows(*parts), NT)))
        for a, term in terms:
            near_total[a] += term
        return 0

    count = counts[group, 0]
    lax.fori_loop(0, (count + NEAR_UNROLL - 1) // NEAR_UNROLL, near_step, 0)

    def far_step(g, _):
        place = plan.far_first + group * plan.far + g * FAR_UNROLL
        terms = []
        for u in range(0, FAR_UNROLL, 2):
            a0, a1 = lists[0, place + u], lists[0, place + u + 1]
            b0, b1 = lists[1, place + u], lists[1, place + u + 1]
            square = dot(far_row[far_first + a0], far_low[b0])
            square += dot(far_row[far_first + a1], far_high[b1])
            both = rows(coeff_low[b0], coeff_high[b1])
            terms.append((a0, a1, dot(matern_of(square), both)))
        for a0, a1, term in terms:
            far_even[a0] += term
            far_odd[a1] += term
        return 0

    count = counts[group, 1]
    lax.fori_loop(0, (count + FAR_UNROLL - 1) // FAR_UNROLL, far_step, 0)


def write_parts(outs, near_total, far_even, far_odd):
    for i, out in enumerate(outs):
        for j in range(8):
            half = slice(j % 2 * LANES, (j % 2 + 1) * LANES)
            part = near_total[4 * i + j // 2, :, half]
            out[j * SAMPLES : (j + 1) * SAMPLES] = part.astype(BF16)
        parts = []
        for l in range(CLUSTERS):
            even, odd = far_even[CLUSTERS * i + l], far_odd[CLUSTERS * i + l]
            parts.append(even[:, :64] + odd[:, 64:])
        for j in range(3):
            pair = lanes(*parts[2 * j : 2 * j + 2])
            out[FAR_ROW + 64 * j : FAR_ROW + 64 * (j + 1)] = pair.astype(BF16)
        pair = lanes(parts[6][:32], parts[6][32:])
        out[FAR_ROW + 192 : FAR_ROW + 224] = pair.astype(BF16)


def clear(totals):
    for total in totals:
        total[...] = jnp.zeros_like(total)


def early_kernel(plan, members, lists, counts, near_row, far_row, *refs):
    blocks, refs = refs[: len(members)], refs[len(members) :]
    prepared, totals = refs[:6], refs[6:]
    clear(totals)
    for i, block in zip(members, blocks):
        prepare(i, block, *prepared)
    work(plan, 0, lists, counts, near_row, far_row, prepared, totals)


def late_kernel(plan, members, lists, counts, near_row, far_row, *refs):
    blocks, refs = refs[: len(members)], refs[len(members) + 9 :]
    prepared, totals, outs = refs[:6], refs[6:9], refs[9:]
    for i, block in zip(members, blocks):
        prepare(i, block, *prepared)
    work(plan, 1, lists, counts, near_row, far_row, prepared, totals)
    write_parts(outs, *totals)


def here_kernel(plan, lists, counts, near_row, far_row, *refs):
    prepared, outs, totals = refs[:6], refs[6:8], refs[8:]
    clear(totals)
    work(plan, 2, lists, counts, near_row, far_row, prepared, totals)
    write_parts(outs, *totals)


def final_kernel(n_col, basis, moves, *refs):
    parts, out = refs[:n_col], refs[n_col]

    def total(first, count):
        return sum(part[first : first + count].astype(F32) for part in parts)

    def turned(first):
        tall = total(first, 64).T
        return lanes(tall[:64], tall[64:])

    top = total(FAR_ROW + 192, 32)
    top = rows(top[:, :64], top[:, 64:]).T
    middle = turned(FAR_ROW + 128) + dot_wide(top, moves[:, 256:384])
    for j in range(2):
        pair = turned(FAR_ROW + 64 * j) + dot_wide(
            middle[:, j * RANK : (j + 1) * RANK], moves[:, j * 128 : (j + 1) * 128]
        )
        for k in range(2):
            l = 2 * j + k
            expanded = dot_wide(
                pair[:, k * RANK : (k + 1) * RANK], basis[:, l * LEAF : (l + 1) * LEAF]
            )
            for h in range(2):
                place = (2 * l + h) * LANES
                near = total((2 * l + h) * SAMPLES, SAMPLES)
                made = near + expanded[:, h * LANES : (h + 1) * LANES]
                out[:, place : place + LANES] = made.astype(BF16)


def exchange(x, axis, offset):
    size = lax.axis_size(axis)
    return lax.ppermute(x, axis, [(i, i ^ offset) for i in range(size)])


def local(
    probes, points, skeleton, leaf_basis, transfer, near_list, near_count, far_list, far_count
):
    n_row = lax.axis_size("row")
    n_col = lax.axis_size("col")
    n_y = n_row // 4
    probes, basis, moves = probes.T, leaf_basis.T, transfer.T
    inputs = (probes, basis, moves, points, skeleton)
    small = pltpu.CompilerParams(vmem_limit_bytes=8 << 20)
    packed, coords = pl.pallas_call(
        pack_kernel,
        out_shape=[
            jax.ShapeDtypeStruct((PACKED_ROWS, LANES), BF16),
            jax.ShapeDtypeStruct((COORD_ROWS, LANES), BF16),
        ],
        in_specs=[VMEM] * 5,
        out_specs=[VMEM] * 2,
        name="pack",
    )(*inputs)

    plan = Plan(near_list.shape[-1], far_list.shape[-1])
    late = list(range(3 * n_y + 1, n_row))
    early = [j for j in range(n_row) if j not in late]
    late_mask = sum(1 << j for j in late)
    width = max(LANES, near_list.shape[-1], far_list.shape[-1])

    def placed(x, row):
        return jnp.pad(x, ((row, 8 - row - x.shape[0]), (0, width - x.shape[1])))

    slots = placed(near_list[0, 0], 0) + placed(far_list[0, 0], 2)
    slots = slots + placed(near_count, 4) + placed(far_count, 5)
    lists, counts, both = pl.pallas_call(
        functools.partial(plan_kernel, n_col, n_y, np.uint32(late_mask).astype(np.int32), plan),
        out_shape=[
            jax.ShapeDtypeStruct((2, plan.size), jnp.int32),
            jax.ShapeDtypeStruct((8, LANES), jnp.int32),
            jax.ShapeDtypeStruct((2 * COORD_ROWS, LANES), BF16),
        ],
        in_specs=[VMEM] * 3,
        out_specs=[VMEM] * 3,
        compiler_params=small,
        cost_estimate=pl.CostEstimate(flops=1 << 30, bytes_accessed=1 << 12, transcendentals=0),
        name="plan",
    )(slots, coords, exchange(coords, "col", 1))

    def along_z(x, planes, flip):
        pairs = [(z * n_y + y, (z ^ flip) * n_y + y) for z in planes for y in range(n_y)]
        return lax.ppermute(x, "row", pairs)

    def pick(inner, outer, name):
        return pl.pallas_call(
            functools.partial(pick_kernel, n_y),
            out_shape=jax.ShapeDtypeStruct((PACKED_ROWS, LANES), BF16),
            in_specs=[VMEM] * 2,
            out_specs=VMEM,
            compiler_params=small,
            name=name,
        )(inner, outer)

    neighbour = along_z(packed, (0, 1, 2, 3), 1)
    inner_a = along_z(packed, (1, 2), 3)
    inner_b = along_z(neighbour, (1, 2), 3)
    block_a = pick(inner_a, along_z(inner_a, (1, 2), 1), "pick_a")
    block_b = pick(inner_b, along_z(inner_b, (1, 2), 1), "pick_b")
    blocks = []
    for block in (packed, neighbour, block_a, block_b):
        blocks += [block] + [exchange(block, "row", y) for y in range(1, n_y)]
    row_coords = [both] + [exchange(both, "col", k) for k in range(2, n_col, 2)]

    row_features = pl.pallas_call(
        functools.partial(row_kernel, n_col),
        out_shape=[
            jax.ShapeDtypeStruct((4 * n_col + 2, LEAF, FEATURES), BF16),
            jax.ShapeDtypeStruct((CLUSTERS * n_col + 2, RANK, FEATURES), BF16),
        ],
        in_specs=[VMEM] * (n_col // 2),
        out_specs=[VMEM] * 2,
        compiler_params=small,
        name="row_side",
    )(*row_coords)

    def sums(targets):
        near = (4 * targets + 1, SAMPLES, LEAF)
        far = (CLUSTERS * targets + 1, RANK, LANES)
        return [near, far, far]

    part = jax.ShapeDtypeStruct((COORD_ROW, LANES), BF16)
    held = [
        jax.ShapeDtypeStruct(shape, BF16)
        for shape in [
            (4 * n_row, SAMPLES, LEAF),
            (4 * n_row, FEATURES, LEAF),
            (CLUSTERS * n_row, RANK, LANES),
            (CLUSTERS * n_row, RANK, LANES),
            (CLUSTERS * n_row, FEATURES, LANES),
            (CLUSTERS * n_row, FEATURES, LANES),
        ]
    ]
    held += [jax.ShapeDtypeStruct(shape, F32) for shape in sums(n_col - 2)]
    params = pltpu.CompilerParams(vmem_limit_bytes=32 << 20)
    cost = pl.CostEstimate(flops=1 << 33, bytes_accessed=1 << 20, transcendentals=0)
    handed = pl.pallas_call(
        functools.partial(early_kernel, plan, early),
        out_shape=held,
        in_specs=[SMEM] * 2 + [VMEM] * (2 + len(early)),
        out_specs=[VMEM] * len(held),
        compiler_params=params,
        cost_estimate=cost,
        name="far_targets_early",
    )(lists, counts, *row_features, *[blocks[j] for j in early])
    first = 4 + len(late)
    handed = pl.pallas_call(
        functools.partial(late_kernel, plan, late),
        out_shape=held + [part] * (n_col - 2),
        in_specs=[SMEM] * 2 + [VMEM] * (first - 2 + len(held)),
        out_specs=[VMEM] * (len(held) + n_col - 2),
        input_output_aliases={first + k: k for k in range(len(held))},
        compiler_params=params,
        cost_estimate=cost,
        name="far_targets_late",
    )(lists, counts, *row_features, *[blocks[j] for j in late], *handed)
    prepared, parts = handed[:6], handed[len(held) :]
    arrived = [exchange(parts[k - 2], "col", k) for k in range(2, n_col)]
    here = pl.pallas_call(
        functools.partial(here_kernel, plan),
        out_shape=[part] * 2,
        in_specs=[SMEM] * 2 + [VMEM] * (2 + len(prepared)),
        out_specs=[VMEM] * 2,
        scratch_shapes=[pltpu.VMEM(shape, F32) for shape in sums(2)],
        compiler_params=params,
        cost_estimate=cost,
        name="near_targets",
    )(lists, counts, *row_features, *prepared)
    arrived += [here[0], exchange(here[1], "col", 1)]
    sample = pl.pallas_call(
        functools.partial(final_kernel, n_col),
        out_shape=jax.ShapeDtypeStruct((SAMPLES, OWN), BF16),
        in_specs=[VMEM] * (2 + n_col),
        out_specs=VMEM,
        compiler_params=pltpu.CompilerParams(vmem_limit_bytes=16 << 20),
        name="final",
    )(basis, moves, *arrived)
    return sample.T


def solution(mesh):
    placed = (
        P(("row", "col"), None),
        P(None, ("row", "col")),
        P(None, ("row", "col")),
        P(("row", "col"), None),
        P(("row", "col"), None),
        P("row", "col", None, None),
        P("row", "col"),
        P("row", "col", None, None),
        P("row", "col"),
    )
    return jax.shard_map(
        local, mesh=mesh, in_specs=placed, out_specs=P(("row", "col"), None), check_vma=False
    )
```

```python
import functools
import math

import jax
import jax.numpy as jnp
import numpy as np
from jax import lax
from jax.experimental import pallas as pl
from jax.experimental.pallas import tpu as pltpu
from jax.sharding import PartitionSpec as P

LEAF = 256
RANK = 64
SAMPLES = 64
OWN = 4 * LEAF
CLUSTERS = 7
LANES = 128
F32 = jnp.float32
BF16 = jnp.bfloat16
FAR_ROW = OWN // LANES * SAMPLES
COORD_ROW = FAR_ROW + CLUSTERS * SAMPLES // 2
COORD_ROWS = 96
PACKED_ROWS = COORD_ROW + COORD_ROWS
FEATURES = 16
CLASSES = 3
NEAR_UNROLL = 4
FAR_UNROLL = 16
RATE = math.sqrt(3.0) / 0.15

ANY = pl.BlockSpec(memory_space=pl.ANY)
VMEM = pl.BlockSpec(memory_space=pltpu.VMEM)
SMEM = pl.BlockSpec(memory_space=pltpu.SMEM)
NN = (((1,), (0,)), ((), ()))
NT = (((1,), (1,)), ((), ()))


def dot(a, b, dims=NN):
    return lax.dot_general(a, b, dims, preferred_element_type=F32)


def dot_wide(a, b):
    high = a.astype(BF16)
    low = (a - high.astype(F32)).astype(BF16)
    return dot(high, b) + dot(low, b)


def lanes(a, b):
    return jnp.concatenate([a, b], axis=1)


def rows(*parts):
    return jnp.concatenate(parts, axis=0)


def features(points):
    norm = points * points
    norm = norm[0:1] + norm[1:2] + norm[2:3]
    high = norm.astype(BF16).astype(F32)
    rest = norm - high
    middle = rest.astype(BF16).astype(F32)
    ones = jnp.ones_like(norm)
    return rows(points, high, middle, rest - middle, ones, ones)


def row_side(made):
    ones = made[6:7]
    return rows(-2.0 * made[0:3], ones, ones, ones, made[3:4], made[4:5])


def matern_of(square):
    square = jnp.maximum(square, 1e-14)
    dist = square * lax.rsqrt(square)
    e = jnp.exp2(dist * (-RATE / math.log(2.0)))
    return ((1.0 + RATE * dist) * e).astype(BF16)


def pack_kernel(probes, basis, moves, points, skeleton, packed, coords):
    near = features(points[...].astype(F32))
    far = features(lanes(skeleton[...].astype(F32), jnp.zeros((3, 64), F32)))
    chunks = [near[:, j * LANES : (j + 1) * LANES] for j in range(8)]
    chunks += [far[:, j * LANES : (j + 1) * LANES] for j in range(4)]
    made = rows(*chunks).astype(BF16)
    packed[COORD_ROW:] = made
    coords[...] = made
    leaves = []
    for l in range(4):
        part = slice(l * LEAF, (l + 1) * LEAF)
        leaves.append(dot(basis[:, part], probes[:, part], NT).astype(BF16))
    middle = [
        dot(moves[:, j * 128 : (j + 1) * 128], rows(*leaves[2 * j : 2 * j + 2])).astype(BF16)
        for j in range(2)
    ]
    top = dot(moves[:, 256:384], rows(*middle)).astype(BF16)
    for j in range(8):
        packed[j * SAMPLES : (j + 1) * SAMPLES] = probes[:, j * LANES : (j + 1) * LANES]
    packed[FAR_ROW : FAR_ROW + 64] = lanes(leaves[0], leaves[1])
    packed[FAR_ROW + 64 : FAR_ROW + 128] = lanes(leaves[2], leaves[3])
    packed[FAR_ROW + 128 : FAR_ROW + 192] = lanes(middle[0], middle[1])
    packed[FAR_ROW + 192 : FAR_ROW + 224] = lanes(top[:32], top[32:])


class Plan:
    def __init__(self, near_most, far_most):
        self.near = near_most + NEAR_UNROLL
        self.far = far_most + FAR_UNROLL
        self.far_first = -(-CLASSES * self.near // LANES) * LANES
        self.size = self.far_first + -(-CLASSES * self.far // LANES) * LANES


def iota(shape, axis):
    return lax.broadcasted_iota(jnp.int32, shape, axis)


def pick_kernel(n_y, inner, outer, out):
    z = lax.axis_index("row") // n_y
    is_inner = (z == 1) | (z == 2)

    @pl.when(is_inner)
    def _():
        out[...] = inner[...]

    @pl.when(jnp.logical_not(is_inner))
    def _():
        out[...] = outer[...]


def join_kernel(count, *refs):
    for mine, other, out in zip(refs[:count], refs[count : 2 * count], refs[2 * count :]):
        out[...] = (mine[...].astype(F32) + other[...].astype(F32)).astype(BF16)


def sort_slots(a_device, a_rest, b_device, b_rest, count, per_device, late_mask, n_col, most, width):
    slots = a_device.shape[1]
    target = a_device ^ lax.axis_index("col")
    source = b_device ^ lax.axis_index("row")
    remote = target >= 2
    is_late = lax.shift_right_logical(jnp.full_like(source, late_mask), source) & 1
    alive = iota((1, slots), 1) < count
    group = jnp.where(alive, jnp.where(remote, is_late, 2), 7)
    row = (target - jnp.where(remote, 2, 0)) * per_device + a_rest
    column = source * per_device + b_rest
    member = jnp.where(iota((8, slots), 0) == group, 1.0, 0.0)
    before = jnp.where(iota((slots, slots), 0) < iota((slots, slots), 1), 1.0, 0.0)
    ahead = dot(member.astype(BF16), before.astype(BF16))
    ahead = jnp.sum(member * ahead, axis=0, keepdims=True).astype(jnp.int32)
    place = jnp.where(alive, group * most + ahead, -1)
    chosen = jnp.where(iota((width, slots), 0) == place, 1.0, 0.0).astype(BF16)
    ones = jnp.ones((6, slots), F32)
    values = rows(row.astype(F32), column.astype(F32), ones).astype(BF16)
    found = dot(values, chosen, NT)
    here = iota((1, width), 1) >= 2 * most
    blank = jnp.where(here, 2.0 * per_device, (n_col - 2.0) * per_device)
    made = rows(found[0:1] + blank * (1.0 - found[2:3]), found[1:2])
    return made.astype(jnp.int32), jnp.sum(member, axis=1, keepdims=True).astype(jnp.int32)


def plan_kernel(n_col, late_mask, plan, slots, packed, mate, _, __, out, counts, again, both):
    again[...] = packed[...]
    both[:COORD_ROWS] = packed[COORD_ROW:]
    both[COORD_ROWS:] = mate[...]
    near_most, far_most = plan.near - NEAR_UNROLL, plan.far - FAR_UNROLL
    a, b = slots[0:1, :near_most], slots[1:2, :near_most]
    near, near_counts = sort_slots(
        lax.shift_right_logical(a, 2), a & 3, lax.shift_right_logical(b, 2), b & 3,
        slots[4:5, 0:1], 4, late_mask, n_col, plan.near, plan.far_first,
    )
    a, b = slots[2:3, :far_most], slots[3:4, :far_most]
    a_device = lax.shift_right_logical(a * 9363, 16)
    b_device = lax.shift_right_logical(b * 9363, 16)
    far, far_counts = sort_slots(
        a_device, a - a_device * CLUSTERS, b_device, b - b_device * CLUSTERS,
        slots[5:6, 0:1], CLUSTERS, late_mask, n_col, plan.far, plan.size - plan.far_first,
    )
    out[:, : plan.far_first] = near
    out[:, plan.far_first :] = far
    counts[...] = jnp.where(iota((8, LANES), 1) == 0, near_counts, far_counts)


def row_kernel(n_col, *refs):
    chips, near_row, far_row = refs[:-2], refs[-2], refs[-1]
    empty = jnp.zeros((8, LANES), F32)
    for i in range(n_col):
        first = i % 2 * COORD_ROWS
        slabs = [chips[i // 2][first + 16 * s : first + 16 * s + 16].astype(F32) for s in range(6)]
        near, far = (4 * i, CLUSTERS * i) if i < 2 else (4 * i + 1, CLUSTERS * i + 1)
        for l in range(4):
            for h in range(2):
                made = row_side(slabs[l][8 * h : 8 * h + 8])
                near_row[near + l, h * LANES : (h + 1) * LANES] = rows(made, empty).T.astype(BF16)
        for c in range(4):
            slab = slabs[4 + c // 2]
            made = row_side(slab[8 * (c % 2) : 8 * (c % 2) + 8])
            tall = rows(made, empty).T.astype(BF16)
            far_row[far + 2 * c] = tall[:64]
            if c < 3:
                far_row[far + 2 * c + 1] = tall[64:]
    for blank in (8, 4 * n_col + 1):
        near_row[blank] = jnp.zeros(near_row.shape[1:], BF16)
    for blank in (2 * CLUSTERS, CLUSTERS * n_col + 1):
        far_row[blank] = jnp.zeros(far_row.shape[1:], BF16)


def prepare(i, block, probes, near_col, coeff_low, coeff_high, far_low, far_high):
    for l in range(4):
        for h in range(2):
            j = 2 * l + h
            half = slice(h * LANES, (h + 1) * LANES)
            probes[4 * i + l, :, half] = block[j * SAMPLES : (j + 1) * SAMPLES]
        slab = block[COORD_ROW + 16 * l : COORD_ROW + 16 * (l + 1)]
        near_col[4 * i + l, :, :LANES] = slab
        near_col[4 * i + l, :, LANES:] = rows(slab[8:], slab[:8])
    slabs = [block[COORD_ROW + 64 + 16 * p : COORD_ROW + 80 + 16 * p] for p in range(2)]
    for k in range(CLUSTERS):
        c, half = k // 2, slice(k % 2 * 64, k % 2 * 64 + 64)
        if k < 6:
            own = block[FAR_ROW + 64 * c : FAR_ROW + 64 * (c + 1)][:, half]
        else:
            own = block[FAR_ROW + 192 : FAR_ROW + 224]
            own = rows(own[:, :64], own[:, 64:])
        empty = jnp.zeros_like(own)
        coeff_low[CLUSTERS * i + k] = lanes(own, empty)
        coeff_high[CLUSTERS * i + k] = lanes(empty, own)
        made = slabs[c // 2].astype(F32)[8 * (c % 2) : 8 * (c % 2) + 8, half]
        empty = jnp.zeros_like(made)
        blank = jnp.zeros((8, LANES), F32)
        far_low[CLUSTERS * i + k] = rows(lanes(made, empty), blank).astype(BF16)
        far_high[CLUSTERS * i + k] = rows(lanes(empty, made), blank).astype(BF16)


def work(plan, group, lists, counts, near_row, far_row, prepared, totals):
    probes, near_col, coeff_low, coeff_high, far_low, far_high = prepared
    near_total, far_even, far_odd = totals
    near_first, far_first = (0, 0) if group == 2 else (9, 2 * CLUSTERS + 1)

    def near_step(g, _):
        place = group * plan.near + g * NEAR_UNROLL
        terms = []
        for u in range(NEAR_UNROLL):
            a, b = lists[0, place + u], lists[1, place + u]
            parts = []
            for q in range(2):
                part = slice(q * LANES, (q + 1) * LANES)
                parts.append(matern_of(dot(near_row[near_first + a, part], near_col[b])))
            terms.append((a, dot(probes[b], rows(*parts), NT)))
        for a, term in terms:
            near_total[a] += term
        return 0

    count = counts[group, 0]
    lax.fori_loop(0, (count + NEAR_UNROLL - 1) // NEAR_UNROLL, near_step, 0)

    def far_step(g, _):
        place = plan.far_first + group * plan.far + g * FAR_UNROLL
        terms = []
        for u in range(0, FAR_UNROLL, 2):
            a0, a1 = lists[0, place + u], lists[0, place + u + 1]
            b0, b1 = lists[1, place + u], lists[1, place + u + 1]
            square = dot(far_row[far_first + a0], far_low[b0])
            square += dot(far_row[far_first + a1], far_high[b1])
            both = rows(coeff_low[b0], coeff_high[b1])
            terms.append((a0, a1, dot(matern_of(square), both)))
        for a0, a1, term in terms:
            far_even[a0] += term
            far_odd[a1] += term
        return 0

    count = counts[group, 1]
    lax.fori_loop(0, (count + FAR_UNROLL - 1) // FAR_UNROLL, far_step, 0)


def write_parts(outs, near_total, far_even, far_odd):
    for i, out in enumerate(outs):
        for j in range(8):
            half = slice(j % 2 * LANES, (j % 2 + 1) * LANES)
            part = near_total[4 * i + j // 2, :, half]
            out[j * SAMPLES : (j + 1) * SAMPLES] = part.astype(BF16)
        parts = []
        for l in range(CLUSTERS):
            even, odd = far_even[CLUSTERS * i + l], far_odd[CLUSTERS * i + l]
            parts.append(even[:, :64] + odd[:, 64:])
        for j in range(3):
            pair = lanes(*parts[2 * j : 2 * j + 2])
            out[FAR_ROW + 64 * j : FAR_ROW + 64 * (j + 1)] = pair.astype(BF16)
        pair = lanes(parts[6][:32], parts[6][32:])
        out[FAR_ROW + 192 : FAR_ROW + 224] = pair.astype(BF16)


def clear(totals):
    for total in totals:
        total[...] = jnp.zeros_like(total)


def early_kernel(plan, members, lists, counts, near_row, far_row, *refs):
    blocks, refs = refs[: len(members)], refs[len(members) :]
    prepared, totals = refs[:6], refs[6:]
    clear(totals)
    for i, block in zip(members, blocks):
        prepare(i, block, *prepared)
    work(plan, 0, lists, counts, near_row, far_row, prepared, totals)


def late_kernel(plan, members, lists, counts, near_row, far_row, *refs):
    blocks, refs = refs[: len(members)], refs[len(members) + 9 :]
    prepared, totals, outs = refs[:6], refs[6:9], refs[9:]
    for i, block in zip(members, blocks):
        prepare(i, block, *prepared)
    work(plan, 1, lists, counts, near_row, far_row, prepared, totals)
    write_parts(outs, *totals)


def here_kernel(plan, lists, counts, near_row, far_row, *refs):
    prepared, outs, totals = refs[:6], refs[7:9], refs[9:]
    clear(totals)
    work(plan, 2, lists, counts, near_row, far_row, prepared, totals)
    write_parts(outs, *totals)


def final_kernel(count, basis, moves, *refs):
    parts, out = refs[:count], refs[count]

    def total(first, count):
        return sum(part[first : first + count].astype(F32) for part in parts)

    def turned(first):
        tall = total(first, 64).T
        return lanes(tall[:64], tall[64:])

    top = total(FAR_ROW + 192, 32)
    top = rows(top[:, :64], top[:, 64:]).T
    middle = turned(FAR_ROW + 128) + dot_wide(top, moves[:, 256:384])
    for j in range(2):
        pair = turned(FAR_ROW + 64 * j) + dot_wide(
            middle[:, j * RANK : (j + 1) * RANK], moves[:, j * 128 : (j + 1) * 128]
        )
        for k in range(2):
            l = 2 * j + k
            expanded = dot_wide(
                pair[:, k * RANK : (k + 1) * RANK], basis[:, l * LEAF : (l + 1) * LEAF]
            )
            for h in range(2):
                place = (2 * l + h) * LANES
                near = total((2 * l + h) * SAMPLES, SAMPLES)
                made = near + expanded[:, h * LANES : (h + 1) * LANES]
                out[:, place : place + LANES] = made.astype(BF16)


def exchange(x, axis, offset):
    size = lax.axis_size(axis)
    return lax.ppermute(x, axis, [(i, i ^ offset) for i in range(size)])


def local(
    probes, points, skeleton, leaf_basis, transfer, near_list, near_count, far_list, far_count
):
    n_row = lax.axis_size("row")
    n_col = lax.axis_size("col")
    n_y = n_row // 4
    probes, basis, moves = probes.T, leaf_basis.T, transfer.T
    inputs = (probes, basis, moves, points, skeleton)
    small = pltpu.CompilerParams(vmem_limit_bytes=8 << 20)
    packed, coords = pl.pallas_call(
        pack_kernel,
        out_shape=[
            jax.ShapeDtypeStruct((PACKED_ROWS, LANES), BF16),
            jax.ShapeDtypeStruct((COORD_ROWS, LANES), BF16),
        ],
        in_specs=[VMEM] * 5,
        out_specs=[VMEM] * 2,
        name="pack",
    )(*inputs)

    plan = Plan(near_list.shape[-1], far_list.shape[-1])
    early = [j for j in range(n_row) if j % n_y == 0 or j < n_y]
    late = [j for j in range(n_row) if j not in early]
    late_mask = sum(1 << j for j in late)
    width = max(LANES, near_list.shape[-1], far_list.shape[-1])

    def placed(x, row):
        return jnp.pad(x, ((row, 8 - row - x.shape[0]), (0, width - x.shape[1])))

    slots = placed(near_list[0, 0], 0) + placed(far_list[0, 0], 2)
    slots = slots + placed(near_count, 4) + placed(far_count, 5)

    def along_z(x, planes, flip):
        pairs = [(z * n_y + y, (z ^ flip) * n_y + y) for z in planes for y in range(n_y)]
        return lax.ppermute(x, "row", pairs)

    own_y = exchange(packed, "row", 1)
    second = along_z(packed, (0, 1, 2, 3), 2)
    neighbour = along_z(packed, (0, 1, 2, 3), 1)
    lists, counts, again, both = pl.pallas_call(
        functools.partial(plan_kernel, n_col, np.uint32(late_mask).astype(np.int32), plan),
        out_shape=[
            jax.ShapeDtypeStruct((2, plan.size), jnp.int32),
            jax.ShapeDtypeStruct((8, LANES), jnp.int32),
            jax.ShapeDtypeStruct((PACKED_ROWS, LANES), BF16),
            jax.ShapeDtypeStruct((2 * COORD_ROWS, LANES), BF16),
        ],
        in_specs=[VMEM] * 3 + [ANY] * 2,
        out_specs=[VMEM] * 4,
        compiler_params=small,
        cost_estimate=pl.CostEstimate(flops=1 << 30, bytes_accessed=1 << 12, transcendentals=0),
        name="plan",
    )(slots, packed, exchange(coords, "col", 1), own_y, neighbour)

    third = pl.pallas_call(
        functools.partial(pick_kernel, n_y),
        out_shape=jax.ShapeDtypeStruct((PACKED_ROWS, LANES), BF16),
        in_specs=[VMEM] * 2,
        out_specs=VMEM,
        compiler_params=small,
        name="pick",
    )(along_z(again, (1, 2), 3), along_z(second, (1, 2), 1))
    blocks = []
    for z, block in enumerate((packed, neighbour, second, third)):
        blocks += [block] + ([own_y] if z == 0 else [exchange(block, "row", 1)])
        blocks += [exchange(block, "row", y) for y in range(2, n_y)]
    row_coords = [both] + [exchange(both, "col", k) for k in range(2, n_col, 2)]

    row_features = pl.pallas_call(
        functools.partial(row_kernel, n_col),
        out_shape=[
            jax.ShapeDtypeStruct((4 * n_col + 2, LEAF, FEATURES), BF16),
            jax.ShapeDtypeStruct((CLUSTERS * n_col + 2, RANK, FEATURES), BF16),
        ],
        in_specs=[VMEM] * (n_col // 2),
        out_specs=[VMEM] * 2,
        compiler_params=small,
        name="row_side",
    )(*row_coords)

    def sums(targets):
        near = (4 * targets + 1, SAMPLES, LEAF)
        far = (CLUSTERS * targets + 1, RANK, LANES)
        return [near, far, far]

    part = jax.ShapeDtypeStruct((COORD_ROW, LANES), BF16)
    held = [
        jax.ShapeDtypeStruct(shape, BF16)
        for shape in [
            (4 * n_row, SAMPLES, LEAF),
            (4 * n_row, FEATURES, LEAF),
            (CLUSTERS * n_row, RANK, LANES),
            (CLUSTERS * n_row, RANK, LANES),
            (CLUSTERS * n_row, FEATURES, LANES),
            (CLUSTERS * n_row, FEATURES, LANES),
        ]
    ]
    held += [jax.ShapeDtypeStruct(shape, F32) for shape in sums(n_col - 2)]
    params = pltpu.CompilerParams(vmem_limit_bytes=32 << 20)
    cost = pl.CostEstimate(flops=1 << 33, bytes_accessed=1 << 20, transcendentals=0)
    handed = pl.pallas_call(
        functools.partial(early_kernel, plan, early),
        out_shape=held,
        in_specs=[SMEM] * 2 + [VMEM] * (2 + len(early)),
        out_specs=[VMEM] * len(held),
        compiler_params=params,
        cost_estimate=cost,
        name="far_targets_early",
    )(lists, counts, *row_features, *[blocks[j] for j in early])
    first = 4 + len(late)
    handed = pl.pallas_call(
        functools.partial(late_kernel, plan, late),
        out_shape=held + [part] * (n_col - 2),
        in_specs=[SMEM] * 2 + [VMEM] * (first - 2 + len(held)),
        out_specs=[VMEM] * (len(held) + n_col - 2),
        input_output_aliases={first + k: k for k in range(len(held))},
        compiler_params=params,
        cost_estimate=cost,
        name="far_targets_late",
    )(lists, counts, *row_features, *[blocks[j] for j in late], *handed)
    prepared, parts = handed[:6], handed[len(held) :]
    mine, other = parts[0::2], [exchange(part, "col", 1) for part in parts[1::2]]
    joined = pl.pallas_call(
        functools.partial(join_kernel, len(mine)),
        out_shape=[part] * len(mine),
        in_specs=[VMEM] * (2 * len(mine)),
        out_specs=[VMEM] * len(mine),
        compiler_params=params,
        name="join",
    )(*mine, *other)
    arrived = [exchange(joined[k], "col", 2 * k + 2) for k in range(len(mine))]
    here = pl.pallas_call(
        functools.partial(here_kernel, plan),
        out_shape=[part] * 2,
        in_specs=[SMEM] * 2 + [VMEM] * (2 + len(prepared)) + [ANY],
        out_specs=[VMEM] * 2,
        scratch_shapes=[pltpu.VMEM(shape, F32) for shape in sums(2)],
        compiler_params=params,
        cost_estimate=cost,
        name="near_targets",
    )(lists, counts, *row_features, *prepared, joined[0])
    arrived += [here[0], exchange(here[1], "col", 1)]
    sample = pl.pallas_call(
        functools.partial(final_kernel, len(arrived)),
        out_shape=jax.ShapeDtypeStruct((SAMPLES, OWN), BF16),
        in_specs=[VMEM] * (2 + len(arrived)),
        out_specs=VMEM,
        compiler_params=pltpu.CompilerParams(vmem_limit_bytes=16 << 20),
        name="final",
    )(basis, moves, *arrived)
    return sample.T


def solution(mesh):
    placed = (
        P(("row", "col"), None),
        P(None, ("row", "col")),
        P(None, ("row", "col")),
        P(("row", "col"), None),
        P(("row", "col"), None),
        P("row", "col", None, None),
        P("row", "col"),
        P("row", "col", None, None),
        P("row", "col"),
    )
    return jax.shard_map(
        local, mesh=mesh, in_specs=placed, out_specs=P(("row", "col"), None), check_vma=False
    )
```

```python
import functools
import math

import jax
import jax.numpy as jnp
import numpy as np
from jax import lax
from jax.experimental import pallas as pl
from jax.experimental.pallas import tpu as pltpu
from jax.sharding import PartitionSpec as P

LEAF = 256
RANK = 64
SAMPLES = 64
OWN = 4 * LEAF
CLUSTERS = 7
LANES = 128
F32 = jnp.float32
BF16 = jnp.bfloat16
FAR_ROW = OWN // LANES * SAMPLES
COORD_ROW = FAR_ROW + CLUSTERS * SAMPLES // 2
COORD_ROWS = 96
PACKED_ROWS = COORD_ROW + COORD_ROWS
FEATURES = 16
CLASSES = 3
NEAR_UNROLL = 4
FAR_UNROLL = 16
RATE = math.sqrt(3.0) / 0.15

ANY = pl.BlockSpec(memory_space=pl.ANY)
VMEM = pl.BlockSpec(memory_space=pltpu.VMEM)
SMEM = pl.BlockSpec(memory_space=pltpu.SMEM)
NN = (((1,), (0,)), ((), ()))
NT = (((1,), (1,)), ((), ()))


def dot(a, b, dims=NN):
    return lax.dot_general(a, b, dims, preferred_element_type=F32)


def dot_wide(a, b):
    high = a.astype(BF16)
    low = (a - high.astype(F32)).astype(BF16)
    return dot(high, b) + dot(low, b)


def lanes(a, b):
    return jnp.concatenate([a, b], axis=1)


def rows(*parts):
    return jnp.concatenate(parts, axis=0)


def features(points):
    norm = points * points
    norm = norm[0:1] + norm[1:2] + norm[2:3]
    high = norm.astype(BF16).astype(F32)
    rest = norm - high
    middle = rest.astype(BF16).astype(F32)
    ones = jnp.ones_like(norm)
    return rows(points, high, middle, rest - middle, ones, ones)


def row_side(made):
    ones = made[6:7]
    return rows(-2.0 * made[0:3], ones, ones, ones, made[3:4], made[4:5])


def matern_of(square):
    square = jnp.maximum(square, 1e-14)
    dist = square * lax.rsqrt(square)
    e = jnp.exp2(dist * (-RATE / math.log(2.0)))
    return ((1.0 + RATE * dist) * e).astype(BF16)


def pack_kernel(probes, basis, moves, points, skeleton, packed, coords):
    near = features(points[...].astype(F32))
    far = features(lanes(skeleton[...].astype(F32), jnp.zeros((3, 64), F32)))
    chunks = [near[:, j * LANES : (j + 1) * LANES] for j in range(8)]
    chunks += [far[:, j * LANES : (j + 1) * LANES] for j in range(4)]
    made = rows(*chunks).astype(BF16)
    packed[COORD_ROW:] = made
    coords[...] = made
    leaves = []
    for l in range(4):
        part = slice(l * LEAF, (l + 1) * LEAF)
        leaves.append(dot(basis[:, part], probes[:, part], NT).astype(BF16))
    middle = [
        dot(moves[:, j * 128 : (j + 1) * 128], rows(*leaves[2 * j : 2 * j + 2])).astype(BF16)
        for j in range(2)
    ]
    top = dot(moves[:, 256:384], rows(*middle)).astype(BF16)
    for j in range(8):
        packed[j * SAMPLES : (j + 1) * SAMPLES] = probes[:, j * LANES : (j + 1) * LANES]
    packed[FAR_ROW : FAR_ROW + 64] = lanes(leaves[0], leaves[1])
    packed[FAR_ROW + 64 : FAR_ROW + 128] = lanes(leaves[2], leaves[3])
    packed[FAR_ROW + 128 : FAR_ROW + 192] = lanes(middle[0], middle[1])
    packed[FAR_ROW + 192 : FAR_ROW + 224] = lanes(top[:32], top[32:])


class Plan:
    def __init__(self, near_most, far_most):
        self.near = near_most + NEAR_UNROLL
        self.far = far_most + FAR_UNROLL
        self.far_first = -(-CLASSES * self.near // LANES) * LANES
        self.size = self.far_first + -(-CLASSES * self.far // LANES) * LANES


def iota(shape, axis):
    return lax.broadcasted_iota(jnp.int32, shape, axis)


def pick_kernel(n_y, inner, outer, out):
    z = lax.axis_index("row") // n_y
    is_inner = (z == 1) | (z == 2)

    @pl.when(is_inner)
    def _():
        out[...] = inner[...]

    @pl.when(jnp.logical_not(is_inner))
    def _():
        out[...] = outer[...]


def tie_kernel(*refs):
    del refs


def tie(x, *others):
    return pl.pallas_call(
        tie_kernel,
        out_shape=jax.ShapeDtypeStruct(x.shape, x.dtype),
        in_specs=[ANY] * (1 + len(others)),
        out_specs=ANY,
        input_output_aliases={0: 0},
        compiler_params=pltpu.CompilerParams(vmem_limit_bytes=1 << 20),
        name="tie",
    )(x, *others)


def join_kernel(count, *refs):
    for mine, other, out in zip(refs[:count], refs[count : 2 * count], refs[2 * count :]):
        out[...] = (mine[...].astype(F32) + other[...].astype(F32)).astype(BF16)


def sort_slots(a_device, a_rest, b_device, b_rest, count, per_device, late_mask, n_col, most, width):
    slots = a_device.shape[1]
    target = a_device ^ lax.axis_index("col")
    source = b_device ^ lax.axis_index("row")
    remote = target >= 2
    is_late = lax.shift_right_logical(jnp.full_like(source, late_mask), source) & 1
    alive = iota((1, slots), 1) < count
    group = jnp.where(alive, jnp.where(remote, is_late, 2), 7)
    row = (target - jnp.where(remote, 2, 0)) * per_device + a_rest
    column = source * per_device + b_rest
    member = jnp.where(iota((8, slots), 0) == group, 1.0, 0.0)
    before = jnp.where(iota((slots, slots), 0) < iota((slots, slots), 1), 1.0, 0.0)
    ahead = dot(member.astype(BF16), before.astype(BF16))
    ahead = jnp.sum(member * ahead, axis=0, keepdims=True).astype(jnp.int32)
    place = jnp.where(alive, group * most + ahead, -1)
    chosen = jnp.where(iota((width, slots), 0) == place, 1.0, 0.0).astype(BF16)
    ones = jnp.ones((6, slots), F32)
    values = rows(row.astype(F32), column.astype(F32), ones).astype(BF16)
    found = dot(values, chosen, NT)
    here = iota((1, width), 1) >= 2 * most
    blank = jnp.where(here, 2.0 * per_device, (n_col - 2.0) * per_device)
    made = rows(found[0:1] + blank * (1.0 - found[2:3]), found[1:2])
    return made.astype(jnp.int32), jnp.sum(member, axis=1, keepdims=True).astype(jnp.int32)


def plan_kernel(n_col, late_mask, plan, slots, packed, mate, _, __, out, counts, again, both):
    again[...] = packed[...]
    both[:COORD_ROWS] = packed[COORD_ROW:]
    both[COORD_ROWS:] = mate[...]
    near_most, far_most = plan.near - NEAR_UNROLL, plan.far - FAR_UNROLL
    a, b = slots[0:1, :near_most], slots[1:2, :near_most]
    near, near_counts = sort_slots(
        lax.shift_right_logical(a, 2), a & 3, lax.shift_right_logical(b, 2), b & 3,
        slots[4:5, 0:1], 4, late_mask, n_col, plan.near, plan.far_first,
    )
    a, b = slots[2:3, :far_most], slots[3:4, :far_most]
    a_device = lax.shift_right_logical(a * 9363, 16)
    b_device = lax.shift_right_logical(b * 9363, 16)
    far, far_counts = sort_slots(
        a_device, a - a_device * CLUSTERS, b_device, b - b_device * CLUSTERS,
        slots[5:6, 0:1], CLUSTERS, late_mask, n_col, plan.far, plan.size - plan.far_first,
    )
    out[:, : plan.far_first] = near
    out[:, plan.far_first :] = far
    counts[...] = jnp.where(iota((8, LANES), 1) == 0, near_counts, far_counts)


def row_kernel(n_col, *refs):
    chips, near_row, far_row = refs[:-2], refs[-2], refs[-1]
    empty = jnp.zeros((8, LANES), F32)
    for i in range(n_col):
        first = i % 2 * COORD_ROWS
        slabs = [chips[i // 2][first + 16 * s : first + 16 * s + 16].astype(F32) for s in range(6)]
        near, far = (4 * i, CLUSTERS * i) if i < 2 else (4 * i + 1, CLUSTERS * i + 1)
        for l in range(4):
            for h in range(2):
                made = row_side(slabs[l][8 * h : 8 * h + 8])
                near_row[near + l, h * LANES : (h + 1) * LANES] = rows(made, empty).T.astype(BF16)
        for c in range(4):
            slab = slabs[4 + c // 2]
            made = row_side(slab[8 * (c % 2) : 8 * (c % 2) + 8])
            tall = rows(made, empty).T.astype(BF16)
            far_row[far + 2 * c] = tall[:64]
            if c < 3:
                far_row[far + 2 * c + 1] = tall[64:]
    for blank in (8, 4 * n_col + 1):
        near_row[blank] = jnp.zeros(near_row.shape[1:], BF16)
    for blank in (2 * CLUSTERS, CLUSTERS * n_col + 1):
        far_row[blank] = jnp.zeros(far_row.shape[1:], BF16)


def prepare(i, block, probes, near_col, coeff_low, coeff_high, far_low, far_high):
    for l in range(4):
        for h in range(2):
            j = 2 * l + h
            half = slice(h * LANES, (h + 1) * LANES)
            probes[4 * i + l, :, half] = block[j * SAMPLES : (j + 1) * SAMPLES]
        slab = block[COORD_ROW + 16 * l : COORD_ROW + 16 * (l + 1)]
        near_col[4 * i + l, :, :LANES] = slab
        near_col[4 * i + l, :, LANES:] = rows(slab[8:], slab[:8])
    slabs = [block[COORD_ROW + 64 + 16 * p : COORD_ROW + 80 + 16 * p] for p in range(2)]
    for k in range(CLUSTERS):
        c, half = k // 2, slice(k % 2 * 64, k % 2 * 64 + 64)
        if k < 6:
            own = block[FAR_ROW + 64 * c : FAR_ROW + 64 * (c + 1)][:, half]
        else:
            own = block[FAR_ROW + 192 : FAR_ROW + 224]
            own = rows(own[:, :64], own[:, 64:])
        empty = jnp.zeros_like(own)
        coeff_low[CLUSTERS * i + k] = lanes(own, empty)
        coeff_high[CLUSTERS * i + k] = lanes(empty, own)
        made = slabs[c // 2].astype(F32)[8 * (c % 2) : 8 * (c % 2) + 8, half]
        empty = jnp.zeros_like(made)
        blank = jnp.zeros((8, LANES), F32)
        far_low[CLUSTERS * i + k] = rows(lanes(made, empty), blank).astype(BF16)
        far_high[CLUSTERS * i + k] = rows(lanes(empty, made), blank).astype(BF16)


def work(plan, group, lists, counts, near_row, far_row, prepared, totals):
    probes, near_col, coeff_low, coeff_high, far_low, far_high = prepared
    near_total, far_even, far_odd = totals
    near_first, far_first = (0, 0) if group == 2 else (9, 2 * CLUSTERS + 1)

    def near_step(g, _):
        place = group * plan.near + g * NEAR_UNROLL
        terms = []
        for u in range(NEAR_UNROLL):
            a, b = lists[0, place + u], lists[1, place + u]
            parts = []
            for q in range(2):
                part = slice(q * LANES, (q + 1) * LANES)
                parts.append(matern_of(dot(near_row[near_first + a, part], near_col[b])))
            terms.append((a, dot(probes[b], rows(*parts), NT)))
        for a, term in terms:
            near_total[a] += term
        return 0

    count = counts[group, 0]
    lax.fori_loop(0, (count + NEAR_UNROLL - 1) // NEAR_UNROLL, near_step, 0)

    def far_step(g, _):
        place = plan.far_first + group * plan.far + g * FAR_UNROLL
        terms = []
        for u in range(0, FAR_UNROLL, 2):
            a0, a1 = lists[0, place + u], lists[0, place + u + 1]
            b0, b1 = lists[1, place + u], lists[1, place + u + 1]
            square = dot(far_row[far_first + a0], far_low[b0])
            square += dot(far_row[far_first + a1], far_high[b1])
            both = rows(coeff_low[b0], coeff_high[b1])
            terms.append((a0, a1, dot(matern_of(square), both)))
        for a0, a1, term in terms:
            far_even[a0] += term
            far_odd[a1] += term
        return 0

    count = counts[group, 1]
    lax.fori_loop(0, (count + FAR_UNROLL - 1) // FAR_UNROLL, far_step, 0)


def write_parts(outs, near_total, far_even, far_odd):
    for i, out in enumerate(outs):
        for j in range(8):
            half = slice(j % 2 * LANES, (j % 2 + 1) * LANES)
            part = near_total[4 * i + j // 2, :, half]
            out[j * SAMPLES : (j + 1) * SAMPLES] = part.astype(BF16)
        parts = []
        for l in range(CLUSTERS):
            even, odd = far_even[CLUSTERS * i + l], far_odd[CLUSTERS * i + l]
            parts.append(even[:, :64] + odd[:, 64:])
        for j in range(3):
            pair = lanes(*parts[2 * j : 2 * j + 2])
            out[FAR_ROW + 64 * j : FAR_ROW + 64 * (j + 1)] = pair.astype(BF16)
        pair = lanes(parts[6][:32], parts[6][32:])
        out[FAR_ROW + 192 : FAR_ROW + 224] = pair.astype(BF16)


def clear(totals):
    for total in totals:
        total[...] = jnp.zeros_like(total)


def early_kernel(plan, members, lists, counts, near_row, far_row, *refs):
    blocks, refs = refs[: len(members)], refs[len(members) :]
    prepared, totals = refs[:6], refs[6:]
    clear(totals)
    for i, block in zip(members, blocks):
        prepare(i, block, *prepared)
    work(plan, 0, lists, counts, near_row, far_row, prepared, totals)


def late_kernel(plan, members, lists, counts, near_row, far_row, *refs):
    blocks, refs = refs[: len(members)], refs[len(members) + 9 :]
    prepared, totals, outs = refs[:6], refs[6:9], refs[9:]
    for i, block in zip(members, blocks):
        prepare(i, block, *prepared)
    work(plan, 1, lists, counts, near_row, far_row, prepared, totals)
    write_parts(outs, *totals)


def here_kernel(plan, lists, counts, near_row, far_row, *refs):
    prepared, outs, totals = refs[:6], refs[7:9], refs[9:]
    clear(totals)
    work(plan, 2, lists, counts, near_row, far_row, prepared, totals)
    write_parts(outs, *totals)


def final_kernel(count, basis, moves, *refs):
    parts, out = refs[:count], refs[count]

    def total(first, count):
        return sum(part[first : first + count].astype(F32) for part in parts)

    def turned(first):
        tall = total(first, 64).T
        return lanes(tall[:64], tall[64:])

    top = total(FAR_ROW + 192, 32)
    top = rows(top[:, :64], top[:, 64:]).T
    middle = turned(FAR_ROW + 128) + dot_wide(top, moves[:, 256:384])
    for j in range(2):
        pair = turned(FAR_ROW + 64 * j) + dot_wide(
            middle[:, j * RANK : (j + 1) * RANK], moves[:, j * 128 : (j + 1) * 128]
        )
        for k in range(2):
            l = 2 * j + k
            expanded = dot_wide(
                pair[:, k * RANK : (k + 1) * RANK], basis[:, l * LEAF : (l + 1) * LEAF]
            )
            for h in range(2):
                place = (2 * l + h) * LANES
                near = total((2 * l + h) * SAMPLES, SAMPLES)
                made = near + expanded[:, h * LANES : (h + 1) * LANES]
                out[:, place : place + LANES] = made.astype(BF16)


def exchange(x, axis, offset):
    size = lax.axis_size(axis)
    return lax.ppermute(x, axis, [(i, i ^ offset) for i in range(size)])


def local(
    probes, points, skeleton, leaf_basis, transfer, near_list, near_count, far_list, far_count
):
    n_row = lax.axis_size("row")
    n_col = lax.axis_size("col")
    n_y = n_row // 4
    probes, basis, moves = probes.T, leaf_basis.T, transfer.T
    inputs = (probes, basis, moves, points, skeleton)
    small = pltpu.CompilerParams(vmem_limit_bytes=8 << 20)
    packed, coords = pl.pallas_call(
        pack_kernel,
        out_shape=[
            jax.ShapeDtypeStruct((PACKED_ROWS, LANES), BF16),
            jax.ShapeDtypeStruct((COORD_ROWS, LANES), BF16),
        ],
        in_specs=[VMEM] * 5,
        out_specs=[VMEM] * 2,
        name="pack",
    )(*inputs)

    plan = Plan(near_list.shape[-1], far_list.shape[-1])
    early = [j for j in range(n_row) if j % n_y == 0 or j < n_y]
    late = [j for j in range(n_row) if j not in early]
    late_mask = sum(1 << j for j in late)
    width = max(LANES, near_list.shape[-1], far_list.shape[-1])

    def placed(x, row):
        return jnp.pad(x, ((row, 8 - row - x.shape[0]), (0, width - x.shape[1])))

    slots = placed(near_list[0, 0], 0) + placed(far_list[0, 0], 2)
    slots = slots + placed(near_count, 4) + placed(far_count, 5)

    def along_z(x, planes, flip):
        pairs = [(z * n_y + y, (z ^ flip) * n_y + y) for z in planes for y in range(n_y)]
        return lax.ppermute(x, "row", pairs)

    own_y = exchange(packed, "row", 1)
    second = along_z(packed, (0, 1, 2, 3), 2)
    neighbour = along_z(packed, (0, 1, 2, 3), 1)
    lists, counts, again, both = pl.pallas_call(
        functools.partial(plan_kernel, n_col, np.uint32(late_mask).astype(np.int32), plan),
        out_shape=[
            jax.ShapeDtypeStruct((2, plan.size), jnp.int32),
            jax.ShapeDtypeStruct((8, LANES), jnp.int32),
            jax.ShapeDtypeStruct((PACKED_ROWS, LANES), BF16),
            jax.ShapeDtypeStruct((2 * COORD_ROWS, LANES), BF16),
        ],
        in_specs=[VMEM] * 3 + [ANY] * 2,
        out_specs=[VMEM] * 4,
        compiler_params=small,
        cost_estimate=pl.CostEstimate(flops=1 << 30, bytes_accessed=1 << 12, transcendentals=0),
        name="plan",
    )(slots, packed, exchange(coords, "col", 1), own_y, neighbour)

    neighbour_y = exchange(neighbour, "row", 1)
    row_coords = [both] + [exchange(both, "col", k) for k in range(2, n_col, 2)]
    second = tie(second, neighbour_y, *row_coords[1:])
    third = pl.pallas_call(
        functools.partial(pick_kernel, n_y),
        out_shape=jax.ShapeDtypeStruct((PACKED_ROWS, LANES), BF16),
        in_specs=[VMEM] * 2,
        out_specs=VMEM,
        compiler_params=small,
        name="pick",
    )(along_z(again, (1, 2), 3), along_z(second, (1, 2), 1))
    blocks = []
    for z, block in enumerate((packed, neighbour, second, third)):
        blocks += [block] + ([own_y, neighbour_y][z : z + 1] or [exchange(block, "row", 1)])
        blocks += [exchange(block, "row", y) for y in range(2, n_y)]

    row_features = pl.pallas_call(
        functools.partial(row_kernel, n_col),
        out_shape=[
            jax.ShapeDtypeStruct((4 * n_col + 2, LEAF, FEATURES), BF16),
            jax.ShapeDtypeStruct((CLUSTERS * n_col + 2, RANK, FEATURES), BF16),
        ],
        in_specs=[VMEM] * (n_col // 2),
        out_specs=[VMEM] * 2,
        compiler_params=small,
        name="row_side",
    )(*row_coords)

    def sums(targets):
        near = (4 * targets + 1, SAMPLES, LEAF)
        far = (CLUSTERS * targets + 1, RANK, LANES)
        return [near, far, far]

    part = jax.ShapeDtypeStruct((COORD_ROW, LANES), BF16)
    held = [
        jax.ShapeDtypeStruct(shape, BF16)
        for shape in [
            (4 * n_row, SAMPLES, LEAF),
            (4 * n_row, FEATURES, LEAF),
            (CLUSTERS * n_row, RANK, LANES),
            (CLUSTERS * n_row, RANK, LANES),
            (CLUSTERS * n_row, FEATURES, LANES),
            (CLUSTERS * n_row, FEATURES, LANES),
        ]
    ]
    held += [jax.ShapeDtypeStruct(shape, F32) for shape in sums(n_col - 2)]
    params = pltpu.CompilerParams(vmem_limit_bytes=32 << 20)
    cost = pl.CostEstimate(flops=1 << 33, bytes_accessed=1 << 20, transcendentals=0)
    handed = pl.pallas_call(
        functools.partial(early_kernel, plan, early),
        out_shape=held,
        in_specs=[SMEM] * 2 + [VMEM] * (2 + len(early)),
        out_specs=[VMEM] * len(held),
        compiler_params=params,
        cost_estimate=cost,
        name="far_targets_early",
    )(lists, counts, *row_features, *[blocks[j] for j in early])
    first = 4 + len(late)
    handed = pl.pallas_call(
        functools.partial(late_kernel, plan, late),
        out_shape=held + [part] * (n_col - 2),
        in_specs=[SMEM] * 2 + [VMEM] * (first - 2 + len(held)),
        out_specs=[VMEM] * (len(held) + n_col - 2),
        input_output_aliases={first + k: k for k in range(len(held))},
        compiler_params=params,
        cost_estimate=cost,
        name="far_targets_late",
    )(lists, counts, *row_features, *[blocks[j] for j in late], *handed)
    prepared, parts = handed[:6], handed[len(held) :]
    mine, other = parts[0::2], [exchange(part, "col", 1) for part in parts[1::2]]
    joined = pl.pallas_call(
        functools.partial(join_kernel, len(mine)),
        out_shape=[part] * len(mine),
        in_specs=[VMEM] * (2 * len(mine)),
        out_specs=[VMEM] * len(mine),
        compiler_params=params,
        name="join",
    )(*mine, *other)
    arrived = [exchange(joined[k], "col", 2 * k + 2) for k in range(len(mine))]
    here = pl.pallas_call(
        functools.partial(here_kernel, plan),
        out_shape=[part] * 2,
        in_specs=[SMEM] * 2 + [VMEM] * (2 + len(prepared)) + [ANY],
        out_specs=[VMEM] * 2,
        scratch_shapes=[pltpu.VMEM(shape, F32) for shape in sums(2)],
        compiler_params=params,
        cost_estimate=cost,
        name="near_targets",
    )(lists, counts, *row_features, *prepared, joined[0])
    arrived += [here[0], exchange(tie(here[1], *arrived), "col", 1)]
    sample = pl.pallas_call(
        functools.partial(final_kernel, len(arrived)),
        out_shape=jax.ShapeDtypeStruct((SAMPLES, OWN), BF16),
        in_specs=[VMEM] * (2 + len(arrived)),
        out_specs=VMEM,
        compiler_params=pltpu.CompilerParams(vmem_limit_bytes=16 << 20),
        name="final",
    )(basis, moves, *arrived)
    return sample.T


def solution(mesh):
    placed = (
        P(("row", "col"), None),
        P(None, ("row", "col")),
        P(None, ("row", "col")),
        P(("row", "col"), None),
        P(("row", "col"), None),
        P("row", "col", None, None),
        P("row", "col"),
        P("row", "col", None, None),
        P("row", "col"),
    )
    return jax.shard_map(
        local, mesh=mesh, in_specs=placed, out_specs=P(("row", "col"), None), check_vma=False
    )
```

```python
import functools
import math

import jax
import jax.numpy as jnp
import numpy as np
from jax import lax
from jax.experimental import pallas as pl
from jax.experimental.pallas import tpu as pltpu
from jax.sharding import PartitionSpec as P

LEAF = 256
RANK = 64
SAMPLES = 64
OWN = 4 * LEAF
CLUSTERS = 7
LANES = 128
F32 = jnp.float32
BF16 = jnp.bfloat16
FAR_ROW = OWN // LANES * SAMPLES
COORD_ROW = FAR_ROW + CLUSTERS * SAMPLES // 2
COORD_ROWS = 96
PACKED_ROWS = COORD_ROW + COORD_ROWS
FEATURES = 16
CLASSES = 3
NEAR_UNROLL = 4
FAR_UNROLL = 16
RATE = math.sqrt(3.0) / 0.15

ANY = pl.BlockSpec(memory_space=pl.ANY)
VMEM = pl.BlockSpec(memory_space=pltpu.VMEM)
SMEM = pl.BlockSpec(memory_space=pltpu.SMEM)
NN = (((1,), (0,)), ((), ()))
NT = (((1,), (1,)), ((), ()))


def dot(a, b, dims=NN):
    return lax.dot_general(a, b, dims, preferred_element_type=F32)


def dot_wide(a, b):
    high = a.astype(BF16)
    low = (a - high.astype(F32)).astype(BF16)
    return dot(high, b) + dot(low, b)


def lanes(a, b):
    return jnp.concatenate([a, b], axis=1)


def rows(*parts):
    return jnp.concatenate(parts, axis=0)


def features(points):
    norm = points * points
    norm = norm[0:1] + norm[1:2] + norm[2:3]
    high = norm.astype(BF16).astype(F32)
    rest = norm - high
    middle = rest.astype(BF16).astype(F32)
    ones = jnp.ones_like(norm)
    return rows(points, high, middle, rest - middle, ones, ones)


def row_side(made):
    ones = made[6:7]
    return rows(-2.0 * made[0:3], ones, ones, ones, made[3:4], made[4:5])


def matern_of(square):
    square = jnp.maximum(square, 1e-14)
    dist = square * lax.rsqrt(square)
    e = jnp.exp2(dist * (-RATE / math.log(2.0)))
    return ((1.0 + RATE * dist) * e).astype(BF16)


def pack_kernel(probes, basis, moves, points, skeleton, packed, coords):
    near = features(points[...].astype(F32))
    far = features(lanes(skeleton[...].astype(F32), jnp.zeros((3, 64), F32)))
    chunks = [near[:, j * LANES : (j + 1) * LANES] for j in range(8)]
    chunks += [far[:, j * LANES : (j + 1) * LANES] for j in range(4)]
    made = rows(*chunks).astype(BF16)
    packed[COORD_ROW:] = made
    coords[...] = made
    leaves = []
    for l in range(4):
        part = slice(l * LEAF, (l + 1) * LEAF)
        leaves.append(dot(basis[:, part], probes[:, part], NT).astype(BF16))
    middle = [
        dot(moves[:, j * 128 : (j + 1) * 128], rows(*leaves[2 * j : 2 * j + 2])).astype(BF16)
        for j in range(2)
    ]
    top = dot(moves[:, 256:384], rows(*middle)).astype(BF16)
    for j in range(8):
        packed[j * SAMPLES : (j + 1) * SAMPLES] = probes[:, j * LANES : (j + 1) * LANES]
    packed[FAR_ROW : FAR_ROW + 64] = lanes(leaves[0], leaves[1])
    packed[FAR_ROW + 64 : FAR_ROW + 128] = lanes(leaves[2], leaves[3])
    packed[FAR_ROW + 128 : FAR_ROW + 192] = lanes(middle[0], middle[1])
    packed[FAR_ROW + 192 : FAR_ROW + 224] = lanes(top[:32], top[32:])


class Plan:
    def __init__(self, near_most, far_most):
        self.near = near_most + NEAR_UNROLL
        self.far = far_most + FAR_UNROLL
        self.far_first = -(-CLASSES * self.near // LANES) * LANES
        self.size = self.far_first + -(-CLASSES * self.far // LANES) * LANES


def iota(shape, axis):
    return lax.broadcasted_iota(jnp.int32, shape, axis)


def pick_kernel(n_y, inner, outer, out):
    z = lax.axis_index("row") // n_y
    is_inner = (z == 1) | (z == 2)

    @pl.when(is_inner)
    def _():
        out[...] = inner[...]

    @pl.when(jnp.logical_not(is_inner))
    def _():
        out[...] = outer[...]


def tie_kernel(*refs):
    del refs


def tie(x, *others):
    return pl.pallas_call(
        tie_kernel,
        out_shape=jax.ShapeDtypeStruct(x.shape, x.dtype),
        in_specs=[ANY] * (1 + len(others)),
        out_specs=ANY,
        input_output_aliases={0: 0},
        compiler_params=pltpu.CompilerParams(vmem_limit_bytes=1 << 20),
        name="tie",
    )(x, *others)


def join_kernel(count, *refs):
    for mine, other, out in zip(refs[:count], refs[count : 2 * count], refs[2 * count :]):
        out[...] = (mine[...].astype(F32) + other[...].astype(F32)).astype(BF16)


def sort_slots(a_device, a_rest, b_device, b_rest, count, per_device, late_mask, n_col, most, width):
    slots = a_device.shape[1]
    target = a_device ^ lax.axis_index("col")
    source = b_device ^ lax.axis_index("row")
    remote = target >= 2
    is_late = lax.shift_right_logical(jnp.full_like(source, late_mask), source) & 1
    alive = iota((1, slots), 1) < count
    group = jnp.where(alive, jnp.where(remote, is_late, 2), 7)
    row = (target - jnp.where(remote, 2, 0)) * per_device + a_rest
    column = source * per_device + b_rest
    member = jnp.where(iota((8, slots), 0) == group, 1.0, 0.0)
    before = jnp.where(iota((slots, slots), 0) < iota((slots, slots), 1), 1.0, 0.0)
    ahead = dot(member.astype(BF16), before.astype(BF16))
    ahead = jnp.sum(member * ahead, axis=0, keepdims=True).astype(jnp.int32)
    place = jnp.where(alive, group * most + ahead, -1)
    chosen = jnp.where(iota((width, slots), 0) == place, 1.0, 0.0).astype(BF16)
    ones = jnp.ones((6, slots), F32)
    values = rows(row.astype(F32), column.astype(F32), ones).astype(BF16)
    found = dot(values, chosen, NT)
    here = iota((1, width), 1) >= 2 * most
    blank = jnp.where(here, 2.0 * per_device, (n_col - 2.0) * per_device)
    made = rows(found[0:1] + blank * (1.0 - found[2:3]), found[1:2])
    return made.astype(jnp.int32), jnp.sum(member, axis=1, keepdims=True).astype(jnp.int32)


def hold_kernel(packed, _, __, out):
    out[...] = packed[...]


def plan_kernel(n_col, late_mask, plan, slots, coords, mate, out, counts, both):
    both[:COORD_ROWS] = coords[...]
    both[COORD_ROWS:] = mate[...]
    near_most, far_most = plan.near - NEAR_UNROLL, plan.far - FAR_UNROLL
    a, b = slots[0:1, :near_most], slots[1:2, :near_most]
    near, near_counts = sort_slots(
        lax.shift_right_logical(a, 2), a & 3, lax.shift_right_logical(b, 2), b & 3,
        slots[4:5, 0:1], 4, late_mask, n_col, plan.near, plan.far_first,
    )
    a, b = slots[2:3, :far_most], slots[3:4, :far_most]
    a_device = lax.shift_right_logical(a * 9363, 16)
    b_device = lax.shift_right_logical(b * 9363, 16)
    far, far_counts = sort_slots(
        a_device, a - a_device * CLUSTERS, b_device, b - b_device * CLUSTERS,
        slots[5:6, 0:1], CLUSTERS, late_mask, n_col, plan.far, plan.size - plan.far_first,
    )
    out[:, : plan.far_first] = near
    out[:, plan.far_first :] = far
    counts[...] = jnp.where(iota((8, LANES), 1) == 0, near_counts, far_counts)


def row_kernel(n_col, *refs):
    chips, near_row, far_row = refs[:-2], refs[-2], refs[-1]
    empty = jnp.zeros((8, LANES), F32)
    for i in range(n_col):
        first = i % 2 * COORD_ROWS
        slabs = [chips[i // 2][first + 16 * s : first + 16 * s + 16].astype(F32) for s in range(6)]
        near, far = (4 * i, CLUSTERS * i) if i < 2 else (4 * i + 1, CLUSTERS * i + 1)
        for l in range(4):
            for h in range(2):
                made = row_side(slabs[l][8 * h : 8 * h + 8])
                near_row[near + l, h * LANES : (h + 1) * LANES] = rows(made, empty).T.astype(BF16)
        for c in range(4):
            slab = slabs[4 + c // 2]
            made = row_side(slab[8 * (c % 2) : 8 * (c % 2) + 8])
            tall = rows(made, empty).T.astype(BF16)
            far_row[far + 2 * c] = tall[:64]
            if c < 3:
                far_row[far + 2 * c + 1] = tall[64:]
    for blank in (8, 4 * n_col + 1):
        near_row[blank] = jnp.zeros(near_row.shape[1:], BF16)
    for blank in (2 * CLUSTERS, CLUSTERS * n_col + 1):
        far_row[blank] = jnp.zeros(far_row.shape[1:], BF16)


def prepare(i, block, probes, near_col, coeff_low, coeff_high, far_low, far_high):
    for l in range(4):
        for h in range(2):
            j = 2 * l + h
            half = slice(h * LANES, (h + 1) * LANES)
            probes[4 * i + l, :, half] = block[j * SAMPLES : (j + 1) * SAMPLES]
        slab = block[COORD_ROW + 16 * l : COORD_ROW + 16 * (l + 1)]
        near_col[4 * i + l, :, :LANES] = slab
        near_col[4 * i + l, :, LANES:] = rows(slab[8:], slab[:8])
    slabs = [block[COORD_ROW + 64 + 16 * p : COORD_ROW + 80 + 16 * p] for p in range(2)]
    for k in range(CLUSTERS):
        c, half = k // 2, slice(k % 2 * 64, k % 2 * 64 + 64)
        if k < 6:
            own = block[FAR_ROW + 64 * c : FAR_ROW + 64 * (c + 1)][:, half]
        else:
            own = block[FAR_ROW + 192 : FAR_ROW + 224]
            own = rows(own[:, :64], own[:, 64:])
        empty = jnp.zeros_like(own)
        coeff_low[CLUSTERS * i + k] = lanes(own, empty)
        coeff_high[CLUSTERS * i + k] = lanes(empty, own)
        made = slabs[c // 2].astype(F32)[8 * (c % 2) : 8 * (c % 2) + 8, half]
        empty = jnp.zeros_like(made)
        blank = jnp.zeros((8, LANES), F32)
        far_low[CLUSTERS * i + k] = rows(lanes(made, empty), blank).astype(BF16)
        far_high[CLUSTERS * i + k] = rows(lanes(empty, made), blank).astype(BF16)


def work(plan, group, lists, counts, near_row, far_row, prepared, totals):
    probes, near_col, coeff_low, coeff_high, far_low, far_high = prepared
    near_total, far_even, far_odd = totals
    near_first, far_first = (0, 0) if group == 2 else (9, 2 * CLUSTERS + 1)

    def near_step(g, _):
        place = group * plan.near + g * NEAR_UNROLL
        terms = []
        for u in range(NEAR_UNROLL):
            a, b = lists[0, place + u], lists[1, place + u]
            parts = []
            for q in range(2):
                part = slice(q * LANES, (q + 1) * LANES)
                parts.append(matern_of(dot(near_row[near_first + a, part], near_col[b])))
            terms.append((a, dot(probes[b], rows(*parts), NT)))
        for a, term in terms:
            near_total[a] += term
        return 0

    count = counts[group, 0]
    lax.fori_loop(0, (count + NEAR_UNROLL - 1) // NEAR_UNROLL, near_step, 0)

    def far_step(g, _):
        place = plan.far_first + group * plan.far + g * FAR_UNROLL
        terms = []
        for u in range(0, FAR_UNROLL, 2):
            a0, a1 = lists[0, place + u], lists[0, place + u + 1]
            b0, b1 = lists[1, place + u], lists[1, place + u + 1]
            square = dot(far_row[far_first + a0], far_low[b0])
            square += dot(far_row[far_first + a1], far_high[b1])
            both = rows(coeff_low[b0], coeff_high[b1])
            terms.append((a0, a1, dot(matern_of(square), both)))
        for a0, a1, term in terms:
            far_even[a0] += term
            far_odd[a1] += term
        return 0

    count = counts[group, 1]
    lax.fori_loop(0, (count + FAR_UNROLL - 1) // FAR_UNROLL, far_step, 0)


def write_parts(outs, near_total, far_even, far_odd):
    for i, out in enumerate(outs):
        for j in range(8):
            half = slice(j % 2 * LANES, (j % 2 + 1) * LANES)
            part = near_total[4 * i + j // 2, :, half]
            out[j * SAMPLES : (j + 1) * SAMPLES] = part.astype(BF16)
        parts = []
        for l in range(CLUSTERS):
            even, odd = far_even[CLUSTERS * i + l], far_odd[CLUSTERS * i + l]
            parts.append(even[:, :64] + odd[:, 64:])
        for j in range(3):
            pair = lanes(*parts[2 * j : 2 * j + 2])
            out[FAR_ROW + 64 * j : FAR_ROW + 64 * (j + 1)] = pair.astype(BF16)
        pair = lanes(parts[6][:32], parts[6][32:])
        out[FAR_ROW + 192 : FAR_ROW + 224] = pair.astype(BF16)


def clear(totals):
    for total in totals:
        total[...] = jnp.zeros_like(total)


def early_kernel(plan, members, lists, counts, near_row, far_row, *refs):
    blocks, refs = refs[: len(members)], refs[len(members) :]
    prepared, totals = refs[:6], refs[6:]
    clear(totals)
    for i, block in zip(members, blocks):
        prepare(i, block, *prepared)
    work(plan, 0, lists, counts, near_row, far_row, prepared, totals)


def late_kernel(plan, members, lists, counts, near_row, far_row, *refs):
    blocks, refs = refs[: len(members)], refs[len(members) + 9 :]
    prepared, totals, outs = refs[:6], refs[6:9], refs[9:]
    for i, block in zip(members, blocks):
        prepare(i, block, *prepared)
    work(plan, 1, lists, counts, near_row, far_row, prepared, totals)
    write_parts(outs, *totals)


def here_kernel(plan, lists, counts, near_row, far_row, *refs):
    prepared, outs, totals = refs[:6], refs[7:9], refs[9:]
    clear(totals)
    work(plan, 2, lists, counts, near_row, far_row, prepared, totals)
    write_parts(outs, *totals)


def final_kernel(count, basis, moves, *refs):
    parts, out = refs[:count], refs[count]

    def total(first, count):
        return sum(part[first : first + count].astype(F32) for part in parts)

    def turned(first):
        tall = total(first, 64).T
        return lanes(tall[:64], tall[64:])

    top = total(FAR_ROW + 192, 32)
    top = rows(top[:, :64], top[:, 64:]).T
    middle = turned(FAR_ROW + 128) + dot_wide(top, moves[:, 256:384])
    for j in range(2):
        pair = turned(FAR_ROW + 64 * j) + dot_wide(
            middle[:, j * RANK : (j + 1) * RANK], moves[:, j * 128 : (j + 1) * 128]
        )
        for k in range(2):
            l = 2 * j + k
            expanded = dot_wide(
                pair[:, k * RANK : (k + 1) * RANK], basis[:, l * LEAF : (l + 1) * LEAF]
            )
            for h in range(2):
                place = (2 * l + h) * LANES
                near = total((2 * l + h) * SAMPLES, SAMPLES)
                made = near + expanded[:, h * LANES : (h + 1) * LANES]
                out[:, place : place + LANES] = made.astype(BF16)


def exchange(x, axis, offset):
    size = lax.axis_size(axis)
    return lax.ppermute(x, axis, [(i, i ^ offset) for i in range(size)])


def local(
    probes, points, skeleton, leaf_basis, transfer, near_list, near_count, far_list, far_count
):
    n_row = lax.axis_size("row")
    n_col = lax.axis_size("col")
    n_y = n_row // 4
    probes, basis, moves = probes.T, leaf_basis.T, transfer.T
    inputs = (probes, basis, moves, points, skeleton)
    small = pltpu.CompilerParams(vmem_limit_bytes=8 << 20)
    packed, coords = pl.pallas_call(
        pack_kernel,
        out_shape=[
            jax.ShapeDtypeStruct((PACKED_ROWS, LANES), BF16),
            jax.ShapeDtypeStruct((COORD_ROWS, LANES), BF16),
        ],
        in_specs=[VMEM] * 5,
        out_specs=[VMEM] * 2,
        name="pack",
    )(*inputs)

    plan = Plan(near_list.shape[-1], far_list.shape[-1])
    early = [j for j in range(n_row) if j % n_y == 0 or j < n_y]
    late = [j for j in range(n_row) if j not in early]
    late_mask = sum(1 << j for j in late)
    width = max(LANES, near_list.shape[-1], far_list.shape[-1])

    def placed(x, row):
        return jnp.pad(x, ((row, 8 - row - x.shape[0]), (0, width - x.shape[1])))

    slots = placed(near_list[0, 0], 0) + placed(far_list[0, 0], 2)
    slots = slots + placed(near_count, 4) + placed(far_count, 5)

    def along_z(x, planes, flip):
        pairs = [(z * n_y + y, (z ^ flip) * n_y + y) for z in planes for y in range(n_y)]
        return lax.ppermute(x, "row", pairs)

    own_y = exchange(packed, "row", 1)
    second = along_z(packed, (0, 1, 2, 3), 2)
    neighbour = along_z(packed, (0, 1, 2, 3), 1)
    lists, counts, both = pl.pallas_call(
        functools.partial(plan_kernel, n_col, np.uint32(late_mask).astype(np.int32), plan),
        out_shape=[
            jax.ShapeDtypeStruct((2, plan.size), jnp.int32),
            jax.ShapeDtypeStruct((8, LANES), jnp.int32),
            jax.ShapeDtypeStruct((2 * COORD_ROWS, LANES), BF16),
        ],
        in_specs=[VMEM] * 3,
        out_specs=[VMEM] * 3,
        compiler_params=small,
        cost_estimate=pl.CostEstimate(flops=1 << 30, bytes_accessed=1 << 12, transcendentals=0),
        name="plan",
    )(slots, coords, exchange(coords, "col", 1))

    again = pl.pallas_call(
        hold_kernel,
        out_shape=jax.ShapeDtypeStruct((PACKED_ROWS, LANES), BF16),
        in_specs=[VMEM, ANY, ANY],
        out_specs=VMEM,
        compiler_params=small,
        name="hold",
    )(packed, own_y, both)
    neighbour = tie(neighbour, again)
    neighbour_y = exchange(neighbour, "row", 1)
    row_coords = [both] + [exchange(both, "col", k) for k in range(2, n_col, 2)]
    second = tie(second, neighbour_y, *row_coords[1:])
    third = pl.pallas_call(
        functools.partial(pick_kernel, n_y),
        out_shape=jax.ShapeDtypeStruct((PACKED_ROWS, LANES), BF16),
        in_specs=[VMEM] * 2,
        out_specs=VMEM,
        compiler_params=small,
        name="pick",
    )(along_z(again, (1, 2), 3), along_z(second, (1, 2), 1))
    blocks = []
    for z, block in enumerate((packed, neighbour, second, third)):
        blocks += [block] + ([own_y, neighbour_y][z : z + 1] or [exchange(block, "row", 1)])
        blocks += [exchange(block, "row", y) for y in range(2, n_y)]

    row_features = pl.pallas_call(
        functools.partial(row_kernel, n_col),
        out_shape=[
            jax.ShapeDtypeStruct((4 * n_col + 2, LEAF, FEATURES), BF16),
            jax.ShapeDtypeStruct((CLUSTERS * n_col + 2, RANK, FEATURES), BF16),
        ],
        in_specs=[VMEM] * (n_col // 2),
        out_specs=[VMEM] * 2,
        compiler_params=small,
        name="row_side",
    )(*row_coords)

    def sums(targets):
        near = (4 * targets + 1, SAMPLES, LEAF)
        far = (CLUSTERS * targets + 1, RANK, LANES)
        return [near, far, far]

    part = jax.ShapeDtypeStruct((COORD_ROW, LANES), BF16)
    held = [
        jax.ShapeDtypeStruct(shape, BF16)
        for shape in [
            (4 * n_row, SAMPLES, LEAF),
            (4 * n_row, FEATURES, LEAF),
            (CLUSTERS * n_row, RANK, LANES),
            (CLUSTERS * n_row, RANK, LANES),
            (CLUSTERS * n_row, FEATURES, LANES),
            (CLUSTERS * n_row, FEATURES, LANES),
        ]
    ]
    held += [jax.ShapeDtypeStruct(shape, F32) for shape in sums(n_col - 2)]
    params = pltpu.CompilerParams(vmem_limit_bytes=32 << 20)
    cost = pl.CostEstimate(flops=1 << 33, bytes_accessed=1 << 20, transcendentals=0)
    handed = pl.pallas_call(
        functools.partial(early_kernel, plan, early),
        out_shape=held,
        in_specs=[SMEM] * 2 + [VMEM] * (2 + len(early)),
        out_specs=[VMEM] * len(held),
        compiler_params=params,
        cost_estimate=cost,
        name="far_targets_early",
    )(lists, counts, *row_features, *[blocks[j] for j in early])
    first = 4 + len(late)
    handed = pl.pallas_call(
        functools.partial(late_kernel, plan, late),
        out_shape=held + [part] * (n_col - 2),
        in_specs=[SMEM] * 2 + [VMEM] * (first - 2 + len(held)),
        out_specs=[VMEM] * (len(held) + n_col - 2),
        input_output_aliases={first + k: k for k in range(len(held))},
        compiler_params=params,
        cost_estimate=cost,
        name="far_targets_late",
    )(lists, counts, *row_features, *[blocks[j] for j in late], *handed)
    prepared, parts = handed[:6], handed[len(held) :]
    mine, other = parts[0::2], [exchange(part, "col", 1) for part in parts[1::2]]
    joined = pl.pallas_call(
        functools.partial(join_kernel, len(mine)),
        out_shape=[part] * len(mine),
        in_specs=[VMEM] * (2 * len(mine)),
        out_specs=[VMEM] * len(mine),
        compiler_params=params,
        name="join",
    )(*mine, *other)
    arrived = [exchange(joined[k], "col", 2 * k + 2) for k in range(len(mine))]
    here = pl.pallas_call(
        functools.partial(here_kernel, plan),
        out_shape=[part] * 2,
        in_specs=[SMEM] * 2 + [VMEM] * (2 + len(prepared)) + [ANY],
        out_specs=[VMEM] * 2,
        scratch_shapes=[pltpu.VMEM(shape, F32) for shape in sums(2)],
        compiler_params=params,
        cost_estimate=cost,
        name="near_targets",
    )(lists, counts, *row_features, *prepared, joined[0])
    arrived += [here[0], exchange(tie(here[1], *arrived), "col", 1)]
    sample = pl.pallas_call(
        functools.partial(final_kernel, len(arrived)),
        out_shape=jax.ShapeDtypeStruct((SAMPLES, OWN), BF16),
        in_specs=[VMEM] * (2 + len(arrived)),
        out_specs=VMEM,
        compiler_params=pltpu.CompilerParams(vmem_limit_bytes=16 << 20),
        name="final",
    )(basis, moves, *arrived)
    return sample.T


def solution(mesh):
    placed = (
        P(("row", "col"), None),
        P(None, ("row", "col")),
        P(None, ("row", "col")),
        P(("row", "col"), None),
        P(("row", "col"), None),
        P("row", "col", None, None),
        P("row", "col"),
        P("row", "col", None, None),
        P("row", "col"),
    )
    return jax.shard_map(
        local, mesh=mesh, in_specs=placed, out_specs=P(("row", "col"), None), check_vma=False
    )
```

```python
import functools
import math

import jax
import jax.numpy as jnp
import numpy as np
from jax import lax
from jax.experimental import pallas as pl
from jax.experimental.pallas import tpu as pltpu
from jax.sharding import PartitionSpec as P

LEAF = 256
RANK = 64
SAMPLES = 64
OWN = 4 * LEAF
CLUSTERS = 7
LANES = 128
F32 = jnp.float32
BF16 = jnp.bfloat16
FAR_ROW = OWN // LANES * SAMPLES
COORD_ROW = FAR_ROW + CLUSTERS * SAMPLES // 2
COORD_ROWS = 96
PACKED_ROWS = COORD_ROW + COORD_ROWS
FEATURES = 16
CLASSES = 3
NEAR_UNROLL = 4
FAR_UNROLL = 16
RATE = math.sqrt(3.0) / 0.15

ANY = pl.BlockSpec(memory_space=pl.ANY)
VMEM = pl.BlockSpec(memory_space=pltpu.VMEM)
SMEM = pl.BlockSpec(memory_space=pltpu.SMEM)
NN = (((1,), (0,)), ((), ()))
NT = (((1,), (1,)), ((), ()))


def dot(a, b, dims=NN):
    return lax.dot_general(a, b, dims, preferred_element_type=F32)


def dot_wide(a, b):
    high = a.astype(BF16)
    low = (a - high.astype(F32)).astype(BF16)
    return dot(high, b) + dot(low, b)


def lanes(a, b):
    return jnp.concatenate([a, b], axis=1)


def rows(*parts):
    return jnp.concatenate(parts, axis=0)


def features(points):
    norm = points * points
    norm = norm[0:1] + norm[1:2] + norm[2:3]
    high = norm.astype(BF16).astype(F32)
    rest = norm - high
    middle = rest.astype(BF16).astype(F32)
    ones = jnp.ones_like(norm)
    return rows(points, high, middle, rest - middle, ones, ones)


def row_side(made):
    ones = made[6:7]
    return rows(-2.0 * made[0:3], ones, ones, ones, made[3:4], made[4:5])


def matern_of(square):
    square = jnp.maximum(square, 1e-14)
    x = (square * lax.rsqrt(square)) * -RATE
    return ((1.0 - x) * jnp.exp(x)).astype(BF16)


def pack_kernel(probes, basis, moves, points, skeleton, packed, coords):
    near = features(points[...].astype(F32))
    far = features(lanes(skeleton[...].astype(F32), jnp.zeros((3, 64), F32)))
    chunks = [near[:, j * LANES : (j + 1) * LANES] for j in range(8)]
    chunks += [far[:, j * LANES : (j + 1) * LANES] for j in range(4)]
    made = rows(*chunks).astype(BF16)
    packed[COORD_ROW:] = made
    coords[...] = made
    leaves = []
    for l in range(4):
        part = slice(l * LEAF, (l + 1) * LEAF)
        leaves.append(dot(basis[:, part], probes[:, part], NT).astype(BF16))
    middle = [
        dot(moves[:, j * 128 : (j + 1) * 128], rows(*leaves[2 * j : 2 * j + 2])).astype(BF16)
        for j in range(2)
    ]
    top = dot(moves[:, 256:384], rows(*middle)).astype(BF16)
    for j in range(8):
        packed[j * SAMPLES : (j + 1) * SAMPLES] = probes[:, j * LANES : (j + 1) * LANES]
    packed[FAR_ROW : FAR_ROW + 64] = lanes(leaves[0], leaves[1])
    packed[FAR_ROW + 64 : FAR_ROW + 128] = lanes(leaves[2], leaves[3])
    packed[FAR_ROW + 128 : FAR_ROW + 192] = lanes(middle[0], middle[1])
    packed[FAR_ROW + 192 : FAR_ROW + 224] = lanes(top[:32], top[32:])


class Plan:
    def __init__(self, near_most, far_most):
        self.near = near_most + NEAR_UNROLL
        self.far = far_most + FAR_UNROLL
        self.far_first = -(-CLASSES * self.near // LANES) * LANES
        self.size = self.far_first + -(-CLASSES * self.far // LANES) * LANES


def iota(shape, axis):
    return lax.broadcasted_iota(jnp.int32, shape, axis)


def pick_kernel(n_y, inner, outer, out):
    z = lax.axis_index("row") // n_y
    is_inner = (z == 1) | (z == 2)

    @pl.when(is_inner)
    def _():
        out[...] = inner[...]

    @pl.when(jnp.logical_not(is_inner))
    def _():
        out[...] = outer[...]


def tie_kernel(*refs):
    del refs


def tie(x, *others):
    return pl.pallas_call(
        tie_kernel,
        out_shape=jax.ShapeDtypeStruct(x.shape, x.dtype),
        in_specs=[ANY] * (1 + len(others)),
        out_specs=ANY,
        input_output_aliases={0: 0},
        compiler_params=pltpu.CompilerParams(vmem_limit_bytes=1 << 20),
        name="tie",
    )(x, *others)


def join_kernel(count, *refs):
    for mine, other, out in zip(refs[:count], refs[count : 2 * count], refs[2 * count :]):
        out[...] = (mine[...].astype(F32) + other[...].astype(F32)).astype(BF16)


def sort_slots(a_device, a_rest, b_device, b_rest, count, per_device, late_mask, n_col, most, width):
    slots = a_device.shape[1]
    target = a_device ^ lax.axis_index("col")
    source = b_device ^ lax.axis_index("row")
    remote = target >= 2
    is_late = lax.shift_right_logical(jnp.full_like(source, late_mask), source) & 1
    alive = iota((1, slots), 1) < count
    group = jnp.where(alive, jnp.where(remote, is_late, 2), 7)
    row = (target - jnp.where(remote, 2, 0)) * per_device + a_rest
    column = source * per_device + b_rest
    member = jnp.where(iota((8, slots), 0) == group, 1.0, 0.0)
    before = jnp.where(iota((slots, slots), 0) < iota((slots, slots), 1), 1.0, 0.0)
    ahead = dot(member.astype(BF16), before.astype(BF16))
    ahead = jnp.sum(member * ahead, axis=0, keepdims=True).astype(jnp.int32)
    place = jnp.where(alive, group * most + ahead, -1)
    chosen = jnp.where(iota((width, slots), 0) == place, 1.0, 0.0).astype(BF16)
    ones = jnp.ones((6, slots), F32)
    values = rows(row.astype(F32), column.astype(F32), ones).astype(BF16)
    found = dot(values, chosen, NT)
    here = iota((1, width), 1) >= 2 * most
    blank = jnp.where(here, 2.0 * per_device, (n_col - 2.0) * per_device)
    made = rows(found[0:1] + blank * (1.0 - found[2:3]), found[1:2])
    return made.astype(jnp.int32), jnp.sum(member, axis=1, keepdims=True).astype(jnp.int32)


def hold_kernel(packed, _, out):
    out[...] = packed[...]


def plan_kernel(n_col, late_mask, plan, slots, coords, mate, out, counts, both):
    both[:COORD_ROWS] = coords[...]
    both[COORD_ROWS:] = mate[...]
    near_most, far_most = plan.near - NEAR_UNROLL, plan.far - FAR_UNROLL
    a, b = slots[0:1, :near_most], slots[1:2, :near_most]
    near, near_counts = sort_slots(
        lax.shift_right_logical(a, 2), a & 3, lax.shift_right_logical(b, 2), b & 3,
        slots[4:5, 0:1], 4, late_mask, n_col, plan.near, plan.far_first,
    )
    a, b = slots[2:3, :far_most], slots[3:4, :far_most]
    a_device = lax.shift_right_logical(a * 9363, 16)
    b_device = lax.shift_right_logical(b * 9363, 16)
    far, far_counts = sort_slots(
        a_device, a - a_device * CLUSTERS, b_device, b - b_device * CLUSTERS,
        slots[5:6, 0:1], CLUSTERS, late_mask, n_col, plan.far, plan.size - plan.far_first,
    )
    out[:, : plan.far_first] = near
    out[:, plan.far_first :] = far
    counts[...] = jnp.where(iota((8, LANES), 1) == 0, near_counts, far_counts)


def row_kernel(n_col, *refs):
    chips, near_row, far_row = refs[:-2], refs[-2], refs[-1]
    empty = jnp.zeros((8, LANES), F32)
    for i in range(n_col):
        first = i % 2 * COORD_ROWS
        slabs = [chips[i // 2][first + 16 * s : first + 16 * s + 16].astype(F32) for s in range(6)]
        near, far = (4 * i, CLUSTERS * i) if i < 2 else (4 * i + 1, CLUSTERS * i + 1)
        for l in range(4):
            for h in range(2):
                made = row_side(slabs[l][8 * h : 8 * h + 8])
                near_row[near + l, h * LANES : (h + 1) * LANES] = rows(made, empty).T.astype(BF16)
        for c in range(4):
            slab = slabs[4 + c // 2]
            made = row_side(slab[8 * (c % 2) : 8 * (c % 2) + 8])
            tall = rows(made, empty).T.astype(BF16)
            far_row[far + 2 * c] = tall[:64]
            if c < 3:
                far_row[far + 2 * c + 1] = tall[64:]
    for blank in (8, 4 * n_col + 1):
        near_row[blank] = jnp.zeros(near_row.shape[1:], BF16)
    for blank in (2 * CLUSTERS, CLUSTERS * n_col + 1):
        far_row[blank] = jnp.zeros(far_row.shape[1:], BF16)


def prepare(i, block, probes, near_col, coeff_low, coeff_high, far_low, far_high):
    for l in range(4):
        for h in range(2):
            j = 2 * l + h
            half = slice(h * LANES, (h + 1) * LANES)
            probes[4 * i + l, :, half] = block[j * SAMPLES : (j + 1) * SAMPLES]
        slab = block[COORD_ROW + 16 * l : COORD_ROW + 16 * (l + 1)]
        near_col[4 * i + l, :, :LANES] = slab
        near_col[4 * i + l, :, LANES:] = rows(slab[8:], slab[:8])
    slabs = [block[COORD_ROW + 64 + 16 * p : COORD_ROW + 80 + 16 * p] for p in range(2)]
    for k in range(CLUSTERS):
        c, half = k // 2, slice(k % 2 * 64, k % 2 * 64 + 64)
        if k < 6:
            own = block[FAR_ROW + 64 * c : FAR_ROW + 64 * (c + 1)][:, half]
        else:
            own = block[FAR_ROW + 192 : FAR_ROW + 224]
            own = rows(own[:, :64], own[:, 64:])
        empty = jnp.zeros_like(own)
        coeff_low[CLUSTERS * i + k] = lanes(own, empty)
        coeff_high[CLUSTERS * i + k] = lanes(empty, own)
        made = slabs[c // 2].astype(F32)[8 * (c % 2) : 8 * (c % 2) + 8, half]
        empty = jnp.zeros_like(made)
        blank = jnp.zeros((8, LANES), F32)
        far_low[CLUSTERS * i + k] = rows(lanes(made, empty), blank).astype(BF16)
        far_high[CLUSTERS * i + k] = rows(lanes(empty, made), blank).astype(BF16)


def work(plan, group, lists, counts, near_row, far_row, prepared, totals):
    probes, near_col, coeff_low, coeff_high, far_low, far_high = prepared
    near_total, far_even, far_odd = totals
    near_first, far_first = (0, 0) if group == 2 else (9, 2 * CLUSTERS + 1)

    def near_step(g, _):
        place = group * plan.near + g * NEAR_UNROLL
        terms = []
        for u in range(NEAR_UNROLL):
            a, b = lists[0, place + u], lists[1, place + u]
            parts = []
            for q in range(2):
                part = slice(q * LANES, (q + 1) * LANES)
                parts.append(matern_of(dot(near_row[near_first + a, part], near_col[b])))
            terms.append((a, dot(probes[b], rows(*parts), NT)))
        for a, term in terms:
            near_total[a] += term
        return 0

    count = counts[group, 0]
    lax.fori_loop(0, (count + NEAR_UNROLL - 1) // NEAR_UNROLL, near_step, 0)

    def far_step(g, _):
        place = plan.far_first + group * plan.far + g * FAR_UNROLL
        terms = []
        for u in range(0, FAR_UNROLL, 2):
            a0, a1 = lists[0, place + u], lists[0, place + u + 1]
            b0, b1 = lists[1, place + u], lists[1, place + u + 1]
            square = dot(far_row[far_first + a0], far_low[b0])
            square += dot(far_row[far_first + a1], far_high[b1])
            both = rows(coeff_low[b0], coeff_high[b1])
            terms.append((a0, a1, dot(matern_of(square), both)))
        for a0, a1, term in terms:
            far_even[a0] += term
            far_odd[a1] += term
        return 0

    count = counts[group, 1]
    lax.fori_loop(0, (count + FAR_UNROLL - 1) // FAR_UNROLL, far_step, 0)


def write_parts(outs, near_total, far_even, far_odd):
    for i, out in enumerate(outs):
        for j in range(8):
            half = slice(j % 2 * LANES, (j % 2 + 1) * LANES)
            part = near_total[4 * i + j // 2, :, half]
            out[j * SAMPLES : (j + 1) * SAMPLES] = part.astype(BF16)
        parts = []
        for l in range(CLUSTERS):
            even, odd = far_even[CLUSTERS * i + l], far_odd[CLUSTERS * i + l]
            parts.append(even[:, :64] + odd[:, 64:])
        for j in range(3):
            pair = lanes(*parts[2 * j : 2 * j + 2])
            out[FAR_ROW + 64 * j : FAR_ROW + 64 * (j + 1)] = pair.astype(BF16)
        pair = lanes(parts[6][:32], parts[6][32:])
        out[FAR_ROW + 192 : FAR_ROW + 224] = pair.astype(BF16)


def clear(totals):
    for total in totals:
        total[...] = jnp.zeros_like(total)


def early_kernel(plan, members, lists, counts, near_row, far_row, *refs):
    blocks, refs = refs[: len(members)], refs[len(members) :]
    prepared, totals = refs[:6], refs[6:]
    clear(totals)
    for i, block in zip(members, blocks):
        prepare(i, block, *prepared)
    work(plan, 0, lists, counts, near_row, far_row, prepared, totals)


def late_kernel(plan, members, lists, counts, near_row, far_row, *refs):
    blocks, refs = refs[: len(members)], refs[len(members) + 9 :]
    prepared, totals, outs = refs[:6], refs[6:9], refs[9:]
    for i, block in zip(members, blocks):
        prepare(i, block, *prepared)
    work(plan, 1, lists, counts, near_row, far_row, prepared, totals)
    write_parts(outs, *totals)


def here_kernel(plan, lists, counts, near_row, far_row, *refs):
    prepared, outs, totals = refs[:6], refs[7:9], refs[9:]
    clear(totals)
    work(plan, 2, lists, counts, near_row, far_row, prepared, totals)
    write_parts(outs, *totals)


def final_kernel(count, basis, moves, *refs):
    parts, out = refs[:count], refs[count]

    def total(first, count):
        return sum(part[first : first + count].astype(F32) for part in parts)

    def turned(first):
        tall = total(first, 64).T
        return lanes(tall[:64], tall[64:])

    top = total(FAR_ROW + 192, 32)
    top = rows(top[:, :64], top[:, 64:]).T
    middle = turned(FAR_ROW + 128) + dot_wide(top, moves[:, 256:384])
    for j in range(2):
        pair = turned(FAR_ROW + 64 * j) + dot_wide(
            middle[:, j * RANK : (j + 1) * RANK], moves[:, j * 128 : (j + 1) * 128]
        )
        for k in range(2):
            l = 2 * j + k
            expanded = dot_wide(
                pair[:, k * RANK : (k + 1) * RANK], basis[:, l * LEAF : (l + 1) * LEAF]
            )
            for h in range(2):
                place = (2 * l + h) * LANES
                near = total((2 * l + h) * SAMPLES, SAMPLES)
                made = near + expanded[:, h * LANES : (h + 1) * LANES]
                out[:, place : place + LANES] = made.astype(BF16)


def exchange(x, axis, offset):
    size = lax.axis_size(axis)
    return lax.ppermute(x, axis, [(i, i ^ offset) for i in range(size)])


def local(
    probes, points, skeleton, leaf_basis, transfer, near_list, near_count, far_list, far_count
):
    n_row = lax.axis_size("row")
    n_col = lax.axis_size("col")
    n_y = n_row // 4
    probes, basis, moves = probes.T, leaf_basis.T, transfer.T
    inputs = (probes, basis, moves, points, skeleton)
    small = pltpu.CompilerParams(vmem_limit_bytes=8 << 20)
    packed, coords = pl.pallas_call(
        pack_kernel,
        out_shape=[
            jax.ShapeDtypeStruct((PACKED_ROWS, LANES), BF16),
            jax.ShapeDtypeStruct((COORD_ROWS, LANES), BF16),
        ],
        in_specs=[VMEM] * 5,
        out_specs=[VMEM] * 2,
        name="pack",
    )(*inputs)

    plan = Plan(near_list.shape[-1], far_list.shape[-1])
    early = [j for j in range(n_row) if j % n_y == 0 or j < n_y]
    late = [j for j in range(n_row) if j not in early]
    late_mask = sum(1 << j for j in late)
    width = max(LANES, near_list.shape[-1], far_list.shape[-1])

    def placed(x, row):
        return jnp.pad(x, ((row, 8 - row - x.shape[0]), (0, width - x.shape[1])))

    slots = placed(near_list[0, 0], 0) + placed(far_list[0, 0], 2)
    slots = slots + placed(near_count, 4) + placed(far_count, 5)

    def along_z(x, planes, flip):
        pairs = [(z * n_y + y, (z ^ flip) * n_y + y) for z in planes for y in range(n_y)]
        return lax.ppermute(x, "row", pairs)

    own_y = exchange(packed, "row", 1)
    second = along_z(packed, (0, 1, 2, 3), 2)
    neighbour = along_z(packed, (0, 1, 2, 3), 1)
    lists, counts, both = pl.pallas_call(
        functools.partial(plan_kernel, n_col, np.uint32(late_mask).astype(np.int32), plan),
        out_shape=[
            jax.ShapeDtypeStruct((2, plan.size), jnp.int32),
            jax.ShapeDtypeStruct((8, LANES), jnp.int32),
            jax.ShapeDtypeStruct((2 * COORD_ROWS, LANES), BF16),
        ],
        in_specs=[VMEM] * 3,
        out_specs=[VMEM] * 3,
        compiler_params=small,
        cost_estimate=pl.CostEstimate(flops=1 << 30, bytes_accessed=1 << 12, transcendentals=0),
        name="plan",
    )(slots, coords, exchange(coords, "col", 1))

    neighbour_y = exchange(neighbour, "row", 1)
    row_coords = [both] + [exchange(both, "col", k) for k in range(2, n_col, 2)]
    second = tie(second, own_y, neighbour_y, *row_coords[1:])
    again = pl.pallas_call(
        hold_kernel,
        out_shape=jax.ShapeDtypeStruct((PACKED_ROWS, LANES), BF16),
        in_specs=[VMEM, ANY],
        out_specs=VMEM,
        compiler_params=small,
        name="hold",
    )(packed, second)
    third = pl.pallas_call(
        functools.partial(pick_kernel, n_y),
        out_shape=jax.ShapeDtypeStruct((PACKED_ROWS, LANES), BF16),
        in_specs=[VMEM] * 2,
        out_specs=VMEM,
        compiler_params=small,
        name="pick",
    )(along_z(again, (1, 2), 3), along_z(second, (1, 2), 1))
    blocks = []
    for z, block in enumerate((packed, neighbour, second, third)):
        blocks += [block] + ([own_y, neighbour_y][z : z + 1] or [exchange(block, "row", 1)])
        blocks += [exchange(block, "row", y) for y in range(2, n_y)]

    row_features = pl.pallas_call(
        functools.partial(row_kernel, n_col),
        out_shape=[
            jax.ShapeDtypeStruct((4 * n_col + 2, LEAF, FEATURES), BF16),
            jax.ShapeDtypeStruct((CLUSTERS * n_col + 2, RANK, FEATURES), BF16),
        ],
        in_specs=[VMEM] * (n_col // 2),
        out_specs=[VMEM] * 2,
        compiler_params=small,
        name="row_side",
    )(*row_coords)

    def sums(targets):
        near = (4 * targets + 1, SAMPLES, LEAF)
        far = (CLUSTERS * targets + 1, RANK, LANES)
        return [near, far, far]

    part = jax.ShapeDtypeStruct((COORD_ROW, LANES), BF16)
    held = [
        jax.ShapeDtypeStruct(shape, BF16)
        for shape in [
            (4 * n_row, SAMPLES, LEAF),
            (4 * n_row, FEATURES, LEAF),
            (CLUSTERS * n_row, RANK, LANES),
            (CLUSTERS * n_row, RANK, LANES),
            (CLUSTERS * n_row, FEATURES, LANES),
            (CLUSTERS * n_row, FEATURES, LANES),
        ]
    ]
    held += [jax.ShapeDtypeStruct(shape, F32) for shape in sums(n_col - 2)]
    params = pltpu.CompilerParams(vmem_limit_bytes=32 << 20)
    cost = pl.CostEstimate(flops=1 << 33, bytes_accessed=1 << 20, transcendentals=0)
    handed = pl.pallas_call(
        functools.partial(early_kernel, plan, early),
        out_shape=held,
        in_specs=[SMEM] * 2 + [VMEM] * (2 + len(early)),
        out_specs=[VMEM] * len(held),
        compiler_params=params,
        cost_estimate=cost,
        name="far_targets_early",
    )(lists, counts, *row_features, *[blocks[j] for j in early])
    first = 4 + len(late)
    handed = pl.pallas_call(
        functools.partial(late_kernel, plan, late),
        out_shape=held + [part] * (n_col - 2),
        in_specs=[SMEM] * 2 + [VMEM] * (first - 2 + len(held)),
        out_specs=[VMEM] * (len(held) + n_col - 2),
        input_output_aliases={first + k: k for k in range(len(held))},
        compiler_params=params,
        cost_estimate=cost,
        name="far_targets_late",
    )(lists, counts, *row_features, *[blocks[j] for j in late], *handed)
    prepared, parts = handed[:6], handed[len(held) :]
    mine, other = parts[0::2], [exchange(part, "col", 1) for part in parts[1::2]]
    joined = pl.pallas_call(
        functools.partial(join_kernel, len(mine)),
        out_shape=[part] * len(mine),
        in_specs=[VMEM] * (2 * len(mine)),
        out_specs=[VMEM] * len(mine),
        compiler_params=params,
        name="join",
    )(*mine, *other)
    arrived = [exchange(joined[k], "col", 2 * k + 2) for k in range(len(mine))]
    here = pl.pallas_call(
        functools.partial(here_kernel, plan),
        out_shape=[part] * 2,
        in_specs=[SMEM] * 2 + [VMEM] * (2 + len(prepared)) + [ANY],
        out_specs=[VMEM] * 2,
        scratch_shapes=[pltpu.VMEM(shape, F32) for shape in sums(2)],
        compiler_params=params,
        cost_estimate=cost,
        name="near_targets",
    )(lists, counts, *row_features, *prepared, joined[0])
    arrived += [here[0], exchange(tie(here[1], *arrived), "col", 1)]
    sample = pl.pallas_call(
        functools.partial(final_kernel, len(arrived)),
        out_shape=jax.ShapeDtypeStruct((SAMPLES, OWN), BF16),
        in_specs=[VMEM] * (2 + len(arrived)),
        out_specs=VMEM,
        compiler_params=pltpu.CompilerParams(vmem_limit_bytes=16 << 20),
        name="final",
    )(basis, moves, *arrived)
    return sample.T


def solution(mesh):
    placed = (
        P(("row", "col"), None),
        P(None, ("row", "col")),
        P(None, ("row", "col")),
        P(("row", "col"), None),
        P(("row", "col"), None),
        P("row", "col", None, None),
        P("row", "col"),
        P("row", "col", None, None),
        P("row", "col"),
    )
    return jax.shard_map(
        local, mesh=mesh, in_specs=placed, out_specs=P(("row", "col"), None), check_vma=False
    )
```

```python
import functools
import math

import jax
import jax.numpy as jnp
import numpy as np
from jax import lax
from jax.experimental import pallas as pl
from jax.experimental.pallas import tpu as pltpu
from jax.sharding import PartitionSpec as P

LEAF = 256
RANK = 64
SAMPLES = 64
OWN = 4 * LEAF
CLUSTERS = 7
LANES = 128
F32 = jnp.float32
BF16 = jnp.bfloat16
FAR_ROW = OWN // LANES * SAMPLES
COORD_ROW = FAR_ROW + CLUSTERS * SAMPLES // 2
COORD_ROWS = 96
PACKED_ROWS = COORD_ROW + COORD_ROWS
FEATURES = 16
CLASSES = 3
NEAR_UNROLL = 8
FAR_UNROLL = 16
RATE = math.sqrt(3.0) / 0.15

ANY = pl.BlockSpec(memory_space=pl.ANY)
VMEM = pl.BlockSpec(memory_space=pltpu.VMEM)
SMEM = pl.BlockSpec(memory_space=pltpu.SMEM)
NN = (((1,), (0,)), ((), ()))
NT = (((1,), (1,)), ((), ()))


def dot(a, b, dims=NN):
    return lax.dot_general(a, b, dims, preferred_element_type=F32)


def dot_wide(a, b):
    high = a.astype(BF16)
    low = (a - high.astype(F32)).astype(BF16)
    return dot(high, b) + dot(low, b)


def lanes(a, b):
    return jnp.concatenate([a, b], axis=1)


def rows(*parts):
    return jnp.concatenate(parts, axis=0)


def features(points):
    norm = points * points
    norm = norm[0:1] + norm[1:2] + norm[2:3]
    high = norm.astype(BF16).astype(F32)
    rest = norm - high
    middle = rest.astype(BF16).astype(F32)
    ones = jnp.ones_like(norm)
    return rows(points, high, middle, rest - middle, ones, ones)


def row_side(made):
    ones = made[6:7]
    return rows(-2.0 * made[0:3], ones, ones, ones, made[3:4], made[4:5])


def matern_of(square):
    square = jnp.maximum(square, 1e-14)
    x = (square * lax.rsqrt(square)) * -RATE
    return ((1.0 - x) * jnp.exp(x)).astype(BF16)


def pack_kernel(probes, basis, moves, points, skeleton, packed, coords):
    near = features(points[...].astype(F32))
    far = features(lanes(skeleton[...].astype(F32), jnp.zeros((3, 64), F32)))
    chunks = [near[:, j * LANES : (j + 1) * LANES] for j in range(8)]
    chunks += [far[:, j * LANES : (j + 1) * LANES] for j in range(4)]
    made = rows(*chunks).astype(BF16)
    packed[COORD_ROW:] = made
    coords[...] = made
    leaves = []
    for l in range(4):
        part = slice(l * LEAF, (l + 1) * LEAF)
        leaves.append(dot(basis[:, part], probes[:, part], NT).astype(BF16))
    middle = [
        dot(moves[:, j * 128 : (j + 1) * 128], rows(*leaves[2 * j : 2 * j + 2])).astype(BF16)
        for j in range(2)
    ]
    top = dot(moves[:, 256:384], rows(*middle)).astype(BF16)
    for j in range(8):
        packed[j * SAMPLES : (j + 1) * SAMPLES] = probes[:, j * LANES : (j + 1) * LANES]
    packed[FAR_ROW : FAR_ROW + 64] = lanes(leaves[0], leaves[1])
    packed[FAR_ROW + 64 : FAR_ROW + 128] = lanes(leaves[2], leaves[3])
    packed[FAR_ROW + 128 : FAR_ROW + 192] = lanes(middle[0], middle[1])
    packed[FAR_ROW + 192 : FAR_ROW + 224] = lanes(top[:32], top[32:])


class Plan:
    def __init__(self, near_most, far_most):
        self.near = near_most + NEAR_UNROLL
        self.far = far_most + FAR_UNROLL
        self.far_first = -(-CLASSES * self.near // LANES) * LANES
        self.size = self.far_first + -(-CLASSES * self.far // LANES) * LANES


def iota(shape, axis):
    return lax.broadcasted_iota(jnp.int32, shape, axis)


def pick_kernel(n_y, inner, outer, out):
    z = lax.axis_index("row") // n_y
    is_inner = (z == 1) | (z == 2)

    @pl.when(is_inner)
    def _():
        out[...] = inner[...]

    @pl.when(jnp.logical_not(is_inner))
    def _():
        out[...] = outer[...]


def tie_kernel(*refs):
    del refs


def tie(x, *others):
    return pl.pallas_call(
        tie_kernel,
        out_shape=jax.ShapeDtypeStruct(x.shape, x.dtype),
        in_specs=[ANY] * (1 + len(others)),
        out_specs=ANY,
        input_output_aliases={0: 0},
        compiler_params=pltpu.CompilerParams(vmem_limit_bytes=1 << 20),
        name="tie",
    )(x, *others)


def join_kernel(count, *refs):
    for mine, other, out in zip(refs[:count], refs[count : 2 * count], refs[2 * count :]):
        out[...] = (mine[...].astype(F32) + other[...].astype(F32)).astype(BF16)


def sort_slots(a_device, a_rest, b_device, b_rest, count, per_device, late_mask, n_col, most, width):
    slots = a_device.shape[1]
    target = a_device ^ lax.axis_index("col")
    source = b_device ^ lax.axis_index("row")
    remote = target >= 2
    is_late = lax.shift_right_logical(jnp.full_like(source, late_mask), source) & 1
    alive = iota((1, slots), 1) < count
    group = jnp.where(alive, jnp.where(remote, is_late, 2), 7)
    row = (target - jnp.where(remote, 2, 0)) * per_device + a_rest
    column = source * per_device + b_rest
    member = jnp.where(iota((8, slots), 0) == group, 1.0, 0.0)
    before = jnp.where(iota((slots, slots), 0) < iota((slots, slots), 1), 1.0, 0.0)
    ahead = dot(member.astype(BF16), before.astype(BF16))
    ahead = jnp.sum(member * ahead, axis=0, keepdims=True).astype(jnp.int32)
    place = jnp.where(alive, group * most + ahead, -1)
    chosen = jnp.where(iota((width, slots), 0) == place, 1.0, 0.0).astype(BF16)
    ones = jnp.ones((6, slots), F32)
    values = rows(row.astype(F32), column.astype(F32), ones).astype(BF16)
    found = dot(values, chosen, NT)
    here = iota((1, width), 1) >= 2 * most
    blank = jnp.where(here, 2.0 * per_device, (n_col - 2.0) * per_device)
    made = rows(found[0:1] + blank * (1.0 - found[2:3]), found[1:2])
    return made.astype(jnp.int32), jnp.sum(member, axis=1, keepdims=True).astype(jnp.int32)


def hold_kernel(packed, _, out):
    out[...] = packed[...]


def plan_kernel(n_col, late_mask, plan, slots, coords, mate, out, counts, both):
    both[:COORD_ROWS] = coords[...]
    both[COORD_ROWS:] = mate[...]
    near_most, far_most = plan.near - NEAR_UNROLL, plan.far - FAR_UNROLL
    a, b = slots[0:1, :near_most], slots[1:2, :near_most]
    near, near_counts = sort_slots(
        lax.shift_right_logical(a, 2), a & 3, lax.shift_right_logical(b, 2), b & 3,
        slots[4:5, 0:1], 4, late_mask, n_col, plan.near, plan.far_first,
    )
    a, b = slots[2:3, :far_most], slots[3:4, :far_most]
    a_device = lax.shift_right_logical(a * 9363, 16)
    b_device = lax.shift_right_logical(b * 9363, 16)
    far, far_counts = sort_slots(
        a_device, a - a_device * CLUSTERS, b_device, b - b_device * CLUSTERS,
        slots[5:6, 0:1], CLUSTERS, late_mask, n_col, plan.far, plan.size - plan.far_first,
    )
    out[:, : plan.far_first] = near
    out[:, plan.far_first :] = far
    counts[...] = jnp.where(iota((8, LANES), 1) == 0, near_counts, far_counts)


def row_kernel(n_col, *refs):
    chips, near_row, far_row = refs[:-3], refs[-2], refs[-1]
    empty = jnp.zeros((8, LANES), F32)
    for i in range(n_col):
        first = i % 2 * COORD_ROWS
        slabs = [chips[i // 2][first + 16 * s : first + 16 * s + 16].astype(F32) for s in range(6)]
        near, far = (4 * i, CLUSTERS * i) if i < 2 else (4 * i + 1, CLUSTERS * i + 1)
        for l in range(4):
            for h in range(2):
                made = row_side(slabs[l][8 * h : 8 * h + 8])
                near_row[near + l, h * LANES : (h + 1) * LANES] = rows(made, empty).T.astype(BF16)
        for c in range(4):
            slab = slabs[4 + c // 2]
            made = row_side(slab[8 * (c % 2) : 8 * (c % 2) + 8])
            tall = rows(made, empty).T.astype(BF16)
            far_row[far + 2 * c] = tall[:64]
            if c < 3:
                far_row[far + 2 * c + 1] = tall[64:]
    for blank in (8, 4 * n_col + 1):
        near_row[blank] = jnp.zeros(near_row.shape[1:], BF16)
    for blank in (2 * CLUSTERS, CLUSTERS * n_col + 1):
        far_row[blank] = jnp.zeros(far_row.shape[1:], BF16)


def prepare(i, block, probes, near_col, coeff_low, coeff_high, far_low, far_high):
    for l in range(4):
        for h in range(2):
            j = 2 * l + h
            half = slice(h * LANES, (h + 1) * LANES)
            probes[4 * i + l, :, half] = block[j * SAMPLES : (j + 1) * SAMPLES]
        slab = block[COORD_ROW + 16 * l : COORD_ROW + 16 * (l + 1)]
        near_col[4 * i + l, :, :LANES] = slab
        near_col[4 * i + l, :, LANES:] = rows(slab[8:], slab[:8])
    slabs = [block[COORD_ROW + 64 + 16 * p : COORD_ROW + 80 + 16 * p] for p in range(2)]
    for k in range(CLUSTERS):
        c, half = k // 2, slice(k % 2 * 64, k % 2 * 64 + 64)
        if k < 6:
            own = block[FAR_ROW + 64 * c : FAR_ROW + 64 * (c + 1)][:, half]
        else:
            own = block[FAR_ROW + 192 : FAR_ROW + 224]
            own = rows(own[:, :64], own[:, 64:])
        empty = jnp.zeros_like(own)
        coeff_low[CLUSTERS * i + k] = lanes(own, empty)
        coeff_high[CLUSTERS * i + k] = lanes(empty, own)
        made = slabs[c // 2].astype(F32)[8 * (c % 2) : 8 * (c % 2) + 8, half]
        empty = jnp.zeros_like(made)
        blank = jnp.zeros((8, LANES), F32)
        far_low[CLUSTERS * i + k] = rows(lanes(made, empty), blank).astype(BF16)
        far_high[CLUSTERS * i + k] = rows(lanes(empty, made), blank).astype(BF16)


def work(plan, group, lists, counts, near_row, far_row, prepared, totals):
    probes, near_col, coeff_low, coeff_high, far_low, far_high = prepared
    near_total, far_even, far_odd = totals
    near_first, far_first = (0, 0) if group == 2 else (9, 2 * CLUSTERS + 1)

    def near_terms(place, slots):
        terms = []
        for u in range(slots):
            a, b = lists[0, place + u], lists[1, place + u]
            parts = []
            for q in range(2):
                part = slice(q * LANES, (q + 1) * LANES)
                parts.append(matern_of(dot(near_row[near_first + a, part], near_col[b])))
            terms.append((a, dot(probes[b], rows(*parts), NT)))
        return terms

    def near_add(terms):
        for a, term in terms:
            near_total[a] += term

    def far_terms(place):
        terms = []
        for u in range(0, FAR_UNROLL, 2):
            a0, a1 = lists[0, place + u], lists[0, place + u + 1]
            b0, b1 = lists[1, place + u], lists[1, place + u + 1]
            square = dot(far_row[far_first + a0], far_low[b0])
            square += dot(far_row[far_first + a1], far_high[b1])
            both = rows(coeff_low[b0], coeff_high[b1])
            terms.append((a0, a1, dot(matern_of(square), both)))
        return terms

    def far_add(terms):
        for a0, a1, term in terms:
            far_even[a0] += term
            far_odd[a1] += term

    half = NEAR_UNROLL // 2
    halves = (counts[group, 0] + half - 1) // half
    near_groups = halves // 2
    far_groups = (counts[group, 1] + FAR_UNROLL - 1) // FAR_UNROLL
    together = jnp.minimum(near_groups, far_groups)
    near_place, far_place = group * plan.near, plan.far_first + group * plan.far

    def joint_step(g, _):
        near = near_terms(near_place + g * NEAR_UNROLL, NEAR_UNROLL)
        far = far_terms(far_place + g * FAR_UNROLL)
        near_add(near)
        far_add(far)
        return 0

    def near_step(g, _):
        near_add(near_terms(near_place + g * NEAR_UNROLL, NEAR_UNROLL))
        return 0

    def far_step(g, _):
        far_add(far_terms(far_place + g * FAR_UNROLL))
        return 0

    lax.fori_loop(0, together, joint_step, 0)
    lax.fori_loop(together, near_groups, near_step, 0)
    lax.fori_loop(together, far_groups, far_step, 0)

    @pl.when(halves % 2 == 1)
    def _():
        near_add(near_terms(near_place + near_groups * NEAR_UNROLL, half))


def write_parts(outs, near_total, far_even, far_odd):
    for i, out in enumerate(outs):
        for j in range(8):
            half = slice(j % 2 * LANES, (j % 2 + 1) * LANES)
            part = near_total[4 * i + j // 2, :, half]
            out[j * SAMPLES : (j + 1) * SAMPLES] = part.astype(BF16)
        parts = []
        for l in range(CLUSTERS):
            even, odd = far_even[CLUSTERS * i + l], far_odd[CLUSTERS * i + l]
            parts.append(even[:, :64] + odd[:, 64:])
        for j in range(3):
            pair = lanes(*parts[2 * j : 2 * j + 2])
            out[FAR_ROW + 64 * j : FAR_ROW + 64 * (j + 1)] = pair.astype(BF16)
        pair = lanes(parts[6][:32], parts[6][32:])
        out[FAR_ROW + 192 : FAR_ROW + 224] = pair.astype(BF16)


def clear(totals):
    for total in totals:
        total[...] = jnp.zeros_like(total)


def early_kernel(plan, members, lists, counts, near_row, far_row, *refs):
    blocks, refs = refs[: len(members)], refs[len(members) :]
    prepared, totals = refs[:6], refs[6:]
    clear(totals)
    for i, block in zip(members, blocks):
        prepare(i, block, *prepared)
    work(plan, 0, lists, counts, near_row, far_row, prepared, totals)


def late_kernel(plan, members, lists, counts, near_row, far_row, *refs):
    blocks, refs = refs[: len(members)], refs[len(members) + 9 :]
    prepared, totals, outs = refs[:6], refs[6:9], refs[9:]
    for i, block in zip(members, blocks):
        prepare(i, block, *prepared)
    work(plan, 1, lists, counts, near_row, far_row, prepared, totals)
    write_parts(outs, *totals)


def here_kernel(plan, lists, counts, near_row, far_row, *refs):
    prepared, outs, totals = refs[:6], refs[7:9], refs[9:]
    clear(totals)
    work(plan, 2, lists, counts, near_row, far_row, prepared, totals)
    write_parts(outs, *totals)


def final_kernel(count, basis, moves, *refs):
    parts, out = refs[:count], refs[count]

    def total(first, count):
        return sum(part[first : first + count].astype(F32) for part in parts)

    def turned(first):
        tall = total(first, 64).T
        return lanes(tall[:64], tall[64:])

    top = total(FAR_ROW + 192, 32)
    top = rows(top[:, :64], top[:, 64:]).T
    middle = turned(FAR_ROW + 128) + dot_wide(top, moves[:, 256:384])
    for j in range(2):
        pair = turned(FAR_ROW + 64 * j) + dot_wide(
            middle[:, j * RANK : (j + 1) * RANK], moves[:, j * 128 : (j + 1) * 128]
        )
        for k in range(2):
            l = 2 * j + k
            expanded = dot_wide(
                pair[:, k * RANK : (k + 1) * RANK], basis[:, l * LEAF : (l + 1) * LEAF]
            )
            for h in range(2):
                place = (2 * l + h) * LANES
                near = total((2 * l + h) * SAMPLES, SAMPLES)
                made = near + expanded[:, h * LANES : (h + 1) * LANES]
                out[:, place : place + LANES] = made.astype(BF16)


def exchange(x, axis, offset):
    size = lax.axis_size(axis)
    return lax.ppermute(x, axis, [(i, i ^ offset) for i in range(size)])


def local(
    probes, points, skeleton, leaf_basis, transfer, near_list, near_count, far_list, far_count
):
    n_row = lax.axis_size("row")
    n_col = lax.axis_size("col")
    n_y = n_row // 4
    probes, basis, moves = probes.T, leaf_basis.T, transfer.T
    inputs = (probes, basis, moves, points, skeleton)
    small = pltpu.CompilerParams(vmem_limit_bytes=8 << 20)
    packed, coords = pl.pallas_call(
        pack_kernel,
        out_shape=[
            jax.ShapeDtypeStruct((PACKED_ROWS, LANES), BF16),
            jax.ShapeDtypeStruct((COORD_ROWS, LANES), BF16),
        ],
        in_specs=[VMEM] * 5,
        out_specs=[VMEM] * 2,
        name="pack",
    )(*inputs)

    plan = Plan(near_list.shape[-1], far_list.shape[-1])
    early = [j for j in range(n_row) if j % n_y == 0 or j < n_y]
    late = [j for j in range(n_row) if j not in early]
    late_mask = sum(1 << j for j in late)
    width = max(LANES, near_list.shape[-1], far_list.shape[-1])

    def placed(x, row):
        return jnp.pad(x, ((row, 8 - row - x.shape[0]), (0, width - x.shape[1])))

    slots = placed(near_list[0, 0], 0) + placed(far_list[0, 0], 2)
    slots = slots + placed(near_count, 4) + placed(far_count, 5)

    def along_z(x, planes, flip):
        pairs = [(z * n_y + y, (z ^ flip) * n_y + y) for z in planes for y in range(n_y)]
        return lax.ppermute(x, "row", pairs)

    own_y = exchange(packed, "row", 1)
    second = along_z(packed, (0, 1, 2, 3), 2)
    neighbour = along_z(packed, (0, 1, 2, 3), 1)
    lists, counts, both = pl.pallas_call(
        functools.partial(plan_kernel, n_col, np.uint32(late_mask).astype(np.int32), plan),
        out_shape=[
            jax.ShapeDtypeStruct((2, plan.size), jnp.int32),
            jax.ShapeDtypeStruct((8, LANES), jnp.int32),
            jax.ShapeDtypeStruct((2 * COORD_ROWS, LANES), BF16),
        ],
        in_specs=[VMEM] * 3,
        out_specs=[VMEM] * 3,
        compiler_params=small,
        cost_estimate=pl.CostEstimate(flops=1 << 30, bytes_accessed=1 << 12, transcendentals=0),
        name="plan",
    )(slots, coords, exchange(coords, "col", 1))

    neighbour_y = exchange(neighbour, "row", 1)
    row_coords = [both] + [exchange(both, "col", k) for k in range(2, n_col, 2)]
    second = tie(second, own_y, neighbour_y, lists)
    again = pl.pallas_call(
        hold_kernel,
        out_shape=jax.ShapeDtypeStruct((PACKED_ROWS, LANES), BF16),
        in_specs=[VMEM, ANY],
        out_specs=VMEM,
        compiler_params=small,
        name="hold",
    )(packed, second)
    third = pl.pallas_call(
        functools.partial(pick_kernel, n_y),
        out_shape=jax.ShapeDtypeStruct((PACKED_ROWS, LANES), BF16),
        in_specs=[VMEM] * 2,
        out_specs=VMEM,
        compiler_params=small,
        name="pick",
    )(along_z(again, (1, 2), 3), along_z(second, (1, 2), 1))
    second_y = exchange(second, "row", 1)
    blocks = []
    for z, block in enumerate((packed, neighbour, second, third)):
        blocks += [block] + ([own_y, neighbour_y, second_y][z : z + 1] or [exchange(block, "row", 1)])
        blocks += [exchange(block, "row", y) for y in range(2, n_y)]

    row_features = pl.pallas_call(
        functools.partial(row_kernel, n_col),
        out_shape=[
            jax.ShapeDtypeStruct((4 * n_col + 2, LEAF, FEATURES), BF16),
            jax.ShapeDtypeStruct((CLUSTERS * n_col + 2, RANK, FEATURES), BF16),
        ],
        in_specs=[VMEM] * (n_col // 2) + [ANY],
        out_specs=[VMEM] * 2,
        compiler_params=small,
        name="row_side",
    )(*row_coords, third)

    def sums(targets):
        near = (4 * targets + 1, SAMPLES, LEAF)
        far = (CLUSTERS * targets + 1, RANK, LANES)
        return [near, far, far]

    part = jax.ShapeDtypeStruct((COORD_ROW, LANES), BF16)
    held = [
        jax.ShapeDtypeStruct(shape, BF16)
        for shape in [
            (4 * n_row, SAMPLES, LEAF),
            (4 * n_row, FEATURES, LEAF),
            (CLUSTERS * n_row, RANK, LANES),
            (CLUSTERS * n_row, RANK, LANES),
            (CLUSTERS * n_row, FEATURES, LANES),
            (CLUSTERS * n_row, FEATURES, LANES),
        ]
    ]
    held += [jax.ShapeDtypeStruct(shape, F32) for shape in sums(n_col - 2)]
    params = pltpu.CompilerParams(vmem_limit_bytes=32 << 20)
    cost = pl.CostEstimate(flops=1 << 33, bytes_accessed=1 << 20, transcendentals=0)
    handed = pl.pallas_call(
        functools.partial(early_kernel, plan, early),
        out_shape=held,
        in_specs=[SMEM] * 2 + [VMEM] * (2 + len(early)),
        out_specs=[VMEM] * len(held),
        compiler_params=params,
        cost_estimate=cost,
        name="far_targets_early",
    )(lists, counts, *row_features, *[blocks[j] for j in early])
    first = 4 + len(late)
    handed = pl.pallas_call(
        functools.partial(late_kernel, plan, late),
        out_shape=held + [part] * (n_col - 2),
        in_specs=[SMEM] * 2 + [VMEM] * (first - 2 + len(held)),
        out_specs=[VMEM] * (len(held) + n_col - 2),
        input_output_aliases={first + k: k for k in range(len(held))},
        compiler_params=params,
        cost_estimate=cost,
        name="far_targets_late",
    )(lists, counts, *row_features, *[blocks[j] for j in late], *handed)
    prepared, parts = handed[:6], handed[len(held) :]
    mine, other = parts[0::2], [exchange(part, "col", 1) for part in parts[1::2]]
    joined = pl.pallas_call(
        functools.partial(join_kernel, len(mine)),
        out_shape=[part] * len(mine),
        in_specs=[VMEM] * (2 * len(mine)),
        out_specs=[VMEM] * len(mine),
        compiler_params=params,
        name="join",
    )(*mine, *other)
    arrived = [exchange(joined[k], "col", 2 * k + 2) for k in range(len(mine))]
    here = pl.pallas_call(
        functools.partial(here_kernel, plan),
        out_shape=[part] * 2,
        in_specs=[SMEM] * 2 + [VMEM] * (2 + len(prepared)) + [ANY],
        out_specs=[VMEM] * 2,
        scratch_shapes=[pltpu.VMEM(shape, F32) for shape in sums(2)],
        compiler_params=params,
        cost_estimate=cost,
        name="near_targets",
    )(lists, counts, *row_features, *prepared, joined[0])
    arrived += [here[0], exchange(tie(here[1], *arrived), "col", 1)]
    sample = pl.pallas_call(
        functools.partial(final_kernel, len(arrived)),
        out_shape=jax.ShapeDtypeStruct((SAMPLES, OWN), BF16),
        in_specs=[VMEM] * (2 + len(arrived)),
        out_specs=VMEM,
        compiler_params=pltpu.CompilerParams(vmem_limit_bytes=16 << 20),
        name="final",
    )(basis, moves, *arrived)
    return sample.T


def solution(mesh):
    placed = (
        P(("row", "col"), None),
        P(None, ("row", "col")),
        P(None, ("row", "col")),
        P(("row", "col"), None),
        P(("row", "col"), None),
        P("row", "col", None, None),
        P("row", "col"),
        P("row", "col", None, None),
        P("row", "col"),
    )
    return jax.shard_map(
        local, mesh=mesh, in_specs=placed, out_specs=P(("row", "col"), None), check_vma=False
    )
```

```python
import functools
import math

import jax
import jax.numpy as jnp
import numpy as np
from jax import lax
from jax.experimental import pallas as pl
from jax.experimental.pallas import tpu as pltpu
from jax.sharding import PartitionSpec as P

LEAF = 256
RANK = 64
SAMPLES = 64
OWN = 4 * LEAF
CLUSTERS = 7
LANES = 128
F32 = jnp.float32
BF16 = jnp.bfloat16
FAR_ROW = OWN // LANES * SAMPLES
COORD_ROW = FAR_ROW + CLUSTERS * SAMPLES // 2
COORD_ROWS = 96
PACKED_ROWS = COORD_ROW + COORD_ROWS
FEATURES = 16
CLASSES = 4
NEAR_UNROLL = 8
FAR_UNROLL = 16
RATE = math.sqrt(3.0) / 0.15

ANY = pl.BlockSpec(memory_space=pl.ANY)
VMEM = pl.BlockSpec(memory_space=pltpu.VMEM)
SMEM = pl.BlockSpec(memory_space=pltpu.SMEM)
NN = (((1,), (0,)), ((), ()))
NT = (((1,), (1,)), ((), ()))


def dot(a, b, dims=NN):
    return lax.dot_general(a, b, dims, preferred_element_type=F32)


def dot_wide(a, b):
    high = a.astype(BF16)
    low = (a - high.astype(F32)).astype(BF16)
    return dot(high, b) + dot(low, b)


def lanes(a, b):
    return jnp.concatenate([a, b], axis=1)


def rows(*parts):
    return jnp.concatenate(parts, axis=0)


def features(points):
    norm = points * points
    norm = norm[0:1] + norm[1:2] + norm[2:3]
    high = norm.astype(BF16).astype(F32)
    rest = norm - high
    middle = rest.astype(BF16).astype(F32)
    ones = jnp.ones_like(norm)
    return rows(points, high, middle, rest - middle, ones, ones)


def row_side(made):
    ones = made[6:7]
    return rows(-2.0 * made[0:3], ones, ones, ones, made[3:4], made[4:5])


def matern_of(square):
    square = jnp.maximum(square, 1e-14)
    x = (square * lax.rsqrt(square)) * -RATE
    return ((1.0 - x) * jnp.exp(x)).astype(BF16)


def pack_kernel(probes, basis, moves, points, skeleton, packed, coords):
    near = features(points[...].astype(F32))
    far = features(lanes(skeleton[...].astype(F32), jnp.zeros((3, 64), F32)))
    chunks = [near[:, j * LANES : (j + 1) * LANES] for j in range(8)]
    chunks += [far[:, j * LANES : (j + 1) * LANES] for j in range(4)]
    made = rows(*chunks).astype(BF16)
    packed[COORD_ROW:] = made
    coords[...] = made
    leaves = []
    for l in range(4):
        part = slice(l * LEAF, (l + 1) * LEAF)
        leaves.append(dot(basis[:, part], probes[:, part], NT).astype(BF16))
    middle = [
        dot(moves[:, j * 128 : (j + 1) * 128], rows(*leaves[2 * j : 2 * j + 2])).astype(BF16)
        for j in range(2)
    ]
    top = dot(moves[:, 256:384], rows(*middle)).astype(BF16)
    for j in range(8):
        packed[j * SAMPLES : (j + 1) * SAMPLES] = probes[:, j * LANES : (j + 1) * LANES]
    packed[FAR_ROW : FAR_ROW + 64] = lanes(leaves[0], leaves[1])
    packed[FAR_ROW + 64 : FAR_ROW + 128] = lanes(leaves[2], leaves[3])
    packed[FAR_ROW + 128 : FAR_ROW + 192] = lanes(middle[0], middle[1])
    packed[FAR_ROW + 192 : FAR_ROW + 224] = lanes(top[:32], top[32:])


class Plan:
    def __init__(self, near_most, far_most):
        self.near = near_most + NEAR_UNROLL
        self.far = far_most + FAR_UNROLL
        self.far_first = -(-CLASSES * self.near // LANES) * LANES
        self.size = self.far_first + -(-CLASSES * self.far // LANES) * LANES


def iota(shape, axis):
    return lax.broadcasted_iota(jnp.int32, shape, axis)


def pick_kernel(n_y, inner, outer, _, out):
    z = lax.axis_index("row") // n_y
    is_inner = (z == 1) | (z == 2)

    @pl.when(is_inner)
    def _():
        out[...] = inner[...]

    @pl.when(jnp.logical_not(is_inner))
    def _():
        out[...] = outer[...]


def tie_kernel(*refs):
    del refs


def tie(x, *others):
    return pl.pallas_call(
        tie_kernel,
        out_shape=jax.ShapeDtypeStruct(x.shape, x.dtype),
        in_specs=[ANY] * (1 + len(others)),
        out_specs=ANY,
        input_output_aliases={0: 0},
        compiler_params=pltpu.CompilerParams(vmem_limit_bytes=1 << 20),
        name="tie",
    )(x, *others)


def join_kernel(count, *refs):
    for mine, other, out in zip(refs[:count], refs[count : 2 * count], refs[2 * count :]):
        out[...] = (mine[...].astype(F32) + other[...].astype(F32)).astype(BF16)


def sort_slots(a_device, a_rest, b_device, b_rest, count, per_device, late_mask, n_col, most, width):
    slots = a_device.shape[1]
    target = a_device ^ lax.axis_index("col")
    source = b_device ^ lax.axis_index("row")
    remote = target >= 2
    is_late = lax.shift_right_logical(jnp.full_like(source, late_mask), source) & 1
    alive = iota((1, slots), 1) < count
    group = jnp.where(alive, jnp.where(remote, 0, 2) + is_late, 7)
    row = (target - jnp.where(remote, 2, 0)) * per_device + a_rest
    column = source * per_device + b_rest
    member = jnp.where(iota((8, slots), 0) == group, 1.0, 0.0)
    before = jnp.where(iota((slots, slots), 0) < iota((slots, slots), 1), 1.0, 0.0)
    ahead = dot(member.astype(BF16), before.astype(BF16))
    ahead = jnp.sum(member * ahead, axis=0, keepdims=True).astype(jnp.int32)
    place = jnp.where(alive, group * most + ahead, -1)
    chosen = jnp.where(iota((width, slots), 0) == place, 1.0, 0.0).astype(BF16)
    ones = jnp.ones((6, slots), F32)
    values = rows(row.astype(F32), column.astype(F32), ones).astype(BF16)
    found = dot(values, chosen, NT)
    here = iota((1, width), 1) >= 2 * most
    blank = jnp.where(here, 2.0 * per_device, (n_col - 2.0) * per_device)
    made = rows(found[0:1] + blank * (1.0 - found[2:3]), found[1:2])
    return made.astype(jnp.int32), jnp.sum(member, axis=1, keepdims=True).astype(jnp.int32)


def hold_kernel(packed, _, out):
    out[...] = packed[...]


def plan_kernel(n_col, late_mask, plan, slots, coords, mate, out, counts, both):
    both[:COORD_ROWS] = coords[...]
    both[COORD_ROWS:] = mate[...]
    near_most, far_most = plan.near - NEAR_UNROLL, plan.far - FAR_UNROLL
    a, b = slots[0:1, :near_most], slots[1:2, :near_most]
    near, near_counts = sort_slots(
        lax.shift_right_logical(a, 2), a & 3, lax.shift_right_logical(b, 2), b & 3,
        slots[4:5, 0:1], 4, late_mask, n_col, plan.near, plan.far_first,
    )
    a, b = slots[2:3, :far_most], slots[3:4, :far_most]
    a_device = lax.shift_right_logical(a * 9363, 16)
    b_device = lax.shift_right_logical(b * 9363, 16)
    far, far_counts = sort_slots(
        a_device, a - a_device * CLUSTERS, b_device, b - b_device * CLUSTERS,
        slots[5:6, 0:1], CLUSTERS, late_mask, n_col, plan.far, plan.size - plan.far_first,
    )
    out[:, : plan.far_first] = near
    out[:, plan.far_first :] = far
    counts[...] = jnp.where(iota((8, LANES), 1) == 0, near_counts, far_counts)


def row_kernel(n_col, *refs):
    chips, near_row, far_row = refs[:-2], refs[-2], refs[-1]
    empty = jnp.zeros((8, LANES), F32)
    for i in range(n_col):
        first = i % 2 * COORD_ROWS
        slabs = [chips[i // 2][first + 16 * s : first + 16 * s + 16].astype(F32) for s in range(6)]
        near, far = (4 * i, CLUSTERS * i) if i < 2 else (4 * i + 1, CLUSTERS * i + 1)
        for l in range(4):
            for h in range(2):
                made = row_side(slabs[l][8 * h : 8 * h + 8])
                near_row[near + l, h * LANES : (h + 1) * LANES] = rows(made, empty).T.astype(BF16)
        for c in range(4):
            slab = slabs[4 + c // 2]
            made = row_side(slab[8 * (c % 2) : 8 * (c % 2) + 8])
            tall = rows(made, empty).T.astype(BF16)
            far_row[far + 2 * c] = tall[:64]
            if c < 3:
                far_row[far + 2 * c + 1] = tall[64:]
    for blank in (8, 4 * n_col + 1):
        near_row[blank] = jnp.zeros(near_row.shape[1:], BF16)
    for blank in (2 * CLUSTERS, CLUSTERS * n_col + 1):
        far_row[blank] = jnp.zeros(far_row.shape[1:], BF16)


def prepare(i, block, probes, near_col, coeff_low, coeff_high, far_low, far_high):
    for l in range(4):
        for h in range(2):
            j = 2 * l + h
            half = slice(h * LANES, (h + 1) * LANES)
            probes[4 * i + l, :, half] = block[j * SAMPLES : (j + 1) * SAMPLES]
        slab = block[COORD_ROW + 16 * l : COORD_ROW + 16 * (l + 1)]
        near_col[4 * i + l, :, :LANES] = slab
        near_col[4 * i + l, :, LANES:] = rows(slab[8:], slab[:8])
    slabs = [block[COORD_ROW + 64 + 16 * p : COORD_ROW + 80 + 16 * p] for p in range(2)]
    for k in range(CLUSTERS):
        c, half = k // 2, slice(k % 2 * 64, k % 2 * 64 + 64)
        if k < 6:
            own = block[FAR_ROW + 64 * c : FAR_ROW + 64 * (c + 1)][:, half]
        else:
            own = block[FAR_ROW + 192 : FAR_ROW + 224]
            own = rows(own[:, :64], own[:, 64:])
        empty = jnp.zeros_like(own)
        coeff_low[CLUSTERS * i + k] = lanes(own, empty)
        coeff_high[CLUSTERS * i + k] = lanes(empty, own)
        made = slabs[c // 2].astype(F32)[8 * (c % 2) : 8 * (c % 2) + 8, half]
        empty = jnp.zeros_like(made)
        blank = jnp.zeros((8, LANES), F32)
        far_low[CLUSTERS * i + k] = rows(lanes(made, empty), blank).astype(BF16)
        far_high[CLUSTERS * i + k] = rows(lanes(empty, made), blank).astype(BF16)


def work(plan, group, lists, counts, near_row, far_row, prepared, totals):
    probes, near_col, coeff_low, coeff_high, far_low, far_high = prepared
    near_total, far_even, far_odd = totals
    near_first, far_first = (0, 0) if group >= 2 else (9, 2 * CLUSTERS + 1)

    def near_terms(place, slots):
        terms = []
        for u in range(slots):
            a, b = lists[0, place + u], lists[1, place + u]
            parts = []
            for q in range(2):
                part = slice(q * LANES, (q + 1) * LANES)
                parts.append(matern_of(dot(near_row[near_first + a, part], near_col[b])))
            terms.append((a, dot(probes[b], rows(*parts), NT)))
        return terms

    def near_add(terms):
        for a, term in terms:
            near_total[a] += term

    def far_terms(place):
        terms = []
        for u in range(0, FAR_UNROLL, 2):
            a0, a1 = lists[0, place + u], lists[0, place + u + 1]
            b0, b1 = lists[1, place + u], lists[1, place + u + 1]
            square = dot(far_row[far_first + a0], far_low[b0])
            square += dot(far_row[far_first + a1], far_high[b1])
            both = rows(coeff_low[b0], coeff_high[b1])
            terms.append((a0, a1, dot(matern_of(square), both)))
        return terms

    def far_add(terms):
        for a0, a1, term in terms:
            far_even[a0] += term
            far_odd[a1] += term

    half = NEAR_UNROLL // 2
    halves = (counts[group, 0] + half - 1) // half
    near_groups = halves // 2
    far_groups = (counts[group, 1] + FAR_UNROLL - 1) // FAR_UNROLL
    together = jnp.minimum(near_groups, far_groups)
    near_place, far_place = group * plan.near, plan.far_first + group * plan.far

    def joint_step(g, _):
        near = near_terms(near_place + g * NEAR_UNROLL, NEAR_UNROLL)
        far = far_terms(far_place + g * FAR_UNROLL)
        near_add(near)
        far_add(far)
        return 0

    def near_step(g, _):
        near_add(near_terms(near_place + g * NEAR_UNROLL, NEAR_UNROLL))
        return 0

    def far_step(g, _):
        far_add(far_terms(far_place + g * FAR_UNROLL))
        return 0

    lax.fori_loop(0, together, joint_step, 0)
    lax.fori_loop(together, near_groups, near_step, 0)
    lax.fori_loop(together, far_groups, far_step, 0)

    @pl.when(halves % 2 == 1)
    def _():
        near_add(near_terms(near_place + near_groups * NEAR_UNROLL, half))


def write_parts(outs, near_total, far_even, far_odd):
    for i, out in enumerate(outs):
        for j in range(8):
            half = slice(j % 2 * LANES, (j % 2 + 1) * LANES)
            part = near_total[4 * i + j // 2, :, half]
            out[j * SAMPLES : (j + 1) * SAMPLES] = part.astype(BF16)
        parts = []
        for l in range(CLUSTERS):
            even, odd = far_even[CLUSTERS * i + l], far_odd[CLUSTERS * i + l]
            parts.append(even[:, :64] + odd[:, 64:])
        for j in range(3):
            pair = lanes(*parts[2 * j : 2 * j + 2])
            out[FAR_ROW + 64 * j : FAR_ROW + 64 * (j + 1)] = pair.astype(BF16)
        pair = lanes(parts[6][:32], parts[6][32:])
        out[FAR_ROW + 192 : FAR_ROW + 224] = pair.astype(BF16)


def clear(totals):
    for total in totals:
        total[...] = jnp.zeros_like(total)


def away_early_kernel(plan, members, lists, counts, near_row, far_row, *refs):
    blocks, refs = refs[: len(members)], refs[len(members) :]
    prepared, totals = refs[:6], refs[6:]
    clear(totals)
    for i, block in zip(members, blocks):
        prepare(i, block, *prepared)
    work(plan, 0, lists, counts, near_row, far_row, prepared, totals)


def here_early_kernel(plan, lists, counts, near_row, far_row, *refs):
    prepared, totals = refs[:6], refs[7:]
    clear(totals)
    work(plan, 2, lists, counts, near_row, far_row, prepared, totals)


def away_late_kernel(plan, members, lists, counts, near_row, far_row, *refs):
    blocks, refs = refs[: len(members)], refs[len(members) + 10 :]
    prepared, totals, outs = refs[:6], refs[6:9], refs[9:]
    for i, block in zip(members, blocks):
        prepare(i, block, *prepared)
    work(plan, 1, lists, counts, near_row, far_row, prepared, totals)
    write_parts(outs, *totals)


def here_late_kernel(plan, lists, counts, near_row, far_row, *refs):
    prepared, refs = refs[:6], refs[10:]
    totals, outs = refs[:3], refs[3:]
    work(plan, 3, lists, counts, near_row, far_row, prepared, totals)
    write_parts(outs, *totals)


def final_kernel(count, basis, moves, *refs):
    parts, out = refs[:count], refs[count]

    def total(first, count):
        return sum(part[first : first + count].astype(F32) for part in parts)

    def turned(first):
        tall = total(first, 64).T
        return lanes(tall[:64], tall[64:])

    top = total(FAR_ROW + 192, 32)
    top = rows(top[:, :64], top[:, 64:]).T
    middle = turned(FAR_ROW + 128) + dot_wide(top, moves[:, 256:384])
    for j in range(2):
        pair = turned(FAR_ROW + 64 * j) + dot_wide(
            middle[:, j * RANK : (j + 1) * RANK], moves[:, j * 128 : (j + 1) * 128]
        )
        for k in range(2):
            l = 2 * j + k
            expanded = dot_wide(
                pair[:, k * RANK : (k + 1) * RANK], basis[:, l * LEAF : (l + 1) * LEAF]
            )
            for h in range(2):
                place = (2 * l + h) * LANES
                near = total((2 * l + h) * SAMPLES, SAMPLES)
                made = near + expanded[:, h * LANES : (h + 1) * LANES]
                out[:, place : place + LANES] = made.astype(BF16)


def exchange(x, axis, offset):
    size = lax.axis_size(axis)
    return lax.ppermute(x, axis, [(i, i ^ offset) for i in range(size)])


def local(
    probes, points, skeleton, leaf_basis, transfer, near_list, near_count, far_list, far_count
):
    n_row = lax.axis_size("row")
    n_col = lax.axis_size("col")
    n_y = n_row // 4
    probes, basis, moves = probes.T, leaf_basis.T, transfer.T
    inputs = (probes, basis, moves, points, skeleton)
    small = pltpu.CompilerParams(vmem_limit_bytes=8 << 20)
    packed, coords = pl.pallas_call(
        pack_kernel,
        out_shape=[
            jax.ShapeDtypeStruct((PACKED_ROWS, LANES), BF16),
            jax.ShapeDtypeStruct((COORD_ROWS, LANES), BF16),
        ],
        in_specs=[VMEM] * 5,
        out_specs=[VMEM] * 2,
        name="pack",
    )(*inputs)

    plan = Plan(near_list.shape[-1], far_list.shape[-1])
    early = list(range(2 * n_y + 1))
    late = list(range(2 * n_y + 1, n_row))
    late_mask = sum(1 << j for j in late)
    width = max(LANES, near_list.shape[-1], far_list.shape[-1])

    def placed(x, row):
        return jnp.pad(x, ((row, 8 - row - x.shape[0]), (0, width - x.shape[1])))

    slots = placed(near_list[0, 0], 0) + placed(far_list[0, 0], 2)
    slots = slots + placed(near_count, 4) + placed(far_count, 5)

    def along_z(x, planes, flip):
        pairs = [(z * n_y + y, (z ^ flip) * n_y + y) for z in planes for y in range(n_y)]
        return lax.ppermute(x, "row", pairs)

    own_y = exchange(packed, "row", 1)
    second = along_z(packed, (0, 1, 2, 3), 2)
    neighbour = along_z(packed, (0, 1, 2, 3), 1)
    lists, counts, both = pl.pallas_call(
        functools.partial(plan_kernel, n_col, np.uint32(late_mask).astype(np.int32), plan),
        out_shape=[
            jax.ShapeDtypeStruct((2, plan.size), jnp.int32),
            jax.ShapeDtypeStruct((8, LANES), jnp.int32),
            jax.ShapeDtypeStruct((2 * COORD_ROWS, LANES), BF16),
        ],
        in_specs=[VMEM] * 3,
        out_specs=[VMEM] * 3,
        compiler_params=small,
        cost_estimate=pl.CostEstimate(flops=1 << 30, bytes_accessed=1 << 12, transcendentals=0),
        name="plan",
    )(slots, coords, exchange(coords, "col", 1))

    row_coords = [both] + [exchange(both, "col", k) for k in range(2, n_col, 2)]
    neighbour = tie(neighbour, lists)
    neighbour_y = exchange(neighbour, "row", 1)
    second = tie(second, own_y, neighbour_y, lists)
    again = pl.pallas_call(
        hold_kernel,
        out_shape=jax.ShapeDtypeStruct((PACKED_ROWS, LANES), BF16),
        in_specs=[VMEM, ANY],
        out_specs=VMEM,
        compiler_params=small,
        name="hold",
    )(packed, second)
    inner, outer = along_z(again, (1, 2), 3), along_z(second, (1, 2), 1)

    def with_y(block, first=None):
        blocks = [block, exchange(block, "row", 1) if first is None else first]
        return blocks + [exchange(block, "row", y) for y in range(2, n_y)]

    blocks = with_y(packed, own_y) + with_y(neighbour, neighbour_y) + with_y(second)

    row_features = pl.pallas_call(
        functools.partial(row_kernel, n_col),
        out_shape=[
            jax.ShapeDtypeStruct((4 * n_col + 2, LEAF, FEATURES), BF16),
            jax.ShapeDtypeStruct((CLUSTERS * n_col + 2, RANK, FEATURES), BF16),
        ],
        in_specs=[VMEM] * (n_col // 2),
        out_specs=[VMEM] * 2,
        compiler_params=small,
        name="row_side",
    )(*row_coords)

    def sums(targets):
        near = (4 * targets + 1, SAMPLES, LEAF)
        far = (CLUSTERS * targets + 1, RANK, LANES)
        return [near, far, far]

    part = jax.ShapeDtypeStruct((COORD_ROW, LANES), BF16)
    held = [
        jax.ShapeDtypeStruct(shape, BF16)
        for shape in [
            (4 * n_row, SAMPLES, LEAF),
            (4 * n_row, FEATURES, LEAF),
            (CLUSTERS * n_row, RANK, LANES),
            (CLUSTERS * n_row, RANK, LANES),
            (CLUSTERS * n_row, FEATURES, LANES),
            (CLUSTERS * n_row, FEATURES, LANES),
        ]
    ]
    held += [jax.ShapeDtypeStruct(shape, F32) for shape in sums(n_col - 2)]
    params = pltpu.CompilerParams(vmem_limit_bytes=32 << 20)
    cost = pl.CostEstimate(flops=1 << 33, bytes_accessed=1 << 20, transcendentals=0)
    local_sums = [jax.ShapeDtypeStruct(shape, F32) for shape in sums(2)]
    handed = pl.pallas_call(
        functools.partial(away_early_kernel, plan, early),
        out_shape=held,
        in_specs=[SMEM] * 2 + [VMEM] * (2 + len(early)),
        out_specs=[VMEM] * len(held),
        compiler_params=params,
        cost_estimate=cost,
        name="away_early",
    )(lists, counts, *row_features, *[blocks[j] for j in early])
    third = pl.pallas_call(
        functools.partial(pick_kernel, n_y),
        out_shape=jax.ShapeDtypeStruct((PACKED_ROWS, LANES), BF16),
        in_specs=[VMEM] * 2 + [ANY],
        out_specs=VMEM,
        compiler_params=small,
        name="pick",
    )(inner, outer, handed[6])
    blocks += with_y(third)
    here_totals = pl.pallas_call(
        functools.partial(here_early_kernel, plan),
        out_shape=local_sums,
        in_specs=[SMEM] * 2 + [VMEM] * 8 + [ANY],
        out_specs=[VMEM] * 3,
        compiler_params=params,
        cost_estimate=cost,
        name="here_early",
    )(lists, counts, *row_features, *handed[:6], third)
    first = 4 + len(late) + 1
    handed = pl.pallas_call(
        functools.partial(away_late_kernel, plan, late),
        out_shape=held + [part] * (n_col - 2),
        in_specs=[SMEM] * 2 + [VMEM] * (2 + len(late)) + [ANY] + [VMEM] * len(held),
        out_specs=[VMEM] * (len(held) + n_col - 2),
        input_output_aliases={first + k: k for k in range(len(held))},
        compiler_params=params,
        cost_estimate=cost,
        name="away_late",
    )(lists, counts, *row_features, *[blocks[j] for j in late], here_totals[0], *handed)
    prepared, parts = handed[:6], handed[len(held) :]
    mine, other = parts[0::2], [exchange(part, "col", 1) for part in parts[1::2]]
    joined = pl.pallas_call(
        functools.partial(join_kernel, len(mine)),
        out_shape=[part] * len(mine),
        in_specs=[VMEM] * (2 * len(mine)),
        out_specs=[VMEM] * len(mine),
        compiler_params=params,
        name="join",
    )(*mine, *other)
    arrived = [exchange(joined[k], "col", 2 * k + 2) for k in range(len(mine))]
    here = pl.pallas_call(
        functools.partial(here_late_kernel, plan),
        out_shape=local_sums + [part] * 2,
        in_specs=[SMEM] * 2 + [VMEM] * 8 + [ANY] + [VMEM] * 3,
        out_specs=[VMEM] * 5,
        input_output_aliases={11 + k: k for k in range(3)},
        compiler_params=params,
        cost_estimate=cost,
        name="here_late",
    )(lists, counts, *row_features, *prepared, joined[0], *here_totals)[3:]
    arrived += [here[0], exchange(tie(here[1], *arrived), "col", 1)]
    sample = pl.pallas_call(
        functools.partial(final_kernel, len(arrived)),
        out_shape=jax.ShapeDtypeStruct((SAMPLES, OWN), BF16),
        in_specs=[VMEM] * (2 + len(arrived)),
        out_specs=VMEM,
        compiler_params=pltpu.CompilerParams(vmem_limit_bytes=16 << 20),
        name="final",
    )(basis, moves, *arrived)
    return sample.T


def solution(mesh):
    placed = (
        P(("row", "col"), None),
        P(None, ("row", "col")),
        P(None, ("row", "col")),
        P(("row", "col"), None),
        P(("row", "col"), None),
        P("row", "col", None, None),
        P("row", "col"),
        P("row", "col", None, None),
        P("row", "col"),
    )
    return jax.shard_map(
        local, mesh=mesh, in_specs=placed, out_specs=P(("row", "col"), None), check_vma=False
    )
```

```python
import functools
import math

import jax
import jax.numpy as jnp
import numpy as np
from jax import lax
from jax.experimental import pallas as pl
from jax.experimental.pallas import tpu as pltpu
from jax.sharding import PartitionSpec as P

LEAF = 256
RANK = 64
SAMPLES = 64
OWN = 4 * LEAF
CLUSTERS = 7
LANES = 128
F32 = jnp.float32
BF16 = jnp.bfloat16
FAR_ROW = OWN // LANES * SAMPLES
COORD_ROW = FAR_ROW + CLUSTERS * SAMPLES // 2
COORD_ROWS = 96
PACKED_ROWS = COORD_ROW + COORD_ROWS
FEATURES = 16
CLASSES = 4
NEAR_UNROLL = 8
FAR_UNROLL = 16
RATE = math.sqrt(3.0) / 0.15

ANY = pl.BlockSpec(memory_space=pl.ANY)
VMEM = pl.BlockSpec(memory_space=pltpu.VMEM)
SMEM = pl.BlockSpec(memory_space=pltpu.SMEM)
NN = (((1,), (0,)), ((), ()))
NT = (((1,), (1,)), ((), ()))


def dot(a, b, dims=NN):
    return lax.dot_general(a, b, dims, preferred_element_type=F32)


def dot_wide(a, b):
    high = a.astype(BF16)
    low = (a - high.astype(F32)).astype(BF16)
    return dot(high, b) + dot(low, b)


def lanes(a, b):
    return jnp.concatenate([a, b], axis=1)


def rows(*parts):
    return jnp.concatenate(parts, axis=0)


def features(points):
    norm = points * points
    norm = norm[0:1] + norm[1:2] + norm[2:3]
    high = norm.astype(BF16).astype(F32)
    rest = norm - high
    middle = rest.astype(BF16).astype(F32)
    ones = jnp.ones_like(norm)
    return rows(points, high, middle, rest - middle, ones, ones)


def row_side(made):
    ones = made[6:7]
    return rows(-2.0 * made[0:3], ones, ones, ones, made[3:4], made[4:5])


def matern_of(square):
    square = jnp.maximum(square, 1e-14)
    x = (square * lax.rsqrt(square)) * -RATE
    return ((1.0 - x) * jnp.exp(x)).astype(BF16)


def pack_kernel(probes, basis, moves, points, skeleton, packed, coords):
    near = features(points[...].astype(F32))
    far = features(lanes(skeleton[...].astype(F32), jnp.zeros((3, 64), F32)))
    chunks = [near[:, j * LANES : (j + 1) * LANES] for j in range(8)]
    chunks += [far[:, j * LANES : (j + 1) * LANES] for j in range(4)]
    made = rows(*chunks).astype(BF16)
    packed[COORD_ROW:] = made
    coords[...] = made
    leaves = []
    for l in range(4):
        part = slice(l * LEAF, (l + 1) * LEAF)
        leaves.append(dot(basis[:, part], probes[:, part], NT).astype(BF16))
    middle = [
        dot(moves[:, j * 128 : (j + 1) * 128], rows(*leaves[2 * j : 2 * j + 2])).astype(BF16)
        for j in range(2)
    ]
    top = dot(moves[:, 256:384], rows(*middle)).astype(BF16)
    for j in range(8):
        packed[j * SAMPLES : (j + 1) * SAMPLES] = probes[:, j * LANES : (j + 1) * LANES]
    packed[FAR_ROW : FAR_ROW + 64] = lanes(leaves[0], leaves[1])
    packed[FAR_ROW + 64 : FAR_ROW + 128] = lanes(leaves[2], leaves[3])
    packed[FAR_ROW + 128 : FAR_ROW + 192] = lanes(middle[0], middle[1])
    packed[FAR_ROW + 192 : FAR_ROW + 224] = lanes(top[:32], top[32:])


class Plan:
    def __init__(self, near_most, far_most):
        self.near = near_most + NEAR_UNROLL
        self.far = far_most + FAR_UNROLL
        self.far_first = -(-CLASSES * self.near // LANES) * LANES
        self.size = self.far_first + -(-CLASSES * self.far // LANES) * LANES


def iota(shape, axis):
    return lax.broadcasted_iota(jnp.int32, shape, axis)


def pick_kernel(n_y, inner, outer, _, out):
    z = lax.axis_index("row") // n_y
    is_inner = (z == 1) | (z == 2)

    @pl.when(is_inner)
    def _():
        out[...] = inner[...]

    @pl.when(jnp.logical_not(is_inner))
    def _():
        out[...] = outer[...]


def tie_kernel(*refs):
    del refs


def tie(x, *others, cost=None):
    return pl.pallas_call(
        tie_kernel,
        out_shape=jax.ShapeDtypeStruct(x.shape, x.dtype),
        in_specs=[ANY] * (1 + len(others)),
        out_specs=ANY,
        input_output_aliases={0: 0},
        compiler_params=pltpu.CompilerParams(vmem_limit_bytes=1 << 20),
        cost_estimate=cost,
        name="tie",
    )(x, *others)


def join_kernel(count, *refs):
    for mine, other, out in zip(refs[:count], refs[count : 2 * count], refs[2 * count :]):
        out[...] = (mine[...].astype(F32) + other[...].astype(F32)).astype(BF16)


def sort_slots(a_device, a_rest, b_device, b_rest, count, per_device, late_mask, n_col, most, width):
    slots = a_device.shape[1]
    target = a_device ^ lax.axis_index("col")
    source = b_device ^ lax.axis_index("row")
    remote = target >= 2
    is_late = lax.shift_right_logical(jnp.full_like(source, late_mask), source) & 1
    alive = iota((1, slots), 1) < count
    group = jnp.where(alive, jnp.where(remote, 0, 2) + is_late, 7)
    row = (target - jnp.where(remote, 2, 0)) * per_device + a_rest
    column = source * per_device + b_rest
    member = jnp.where(iota((8, slots), 0) == group, 1.0, 0.0)
    before = jnp.where(iota((slots, slots), 0) < iota((slots, slots), 1), 1.0, 0.0)
    ahead = dot(member.astype(BF16), before.astype(BF16))
    ahead = jnp.sum(member * ahead, axis=0, keepdims=True).astype(jnp.int32)
    place = jnp.where(alive, group * most + ahead, -1)
    chosen = jnp.where(iota((width, slots), 0) == place, 1.0, 0.0).astype(BF16)
    ones = jnp.ones((6, slots), F32)
    values = rows(row.astype(F32), column.astype(F32), ones).astype(BF16)
    found = dot(values, chosen, NT)
    here = iota((1, width), 1) >= 2 * most
    blank = jnp.where(here, 2.0 * per_device, (n_col - 2.0) * per_device)
    made = rows(found[0:1] + blank * (1.0 - found[2:3]), found[1:2])
    return made.astype(jnp.int32), jnp.sum(member, axis=1, keepdims=True).astype(jnp.int32)


def plan_kernel(n_col, late_mask, plan, slots, coords, mate, out, counts, both):
    both[:COORD_ROWS] = coords[...]
    both[COORD_ROWS:] = mate[...]
    near_most, far_most = plan.near - NEAR_UNROLL, plan.far - FAR_UNROLL
    a, b = slots[0:1, :near_most], slots[1:2, :near_most]
    near, near_counts = sort_slots(
        lax.shift_right_logical(a, 2), a & 3, lax.shift_right_logical(b, 2), b & 3,
        slots[4:5, 0:1], 4, late_mask, n_col, plan.near, plan.far_first,
    )
    a, b = slots[2:3, :far_most], slots[3:4, :far_most]
    a_device = lax.shift_right_logical(a * 9363, 16)
    b_device = lax.shift_right_logical(b * 9363, 16)
    far, far_counts = sort_slots(
        a_device, a - a_device * CLUSTERS, b_device, b - b_device * CLUSTERS,
        slots[5:6, 0:1], CLUSTERS, late_mask, n_col, plan.far, plan.size - plan.far_first,
    )
    out[:, : plan.far_first] = near
    out[:, plan.far_first :] = far
    counts[...] = jnp.where(iota((8, LANES), 1) == 0, near_counts, far_counts)


def row_kernel(n_col, *refs):
    chips, near_row, far_row = refs[:-2], refs[-2], refs[-1]
    empty = jnp.zeros((8, LANES), F32)
    for i in range(n_col):
        first = i % 2 * COORD_ROWS
        slabs = [chips[i // 2][first + 16 * s : first + 16 * s + 16].astype(F32) for s in range(6)]
        near, far = (4 * i, CLUSTERS * i) if i < 2 else (4 * i + 1, CLUSTERS * i + 1)
        for l in range(4):
            for h in range(2):
                made = row_side(slabs[l][8 * h : 8 * h + 8])
                near_row[near + l, h * LANES : (h + 1) * LANES] = rows(made, empty).T.astype(BF16)
        for c in range(4):
            slab = slabs[4 + c // 2]
            made = row_side(slab[8 * (c % 2) : 8 * (c % 2) + 8])
            tall = rows(made, empty).T.astype(BF16)
            far_row[far + 2 * c] = tall[:64]
            if c < 3:
                far_row[far + 2 * c + 1] = tall[64:]
    for blank in (8, 4 * n_col + 1):
        near_row[blank] = jnp.zeros(near_row.shape[1:], BF16)
    for blank in (2 * CLUSTERS, CLUSTERS * n_col + 1):
        far_row[blank] = jnp.zeros(far_row.shape[1:], BF16)


def prepare(i, block, probes, near_col, coeff_low, coeff_high, far_low, far_high):
    for l in range(4):
        for h in range(2):
            j = 2 * l + h
            half = slice(h * LANES, (h + 1) * LANES)
            probes[4 * i + l, :, half] = block[j * SAMPLES : (j + 1) * SAMPLES]
        slab = block[COORD_ROW + 16 * l : COORD_ROW + 16 * (l + 1)]
        near_col[4 * i + l, :, :LANES] = slab
        near_col[4 * i + l, :, LANES:] = rows(slab[8:], slab[:8])
    slabs = [block[COORD_ROW + 64 + 16 * p : COORD_ROW + 80 + 16 * p] for p in range(2)]
    for k in range(CLUSTERS):
        c, half = k // 2, slice(k % 2 * 64, k % 2 * 64 + 64)
        if k < 6:
            own = block[FAR_ROW + 64 * c : FAR_ROW + 64 * (c + 1)][:, half]
        else:
            own = block[FAR_ROW + 192 : FAR_ROW + 224]
            own = rows(own[:, :64], own[:, 64:])
        empty = jnp.zeros_like(own)
        coeff_low[CLUSTERS * i + k] = lanes(own, empty)
        coeff_high[CLUSTERS * i + k] = lanes(empty, own)
        made = slabs[c // 2].astype(F32)[8 * (c % 2) : 8 * (c % 2) + 8, half]
        empty = jnp.zeros_like(made)
        blank = jnp.zeros((8, LANES), F32)
        far_low[CLUSTERS * i + k] = rows(lanes(made, empty), blank).astype(BF16)
        far_high[CLUSTERS * i + k] = rows(lanes(empty, made), blank).astype(BF16)


def work(plan, group, lists, counts, near_row, far_row, prepared, totals):
    probes, near_col, coeff_low, coeff_high, far_low, far_high = prepared
    near_total, far_even, far_odd = totals
    near_first, far_first = (0, 0) if group >= 2 else (9, 2 * CLUSTERS + 1)

    def near_terms(place, slots):
        terms = []
        for u in range(slots):
            a, b = lists[0, place + u], lists[1, place + u]
            parts = []
            for q in range(2):
                part = slice(q * LANES, (q + 1) * LANES)
                parts.append(matern_of(dot(near_row[near_first + a, part], near_col[b])))
            terms.append((a, dot(probes[b], rows(*parts), NT)))
        return terms

    def near_add(terms):
        for a, term in terms:
            near_total[a] += term

    def far_terms(place):
        terms = []
        for u in range(0, FAR_UNROLL, 2):
            a0, a1 = lists[0, place + u], lists[0, place + u + 1]
            b0, b1 = lists[1, place + u], lists[1, place + u + 1]
            square = dot(far_row[far_first + a0], far_low[b0])
            square += dot(far_row[far_first + a1], far_high[b1])
            both = rows(coeff_low[b0], coeff_high[b1])
            terms.append((a0, a1, dot(matern_of(square), both)))
        return terms

    def far_add(terms):
        for a0, a1, term in terms:
            far_even[a0] += term
            far_odd[a1] += term

    half = NEAR_UNROLL // 2
    halves = (counts[group, 0] + half - 1) // half
    near_groups = halves // 2
    far_groups = (counts[group, 1] + FAR_UNROLL - 1) // FAR_UNROLL
    together = jnp.minimum(near_groups, far_groups)
    near_place, far_place = group * plan.near, plan.far_first + group * plan.far

    def joint_step(g, _):
        near = near_terms(near_place + g * NEAR_UNROLL, NEAR_UNROLL)
        far = far_terms(far_place + g * FAR_UNROLL)
        near_add(near)
        far_add(far)
        return 0

    def near_step(g, _):
        near_add(near_terms(near_place + g * NEAR_UNROLL, NEAR_UNROLL))
        return 0

    def far_step(g, _):
        far_add(far_terms(far_place + g * FAR_UNROLL))
        return 0

    lax.fori_loop(0, together, joint_step, 0)
    lax.fori_loop(together, near_groups, near_step, 0)
    lax.fori_loop(together, far_groups, far_step, 0)

    @pl.when(halves % 2 == 1)
    def _():
        near_add(near_terms(near_place + near_groups * NEAR_UNROLL, half))


def write_parts(outs, near_total, far_even, far_odd):
    for i, out in enumerate(outs):
        for j in range(8):
            half = slice(j % 2 * LANES, (j % 2 + 1) * LANES)
            part = near_total[4 * i + j // 2, :, half]
            out[j * SAMPLES : (j + 1) * SAMPLES] = part.astype(BF16)
        parts = []
        for l in range(CLUSTERS):
            even, odd = far_even[CLUSTERS * i + l], far_odd[CLUSTERS * i + l]
            parts.append(even[:, :64] + odd[:, 64:])
        for j in range(3):
            pair = lanes(*parts[2 * j : 2 * j + 2])
            out[FAR_ROW + 64 * j : FAR_ROW + 64 * (j + 1)] = pair.astype(BF16)
        pair = lanes(parts[6][:32], parts[6][32:])
        out[FAR_ROW + 192 : FAR_ROW + 224] = pair.astype(BF16)


def clear(totals):
    for total in totals:
        total[...] = jnp.zeros_like(total)


def away_early_kernel(plan, members, lists, counts, near_row, far_row, *refs):
    blocks, refs = refs[: len(members)], refs[len(members) :]
    prepared, totals = refs[:6], refs[6:]
    clear(totals)
    for i, block in zip(members, blocks):
        prepare(i, block, *prepared)
    work(plan, 0, lists, counts, near_row, far_row, prepared, totals)


def here_early_kernel(plan, lists, counts, near_row, far_row, *refs):
    prepared, totals = refs[:6], refs[7:]
    clear(totals)
    work(plan, 2, lists, counts, near_row, far_row, prepared, totals)


def away_late_kernel(plan, members, lists, counts, near_row, far_row, *refs):
    blocks, refs = refs[: len(members)], refs[len(members) + 10 :]
    prepared, totals, outs = refs[:6], refs[6:9], refs[9:]
    for i, block in zip(members, blocks):
        prepare(i, block, *prepared)
    work(plan, 1, lists, counts, near_row, far_row, prepared, totals)
    write_parts(outs, *totals)


def here_late_kernel(plan, lists, counts, near_row, far_row, *refs):
    prepared, refs = refs[:6], refs[10:]
    totals, outs = refs[:3], refs[3:]
    work(plan, 3, lists, counts, near_row, far_row, prepared, totals)
    write_parts(outs, *totals)


def final_kernel(count, basis, moves, *refs):
    parts, out = refs[:count], refs[count]

    def total(first, count):
        return sum(part[first : first + count].astype(F32) for part in parts)

    def turned(first):
        tall = total(first, 64).T
        return lanes(tall[:64], tall[64:])

    top = total(FAR_ROW + 192, 32)
    top = rows(top[:, :64], top[:, 64:]).T
    middle = turned(FAR_ROW + 128) + dot_wide(top, moves[:, 256:384])
    for j in range(2):
        pair = turned(FAR_ROW + 64 * j) + dot_wide(
            middle[:, j * RANK : (j + 1) * RANK], moves[:, j * 128 : (j + 1) * 128]
        )
        for k in range(2):
            l = 2 * j + k
            expanded = dot_wide(
                pair[:, k * RANK : (k + 1) * RANK], basis[:, l * LEAF : (l + 1) * LEAF]
            )
            for h in range(2):
                place = (2 * l + h) * LANES
                near = total((2 * l + h) * SAMPLES, SAMPLES)
                made = near + expanded[:, h * LANES : (h + 1) * LANES]
                out[:, place : place + LANES] = made.astype(BF16)


def exchange(x, axis, offset):
    size = lax.axis_size(axis)
    return lax.ppermute(x, axis, [(i, i ^ offset) for i in range(size)])


def local(
    probes, points, skeleton, leaf_basis, transfer, near_list, near_count, far_list, far_count
):
    n_row = lax.axis_size("row")
    n_col = lax.axis_size("col")
    n_y = n_row // 4
    probes, basis, moves = probes.T, leaf_basis.T, transfer.T
    inputs = (probes, basis, moves, points, skeleton)
    small = pltpu.CompilerParams(vmem_limit_bytes=8 << 20)
    packed, coords = pl.pallas_call(
        pack_kernel,
        out_shape=[
            jax.ShapeDtypeStruct((PACKED_ROWS, LANES), BF16),
            jax.ShapeDtypeStruct((COORD_ROWS, LANES), BF16),
        ],
        in_specs=[VMEM] * 5,
        out_specs=[VMEM] * 2,
        name="pack",
    )(*inputs)

    plan = Plan(near_list.shape[-1], far_list.shape[-1])
    early = list(range(2 * n_y + 1))
    late = list(range(2 * n_y + 1, n_row))
    late_mask = sum(1 << j for j in late)
    width = max(LANES, near_list.shape[-1], far_list.shape[-1])

    def placed(x, row):
        return jnp.pad(x, ((row, 8 - row - x.shape[0]), (0, width - x.shape[1])))

    slots = placed(near_list[0, 0], 0) + placed(far_list[0, 0], 2)
    slots = slots + placed(near_count, 4) + placed(far_count, 5)

    def along_z(x, planes, flip):
        pairs = [(z * n_y + y, (z ^ flip) * n_y + y) for z in planes for y in range(n_y)]
        return lax.ppermute(x, "row", pairs)

    own_y = exchange(packed, "row", 1)
    second = along_z(packed, (0, 1, 2, 3), 2)
    neighbour = along_z(packed, (0, 1, 2, 3), 1)
    lists, counts, both = pl.pallas_call(
        functools.partial(plan_kernel, n_col, np.uint32(late_mask).astype(np.int32), plan),
        out_shape=[
            jax.ShapeDtypeStruct((2, plan.size), jnp.int32),
            jax.ShapeDtypeStruct((8, LANES), jnp.int32),
            jax.ShapeDtypeStruct((2 * COORD_ROWS, LANES), BF16),
        ],
        in_specs=[VMEM] * 3,
        out_specs=[VMEM] * 3,
        compiler_params=small,
        cost_estimate=pl.CostEstimate(flops=1 << 30, bytes_accessed=1 << 12, transcendentals=0),
        name="plan",
    )(slots, coords, exchange(coords, "col", 1))

    row_coords = [both] + [exchange(both, "col", k) for k in range(2, n_col, 2)]
    neighbour = tie(neighbour, lists)
    neighbour_y = exchange(neighbour, "row", 1)
    second = tie(second, own_y, neighbour_y, lists)
    inner, outer = along_z(packed, (1, 2), 3), along_z(second, (1, 2), 1)

    def with_y(block, first=None):
        blocks = [block, exchange(block, "row", 1) if first is None else first]
        return blocks + [exchange(block, "row", y) for y in range(2, n_y)]

    blocks = with_y(packed, own_y) + with_y(neighbour, neighbour_y) + with_y(second)

    row_features = pl.pallas_call(
        functools.partial(row_kernel, n_col),
        out_shape=[
            jax.ShapeDtypeStruct((4 * n_col + 2, LEAF, FEATURES), BF16),
            jax.ShapeDtypeStruct((CLUSTERS * n_col + 2, RANK, FEATURES), BF16),
        ],
        in_specs=[VMEM] * (n_col // 2),
        out_specs=[VMEM] * 2,
        compiler_params=small,
        name="row_side",
    )(*row_coords)

    def sums(targets):
        near = (4 * targets + 1, SAMPLES, LEAF)
        far = (CLUSTERS * targets + 1, RANK, LANES)
        return [near, far, far]

    part = jax.ShapeDtypeStruct((COORD_ROW, LANES), BF16)
    held = [
        jax.ShapeDtypeStruct(shape, BF16)
        for shape in [
            (4 * n_row, SAMPLES, LEAF),
            (4 * n_row, FEATURES, LEAF),
            (CLUSTERS * n_row, RANK, LANES),
            (CLUSTERS * n_row, RANK, LANES),
            (CLUSTERS * n_row, FEATURES, LANES),
            (CLUSTERS * n_row, FEATURES, LANES),
        ]
    ]
    held += [jax.ShapeDtypeStruct(shape, F32) for shape in sums(n_col - 2)]
    params = pltpu.CompilerParams(vmem_limit_bytes=32 << 20)
    cost = pl.CostEstimate(flops=1 << 33, bytes_accessed=1 << 20, transcendentals=0)
    local_sums = [jax.ShapeDtypeStruct(shape, F32) for shape in sums(2)]
    handed = pl.pallas_call(
        functools.partial(away_early_kernel, plan, early),
        out_shape=held,
        in_specs=[SMEM] * 2 + [VMEM] * (2 + len(early)),
        out_specs=[VMEM] * len(held),
        compiler_params=params,
        cost_estimate=cost,
        name="away_early",
    )(lists, counts, *row_features, *[blocks[j] for j in early])
    third = pl.pallas_call(
        functools.partial(pick_kernel, n_y),
        out_shape=jax.ShapeDtypeStruct((PACKED_ROWS, LANES), BF16),
        in_specs=[VMEM] * 2 + [ANY],
        out_specs=VMEM,
        compiler_params=small,
        name="pick",
    )(inner, outer, handed[6])
    blocks += with_y(third)
    here_totals = pl.pallas_call(
        functools.partial(here_early_kernel, plan),
        out_shape=local_sums,
        in_specs=[SMEM] * 2 + [VMEM] * 8 + [ANY],
        out_specs=[VMEM] * 3,
        compiler_params=params,
        cost_estimate=cost,
        name="here_early",
    )(lists, counts, *row_features, *handed[:6], third)
    first = 4 + len(late) + 1
    handed = pl.pallas_call(
        functools.partial(away_late_kernel, plan, late),
        out_shape=held + [part] * (n_col - 2),
        in_specs=[SMEM] * 2 + [VMEM] * (2 + len(late)) + [ANY] + [VMEM] * len(held),
        out_specs=[VMEM] * (len(held) + n_col - 2),
        input_output_aliases={first + k: k for k in range(len(held))},
        compiler_params=params,
        cost_estimate=cost,
        name="away_late",
    )(lists, counts, *row_features, *[blocks[j] for j in late], here_totals[0], *handed)
    prepared, parts = handed[:6], handed[len(held) :]
    mine, other = parts[0::2], [exchange(part, "col", 1) for part in parts[1::2]]
    joined = pl.pallas_call(
        functools.partial(join_kernel, len(mine)),
        out_shape=[part] * len(mine),
        in_specs=[VMEM] * (2 * len(mine)),
        out_specs=[VMEM] * len(mine),
        compiler_params=params,
        name="join",
    )(*mine, *other)
    arrived = [exchange(joined[k], "col", 2 * k + 2) for k in range(len(mine))]
    here = pl.pallas_call(
        functools.partial(here_late_kernel, plan),
        out_shape=local_sums + [part] * 2,
        in_specs=[SMEM] * 2 + [VMEM] * 8 + [ANY] + [VMEM] * 3,
        out_specs=[VMEM] * 5,
        input_output_aliases={11 + k: k for k in range(3)},
        compiler_params=params,
        cost_estimate=cost,
        name="here_late",
    )(lists, counts, *row_features, *prepared, joined[0], *here_totals)[3:]
    arrived = [tie(x, cost=cost) for x in arrived]
    arrived += [here[0], exchange(here[1], "col", 1)]
    sample = pl.pallas_call(
        functools.partial(final_kernel, len(arrived)),
        out_shape=jax.ShapeDtypeStruct((SAMPLES, OWN), BF16),
        in_specs=[VMEM] * (2 + len(arrived)),
        out_specs=VMEM,
        compiler_params=pltpu.CompilerParams(vmem_limit_bytes=16 << 20),
        name="final",
    )(basis, moves, *arrived)
    return sample.T


def solution(mesh):
    placed = (
        P(("row", "col"), None),
        P(None, ("row", "col")),
        P(None, ("row", "col")),
        P(("row", "col"), None),
        P(("row", "col"), None),
        P("row", "col", None, None),
        P("row", "col"),
        P("row", "col", None, None),
        P("row", "col"),
    )
    return jax.shard_map(
        local, mesh=mesh, in_specs=placed, out_specs=P(("row", "col"), None), check_vma=False
    )
```

```python
import functools
import math

import jax
import jax.numpy as jnp
from jax import lax
from jax.experimental import pallas as pl
from jax.experimental.pallas import tpu as pltpu
from jax.sharding import PartitionSpec as P

LEAF = 256
RANK = 64
SAMPLES = 64
OWN = 4 * LEAF
CLUSTERS = 7
LANES = 128
F32 = jnp.float32
BF16 = jnp.bfloat16
FAR_ROW = OWN // LANES * SAMPLES
COORD_ROW = FAR_ROW + CLUSTERS * SAMPLES // 2
COORD_ROWS = 96
PACKED_ROWS = COORD_ROW + COORD_ROWS
FEATURES = 16
CLASSES = 4
NEAR_UNROLL = 8
FAR_UNROLL = 16
RATE = math.sqrt(3.0) / 0.15
HERE_UNITS = 1

ANY = pl.BlockSpec(memory_space=pl.ANY)
VMEM = pl.BlockSpec(memory_space=pltpu.VMEM)
SMEM = pl.BlockSpec(memory_space=pltpu.SMEM)
NN = (((1,), (0,)), ((), ()))
NT = (((1,), (1,)), ((), ()))


def dot(a, b, dims=NN):
    return lax.dot_general(a, b, dims, preferred_element_type=F32)


def dot_wide(a, b):
    high = a.astype(BF16)
    low = (a - high.astype(F32)).astype(BF16)
    return dot(high, b) + dot(low, b)


def lanes(a, b):
    return jnp.concatenate([a, b], axis=1)


def rows(*parts):
    return jnp.concatenate(parts, axis=0)


def features(points):
    norm = points * points
    norm = norm[0:1] + norm[1:2] + norm[2:3]
    high = norm.astype(BF16).astype(F32)
    rest = norm - high
    middle = rest.astype(BF16).astype(F32)
    ones = jnp.ones_like(norm)
    return rows(points, high, middle, rest - middle, ones, ones)


def row_side(made):
    ones = made[6:7]
    return rows(-2.0 * made[0:3], ones, ones, ones, made[3:4], made[4:5])


def matern_of(square):
    square = jnp.maximum(square, 1e-14)
    x = (square * lax.rsqrt(square)) * -RATE
    return ((1.0 - x) * jnp.exp(x)).astype(BF16)


def pack_kernel(probes, basis, moves, points, skeleton, packed, coords):
    near = features(points[...].astype(F32))
    far = features(lanes(skeleton[...].astype(F32), jnp.zeros((3, 64), F32)))
    chunks = [near[:, j * LANES : (j + 1) * LANES] for j in range(8)]
    chunks += [far[:, j * LANES : (j + 1) * LANES] for j in range(4)]
    made = rows(*chunks).astype(BF16)
    packed[COORD_ROW:] = made
    coords[...] = made
    leaves = []
    for l in range(4):
        part = slice(l * LEAF, (l + 1) * LEAF)
        leaves.append(dot(basis[:, part], probes[:, part], NT).astype(BF16))
    middle = [
        dot(moves[:, j * 128 : (j + 1) * 128], rows(*leaves[2 * j : 2 * j + 2])).astype(BF16)
        for j in range(2)
    ]
    top = dot(moves[:, 256:384], rows(*middle)).astype(BF16)
    for j in range(8):
        packed[j * SAMPLES : (j + 1) * SAMPLES] = probes[:, j * LANES : (j + 1) * LANES]
    packed[FAR_ROW : FAR_ROW + 64] = lanes(leaves[0], leaves[1])
    packed[FAR_ROW + 64 : FAR_ROW + 128] = lanes(leaves[2], leaves[3])
    packed[FAR_ROW + 128 : FAR_ROW + 192] = lanes(middle[0], middle[1])
    packed[FAR_ROW + 192 : FAR_ROW + 224] = lanes(top[:32], top[32:])


class Plan:
    def __init__(self, near_most, far_most):
        self.near = near_most + NEAR_UNROLL
        self.far = far_most + FAR_UNROLL
        self.far_first = -(-CLASSES * self.near // LANES) * LANES
        self.size = self.far_first + -(-CLASSES * self.far // LANES) * LANES


def iota(shape, axis):
    return lax.broadcasted_iota(jnp.int32, shape, axis)


def tie_kernel(*refs):
    del refs


def tie(x, *others, cost=None):
    return pl.pallas_call(
        tie_kernel,
        out_shape=jax.ShapeDtypeStruct(x.shape, x.dtype),
        in_specs=[ANY] * (1 + len(others)),
        out_specs=ANY,
        input_output_aliases={0: 0},
        compiler_params=pltpu.CompilerParams(vmem_limit_bytes=1 << 20),
        cost_estimate=cost,
        name="tie",
    )(x, *others)


def join_kernel(count, *refs):
    for mine, other, out in zip(refs[:count], refs[count : 2 * count], refs[2 * count :]):
        out[...] = (mine[...].astype(F32) + other[...].astype(F32)).astype(BF16)


def sort_slots(a_device, a_rest, b_device, b_rest, count, per_device, n_col, n_y, most, width):
    slots = a_device.shape[1]
    target = a_device ^ lax.axis_index("col")
    source = b_device ^ lax.axis_index("row")
    remote = target >= 2
    stage = jnp.where(source > 3 * n_y, 2, jnp.where(source > 2 * n_y, 1, 0))
    group = jnp.where(remote, stage, jnp.where(stage == 2, 4, 3))
    alive = iota((1, slots), 1) < count
    group = jnp.where(alive, group, 7)
    row = (target - jnp.where(remote, 2, 0)) * per_device + a_rest
    column = source * per_device + b_rest
    member = jnp.where(iota((8, slots), 0) == group, 1.0, 0.0)
    before = jnp.where(iota((slots, slots), 0) < iota((slots, slots), 1), 1.0, 0.0)
    ahead = dot(member.astype(BF16), before.astype(BF16))
    ahead = jnp.sum(member * ahead, axis=0, keepdims=True)
    sizes = jnp.sum(member, axis=1, keepdims=True)
    ahead = (ahead + jnp.where(group == 4, sizes[3:4], 0.0)).astype(jnp.int32)
    place = jnp.where(alive, jnp.minimum(group, 3) * most + ahead, -1)
    chosen = jnp.where(iota((width, slots), 0) == place, 1.0, 0.0).astype(BF16)
    ones = jnp.ones((6, slots), F32)
    values = rows(row.astype(F32), column.astype(F32), ones).astype(BF16)
    found = dot(values, chosen, NT)
    here = iota((1, width), 1) >= 3 * most
    blank = jnp.where(here, 2.0 * per_device, (n_col - 2.0) * per_device)
    made = rows(found[0:1] + blank * (1.0 - found[2:3]), found[1:2])
    return made.astype(jnp.int32), sizes.astype(jnp.int32)


def plan_kernel(n_col, n_y, plan, slots, coords, mate, out, counts, both):
    both[:COORD_ROWS] = coords[...]
    both[COORD_ROWS:] = mate[...]
    near_most, far_most = plan.near - NEAR_UNROLL, plan.far - FAR_UNROLL
    a, b = slots[0:1, :near_most], slots[1:2, :near_most]
    near, near_counts = sort_slots(
        lax.shift_right_logical(a, 2), a & 3, lax.shift_right_logical(b, 2), b & 3,
        slots[4:5, 0:1], 4, n_col, n_y, plan.near, plan.far_first,
    )
    a, b = slots[2:3, :far_most], slots[3:4, :far_most]
    a_device = lax.shift_right_logical(a * 9363, 16)
    b_device = lax.shift_right_logical(b * 9363, 16)
    far, far_counts = sort_slots(
        a_device, a - a_device * CLUSTERS, b_device, b - b_device * CLUSTERS,
        slots[5:6, 0:1], CLUSTERS, n_col, n_y, plan.far, plan.size - plan.far_first,
    )
    out[:, : plan.far_first] = near
    out[:, plan.far_first :] = far
    counts[...] = jnp.where(iota((8, LANES), 1) == 0, near_counts, far_counts)


def row_kernel(n_col, *refs):
    chips, near_row, far_row = refs[:-2], refs[-2], refs[-1]
    empty = jnp.zeros((8, LANES), F32)
    for i in range(n_col):
        first = i % 2 * COORD_ROWS
        slabs = [chips[i // 2][first + 16 * s : first + 16 * s + 16].astype(F32) for s in range(6)]
        near, far = (4 * i, CLUSTERS * i) if i < 2 else (4 * i + 1, CLUSTERS * i + 1)
        for l in range(4):
            for h in range(2):
                made = row_side(slabs[l][8 * h : 8 * h + 8])
                near_row[near + l, h * LANES : (h + 1) * LANES] = rows(made, empty).T.astype(BF16)
        for c in range(4):
            slab = slabs[4 + c // 2]
            made = row_side(slab[8 * (c % 2) : 8 * (c % 2) + 8])
            tall = rows(made, empty).T.astype(BF16)
            far_row[far + 2 * c] = tall[:64]
            if c < 3:
                far_row[far + 2 * c + 1] = tall[64:]
    for blank in (8, 4 * n_col + 1):
        near_row[blank] = jnp.zeros(near_row.shape[1:], BF16)
    for blank in (2 * CLUSTERS, CLUSTERS * n_col + 1):
        far_row[blank] = jnp.zeros(far_row.shape[1:], BF16)


def prepare(i, block, probes, near_col, coeff_low, coeff_high, far_low, far_high):
    for l in range(4):
        for h in range(2):
            j = 2 * l + h
            half = slice(h * LANES, (h + 1) * LANES)
            probes[4 * i + l, :, half] = block[j * SAMPLES : (j + 1) * SAMPLES]
        slab = block[COORD_ROW + 16 * l : COORD_ROW + 16 * (l + 1)]
        near_col[4 * i + l, :, :LANES] = slab
        near_col[4 * i + l, :, LANES:] = rows(slab[8:], slab[:8])
    slabs = [block[COORD_ROW + 64 + 16 * p : COORD_ROW + 80 + 16 * p] for p in range(2)]
    for k in range(CLUSTERS):
        c, half = k // 2, slice(k % 2 * 64, k % 2 * 64 + 64)
        if k < 6:
            own = block[FAR_ROW + 64 * c : FAR_ROW + 64 * (c + 1)][:, half]
        else:
            own = block[FAR_ROW + 192 : FAR_ROW + 224]
            own = rows(own[:, :64], own[:, 64:])
        empty = jnp.zeros_like(own)
        coeff_low[CLUSTERS * i + k] = lanes(own, empty)
        coeff_high[CLUSTERS * i + k] = lanes(empty, own)
        made = slabs[c // 2].astype(F32)[8 * (c % 2) : 8 * (c % 2) + 8, half]
        empty = jnp.zeros_like(made)
        blank = jnp.zeros((8, LANES), F32)
        far_low[CLUSTERS * i + k] = rows(lanes(made, empty), blank).astype(BF16)
        far_high[CLUSTERS * i + k] = rows(lanes(empty, made), blank).astype(BF16)


def work(plan, group, lists, counts, near_row, far_row, prepared, totals, part=None):
    probes, near_col, coeff_low, coeff_high, far_low, far_high = prepared
    near_total, far_even, far_odd = totals
    near_first, far_first = (0, 0) if group == 3 else (9, 2 * CLUSTERS + 1)

    def near_terms(place, slots):
        terms = []
        for u in range(slots):
            a, b = lists[0, place + u], lists[1, place + u]
            parts = []
            for q in range(2):
                part = slice(q * LANES, (q + 1) * LANES)
                parts.append(matern_of(dot(near_row[near_first + a, part], near_col[b])))
            terms.append((a, dot(probes[b], rows(*parts), NT)))
        return terms

    def near_add(terms):
        for a, term in terms:
            near_total[a] += term

    def far_terms(place):
        terms = []
        for u in range(0, FAR_UNROLL, 2):
            a0, a1 = lists[0, place + u], lists[0, place + u + 1]
            b0, b1 = lists[1, place + u], lists[1, place + u + 1]
            square = dot(far_row[far_first + a0], far_low[b0])
            square += dot(far_row[far_first + a1], far_high[b1])
            both = rows(coeff_low[b0], coeff_high[b1])
            terms.append((a0, a1, dot(matern_of(square), both)))
        return terms

    def far_add(terms):
        for a0, a1, term in terms:
            far_even[a0] += term
            far_odd[a1] += term

    half = NEAR_UNROLL // 2
    near_count, far_count = counts[group, 0], counts[group, 1]
    near_from = far_from = 0
    if group == 3:
        near_first_part = jnp.minimum(near_count // NEAR_UNROLL, HERE_UNITS)
        far_first_part = jnp.minimum(far_count // FAR_UNROLL, HERE_UNITS)
        near_count, far_count = near_count + counts[4, 0], far_count + counts[4, 1]
        if part == 0:
            near_count, far_count = near_first_part * NEAR_UNROLL, far_first_part * FAR_UNROLL
        else:
            near_from, far_from = near_first_part, far_first_part
            near_count -= near_from * NEAR_UNROLL
            far_count -= far_from * FAR_UNROLL
    halves = (near_count + half - 1) // half
    near_groups = halves // 2
    far_groups = (far_count + FAR_UNROLL - 1) // FAR_UNROLL
    together = jnp.minimum(near_groups, far_groups)
    near_place = group * plan.near + near_from * NEAR_UNROLL
    far_place = plan.far_first + group * plan.far + far_from * FAR_UNROLL

    def joint_step(g, _):
        near = near_terms(near_place + g * NEAR_UNROLL, NEAR_UNROLL)
        far = far_terms(far_place + g * FAR_UNROLL)
        near_add(near)
        far_add(far)
        return 0

    def near_step(g, _):
        near_add(near_terms(near_place + g * NEAR_UNROLL, NEAR_UNROLL))
        return 0

    def far_step(g, _):
        far_add(far_terms(far_place + g * FAR_UNROLL))
        return 0

    lax.fori_loop(0, together, joint_step, 0)
    lax.fori_loop(together, near_groups, near_step, 0)
    lax.fori_loop(together, far_groups, far_step, 0)

    if part == 0:
        return

    @pl.when(halves % 2 == 1)
    def _():
        near_add(near_terms(near_place + near_groups * NEAR_UNROLL, half))


def write_parts(outs, near_total, far_even, far_odd):
    for i, out in enumerate(outs):
        for j in range(8):
            half = slice(j % 2 * LANES, (j % 2 + 1) * LANES)
            part = near_total[4 * i + j // 2, :, half]
            out[j * SAMPLES : (j + 1) * SAMPLES] = part.astype(BF16)
        parts = []
        for l in range(CLUSTERS):
            even, odd = far_even[CLUSTERS * i + l], far_odd[CLUSTERS * i + l]
            parts.append(even[:, :64] + odd[:, 64:])
        for j in range(3):
            pair = lanes(*parts[2 * j : 2 * j + 2])
            out[FAR_ROW + 64 * j : FAR_ROW + 64 * (j + 1)] = pair.astype(BF16)
        pair = lanes(parts[6][:32], parts[6][32:])
        out[FAR_ROW + 192 : FAR_ROW + 224] = pair.astype(BF16)


def clear(totals):
    for total in totals:
        total[...] = jnp.zeros_like(total)


def early_kernel(plan, members, lists, counts, near_row, far_row, *refs):
    blocks, refs = refs[: len(members)], refs[len(members) :]
    prepared, totals = refs[:6], refs[6:]
    clear(totals)
    for i, block in zip(members, blocks):
        prepare(i, block, *prepared)
    work(plan, 0, lists, counts, near_row, far_row, prepared, totals)


def mid_kernel(plan, members, lists, counts, near_row, far_row, *refs):
    blocks, refs = refs[: len(members)], refs[len(members) + 9 :]
    prepared, totals, here = refs[:6], refs[6:9], refs[9:]
    clear(here)
    for i, block in zip(members, blocks):
        prepare(i, block, *prepared)
    work(plan, 1, lists, counts, near_row, far_row, prepared, totals)
    work(plan, 3, lists, counts, near_row, far_row, prepared, here, 0)


def late_kernel(plan, members, lists, counts, near_row, far_row, *refs):
    blocks, refs = refs[: len(members)], refs[len(members) + 9 :]
    prepared, totals, outs = refs[:6], refs[6:9], refs[9:]
    for i, block in zip(members, blocks):
        prepare(i, block, *prepared)
    work(plan, 2, lists, counts, near_row, far_row, prepared, totals)
    write_parts(outs, *totals)


def here_kernel(plan, lists, counts, near_row, far_row, *refs):
    prepared, refs = refs[:6], refs[10:]
    totals, outs = refs[:3], refs[3:]
    work(plan, 3, lists, counts, near_row, far_row, prepared, totals, 1)
    write_parts(outs, *totals)


def final_kernel(count, basis, moves, *refs):
    parts, out = refs[:count], refs[count]

    def total(first, count):
        return sum(part[first : first + count].astype(F32) for part in parts)

    def turned(first):
        tall = total(first, 64).T
        return lanes(tall[:64], tall[64:])

    top = total(FAR_ROW + 192, 32)
    top = rows(top[:, :64], top[:, 64:]).T
    middle = turned(FAR_ROW + 128) + dot_wide(top, moves[:, 256:384])
    for j in range(2):
        pair = turned(FAR_ROW + 64 * j) + dot_wide(
            middle[:, j * RANK : (j + 1) * RANK], moves[:, j * 128 : (j + 1) * 128]
        )
        for k in range(2):
            l = 2 * j + k
            expanded = dot_wide(
                pair[:, k * RANK : (k + 1) * RANK], basis[:, l * LEAF : (l + 1) * LEAF]
            )
            for h in range(2):
                place = (2 * l + h) * LANES
                near = total((2 * l + h) * SAMPLES, SAMPLES)
                made = near + expanded[:, h * LANES : (h + 1) * LANES]
                out[:, place : place + LANES] = made.astype(BF16)


def exchange(x, axis, offset):
    size = lax.axis_size(axis)
    return lax.ppermute(x, axis, [(i, i ^ offset) for i in range(size)])


def local(
    probes, points, skeleton, leaf_basis, transfer, near_list, near_count, far_list, far_count
):
    n_row = lax.axis_size("row")
    n_col = lax.axis_size("col")
    n_y = n_row // 4
    probes, basis, moves = probes.T, leaf_basis.T, transfer.T
    inputs = (probes, basis, moves, points, skeleton)
    small = pltpu.CompilerParams(vmem_limit_bytes=8 << 20)
    packed, coords = pl.pallas_call(
        pack_kernel,
        out_shape=[
            jax.ShapeDtypeStruct((PACKED_ROWS, LANES), BF16),
            jax.ShapeDtypeStruct((COORD_ROWS, LANES), BF16),
        ],
        in_specs=[VMEM] * 5,
        out_specs=[VMEM] * 2,
        name="pack",
    )(*inputs)

    plan = Plan(near_list.shape[-1], far_list.shape[-1])
    width = max(LANES, near_list.shape[-1], far_list.shape[-1])

    def placed(x, row):
        return jnp.pad(x, ((row, 8 - row - x.shape[0]), (0, width - x.shape[1])))

    slots = placed(near_list[0, 0], 0) + placed(far_list[0, 0], 2)
    slots = slots + placed(near_count, 4) + placed(far_count, 5)

    def along_z(x, planes, flip):
        pairs = [(z * n_y + y, (z ^ flip) * n_y + y) for z in planes for y in range(n_y)]
        return lax.ppermute(x, "row", pairs)

    own_y = exchange(packed, "row", 1)
    second = along_z(packed, (0, 1, 2, 3), 2)
    neighbour = along_z(packed, (0, 1, 2, 3), 1)
    lists, counts, both = pl.pallas_call(
        functools.partial(plan_kernel, n_col, n_y, plan),
        out_shape=[
            jax.ShapeDtypeStruct((2, plan.size), jnp.int32),
            jax.ShapeDtypeStruct((8, LANES), jnp.int32),
            jax.ShapeDtypeStruct((2 * COORD_ROWS, LANES), BF16),
        ],
        in_specs=[VMEM] * 3,
        out_specs=[VMEM] * 3,
        compiler_params=small,
        cost_estimate=pl.CostEstimate(flops=1 << 30, bytes_accessed=1 << 12, transcendentals=0),
        name="plan",
    )(slots, coords, exchange(coords, "col", 1))

    row_coords = [both] + [exchange(both, "col", k) for k in range(2, n_col, 2)]
    neighbour = tie(neighbour, lists)
    neighbour_y = exchange(neighbour, "row", 1)
    second = tie(second, own_y, neighbour_y, lists)
    def with_y(block, first=None):
        blocks = [block, exchange(block, "row", 1) if first is None else first]
        return blocks + [exchange(block, "row", y) for y in range(2, n_y)]

    blocks = with_y(packed, own_y) + with_y(neighbour, neighbour_y) + with_y(second)

    row_features = pl.pallas_call(
        functools.partial(row_kernel, n_col),
        out_shape=[
            jax.ShapeDtypeStruct((4 * n_col + 2, LEAF, FEATURES), BF16),
            jax.ShapeDtypeStruct((CLUSTERS * n_col + 2, RANK, FEATURES), BF16),
        ],
        in_specs=[VMEM] * (n_col // 2),
        out_specs=[VMEM] * 2,
        compiler_params=small,
        name="row_side",
    )(*row_coords)

    def sums(targets):
        near = (4 * targets + 1, SAMPLES, LEAF)
        far = (CLUSTERS * targets + 1, RANK, LANES)
        return [near, far, far]

    part = jax.ShapeDtypeStruct((COORD_ROW, LANES), BF16)
    held = [
        jax.ShapeDtypeStruct(shape, BF16)
        for shape in [
            (4 * n_row, SAMPLES, LEAF),
            (4 * n_row, FEATURES, LEAF),
            (CLUSTERS * n_row, RANK, LANES),
            (CLUSTERS * n_row, RANK, LANES),
            (CLUSTERS * n_row, FEATURES, LANES),
            (CLUSTERS * n_row, FEATURES, LANES),
        ]
    ]
    held += [jax.ShapeDtypeStruct(shape, F32) for shape in sums(n_col - 2)]
    params = pltpu.CompilerParams(vmem_limit_bytes=32 << 20)
    cost = pl.CostEstimate(flops=1 << 33, bytes_accessed=1 << 20, transcendentals=0)
    local_sums = [jax.ShapeDtypeStruct(shape, F32) for shape in sums(2)]
    def stage(kernel, members, out_shape, name):
        first = 4 + len(members)
        return pl.pallas_call(
            functools.partial(kernel, plan, members),
            out_shape=out_shape,
            in_specs=[SMEM] * 2 + [VMEM] * (2 + len(members) + len(handed)),
            out_specs=[VMEM] * len(out_shape),
            input_output_aliases={first + k: k for k in range(len(handed))},
            compiler_params=params,
            cost_estimate=cost,
            name=name,
        )(lists, counts, *row_features, *[blocks[j] for j in members], *handed)

    handed = []
    handed = stage(early_kernel, list(range(2 * n_y + 1)), held, "early")
    third = tie(along_z(second, (0, 1, 2, 3), 1), handed[6])
    blocks += with_y(third)
    mid = stage(mid_kernel, list(range(2 * n_y + 1, 3 * n_y + 1)), held + local_sums, "mid")
    handed, here_totals = mid[: len(held)], mid[len(held) :]
    handed = stage(late_kernel, list(range(3 * n_y + 1, n_row)), held + [part] * (n_col - 2), "late")
    prepared, parts = handed[:6], handed[len(held) :]
    mine, other = parts[0::2], [exchange(part, "col", 1) for part in parts[1::2]]
    joined = pl.pallas_call(
        functools.partial(join_kernel, len(mine)),
        out_shape=[part] * len(mine),
        in_specs=[VMEM] * (2 * len(mine)),
        out_specs=[VMEM] * len(mine),
        compiler_params=params,
        name="join",
    )(*mine, *other)
    arrived = [exchange(joined[k], "col", 2 * k + 2) for k in range(len(mine))]
    here = pl.pallas_call(
        functools.partial(here_kernel, plan),
        out_shape=local_sums + [part] * 2,
        in_specs=[SMEM] * 2 + [VMEM] * 8 + [ANY] + [VMEM] * 3,
        out_specs=[VMEM] * 5,
        input_output_aliases={11 + k: k for k in range(3)},
        compiler_params=params,
        cost_estimate=cost,
        name="here",
    )(lists, counts, *row_features, *prepared, joined[0], *here_totals)[3:]
    arrived = [tie(x, cost=cost) for x in arrived]
    arrived += [here[0], exchange(here[1], "col", 1)]
    sample = pl.pallas_call(
        functools.partial(final_kernel, len(arrived)),
        out_shape=jax.ShapeDtypeStruct((SAMPLES, OWN), BF16),
        in_specs=[VMEM] * (2 + len(arrived)),
        out_specs=VMEM,
        compiler_params=pltpu.CompilerParams(vmem_limit_bytes=16 << 20),
        name="final",
    )(basis, moves, *arrived)
    return sample.T


def solution(mesh):
    placed = (
        P(("row", "col"), None),
        P(None, ("row", "col")),
        P(None, ("row", "col")),
        P(("row", "col"), None),
        P(("row", "col"), None),
        P("row", "col", None, None),
        P("row", "col"),
        P("row", "col", None, None),
        P("row", "col"),
    )
    return jax.shard_map(
        local, mesh=mesh, in_specs=placed, out_specs=P(("row", "col"), None), check_vma=False
    )
```

```python
import functools
import math

import jax
import jax.numpy as jnp
from jax import lax
from jax.experimental import pallas as pl
from jax.experimental.pallas import tpu as pltpu
from jax.sharding import PartitionSpec as P

LEAF = 256
RANK = 64
SAMPLES = 64
OWN = 4 * LEAF
CLUSTERS = 7
LANES = 128
F32 = jnp.float32
BF16 = jnp.bfloat16
FAR_ROW = OWN // LANES * SAMPLES
COORD_ROW = FAR_ROW + CLUSTERS * SAMPLES // 2
COORD_ROWS = 96
PACKED_ROWS = COORD_ROW + COORD_ROWS
FEATURES = 16
CLASSES = 2
NEAR_UNROLL = 8
FAR_UNROLL = 16
RATE = math.sqrt(3.0) / 0.15
EARLY_UNITS = 1
HERE_UNITS = 1

ANY = pl.BlockSpec(memory_space=pl.ANY)
VMEM = pl.BlockSpec(memory_space=pltpu.VMEM)
SMEM = pl.BlockSpec(memory_space=pltpu.SMEM)
NN = (((1,), (0,)), ((), ()))
NT = (((1,), (1,)), ((), ()))


def dot(a, b, dims=NN):
    return lax.dot_general(a, b, dims, preferred_element_type=F32)


def dot_wide(a, b):
    high = a.astype(BF16)
    low = (a - high.astype(F32)).astype(BF16)
    return dot(high, b) + dot(low, b)


def lanes(a, b):
    return jnp.concatenate([a, b], axis=1)


def rows(*parts):
    return jnp.concatenate(parts, axis=0)


def features(points):
    norm = points * points
    norm = norm[0:1] + norm[1:2] + norm[2:3]
    high = norm.astype(BF16).astype(F32)
    rest = norm - high
    middle = rest.astype(BF16).astype(F32)
    ones = jnp.ones_like(norm)
    return rows(points, high, middle, rest - middle, ones, ones)


def row_side(made):
    ones = made[6:7]
    return rows(-2.0 * made[0:3], ones, ones, ones, made[3:4], made[4:5])


def matern_of(square):
    square = jnp.maximum(square, 1e-14)
    x = (square * lax.rsqrt(square)) * -RATE
    return ((1.0 - x) * jnp.exp(x)).astype(BF16)


def pack_kernel(probes, basis, moves, points, skeleton, packed, coords):
    near = features(points[...].astype(F32))
    far = features(lanes(skeleton[...].astype(F32), jnp.zeros((3, 64), F32)))
    chunks = [near[:, j * LANES : (j + 1) * LANES] for j in range(8)]
    chunks += [far[:, j * LANES : (j + 1) * LANES] for j in range(4)]
    made = rows(*chunks).astype(BF16)
    packed[COORD_ROW:] = made
    coords[...] = made
    leaves = []
    for l in range(4):
        part = slice(l * LEAF, (l + 1) * LEAF)
        leaves.append(dot(basis[:, part], probes[:, part], NT).astype(BF16))
    middle = [
        dot(moves[:, j * 128 : (j + 1) * 128], rows(*leaves[2 * j : 2 * j + 2])).astype(BF16)
        for j in range(2)
    ]
    top = dot(moves[:, 256:384], rows(*middle)).astype(BF16)
    for j in range(8):
        packed[j * SAMPLES : (j + 1) * SAMPLES] = probes[:, j * LANES : (j + 1) * LANES]
    packed[FAR_ROW : FAR_ROW + 64] = lanes(leaves[0], leaves[1])
    packed[FAR_ROW + 64 : FAR_ROW + 128] = lanes(leaves[2], leaves[3])
    packed[FAR_ROW + 128 : FAR_ROW + 192] = lanes(middle[0], middle[1])
    packed[FAR_ROW + 192 : FAR_ROW + 224] = lanes(top[:32], top[32:])


class Plan:
    def __init__(self, near_most, far_most):
        self.near = near_most + NEAR_UNROLL
        self.far = far_most + FAR_UNROLL
        self.far_first = -(-CLASSES * self.near // LANES) * LANES
        self.size = self.far_first + -(-CLASSES * self.far // LANES) * LANES


def iota(shape, axis):
    return lax.broadcasted_iota(jnp.int32, shape, axis)


def tie_kernel(*refs):
    del refs


def tie(x, *others, cost=None):
    return pl.pallas_call(
        tie_kernel,
        out_shape=jax.ShapeDtypeStruct(x.shape, x.dtype),
        in_specs=[ANY] * (1 + len(others)),
        out_specs=ANY,
        input_output_aliases={0: 0},
        compiler_params=pltpu.CompilerParams(vmem_limit_bytes=1 << 20),
        cost_estimate=cost,
        name="tie",
    )(x, *others)


def join_kernel(count, *refs):
    for mine, other, out in zip(refs[:count], refs[count : 2 * count], refs[2 * count :]):
        out[...] = (mine[...].astype(F32) + other[...].astype(F32)).astype(BF16)


def sort_slots(a_device, a_rest, b_device, b_rest, count, per_device, n_col, n_y, most, width):
    slots = a_device.shape[1]
    target = a_device ^ lax.axis_index("col")
    source = b_device ^ lax.axis_index("row")
    remote = target >= 2
    stage = jnp.where(source > 3 * n_y, 2, jnp.where(source > 2 * n_y, 1, 0))
    group = jnp.where(remote, stage, jnp.where(stage == 2, 4, 3))
    alive = iota((1, slots), 1) < count
    group = jnp.where(alive, group, 7)
    row = (target - jnp.where(remote, 2, 0)) * per_device + a_rest
    column = source * per_device + b_rest
    member = jnp.where(iota((8, slots), 0) == group, 1.0, 0.0)
    before = jnp.where(iota((slots, slots), 0) < iota((slots, slots), 1), 1.0, 0.0)
    ahead = dot(member.astype(BF16), before.astype(BF16))
    ahead = jnp.sum(member * ahead, axis=0, keepdims=True)
    sizes = jnp.sum(member, axis=1, keepdims=True)
    ahead += jnp.where(group == 4, sizes[3:4], 0.0)
    ahead += jnp.where((group == 1) | (group == 2), sizes[0:1], 0.0)
    ahead += jnp.where(group == 2, sizes[1:2], 0.0)
    place = jnp.where(alive, jnp.where(remote, 0, most) + ahead.astype(jnp.int32), -1)
    chosen = jnp.where(iota((width, slots), 0) == place, 1.0, 0.0).astype(BF16)
    ones = jnp.ones((6, slots), F32)
    values = rows(row.astype(F32), column.astype(F32), ones).astype(BF16)
    found = dot(values, chosen, NT)
    here = iota((1, width), 1) >= most
    blank = jnp.where(here, 2.0 * per_device, (n_col - 2.0) * per_device)
    made = rows(found[0:1] + blank * (1.0 - found[2:3]), found[1:2])
    return made.astype(jnp.int32), sizes.astype(jnp.int32)


def plan_kernel(n_col, n_y, plan, slots, coords, mate, out, counts, both):
    both[:COORD_ROWS] = coords[...]
    both[COORD_ROWS:] = mate[...]
    near_most, far_most = plan.near - NEAR_UNROLL, plan.far - FAR_UNROLL
    a, b = slots[0:1, :near_most], slots[1:2, :near_most]
    near, near_counts = sort_slots(
        lax.shift_right_logical(a, 2), a & 3, lax.shift_right_logical(b, 2), b & 3,
        slots[4:5, 0:1], 4, n_col, n_y, plan.near, plan.far_first,
    )
    a, b = slots[2:3, :far_most], slots[3:4, :far_most]
    a_device = lax.shift_right_logical(a * 9363, 16)
    b_device = lax.shift_right_logical(b * 9363, 16)
    far, far_counts = sort_slots(
        a_device, a - a_device * CLUSTERS, b_device, b - b_device * CLUSTERS,
        slots[5:6, 0:1], CLUSTERS, n_col, n_y, plan.far, plan.size - plan.far_first,
    )
    out[:, : plan.far_first] = near
    out[:, plan.far_first :] = far
    counts[...] = jnp.where(iota((8, LANES), 1) == 0, near_counts, far_counts)


def row_kernel(n_col, *refs):
    chips, near_row, far_row = refs[:-3], refs[-2], refs[-1]
    empty = jnp.zeros((8, LANES), F32)
    for i in range(n_col):
        first = i % 2 * COORD_ROWS
        slabs = [chips[i // 2][first + 16 * s : first + 16 * s + 16].astype(F32) for s in range(6)]
        near, far = (4 * i, CLUSTERS * i) if i < 2 else (4 * i + 1, CLUSTERS * i + 1)
        for l in range(4):
            for h in range(2):
                made = row_side(slabs[l][8 * h : 8 * h + 8])
                near_row[near + l, h * LANES : (h + 1) * LANES] = rows(made, empty).T.astype(BF16)
        for c in range(4):
            slab = slabs[4 + c // 2]
            made = row_side(slab[8 * (c % 2) : 8 * (c % 2) + 8])
            tall = rows(made, empty).T.astype(BF16)
            far_row[far + 2 * c] = tall[:64]
            if c < 3:
                far_row[far + 2 * c + 1] = tall[64:]
    for blank in (8, 4 * n_col + 1):
        near_row[blank] = jnp.zeros(near_row.shape[1:], BF16)
    for blank in (2 * CLUSTERS, CLUSTERS * n_col + 1):
        far_row[blank] = jnp.zeros(far_row.shape[1:], BF16)


def prepare(i, block, probes, near_col, coeff_low, coeff_high, far_low, far_high):
    for l in range(4):
        for h in range(2):
            j = 2 * l + h
            half = slice(h * LANES, (h + 1) * LANES)
            probes[4 * i + l, :, half] = block[j * SAMPLES : (j + 1) * SAMPLES]
        slab = block[COORD_ROW + 16 * l : COORD_ROW + 16 * (l + 1)]
        near_col[4 * i + l, :, :LANES] = slab
        near_col[4 * i + l, :, LANES:] = rows(slab[8:], slab[:8])
    slabs = [block[COORD_ROW + 64 + 16 * p : COORD_ROW + 80 + 16 * p] for p in range(2)]
    for k in range(CLUSTERS):
        c, half = k // 2, slice(k % 2 * 64, k % 2 * 64 + 64)
        if k < 6:
            own = block[FAR_ROW + 64 * c : FAR_ROW + 64 * (c + 1)][:, half]
        else:
            own = block[FAR_ROW + 192 : FAR_ROW + 224]
            own = rows(own[:, :64], own[:, 64:])
        empty = jnp.zeros_like(own)
        coeff_low[CLUSTERS * i + k] = lanes(own, empty)
        coeff_high[CLUSTERS * i + k] = lanes(empty, own)
        made = slabs[c // 2].astype(F32)[8 * (c % 2) : 8 * (c % 2) + 8, half]
        empty = jnp.zeros_like(made)
        blank = jnp.zeros((8, LANES), F32)
        far_low[CLUSTERS * i + k] = rows(lanes(made, empty), blank).astype(BF16)
        far_high[CLUSTERS * i + k] = rows(lanes(empty, made), blank).astype(BF16)


def work(plan, here, stage, lists, counts, near_row, far_row, prepared, totals):
    probes, near_col, coeff_low, coeff_high, far_low, far_high = prepared
    near_total, far_even, far_odd = totals
    near_first, far_first = (0, 0) if here else (9, 2 * CLUSTERS + 1)

    def near_terms(place, slots):
        terms = []
        for u in range(slots):
            a, b = lists[0, place + u], lists[1, place + u]
            parts = []
            for q in range(2):
                part = slice(q * LANES, (q + 1) * LANES)
                parts.append(matern_of(dot(near_row[near_first + a, part], near_col[b])))
            terms.append((a, dot(probes[b], rows(*parts), NT)))
        return terms

    def near_add(terms):
        for a, term in terms:
            near_total[a] += term

    def far_terms(place):
        terms = []
        for u in range(0, FAR_UNROLL, 2):
            a0, a1 = lists[0, place + u], lists[0, place + u + 1]
            b0, b1 = lists[1, place + u], lists[1, place + u + 1]
            square = dot(far_row[far_first + a0], far_low[b0])
            square += dot(far_row[far_first + a1], far_high[b1])
            both = rows(coeff_low[b0], coeff_high[b1])
            terms.append((a0, a1, dot(matern_of(square), both)))
        return terms

    def far_add(terms):
        for a0, a1, term in terms:
            far_even[a0] += term
            far_odd[a1] += term

    half = NEAR_UNROLL // 2

    def bounds(kind, unroll):
        sizes = [counts[k, kind] for k in ((3, 4) if here else (0, 1, 2))]
        ends = [jnp.minimum(sizes[0] // unroll, HERE_UNITS if here else EARLY_UNITS)]
        if not here:
            ends.append((sizes[0] + sizes[1]) // unroll)
        first = ends[stage - 1] if stage else 0
        if stage < len(ends):
            return first, (ends[stage] - first) * unroll
        return first, sum(sizes) - first * unroll

    near_from, near_count = bounds(0, NEAR_UNROLL)
    far_from, far_count = bounds(1, FAR_UNROLL)
    halves = (near_count + half - 1) // half
    near_groups = halves // 2
    far_groups = (far_count + FAR_UNROLL - 1) // FAR_UNROLL
    together = jnp.minimum(near_groups, far_groups)
    near_place = here * plan.near + near_from * NEAR_UNROLL
    far_place = plan.far_first + here * plan.far + far_from * FAR_UNROLL

    def joint_step(g, _):
        near = near_terms(near_place + g * NEAR_UNROLL, NEAR_UNROLL)
        far = far_terms(far_place + g * FAR_UNROLL)
        near_add(near)
        far_add(far)
        return 0

    def near_step(g, _):
        near_add(near_terms(near_place + g * NEAR_UNROLL, NEAR_UNROLL))
        return 0

    def far_step(g, _):
        far_add(far_terms(far_place + g * FAR_UNROLL))
        return 0

    lax.fori_loop(0, together, joint_step, 0)
    lax.fori_loop(together, near_groups, near_step, 0)
    lax.fori_loop(together, far_groups, far_step, 0)

    if stage < (1 if here else 2):
        return

    @pl.when(halves % 2 == 1)
    def _():
        near_add(near_terms(near_place + near_groups * NEAR_UNROLL, half))


def write_parts(outs, near_total, far_even, far_odd):
    for i, out in enumerate(outs):
        for j in range(8):
            half = slice(j % 2 * LANES, (j % 2 + 1) * LANES)
            part = near_total[4 * i + j // 2, :, half]
            out[j * SAMPLES : (j + 1) * SAMPLES] = part.astype(BF16)
        parts = []
        for l in range(CLUSTERS):
            even, odd = far_even[CLUSTERS * i + l], far_odd[CLUSTERS * i + l]
            parts.append(even[:, :64] + odd[:, 64:])
        for j in range(3):
            pair = lanes(*parts[2 * j : 2 * j + 2])
            out[FAR_ROW + 64 * j : FAR_ROW + 64 * (j + 1)] = pair.astype(BF16)
        pair = lanes(parts[6][:32], parts[6][32:])
        out[FAR_ROW + 192 : FAR_ROW + 224] = pair.astype(BF16)


def clear(totals):
    for total in totals:
        total[...] = jnp.zeros_like(total)


def early_kernel(plan, members, lists, counts, near_row, far_row, *refs):
    blocks, refs = refs[: len(members)], refs[len(members) :]
    prepared, totals = refs[:6], refs[6:]
    clear(totals)
    for i, block in zip(members, blocks):
        prepare(i, block, *prepared)
    work(plan, 0, 0, lists, counts, near_row, far_row, prepared, totals)


def mid_kernel(plan, members, lists, counts, near_row, far_row, *refs):
    blocks, refs = refs[: len(members)], refs[len(members) + 9 :]
    prepared, totals, here = refs[:6], refs[6:9], refs[9:]
    clear(here)
    for i, block in zip(members, blocks):
        prepare(i, block, *prepared)
    work(plan, 0, 1, lists, counts, near_row, far_row, prepared, totals)
    work(plan, 1, 0, lists, counts, near_row, far_row, prepared, here)


def late_kernel(plan, members, lists, counts, near_row, far_row, *refs):
    blocks, refs = refs[: len(members)], refs[len(members) + 9 :]
    prepared, totals, outs = refs[:6], refs[6:9], refs[9:]
    for i, block in zip(members, blocks):
        prepare(i, block, *prepared)
    work(plan, 0, 2, lists, counts, near_row, far_row, prepared, totals)
    write_parts(outs, *totals)


def here_kernel(plan, lists, counts, near_row, far_row, *refs):
    prepared, refs = refs[:6], refs[10:]
    totals, outs = refs[:3], refs[3:]
    work(plan, 1, 1, lists, counts, near_row, far_row, prepared, totals)
    write_parts(outs, *totals)


def final_kernel(count, basis, moves, *refs):
    parts, out = refs[:count], refs[count]

    def total(first, count):
        return sum(part[first : first + count].astype(F32) for part in parts)

    def turned(first):
        tall = total(first, 64).T
        return lanes(tall[:64], tall[64:])

    top = total(FAR_ROW + 192, 32)
    top = rows(top[:, :64], top[:, 64:]).T
    middle = turned(FAR_ROW + 128) + dot_wide(top, moves[:, 256:384])
    for j in range(2):
        pair = turned(FAR_ROW + 64 * j) + dot_wide(
            middle[:, j * RANK : (j + 1) * RANK], moves[:, j * 128 : (j + 1) * 128]
        )
        for k in range(2):
            l = 2 * j + k
            expanded = dot_wide(
                pair[:, k * RANK : (k + 1) * RANK], basis[:, l * LEAF : (l + 1) * LEAF]
            )
            for h in range(2):
                place = (2 * l + h) * LANES
                near = total((2 * l + h) * SAMPLES, SAMPLES)
                made = near + expanded[:, h * LANES : (h + 1) * LANES]
                out[:, place : place + LANES] = made.astype(BF16)


def exchange(x, axis, offset):
    size = lax.axis_size(axis)
    return lax.ppermute(x, axis, [(i, i ^ offset) for i in range(size)])


def local(
    probes, points, skeleton, leaf_basis, transfer, near_list, near_count, far_list, far_count
):
    n_row = lax.axis_size("row")
    n_col = lax.axis_size("col")
    n_y = n_row // 4
    probes, basis, moves = probes.T, leaf_basis.T, transfer.T
    inputs = (probes, basis, moves, points, skeleton)
    small = pltpu.CompilerParams(vmem_limit_bytes=8 << 20)
    packed, coords = pl.pallas_call(
        pack_kernel,
        out_shape=[
            jax.ShapeDtypeStruct((PACKED_ROWS, LANES), BF16),
            jax.ShapeDtypeStruct((COORD_ROWS, LANES), BF16),
        ],
        in_specs=[VMEM] * 5,
        out_specs=[VMEM] * 2,
        name="pack",
    )(*inputs)

    plan = Plan(near_list.shape[-1], far_list.shape[-1])
    width = max(LANES, near_list.shape[-1], far_list.shape[-1])

    def placed(x, row):
        return jnp.pad(x, ((row, 8 - row - x.shape[0]), (0, width - x.shape[1])))

    slots = placed(near_list[0, 0], 0) + placed(far_list[0, 0], 2)
    slots = slots + placed(near_count, 4) + placed(far_count, 5)

    def along_z(x, planes, flip):
        pairs = [(z * n_y + y, (z ^ flip) * n_y + y) for z in planes for y in range(n_y)]
        return lax.ppermute(x, "row", pairs)

    own_y = exchange(packed, "row", 1)
    second = along_z(packed, (0, 1, 2, 3), 2)
    neighbour = along_z(packed, (0, 1, 2, 3), 1)
    lists, counts, both = pl.pallas_call(
        functools.partial(plan_kernel, n_col, n_y, plan),
        out_shape=[
            jax.ShapeDtypeStruct((2, plan.size), jnp.int32),
            jax.ShapeDtypeStruct((8, LANES), jnp.int32),
            jax.ShapeDtypeStruct((2 * COORD_ROWS, LANES), BF16),
        ],
        in_specs=[VMEM] * 3,
        out_specs=[VMEM] * 3,
        compiler_params=small,
        cost_estimate=pl.CostEstimate(flops=1 << 30, bytes_accessed=1 << 12, transcendentals=0),
        name="plan",
    )(slots, coords, exchange(coords, "col", 1))

    row_coords = [both] + [exchange(both, "col", k) for k in range(2, n_col, 2)]
    neighbour = tie(neighbour, lists)
    neighbour_y = exchange(neighbour, "row", 1)
    second = tie(second, own_y, neighbour, lists)
    def with_y(block, first=None):
        blocks = [block, exchange(block, "row", 1) if first is None else first]
        return blocks + [exchange(block, "row", y) for y in range(2, n_y)]

    blocks = with_y(packed, own_y) + with_y(neighbour, neighbour_y) + with_y(second)

    row_features = pl.pallas_call(
        functools.partial(row_kernel, n_col),
        out_shape=[
            jax.ShapeDtypeStruct((4 * n_col + 2, LEAF, FEATURES), BF16),
            jax.ShapeDtypeStruct((CLUSTERS * n_col + 2, RANK, FEATURES), BF16),
        ],
        in_specs=[VMEM] * (n_col // 2) + [ANY],
        out_specs=[VMEM] * 2,
        compiler_params=small,
        name="row_side",
    )(*row_coords, second)

    def sums(targets):
        near = (4 * targets + 1, SAMPLES, LEAF)
        far = (CLUSTERS * targets + 1, RANK, LANES)
        return [near, far, far]

    part = jax.ShapeDtypeStruct((COORD_ROW, LANES), BF16)
    held = [
        jax.ShapeDtypeStruct(shape, BF16)
        for shape in [
            (4 * n_row, SAMPLES, LEAF),
            (4 * n_row, FEATURES, LEAF),
            (CLUSTERS * n_row, RANK, LANES),
            (CLUSTERS * n_row, RANK, LANES),
            (CLUSTERS * n_row, FEATURES, LANES),
            (CLUSTERS * n_row, FEATURES, LANES),
        ]
    ]
    held += [jax.ShapeDtypeStruct(shape, F32) for shape in sums(n_col - 2)]
    params = pltpu.CompilerParams(vmem_limit_bytes=32 << 20)
    cost = pl.CostEstimate(flops=1 << 33, bytes_accessed=1 << 20, transcendentals=0)
    local_sums = [jax.ShapeDtypeStruct(shape, F32) for shape in sums(2)]
    def stage(kernel, members, out_shape, name, cost=cost):
        first = 4 + len(members)
        return pl.pallas_call(
            functools.partial(kernel, plan, members),
            out_shape=out_shape,
            in_specs=[SMEM] * 2 + [VMEM] * (2 + len(members) + len(handed)),
            out_specs=[VMEM] * len(out_shape),
            input_output_aliases={first + k: k for k in range(len(handed))},
            compiler_params=params,
            cost_estimate=cost,
            name=name,
        )(lists, counts, *row_features, *[blocks[j] for j in members], *handed)

    handed = []
    handed = stage(early_kernel, list(range(2 * n_y + 1)), held, "early")
    third = tie(along_z(second, (0, 1, 2, 3), 1), handed[6])
    blocks += with_y(third)
    mid = stage(mid_kernel, list(range(2 * n_y + 1, 3 * n_y + 1)), held + local_sums, "mid")
    handed, here_totals = mid[: len(held)], mid[len(held) :]
    handed = stage(late_kernel, list(range(3 * n_y + 1, n_row)), held + [part] * (n_col - 2), "late")
    prepared, parts = handed[:6], handed[len(held) :]
    mine, other = parts[0::2], [exchange(part, "col", 1) for part in parts[1::2]]
    joined = pl.pallas_call(
        functools.partial(join_kernel, len(mine)),
        out_shape=[part] * len(mine),
        in_specs=[VMEM] * (2 * len(mine)),
        out_specs=[VMEM] * len(mine),
        compiler_params=params,
        name="join",
    )(*mine, *other)
    arrived = [exchange(joined[k], "col", 2 * k + 2) for k in range(len(mine))]
    here = pl.pallas_call(
        functools.partial(here_kernel, plan),
        out_shape=local_sums + [part] * 2,
        in_specs=[SMEM] * 2 + [VMEM] * 8 + [ANY] + [VMEM] * 3,
        out_specs=[VMEM] * 5,
        input_output_aliases={11 + k: k for k in range(3)},
        compiler_params=params,
        cost_estimate=cost,
        name="here",
    )(lists, counts, *row_features, *prepared, joined[0], *here_totals)[3:]
    arrived = [tie(x, cost=cost) for x in arrived]
    arrived += [here[0], exchange(here[1], "col", 1)]
    sample = pl.pallas_call(
        functools.partial(final_kernel, len(arrived)),
        out_shape=jax.ShapeDtypeStruct((SAMPLES, OWN), BF16),
        in_specs=[VMEM] * (2 + len(arrived)),
        out_specs=VMEM,
        compiler_params=pltpu.CompilerParams(vmem_limit_bytes=16 << 20),
        name="final",
    )(basis, moves, *arrived)
    return sample.T


def solution(mesh):
    placed = (
        P(("row", "col"), None),
        P(None, ("row", "col")),
        P(None, ("row", "col")),
        P(("row", "col"), None),
        P(("row", "col"), None),
        P("row", "col", None, None),
        P("row", "col"),
        P("row", "col", None, None),
        P("row", "col"),
    )
    return jax.shard_map(
        local, mesh=mesh, in_specs=placed, out_specs=P(("row", "col"), None), check_vma=False
    )
```

```python
import functools
import math

import jax
import jax.numpy as jnp
from jax import lax
from jax.experimental import pallas as pl
from jax.experimental.pallas import tpu as pltpu
from jax.sharding import PartitionSpec as P

LEAF = 256
RANK = 64
SAMPLES = 64
OWN = 4 * LEAF
CLUSTERS = 7
LANES = 128
F32 = jnp.float32
BF16 = jnp.bfloat16
FAR_ROW = OWN // LANES * SAMPLES
COORD_ROW = FAR_ROW + CLUSTERS * SAMPLES // 2
COORD_ROWS = 96
PACKED_ROWS = COORD_ROW + COORD_ROWS
FEATURES = 16
CLASSES = 2
NEAR_UNROLL = 8
FAR_UNROLL = 16
RATE = math.sqrt(3.0) / 0.15
EARLY_UNITS = 1
HERE_UNITS = 1

ANY = pl.BlockSpec(memory_space=pl.ANY)
VMEM = pl.BlockSpec(memory_space=pltpu.VMEM)
SMEM = pl.BlockSpec(memory_space=pltpu.SMEM)
NN = (((1,), (0,)), ((), ()))
NT = (((1,), (1,)), ((), ()))


def dot(a, b, dims=NN):
    return lax.dot_general(a, b, dims, preferred_element_type=F32)


def dot_wide(a, b):
    high = a.astype(BF16)
    low = (a - high.astype(F32)).astype(BF16)
    return dot(high, b) + dot(low, b)


def lanes(a, b):
    return jnp.concatenate([a, b], axis=1)


def rows(*parts):
    return jnp.concatenate(parts, axis=0)


def features(points):
    norm = points * points
    norm = norm[0:1] + norm[1:2] + norm[2:3]
    high = norm.astype(BF16).astype(F32)
    rest = norm - high
    middle = rest.astype(BF16).astype(F32)
    ones = jnp.ones_like(norm)
    return rows(points, high, middle, rest - middle, ones, ones)


def row_side(made):
    ones = made[6:7]
    return rows(-2.0 * made[0:3], ones, ones, ones, made[3:4], made[4:5])


def matern_of(square):
    square = jnp.maximum(square, 1e-14)
    x = (square * lax.rsqrt(square)) * -RATE
    return ((1.0 - x) * jnp.exp(x)).astype(BF16)


def pack_kernel(probes, basis, moves, points, skeleton, packed, coords):
    near = features(points[...].astype(F32))
    far = features(lanes(skeleton[...].astype(F32), jnp.zeros((3, 64), F32)))
    chunks = [near[:, j * LANES : (j + 1) * LANES] for j in range(8)]
    chunks += [far[:, j * LANES : (j + 1) * LANES] for j in range(4)]
    made = rows(*chunks).astype(BF16)
    packed[COORD_ROW:] = made
    coords[...] = made
    leaves = []
    for l in range(4):
        part = slice(l * LEAF, (l + 1) * LEAF)
        leaves.append(dot(basis[:, part], probes[:, part], NT).astype(BF16))
    middle = [
        dot(moves[:, j * 128 : (j + 1) * 128], rows(*leaves[2 * j : 2 * j + 2])).astype(BF16)
        for j in range(2)
    ]
    top = dot(moves[:, 256:384], rows(*middle)).astype(BF16)
    for j in range(8):
        packed[j * SAMPLES : (j + 1) * SAMPLES] = probes[:, j * LANES : (j + 1) * LANES]
    packed[FAR_ROW : FAR_ROW + 64] = lanes(leaves[0], leaves[1])
    packed[FAR_ROW + 64 : FAR_ROW + 128] = lanes(leaves[2], leaves[3])
    packed[FAR_ROW + 128 : FAR_ROW + 192] = lanes(middle[0], middle[1])
    packed[FAR_ROW + 192 : FAR_ROW + 224] = lanes(top[:32], top[32:])


class Plan:
    def __init__(self, near_most, far_most):
        self.near = near_most + NEAR_UNROLL
        self.far = far_most + FAR_UNROLL
        self.far_first = -(-CLASSES * self.near // LANES) * LANES
        self.size = self.far_first + -(-CLASSES * self.far // LANES) * LANES


def iota(shape, axis):
    return lax.broadcasted_iota(jnp.int32, shape, axis)


def tie_kernel(*refs):
    del refs


def tie(x, *others, cost=None):
    return pl.pallas_call(
        tie_kernel,
        out_shape=jax.ShapeDtypeStruct(x.shape, x.dtype),
        in_specs=[ANY] * (1 + len(others)),
        out_specs=ANY,
        input_output_aliases={0: 0},
        compiler_params=pltpu.CompilerParams(vmem_limit_bytes=1 << 20),
        cost_estimate=cost,
        name="tie",
    )(x, *others)


def join_kernel(count, *refs):
    for mine, other, out in zip(refs[:count], refs[count : 2 * count], refs[2 * count :]):
        out[...] = (mine[...].astype(F32) + other[...].astype(F32)).astype(BF16)


def sort_slots(a_device, a_rest, b_device, b_rest, count, per_device, n_col, n_y, most, width):
    slots = a_device.shape[1]
    target = a_device ^ lax.axis_index("col")
    source = b_device ^ lax.axis_index("row")
    remote = target >= 2
    stage = jnp.where(source > 3 * n_y, 2, jnp.where(source > 2 * n_y, 1, 0))
    group = jnp.where(remote, stage, jnp.where(stage == 2, 4, 3))
    alive = iota((1, slots), 1) < count
    group = jnp.where(alive, group, 7)
    row = (target - jnp.where(remote, 2, 0)) * per_device + a_rest
    column = source * per_device + b_rest
    member = jnp.where(iota((8, slots), 0) == group, 1.0, 0.0)
    before = jnp.where(iota((slots, slots), 0) < iota((slots, slots), 1), 1.0, 0.0)
    ahead = dot(member.astype(BF16), before.astype(BF16))
    ahead = jnp.sum(member * ahead, axis=0, keepdims=True)
    sizes = jnp.sum(member, axis=1, keepdims=True)
    ahead += jnp.where(group == 4, sizes[3:4], 0.0)
    ahead += jnp.where((group == 1) | (group == 2), sizes[0:1], 0.0)
    ahead += jnp.where(group == 2, sizes[1:2], 0.0)
    place = jnp.where(alive, jnp.where(remote, 0, most) + ahead.astype(jnp.int32), -1)
    chosen = jnp.where(iota((width, slots), 0) == place, 1.0, 0.0).astype(BF16)
    ones = jnp.ones((6, slots), F32)
    values = rows(row.astype(F32), column.astype(F32), ones).astype(BF16)
    found = dot(values, chosen, NT)
    here = iota((1, width), 1) >= most
    blank = jnp.where(here, 2.0 * per_device, (n_col - 2.0) * per_device)
    made = rows(found[0:1] + blank * (1.0 - found[2:3]), found[1:2])
    return made.astype(jnp.int32), sizes.astype(jnp.int32)


def plan_kernel(n_col, n_y, plan, slots, coords, mate, out, counts, both):
    both[:COORD_ROWS] = coords[...]
    both[COORD_ROWS:] = mate[...]
    near_most, far_most = plan.near - NEAR_UNROLL, plan.far - FAR_UNROLL
    a, b = slots[0:1, :near_most], slots[1:2, :near_most]
    near, near_counts = sort_slots(
        lax.shift_right_logical(a, 2), a & 3, lax.shift_right_logical(b, 2), b & 3,
        slots[4:5, 0:1], 4, n_col, n_y, plan.near, plan.far_first,
    )
    a, b = slots[2:3, :far_most], slots[3:4, :far_most]
    a_device = lax.shift_right_logical(a * 9363, 16)
    b_device = lax.shift_right_logical(b * 9363, 16)
    far, far_counts = sort_slots(
        a_device, a - a_device * CLUSTERS, b_device, b - b_device * CLUSTERS,
        slots[5:6, 0:1], CLUSTERS, n_col, n_y, plan.far, plan.size - plan.far_first,
    )
    out[:, : plan.far_first] = near
    out[:, plan.far_first :] = far
    counts[...] = jnp.where(iota((8, LANES), 1) == 0, near_counts, far_counts)


def row_kernel(n_col, *refs):
    chips, near_row, far_row = refs[:-3], refs[-2], refs[-1]
    empty = jnp.zeros((8, LANES), F32)
    for i in range(n_col):
        first = i % 2 * COORD_ROWS
        slabs = [chips[i // 2][first + 16 * s : first + 16 * s + 16].astype(F32) for s in range(6)]
        near, far = (4 * i, CLUSTERS * i) if i < 2 else (4 * i + 1, CLUSTERS * i + 1)
        for l in range(4):
            for h in range(2):
                made = row_side(slabs[l][8 * h : 8 * h + 8])
                near_row[near + l, :, h * LANES : (h + 1) * LANES] = rows(made, empty).astype(BF16)
        for c in range(4):
            slab = slabs[4 + c // 2]
            made = row_side(slab[8 * (c % 2) : 8 * (c % 2) + 8])
            tall = rows(made, empty).T.astype(BF16)
            far_row[far + 2 * c] = tall[:64]
            if c < 3:
                far_row[far + 2 * c + 1] = tall[64:]
    for blank in (8, 4 * n_col + 1):
        near_row[blank] = jnp.zeros(near_row.shape[1:], BF16)
    for blank in (2 * CLUSTERS, CLUSTERS * n_col + 1):
        far_row[blank] = jnp.zeros(far_row.shape[1:], BF16)


def prepare(i, block, probes, near_col, coeff_low, coeff_high, far_low, far_high):
    for l in range(4):
        for h in range(2):
            j = 2 * l + h
            half = slice(h * LANES, (h + 1) * LANES)
            probes[4 * i + l, :, half] = block[j * SAMPLES : (j + 1) * SAMPLES]
        slab = block[COORD_ROW + 16 * l : COORD_ROW + 16 * (l + 1)]
        slab = slab.astype(F32)
        near_col[4 * i + l, :LANES] = slab.T.astype(BF16)
        near_col[4 * i + l, LANES:] = rows(slab[8:], slab[:8]).T.astype(BF16)
    slabs = [block[COORD_ROW + 64 + 16 * p : COORD_ROW + 80 + 16 * p] for p in range(2)]
    for k in range(CLUSTERS):
        c, half = k // 2, slice(k % 2 * 64, k % 2 * 64 + 64)
        if k < 6:
            own = block[FAR_ROW + 64 * c : FAR_ROW + 64 * (c + 1)][:, half]
        else:
            own = block[FAR_ROW + 192 : FAR_ROW + 224]
            own = rows(own[:, :64], own[:, 64:])
        empty = jnp.zeros_like(own)
        coeff_low[CLUSTERS * i + k] = lanes(own, empty)
        coeff_high[CLUSTERS * i + k] = lanes(empty, own)
        made = slabs[c // 2].astype(F32)[8 * (c % 2) : 8 * (c % 2) + 8, half]
        empty = jnp.zeros_like(made)
        blank = jnp.zeros((8, LANES), F32)
        far_low[CLUSTERS * i + k] = rows(lanes(made, empty), blank).astype(BF16)
        far_high[CLUSTERS * i + k] = rows(lanes(empty, made), blank).astype(BF16)


def work(plan, here, stage, lists, counts, near_row, far_row, prepared, totals):
    probes, near_col, coeff_low, coeff_high, far_low, far_high = prepared
    near_total, far_even, far_odd = totals
    near_first, far_first = (0, 0) if here else (9, 2 * CLUSTERS + 1)

    def near_terms(place, slots):
        terms = []
        for u in range(slots):
            a, b = lists[0, place + u], lists[1, place + u]
            parts = []
            for q in range(2):
                part = slice(q * LANES, (q + 1) * LANES)
                parts.append(matern_of(dot(near_col[b, part], near_row[near_first + a])))
            terms.append((a, dot(probes[b], rows(*parts))))
        return terms

    def near_add(terms):
        for a, term in terms:
            near_total[a] += term

    def far_terms(place):
        terms = []
        for u in range(0, FAR_UNROLL, 2):
            a0, a1 = lists[0, place + u], lists[0, place + u + 1]
            b0, b1 = lists[1, place + u], lists[1, place + u + 1]
            square = dot(far_row[far_first + a0], far_low[b0])
            square += dot(far_row[far_first + a1], far_high[b1])
            both = rows(coeff_low[b0], coeff_high[b1])
            terms.append((a0, a1, dot(matern_of(square), both)))
        return terms

    def far_add(terms):
        for a0, a1, term in terms:
            far_even[a0] += term
            far_odd[a1] += term

    half = NEAR_UNROLL // 2

    def bounds(kind, unroll):
        sizes = [counts[k, kind] for k in ((3, 4) if here else (0, 1, 2))]
        ends = [jnp.minimum(sizes[0] // unroll, HERE_UNITS if here else EARLY_UNITS)]
        if not here:
            ends.append((sizes[0] + sizes[1]) // unroll)
        first = ends[stage - 1] if stage else 0
        if stage < len(ends):
            return first, (ends[stage] - first) * unroll
        return first, sum(sizes) - first * unroll

    near_from, near_count = bounds(0, NEAR_UNROLL)
    far_from, far_count = bounds(1, FAR_UNROLL)
    halves = (near_count + half - 1) // half
    near_groups = halves // 2
    far_groups = (far_count + FAR_UNROLL - 1) // FAR_UNROLL
    together = jnp.minimum(near_groups, far_groups)
    near_place = here * plan.near + near_from * NEAR_UNROLL
    far_place = plan.far_first + here * plan.far + far_from * FAR_UNROLL

    def joint_step(g, _):
        near = near_terms(near_place + g * NEAR_UNROLL, NEAR_UNROLL)
        far = far_terms(far_place + g * FAR_UNROLL)
        near_add(near)
        far_add(far)
        return 0

    def near_step(g, _):
        near_add(near_terms(near_place + g * NEAR_UNROLL, NEAR_UNROLL))
        return 0

    def far_step(g, _):
        far_add(far_terms(far_place + g * FAR_UNROLL))
        return 0

    lax.fori_loop(0, together, joint_step, 0)
    lax.fori_loop(together, near_groups, near_step, 0)
    lax.fori_loop(together, far_groups, far_step, 0)

    if stage < (1 if here else 2):
        return

    @pl.when(halves % 2 == 1)
    def _():
        near_add(near_terms(near_place + near_groups * NEAR_UNROLL, half))


def write_parts(outs, near_total, far_even, far_odd):
    for i, out in enumerate(outs):
        for j in range(8):
            half = slice(j % 2 * LANES, (j % 2 + 1) * LANES)
            part = near_total[4 * i + j // 2, :, half]
            out[j * SAMPLES : (j + 1) * SAMPLES] = part.astype(BF16)
        parts = []
        for l in range(CLUSTERS):
            even, odd = far_even[CLUSTERS * i + l], far_odd[CLUSTERS * i + l]
            parts.append(even[:, :64] + odd[:, 64:])
        for j in range(3):
            pair = lanes(*parts[2 * j : 2 * j + 2])
            out[FAR_ROW + 64 * j : FAR_ROW + 64 * (j + 1)] = pair.astype(BF16)
        pair = lanes(parts[6][:32], parts[6][32:])
        out[FAR_ROW + 192 : FAR_ROW + 224] = pair.astype(BF16)


def clear(totals):
    for total in totals:
        total[...] = jnp.zeros_like(total)


def early_kernel(plan, members, lists, counts, near_row, far_row, *refs):
    blocks, refs = refs[: len(members)], refs[len(members) :]
    prepared, totals = refs[:6], refs[6:]
    clear(totals)
    for i, block in zip(members, blocks):
        prepare(i, block, *prepared)
    work(plan, 0, 0, lists, counts, near_row, far_row, prepared, totals)


def mid_kernel(plan, members, lists, counts, near_row, far_row, *refs):
    blocks, refs = refs[: len(members)], refs[len(members) + 9 :]
    prepared, totals, here = refs[:6], refs[6:9], refs[9:]
    clear(here)
    for i, block in zip(members, blocks):
        prepare(i, block, *prepared)
    work(plan, 0, 1, lists, counts, near_row, far_row, prepared, totals)
    work(plan, 1, 0, lists, counts, near_row, far_row, prepared, here)


def late_kernel(plan, members, lists, counts, near_row, far_row, *refs):
    blocks, refs = refs[: len(members)], refs[len(members) + 9 :]
    prepared, totals, outs = refs[:6], refs[6:9], refs[9:]
    for i, block in zip(members, blocks):
        prepare(i, block, *prepared)
    work(plan, 0, 2, lists, counts, near_row, far_row, prepared, totals)
    write_parts(outs, *totals)


def here_kernel(plan, lists, counts, near_row, far_row, *refs):
    prepared, refs = refs[:6], refs[10:]
    totals, outs = refs[:3], refs[3:]
    work(plan, 1, 1, lists, counts, near_row, far_row, prepared, totals)
    write_parts(outs, *totals)


def final_kernel(count, basis, moves, *refs):
    parts, out = refs[:count], refs[count]

    def total(first, count):
        return sum(part[first : first + count].astype(F32) for part in parts)

    def turned(first):
        tall = total(first, 64).T
        return lanes(tall[:64], tall[64:])

    top = total(FAR_ROW + 192, 32)
    top = rows(top[:, :64], top[:, 64:]).T
    middle = turned(FAR_ROW + 128) + dot_wide(top, moves[:, 256:384])
    for j in range(2):
        pair = turned(FAR_ROW + 64 * j) + dot_wide(
            middle[:, j * RANK : (j + 1) * RANK], moves[:, j * 128 : (j + 1) * 128]
        )
        for k in range(2):
            l = 2 * j + k
            expanded = dot_wide(
                pair[:, k * RANK : (k + 1) * RANK], basis[:, l * LEAF : (l + 1) * LEAF]
            )
            for h in range(2):
                place = (2 * l + h) * LANES
                near = total((2 * l + h) * SAMPLES, SAMPLES)
                made = near + expanded[:, h * LANES : (h + 1) * LANES]
                out[:, place : place + LANES] = made.astype(BF16)


def exchange(x, axis, offset):
    size = lax.axis_size(axis)
    return lax.ppermute(x, axis, [(i, i ^ offset) for i in range(size)])


def local(
    probes, points, skeleton, leaf_basis, transfer, near_list, near_count, far_list, far_count
):
    n_row = lax.axis_size("row")
    n_col = lax.axis_size("col")
    n_y = n_row // 4
    probes, basis, moves = probes.T, leaf_basis.T, transfer.T
    inputs = (probes, basis, moves, points, skeleton)
    small = pltpu.CompilerParams(vmem_limit_bytes=8 << 20)
    packed, coords = pl.pallas_call(
        pack_kernel,
        out_shape=[
            jax.ShapeDtypeStruct((PACKED_ROWS, LANES), BF16),
            jax.ShapeDtypeStruct((COORD_ROWS, LANES), BF16),
        ],
        in_specs=[VMEM] * 5,
        out_specs=[VMEM] * 2,
        name="pack",
    )(*inputs)

    plan = Plan(near_list.shape[-1], far_list.shape[-1])
    width = max(LANES, near_list.shape[-1], far_list.shape[-1])

    def placed(x, row):
        return jnp.pad(x, ((row, 8 - row - x.shape[0]), (0, width - x.shape[1])))

    slots = placed(near_list[0, 0], 0) + placed(far_list[0, 0], 2)
    slots = slots + placed(near_count, 4) + placed(far_count, 5)

    def along_z(x, planes, flip):
        pairs = [(z * n_y + y, (z ^ flip) * n_y + y) for z in planes for y in range(n_y)]
        return lax.ppermute(x, "row", pairs)

    own_y = exchange(packed, "row", 1)
    second = along_z(packed, (0, 1, 2, 3), 2)
    neighbour = along_z(packed, (0, 1, 2, 3), 1)
    lists, counts, both = pl.pallas_call(
        functools.partial(plan_kernel, n_col, n_y, plan),
        out_shape=[
            jax.ShapeDtypeStruct((2, plan.size), jnp.int32),
            jax.ShapeDtypeStruct((8, LANES), jnp.int32),
            jax.ShapeDtypeStruct((2 * COORD_ROWS, LANES), BF16),
        ],
        in_specs=[VMEM] * 3,
        out_specs=[VMEM] * 3,
        compiler_params=small,
        cost_estimate=pl.CostEstimate(flops=1 << 30, bytes_accessed=1 << 12, transcendentals=0),
        name="plan",
    )(slots, coords, exchange(coords, "col", 1))

    row_coords = [both] + [exchange(both, "col", k) for k in range(2, n_col, 2)]
    neighbour = tie(neighbour, lists)
    neighbour_y = exchange(neighbour, "row", 1)
    second = tie(second, own_y, neighbour, lists)
    def with_y(block, first=None):
        blocks = [block, exchange(block, "row", 1) if first is None else first]
        return blocks + [exchange(block, "row", y) for y in range(2, n_y)]

    blocks = with_y(packed, own_y) + with_y(neighbour, neighbour_y) + with_y(second)

    row_features = pl.pallas_call(
        functools.partial(row_kernel, n_col),
        out_shape=[
            jax.ShapeDtypeStruct((4 * n_col + 2, FEATURES, LEAF), BF16),
            jax.ShapeDtypeStruct((CLUSTERS * n_col + 2, RANK, FEATURES), BF16),
        ],
        in_specs=[VMEM] * (n_col // 2) + [ANY],
        out_specs=[VMEM] * 2,
        compiler_params=small,
        name="row_side",
    )(*row_coords, second)

    def sums(targets):
        near = (4 * targets + 1, SAMPLES, LEAF)
        far = (CLUSTERS * targets + 1, RANK, LANES)
        return [near, far, far]

    part = jax.ShapeDtypeStruct((COORD_ROW, LANES), BF16)
    held = [
        jax.ShapeDtypeStruct(shape, BF16)
        for shape in [
            (4 * n_row, SAMPLES, LEAF),
            (4 * n_row, LEAF, FEATURES),
            (CLUSTERS * n_row, RANK, LANES),
            (CLUSTERS * n_row, RANK, LANES),
            (CLUSTERS * n_row, FEATURES, LANES),
            (CLUSTERS * n_row, FEATURES, LANES),
        ]
    ]
    held += [jax.ShapeDtypeStruct(shape, F32) for shape in sums(n_col - 2)]
    params = pltpu.CompilerParams(vmem_limit_bytes=32 << 20)
    cost = pl.CostEstimate(flops=1 << 33, bytes_accessed=1 << 20, transcendentals=0)
    local_sums = [jax.ShapeDtypeStruct(shape, F32) for shape in sums(2)]
    def stage(kernel, members, out_shape, name, cost=cost):
        first = 4 + len(members)
        return pl.pallas_call(
            functools.partial(kernel, plan, members),
            out_shape=out_shape,
            in_specs=[SMEM] * 2 + [VMEM] * (2 + len(members) + len(handed)),
            out_specs=[VMEM] * len(out_shape),
            input_output_aliases={first + k: k for k in range(len(handed))},
            compiler_params=params,
            cost_estimate=cost,
            name=name,
        )(lists, counts, *row_features, *[blocks[j] for j in members], *handed)

    handed = []
    handed = stage(early_kernel, list(range(2 * n_y + 1)), held, "early")
    third = tie(along_z(second, (0, 1, 2, 3), 1), handed[6])
    blocks += with_y(third)
    mid = stage(mid_kernel, list(range(2 * n_y + 1, 3 * n_y + 1)), held + local_sums, "mid")
    handed, here_totals = mid[: len(held)], mid[len(held) :]
    handed = stage(late_kernel, list(range(3 * n_y + 1, n_row)), held + [part] * (n_col - 2), "late")
    prepared, parts = handed[:6], handed[len(held) :]
    mine, other = parts[0::2], [exchange(part, "col", 1) for part in parts[1::2]]
    joined = pl.pallas_call(
        functools.partial(join_kernel, len(mine)),
        out_shape=[part] * len(mine),
        in_specs=[VMEM] * (2 * len(mine)),
        out_specs=[VMEM] * len(mine),
        compiler_params=params,
        name="join",
    )(*mine, *other)
    arrived = [exchange(joined[k], "col", 2 * k + 2) for k in range(len(mine))]
    here = pl.pallas_call(
        functools.partial(here_kernel, plan),
        out_shape=local_sums + [part] * 2,
        in_specs=[SMEM] * 2 + [VMEM] * 8 + [ANY] + [VMEM] * 3,
        out_specs=[VMEM] * 5,
        input_output_aliases={11 + k: k for k in range(3)},
        compiler_params=params,
        cost_estimate=cost,
        name="here",
    )(lists, counts, *row_features, *prepared, joined[0], *here_totals)[3:]
    arrived = [tie(x, cost=cost) for x in arrived]
    arrived += [here[0], exchange(here[1], "col", 1)]
    sample = pl.pallas_call(
        functools.partial(final_kernel, len(arrived)),
        out_shape=jax.ShapeDtypeStruct((SAMPLES, OWN), BF16),
        in_specs=[VMEM] * (2 + len(arrived)),
        out_specs=VMEM,
        compiler_params=pltpu.CompilerParams(vmem_limit_bytes=16 << 20),
        name="final",
    )(basis, moves, *arrived)
    return sample.T


def solution(mesh):
    placed = (
        P(("row", "col"), None),
        P(None, ("row", "col")),
        P(None, ("row", "col")),
        P(("row", "col"), None),
        P(("row", "col"), None),
        P("row", "col", None, None),
        P("row", "col"),
        P("row", "col", None, None),
        P("row", "col"),
    )
    return jax.shard_map(
        local, mesh=mesh, in_specs=placed, out_specs=P(("row", "col"), None), check_vma=False
    )
```

```python
import functools
import math

import jax
import jax.numpy as jnp
from jax import lax
from jax.experimental import pallas as pl
from jax.experimental.pallas import tpu as pltpu
from jax.sharding import PartitionSpec as P

LEAF = 256
RANK = 64
SAMPLES = 64
OWN = 4 * LEAF
CLUSTERS = 7
LANES = 128
F32 = jnp.float32
BF16 = jnp.bfloat16
FAR_ROW = OWN // LANES * SAMPLES
COORD_ROW = FAR_ROW + CLUSTERS * SAMPLES // 2
COORD_ROWS = 96
PACKED_ROWS = COORD_ROW + COORD_ROWS
FEATURES = 16
CLASSES = 2
NEAR_UNROLL = 8
FAR_UNROLL = 16
RATE = math.sqrt(3.0) / 0.15
EARLY_UNITS = 1
HERE_UNITS = 1

ANY = pl.BlockSpec(memory_space=pl.ANY)
VMEM = pl.BlockSpec(memory_space=pltpu.VMEM)
SMEM = pl.BlockSpec(memory_space=pltpu.SMEM)
NN = (((1,), (0,)), ((), ()))
NT = (((1,), (1,)), ((), ()))


def dot(a, b, dims=NN):
    return lax.dot_general(a, b, dims, preferred_element_type=F32)


def dot_wide(a, b):
    high = a.astype(BF16)
    low = (a - high.astype(F32)).astype(BF16)
    return dot(high, b) + dot(low, b)


def lanes(a, b):
    return jnp.concatenate([a, b], axis=1)


def rows(*parts):
    return jnp.concatenate(parts, axis=0)


def features(points):
    norm = points * points
    norm = norm[0:1] + norm[1:2] + norm[2:3]
    high = norm.astype(BF16).astype(F32)
    rest = norm - high
    middle = rest.astype(BF16).astype(F32)
    ones = jnp.ones_like(norm)
    return rows(points, high, middle, rest - middle, ones, ones)


def row_side(made):
    ones = made[6:7]
    return rows(-2.0 * made[0:3], ones, ones, ones, made[3:4], made[4:5])


def matern_of(square):
    square = jnp.maximum(square, 1e-14)
    x = (square * lax.rsqrt(square)) * -RATE
    return ((1.0 - x) * jnp.exp(x)).astype(BF16)


def pack_kernel(probes, basis, moves, points, skeleton, packed, coords):
    near = features(points[...].astype(F32))
    far = features(lanes(skeleton[...].astype(F32), jnp.zeros((3, 64), F32)))
    chunks = [near[:, j * LANES : (j + 1) * LANES] for j in range(8)]
    chunks += [far[:, j * LANES : (j + 1) * LANES] for j in range(4)]
    made = rows(*chunks).astype(BF16)
    packed[COORD_ROW:] = made
    coords[...] = made
    leaves = []
    for l in range(4):
        part = slice(l * LEAF, (l + 1) * LEAF)
        leaves.append(dot(basis[:, part], probes[:, part], NT).astype(BF16))
    middle = [
        dot(moves[:, j * 128 : (j + 1) * 128], rows(*leaves[2 * j : 2 * j + 2])).astype(BF16)
        for j in range(2)
    ]
    top = dot(moves[:, 256:384], rows(*middle)).astype(BF16)
    for j in range(8):
        packed[j * SAMPLES : (j + 1) * SAMPLES] = probes[:, j * LANES : (j + 1) * LANES]
    packed[FAR_ROW : FAR_ROW + 64] = lanes(leaves[0], leaves[1])
    packed[FAR_ROW + 64 : FAR_ROW + 128] = lanes(leaves[2], leaves[3])
    packed[FAR_ROW + 128 : FAR_ROW + 192] = lanes(middle[0], middle[1])
    packed[FAR_ROW + 192 : FAR_ROW + 224] = lanes(top[:32], top[32:])


class Plan:
    def __init__(self, near_most, far_most):
        self.near = near_most + NEAR_UNROLL
        self.far = far_most + FAR_UNROLL
        self.far_first = -(-CLASSES * self.near // LANES) * LANES
        self.size = self.far_first + -(-CLASSES * self.far // LANES) * LANES


def iota(shape, axis):
    return lax.broadcasted_iota(jnp.int32, shape, axis)


def tie_kernel(*refs):
    del refs


def tie(x, *others, cost=None):
    return pl.pallas_call(
        tie_kernel,
        out_shape=jax.ShapeDtypeStruct(x.shape, x.dtype),
        in_specs=[ANY] * (1 + len(others)),
        out_specs=ANY,
        input_output_aliases={0: 0},
        compiler_params=pltpu.CompilerParams(vmem_limit_bytes=1 << 20),
        cost_estimate=cost,
        name="tie",
    )(x, *others)


def join_kernel(count, *refs):
    for mine, other, out in zip(refs[:count], refs[count : 2 * count], refs[2 * count :]):
        out[...] = (mine[...].astype(F32) + other[...].astype(F32)).astype(BF16)


def sort_slots(a_device, a_rest, b_device, b_rest, count, per_device, n_col, n_y, most, width):
    slots = a_device.shape[1]
    target = a_device ^ lax.axis_index("col")
    source = b_device ^ lax.axis_index("row")
    remote = target >= 2
    stage = jnp.where(source > 3 * n_y, 2, jnp.where(source > 2 * n_y, 1, 0))
    group = jnp.where(remote, stage, jnp.where(stage == 0, 3, 4))
    alive = iota((1, slots), 1) < count
    group = jnp.where(alive, group, 7)
    row = (target - jnp.where(remote, 2, 0)) * per_device + a_rest
    column = source * per_device + b_rest
    member = jnp.where(iota((8, slots), 0) == group, 1.0, 0.0)
    before = jnp.where(iota((slots, slots), 0) < iota((slots, slots), 1), 1.0, 0.0)
    ahead = dot(member.astype(BF16), before.astype(BF16))
    ahead = jnp.sum(member * ahead, axis=0, keepdims=True)
    sizes = jnp.sum(member, axis=1, keepdims=True)
    ahead += jnp.where(group == 4, sizes[3:4], 0.0)
    ahead += jnp.where((group == 1) | (group == 2), sizes[0:1], 0.0)
    ahead += jnp.where(group == 2, sizes[1:2], 0.0)
    place = jnp.where(alive, jnp.where(remote, 0, most) + ahead.astype(jnp.int32), -1)
    chosen = jnp.where(iota((width, slots), 0) == place, 1.0, 0.0).astype(BF16)
    ones = jnp.ones((6, slots), F32)
    values = rows(row.astype(F32), column.astype(F32), ones).astype(BF16)
    found = dot(values, chosen, NT)
    here = iota((1, width), 1) >= most
    blank = jnp.where(here, 2.0 * per_device, (n_col - 2.0) * per_device)
    made = rows(found[0:1] + blank * (1.0 - found[2:3]), found[1:2])
    return made.astype(jnp.int32), sizes.astype(jnp.int32)


def plan_kernel(n_col, n_y, plan, slots, coords, mate, out, counts, both):
    both[:COORD_ROWS] = coords[...]
    both[COORD_ROWS:] = mate[...]
    near_most, far_most = plan.near - NEAR_UNROLL, plan.far - FAR_UNROLL
    a, b = slots[0:1, :near_most], slots[1:2, :near_most]
    near, near_counts = sort_slots(
        lax.shift_right_logical(a, 2), a & 3, lax.shift_right_logical(b, 2), b & 3,
        slots[4:5, 0:1], 4, n_col, n_y, plan.near, plan.far_first,
    )
    a, b = slots[2:3, :far_most], slots[3:4, :far_most]
    a_device = lax.shift_right_logical(a * 9363, 16)
    b_device = lax.shift_right_logical(b * 9363, 16)
    far, far_counts = sort_slots(
        a_device, a - a_device * CLUSTERS, b_device, b - b_device * CLUSTERS,
        slots[5:6, 0:1], CLUSTERS, n_col, n_y, plan.far, plan.size - plan.far_first,
    )
    out[:, : plan.far_first] = near
    out[:, plan.far_first :] = far
    counts[...] = jnp.where(iota((8, LANES), 1) == 0, near_counts, far_counts)


def row_kernel(n_col, *refs):
    chips, near_row, far_row = refs[:-3], refs[-2], refs[-1]
    empty = jnp.zeros((8, LANES), F32)
    for i in range(n_col):
        first = i % 2 * COORD_ROWS
        slabs = [chips[i // 2][first + 16 * s : first + 16 * s + 16].astype(F32) for s in range(6)]
        near, far = (4 * i, CLUSTERS * i) if i < 2 else (4 * i + 1, CLUSTERS * i + 1)
        for l in range(4):
            for h in range(2):
                made = row_side(slabs[l][8 * h : 8 * h + 8])
                near_row[near + l, h * LANES : (h + 1) * LANES] = rows(made, empty).T.astype(BF16)
        for c in range(4):
            slab = slabs[4 + c // 2]
            made = row_side(slab[8 * (c % 2) : 8 * (c % 2) + 8])
            tall = rows(made, empty).T.astype(BF16)
            far_row[far + 2 * c] = tall[:64]
            if c < 3:
                far_row[far + 2 * c + 1] = tall[64:]
    for blank in (8, 4 * n_col + 1):
        near_row[blank] = jnp.zeros(near_row.shape[1:], BF16)
    for blank in (2 * CLUSTERS, CLUSTERS * n_col + 1):
        far_row[blank] = jnp.zeros(far_row.shape[1:], BF16)


def prepare(i, block, probes, near_col, coeff_low, coeff_high, far_low, far_high):
    for l in range(4):
        for h in range(2):
            j = 2 * l + h
            half = slice(h * LANES, (h + 1) * LANES)
            probes[4 * i + l, :, half] = block[j * SAMPLES : (j + 1) * SAMPLES]
        slab = block[COORD_ROW + 16 * l : COORD_ROW + 16 * (l + 1)]
        near_col[4 * i + l, :, :LANES] = slab
        near_col[4 * i + l, :, LANES:] = rows(slab[8:], slab[:8])
    slabs = [block[COORD_ROW + 64 + 16 * p : COORD_ROW + 80 + 16 * p] for p in range(2)]
    for k in range(CLUSTERS):
        c, half = k // 2, slice(k % 2 * 64, k % 2 * 64 + 64)
        if k < 6:
            own = block[FAR_ROW + 64 * c : FAR_ROW + 64 * (c + 1)][:, half]
        else:
            own = block[FAR_ROW + 192 : FAR_ROW + 224]
            own = rows(own[:, :64], own[:, 64:])
        empty = jnp.zeros_like(own)
        coeff_low[CLUSTERS * i + k] = lanes(own, empty)
        coeff_high[CLUSTERS * i + k] = lanes(empty, own)
        made = slabs[c // 2].astype(F32)[8 * (c % 2) : 8 * (c % 2) + 8, half]
        empty = jnp.zeros_like(made)
        blank = jnp.zeros((8, LANES), F32)
        far_low[CLUSTERS * i + k] = rows(lanes(made, empty), blank).astype(BF16)
        far_high[CLUSTERS * i + k] = rows(lanes(empty, made), blank).astype(BF16)


def work(plan, here, stage, lists, counts, near_row, far_row, prepared, totals):
    probes, near_col, coeff_low, coeff_high, far_low, far_high = prepared
    near_total, far_even, far_odd = totals
    near_first, far_first = (0, 0) if here else (9, 2 * CLUSTERS + 1)

    def near_terms(place, slots):
        terms = []
        for u in range(slots):
            a, b = lists[0, place + u], lists[1, place + u]
            parts = []
            for q in range(2):
                part = slice(q * LANES, (q + 1) * LANES)
                parts.append(matern_of(dot(near_row[near_first + a, part], near_col[b])))
            terms.append((a, dot(probes[b], rows(*parts), NT)))
        return terms

    def near_add(terms):
        for a, term in terms:
            near_total[a] += term

    def far_terms(place):
        terms = []
        for u in range(0, FAR_UNROLL, 2):
            a0, a1 = lists[0, place + u], lists[0, place + u + 1]
            b0, b1 = lists[1, place + u], lists[1, place + u + 1]
            square = dot(far_row[far_first + a0], far_low[b0])
            square += dot(far_row[far_first + a1], far_high[b1])
            both = rows(coeff_low[b0], coeff_high[b1])
            terms.append((a0, a1, dot(matern_of(square), both)))
        return terms

    def far_add(terms):
        for a0, a1, term in terms:
            far_even[a0] += term
            far_odd[a1] += term

    half = NEAR_UNROLL // 2

    def bounds(kind, unroll):
        sizes = [counts[k, kind] for k in ((3, 4) if here else (0, 1, 2))]
        ends = [jnp.minimum(sizes[0] // unroll, HERE_UNITS if here else EARLY_UNITS)]
        if not here:
            ends += [sizes[0] // unroll, (sizes[0] + sizes[1]) // unroll]
        first = ends[stage - 1] if stage else 0
        if stage < len(ends):
            return first, (ends[stage] - first) * unroll
        return first, sum(sizes) - first * unroll

    near_from, near_count = bounds(0, NEAR_UNROLL)
    far_from, far_count = bounds(1, FAR_UNROLL)
    halves = (near_count + half - 1) // half
    near_groups = halves // 2
    far_groups = (far_count + FAR_UNROLL - 1) // FAR_UNROLL
    together = jnp.minimum(near_groups, far_groups)
    near_place = here * plan.near + near_from * NEAR_UNROLL
    far_place = plan.far_first + here * plan.far + far_from * FAR_UNROLL

    def joint_step(g, _):
        near = near_terms(near_place + g * NEAR_UNROLL, NEAR_UNROLL)
        far = far_terms(far_place + g * FAR_UNROLL)
        near_add(near)
        far_add(far)
        return 0

    def near_step(g, _):
        near_add(near_terms(near_place + g * NEAR_UNROLL, NEAR_UNROLL))
        return 0

    def far_step(g, _):
        far_add(far_terms(far_place + g * FAR_UNROLL))
        return 0

    lax.fori_loop(0, together, joint_step, 0)
    lax.fori_loop(together, near_groups, near_step, 0)
    lax.fori_loop(together, far_groups, far_step, 0)

    if stage < (1 if here else 3):
        return

    @pl.when(halves % 2 == 1)
    def _():
        near_add(near_terms(near_place + near_groups * NEAR_UNROLL, half))


def write_parts(outs, near_total, far_even, far_odd):
    for i, out in enumerate(outs):
        for j in range(8):
            half = slice(j % 2 * LANES, (j % 2 + 1) * LANES)
            part = near_total[4 * i + j // 2, :, half]
            out[j * SAMPLES : (j + 1) * SAMPLES] = part.astype(BF16)
        parts = []
        for l in range(CLUSTERS):
            even, odd = far_even[CLUSTERS * i + l], far_odd[CLUSTERS * i + l]
            parts.append(even[:, :64] + odd[:, 64:])
        for j in range(3):
            pair = lanes(*parts[2 * j : 2 * j + 2])
            out[FAR_ROW + 64 * j : FAR_ROW + 64 * (j + 1)] = pair.astype(BF16)
        pair = lanes(parts[6][:32], parts[6][32:])
        out[FAR_ROW + 192 : FAR_ROW + 224] = pair.astype(BF16)


def clear(totals):
    for total in totals:
        total[...] = jnp.zeros_like(total)


def early_kernel(plan, copied, members, lists, counts, near_row, far_row, *refs):
    blocks, refs = refs[: len(members)], refs[len(members) :]
    prepared, totals = refs[:6], refs[6:]
    clear(totals)
    for i, block in zip(members, blocks):
        prepare(i, block, *prepared)
    work(plan, 0, 0, lists, counts, near_row, far_row, prepared, totals)


def carry(before, after, copied):
    if copied:
        for old, new in zip(before, after):
            new[...] = old[...]


def second_kernel(plan, copied, members, lists, counts, near_row, far_row, *refs):
    before, refs = refs[:9], refs[9:]
    prepared, totals, here = refs[:6], refs[6:9], refs[9:]
    carry(before, refs, copied)
    clear(here)
    work(plan, 0, 1, lists, counts, near_row, far_row, prepared, totals)
    work(plan, 1, 0, lists, counts, near_row, far_row, prepared, here)


def mid_kernel(plan, copied, members, lists, counts, near_row, far_row, *refs):
    blocks, before, refs = refs[: len(members)], refs[len(members) :][:9], refs[len(members) + 9 :]
    prepared, totals = refs[:6], refs[6:9]
    carry(before, refs, copied)
    for i, block in zip(members, blocks):
        prepare(i, block, *prepared)
    work(plan, 0, 2, lists, counts, near_row, far_row, prepared, totals)


def late_kernel(plan, copied, members, lists, counts, near_row, far_row, *refs):
    blocks, before, refs = refs[: len(members)], refs[len(members) :][:9], refs[len(members) + 9 :]
    prepared, totals, outs = refs[:6], refs[6:9], refs[9:]
    carry(before, refs, copied)
    for i, block in zip(members, blocks):
        prepare(i, block, *prepared)
    work(plan, 0, 3, lists, counts, near_row, far_row, prepared, totals)
    write_parts(outs, *totals)


def here_kernel(plan, copied, lists, counts, near_row, far_row, *refs):
    prepared, before, refs = refs[:6], refs[7:10], refs[10:]
    totals, outs = refs[:3], refs[3:]
    carry(before, refs, copied)
    work(plan, 1, 1, lists, counts, near_row, far_row, prepared, totals)
    write_parts(outs, *totals)


def final_kernel(count, basis, moves, *refs):
    parts, out = refs[:count], refs[count]

    def total(first, count):
        return sum(part[first : first + count].astype(F32) for part in parts)

    def turned(first):
        tall = total(first, 64).T
        return lanes(tall[:64], tall[64:])

    top = total(FAR_ROW + 192, 32)
    top = rows(top[:, :64], top[:, 64:]).T
    middle = turned(FAR_ROW + 128) + dot_wide(top, moves[:, 256:384])
    for j in range(2):
        pair = turned(FAR_ROW + 64 * j) + dot_wide(
            middle[:, j * RANK : (j + 1) * RANK], moves[:, j * 128 : (j + 1) * 128]
        )
        for k in range(2):
            l = 2 * j + k
            expanded = dot_wide(
                pair[:, k * RANK : (k + 1) * RANK], basis[:, l * LEAF : (l + 1) * LEAF]
            )
            for h in range(2):
                place = (2 * l + h) * LANES
                near = total((2 * l + h) * SAMPLES, SAMPLES)
                made = near + expanded[:, h * LANES : (h + 1) * LANES]
                out[:, place : place + LANES] = made.astype(BF16)


def exchange(x, axis, offset):
    size = lax.axis_size(axis)
    return lax.ppermute(x, axis, [(i, i ^ offset) for i in range(size)])


def local(
    probes, points, skeleton, leaf_basis, transfer, near_list, near_count, far_list, far_count
):
    n_row = lax.axis_size("row")
    n_col = lax.axis_size("col")
    n_y = n_row // 4
    probes, basis, moves = probes.T, leaf_basis.T, transfer.T
    inputs = (probes, basis, moves, points, skeleton)
    small = pltpu.CompilerParams(vmem_limit_bytes=8 << 20)
    packed, coords = pl.pallas_call(
        pack_kernel,
        out_shape=[
            jax.ShapeDtypeStruct((PACKED_ROWS, LANES), BF16),
            jax.ShapeDtypeStruct((COORD_ROWS, LANES), BF16),
        ],
        in_specs=[VMEM] * 5,
        out_specs=[VMEM] * 2,
        name="pack",
    )(*inputs)

    plan = Plan(near_list.shape[-1], far_list.shape[-1])
    width = max(LANES, near_list.shape[-1], far_list.shape[-1])

    def placed(x, row):
        return jnp.pad(x, ((row, 8 - row - x.shape[0]), (0, width - x.shape[1])))

    slots = placed(near_list[0, 0], 0) + placed(far_list[0, 0], 2)
    slots = slots + placed(near_count, 4) + placed(far_count, 5)

    def along_z(x, planes, flip):
        pairs = [(z * n_y + y, (z ^ flip) * n_y + y) for z in planes for y in range(n_y)]
        return lax.ppermute(x, "row", pairs)

    own_y = exchange(packed, "row", 1)
    second = along_z(packed, (0, 1, 2, 3), 2)
    neighbour = along_z(packed, (0, 1, 2, 3), 1)
    lists, counts, both = pl.pallas_call(
        functools.partial(plan_kernel, n_col, n_y, plan),
        out_shape=[
            jax.ShapeDtypeStruct((2, plan.size), jnp.int32),
            jax.ShapeDtypeStruct((8, LANES), jnp.int32),
            jax.ShapeDtypeStruct((2 * COORD_ROWS, LANES), BF16),
        ],
        in_specs=[VMEM] * 3,
        out_specs=[VMEM] * 3,
        compiler_params=small,
        cost_estimate=pl.CostEstimate(flops=1 << 30, bytes_accessed=1 << 12, transcendentals=0),
        name="plan",
    )(slots, coords, exchange(coords, "col", 1))

    row_coords = [both] + [exchange(both, "col", k) for k in range(2, n_col, 2)]
    neighbour = tie(neighbour, lists)
    neighbour_y = exchange(neighbour, "row", 1)
    second = tie(second, own_y, neighbour, lists)
    def with_y(block, first=None):
        blocks = [block, exchange(block, "row", 1) if first is None else first]
        return blocks + [exchange(block, "row", y) for y in range(2, n_y)]

    blocks = with_y(packed, own_y) + with_y(neighbour, neighbour_y) + with_y(second)

    row_features = pl.pallas_call(
        functools.partial(row_kernel, n_col),
        out_shape=[
            jax.ShapeDtypeStruct((4 * n_col + 2, LEAF, FEATURES), BF16),
            jax.ShapeDtypeStruct((CLUSTERS * n_col + 2, RANK, FEATURES), BF16),
        ],
        in_specs=[VMEM] * (n_col // 2) + [ANY],
        out_specs=[VMEM] * 2,
        compiler_params=small,
        name="row_side",
    )(*row_coords, second)

    def sums(targets):
        near = (4 * targets + 1, SAMPLES, LEAF)
        far = (CLUSTERS * targets + 1, RANK, LANES)
        return [near, far, far]

    part = jax.ShapeDtypeStruct((COORD_ROW, LANES), BF16)
    held = [
        jax.ShapeDtypeStruct(shape, BF16)
        for shape in [
            (4 * n_row, SAMPLES, LEAF),
            (4 * n_row, FEATURES, LEAF),
            (CLUSTERS * n_row, RANK, LANES),
            (CLUSTERS * n_row, RANK, LANES),
            (CLUSTERS * n_row, FEATURES, LANES),
            (CLUSTERS * n_row, FEATURES, LANES),
        ]
    ]
    held += [jax.ShapeDtypeStruct(shape, F32) for shape in sums(n_col - 2)]
    params = pltpu.CompilerParams(vmem_limit_bytes=32 << 20)
    cost = pl.CostEstimate(flops=1 << 33, bytes_accessed=1 << 20, transcendentals=0)
    local_sums = [jax.ShapeDtypeStruct(shape, F32) for shape in sums(2)]
    copied = sum(math.prod(x.shape) * x.dtype.itemsize for x in held) > 8 << 20

    def stage(kernel, members, out_shape, name):
        first = 4 + len(members)
        return pl.pallas_call(
            functools.partial(kernel, plan, copied, members),
            out_shape=out_shape,
            in_specs=[SMEM] * 2 + [VMEM] * (2 + len(members) + len(handed)),
            out_specs=[VMEM] * len(out_shape),
            input_output_aliases={first + k: k for k in range(len(handed))},
            compiler_params=params,
            cost_estimate=cost,
            name=name,
        )(lists, counts, *row_features, *[blocks[j] for j in members], *handed)

    handed = []
    handed = stage(early_kernel, list(range(2 * n_y + 1)), held, "early")
    third = tie(along_z(second, (0, 1, 2, 3), 1), handed[6])
    blocks += with_y(third)
    both_sums = stage(second_kernel, [], held + local_sums, "second")
    handed, here_totals = both_sums[: len(held)], both_sums[len(held) :]
    handed = stage(mid_kernel, list(range(2 * n_y + 1, 3 * n_y + 1)), held, "mid")
    handed = stage(late_kernel, list(range(3 * n_y + 1, n_row)), held + [part] * (n_col - 2), "late")
    prepared, parts = handed[:6], handed[len(held) :]
    mine, other = parts[0::2], [exchange(part, "col", 1) for part in parts[1::2]]
    joined = pl.pallas_call(
        functools.partial(join_kernel, len(mine)),
        out_shape=[part] * len(mine),
        in_specs=[VMEM] * (2 * len(mine)),
        out_specs=[VMEM] * len(mine),
        compiler_params=params,
        name="join",
    )(*mine, *other)
    arrived = [exchange(joined[k], "col", 2 * k + 2) for k in range(len(mine))]
    here = pl.pallas_call(
        functools.partial(here_kernel, plan, copied),
        out_shape=local_sums + [part] * 2,
        in_specs=[SMEM] * 2 + [VMEM] * 8 + [ANY] + [VMEM] * 3,
        out_specs=[VMEM] * 5,
        input_output_aliases={11 + k: k for k in range(3)},
        compiler_params=params,
        cost_estimate=cost,
        name="here",
    )(lists, counts, *row_features, *prepared, joined[0], *here_totals)[3:]
    arrived = [tie(x, cost=cost) for x in arrived]
    arrived += [here[0], exchange(here[1], "col", 1)]
    sample = pl.pallas_call(
        functools.partial(final_kernel, len(arrived)),
        out_shape=jax.ShapeDtypeStruct((SAMPLES, OWN), BF16),
        in_specs=[VMEM] * (2 + len(arrived)),
        out_specs=VMEM,
        compiler_params=pltpu.CompilerParams(vmem_limit_bytes=16 << 20),
        name="final",
    )(basis, moves, *arrived)
    return sample.T


def solution(mesh):
    placed = (
        P(("row", "col"), None),
        P(None, ("row", "col")),
        P(None, ("row", "col")),
        P(("row", "col"), None),
        P(("row", "col"), None),
        P("row", "col", None, None),
        P("row", "col"),
        P("row", "col", None, None),
        P("row", "col"),
    )
    return jax.shard_map(
        local, mesh=mesh, in_specs=placed, out_specs=P(("row", "col"), None), check_vma=False
    )
```

```python
import functools
import math

import jax
import jax.numpy as jnp
from jax import lax
from jax.experimental import pallas as pl
from jax.experimental.pallas import tpu as pltpu
from jax.sharding import PartitionSpec as P

LEAF = 256
RANK = 64
SAMPLES = 64
OWN = 4 * LEAF
CLUSTERS = 7
LANES = 128
F32 = jnp.float32
BF16 = jnp.bfloat16
FAR_ROW = OWN // LANES * SAMPLES
COORD_ROW = FAR_ROW + CLUSTERS * SAMPLES // 2
COORD_ROWS = 96
PACKED_ROWS = COORD_ROW + COORD_ROWS
FEATURES = 16
CLASSES = 2
NEAR_UNROLL = 8
FAR_UNROLL = 16
RATE = math.sqrt(3.0) / 0.15
EARLY_UNITS = 1
HERE_UNITS = 1

ANY = pl.BlockSpec(memory_space=pl.ANY)
VMEM = pl.BlockSpec(memory_space=pltpu.VMEM)
SMEM = pl.BlockSpec(memory_space=pltpu.SMEM)
NN = (((1,), (0,)), ((), ()))
NT = (((1,), (1,)), ((), ()))


def dot(a, b, dims=NN):
    return lax.dot_general(a, b, dims, preferred_element_type=F32)


def dot_wide(a, b):
    high = a.astype(BF16)
    low = (a - high.astype(F32)).astype(BF16)
    return dot(high, b) + dot(low, b)


def lanes(a, b):
    return jnp.concatenate([a, b], axis=1)


def rows(*parts):
    return jnp.concatenate(parts, axis=0)


def features(points):
    norm = points * points
    norm = norm[0:1] + norm[1:2] + norm[2:3]
    high = norm.astype(BF16).astype(F32)
    rest = norm - high
    middle = rest.astype(BF16).astype(F32)
    ones = jnp.ones_like(norm)
    return rows(points, high, middle, rest - middle, ones, ones)


def row_side(made):
    ones = made[6:7]
    return rows(-2.0 * made[0:3], ones, ones, ones, made[3:4], made[4:5])


def matern_of(square):
    square = jnp.maximum(square, 1e-14)
    x = (square * lax.rsqrt(square)) * -RATE
    return ((1.0 - x) * jnp.exp(x)).astype(BF16)


def pack_kernel(probes, basis, moves, points, skeleton, packed, coords):
    near = features(points[...].astype(F32))
    far = features(lanes(skeleton[...].astype(F32), jnp.zeros((3, 64), F32)))
    chunks = [near[:, j * LANES : (j + 1) * LANES] for j in range(8)]
    chunks += [far[:, j * LANES : (j + 1) * LANES] for j in range(4)]
    made = rows(*chunks).astype(BF16)
    packed[COORD_ROW:] = made
    coords[...] = made
    leaves = []
    for l in range(4):
        part = slice(l * LEAF, (l + 1) * LEAF)
        leaves.append(dot(basis[:, part], probes[:, part], NT).astype(BF16))
    middle = [
        dot(moves[:, j * 128 : (j + 1) * 128], rows(*leaves[2 * j : 2 * j + 2])).astype(BF16)
        for j in range(2)
    ]
    top = dot(moves[:, 256:384], rows(*middle)).astype(BF16)
    for j in range(8):
        packed[j * SAMPLES : (j + 1) * SAMPLES] = probes[:, j * LANES : (j + 1) * LANES]
    packed[FAR_ROW : FAR_ROW + 64] = lanes(leaves[0], leaves[1])
    packed[FAR_ROW + 64 : FAR_ROW + 128] = lanes(leaves[2], leaves[3])
    packed[FAR_ROW + 128 : FAR_ROW + 192] = lanes(middle[0], middle[1])
    packed[FAR_ROW + 192 : FAR_ROW + 224] = lanes(top[:32], top[32:])


class Plan:
    def __init__(self, near_most, far_most):
        self.near = near_most + NEAR_UNROLL
        self.far = far_most + FAR_UNROLL
        self.far_first = -(-CLASSES * self.near // LANES) * LANES
        self.size = self.far_first + -(-CLASSES * self.far // LANES) * LANES


def iota(shape, axis):
    return lax.broadcasted_iota(jnp.int32, shape, axis)


def tie_kernel(*refs):
    del refs


def tie(x, *others, cost=None):
    return pl.pallas_call(
        tie_kernel,
        out_shape=jax.ShapeDtypeStruct(x.shape, x.dtype),
        in_specs=[ANY] * (1 + len(others)),
        out_specs=ANY,
        input_output_aliases={0: 0},
        compiler_params=pltpu.CompilerParams(vmem_limit_bytes=1 << 20),
        cost_estimate=cost,
        name="tie",
    )(x, *others)


def join_kernel(count, *refs):
    for mine, other, out in zip(refs[:count], refs[count : 2 * count], refs[2 * count :]):
        out[...] = (mine[...].astype(F32) + other[...].astype(F32)).astype(BF16)


def sort_slots(a_device, a_rest, b_device, b_rest, count, per_device, n_col, n_y, most, width):
    slots = a_device.shape[1]
    target = a_device ^ lax.axis_index("col")
    source = b_device ^ lax.axis_index("row")
    remote = target >= 2
    stage = jnp.where(source > 3 * n_y, 2, jnp.where(source > 2 * n_y, 1, 0))
    group = jnp.where(remote, stage, jnp.where(stage == 0, 3, 4))
    alive = iota((1, slots), 1) < count
    group = jnp.where(alive, group, 7)
    row = (target - jnp.where(remote, 2, 0)) * per_device + a_rest
    column = source * per_device + b_rest
    member = jnp.where(iota((8, slots), 0) == group, 1.0, 0.0)
    before = jnp.where(iota((slots, slots), 0) < iota((slots, slots), 1), 1.0, 0.0)
    ahead = dot(member.astype(BF16), before.astype(BF16))
    ahead = jnp.sum(member * ahead, axis=0, keepdims=True)
    sizes = jnp.sum(member, axis=1, keepdims=True)
    ahead += jnp.where(group == 4, sizes[3:4], 0.0)
    ahead += jnp.where((group == 1) | (group == 2), sizes[0:1], 0.0)
    ahead += jnp.where(group == 2, sizes[1:2], 0.0)
    place = jnp.where(alive, jnp.where(remote, 0, most) + ahead.astype(jnp.int32), -1)
    chosen = jnp.where(iota((width, slots), 0) == place, 1.0, 0.0).astype(BF16)
    ones = jnp.ones((6, slots), F32)
    values = rows(row.astype(F32), column.astype(F32), ones).astype(BF16)
    found = dot(values, chosen, NT)
    here = iota((1, width), 1) >= most
    blank = jnp.where(here, 2.0 * per_device, (n_col - 2.0) * per_device)
    made = rows(found[0:1] + blank * (1.0 - found[2:3]), found[1:2])
    return made.astype(jnp.int32), sizes.astype(jnp.int32)


def plan_kernel(n_col, n_y, plan, slots, coords, mate, out, counts, both):
    both[:COORD_ROWS] = coords[...]
    both[COORD_ROWS:] = mate[...]
    near_most, far_most = plan.near - NEAR_UNROLL, plan.far - FAR_UNROLL
    a, b = slots[0:1, :near_most], slots[1:2, :near_most]
    near, near_counts = sort_slots(
        lax.shift_right_logical(a, 2), a & 3, lax.shift_right_logical(b, 2), b & 3,
        slots[4:5, 0:1], 4, n_col, n_y, plan.near, plan.far_first,
    )
    a, b = slots[2:3, :far_most], slots[3:4, :far_most]
    a_device = lax.shift_right_logical(a * 9363, 16)
    b_device = lax.shift_right_logical(b * 9363, 16)
    far, far_counts = sort_slots(
        a_device, a - a_device * CLUSTERS, b_device, b - b_device * CLUSTERS,
        slots[5:6, 0:1], CLUSTERS, n_col, n_y, plan.far, plan.size - plan.far_first,
    )
    out[:, : plan.far_first] = near
    out[:, plan.far_first :] = far
    counts[...] = jnp.where(iota((8, LANES), 1) == 0, near_counts, far_counts)


def row_kernel(n_col, *refs):
    chips, near_row, far_row = refs[:-3], refs[-2], refs[-1]
    empty = jnp.zeros((8, LANES), F32)
    for i in range(n_col):
        first = i % 2 * COORD_ROWS
        slabs = [chips[i // 2][first + 16 * s : first + 16 * s + 16].astype(F32) for s in range(6)]
        near, far = (4 * i, CLUSTERS * i) if i < 2 else (4 * i + 1, CLUSTERS * i + 1)
        for l in range(4):
            for h in range(2):
                made = row_side(slabs[l][8 * h : 8 * h + 8])
                near_row[near + l, h * LANES : (h + 1) * LANES] = rows(made, empty).T.astype(BF16)
        for c in range(4):
            slab = slabs[4 + c // 2]
            made = row_side(slab[8 * (c % 2) : 8 * (c % 2) + 8])
            tall = rows(made, empty).T.astype(BF16)
            far_row[far + 2 * c] = tall[:64]
            if c < 3:
                far_row[far + 2 * c + 1] = tall[64:]
    for blank in (8, 4 * n_col + 1):
        near_row[blank] = jnp.zeros(near_row.shape[1:], BF16)
    for blank in (2 * CLUSTERS, CLUSTERS * n_col + 1):
        far_row[blank] = jnp.zeros(far_row.shape[1:], BF16)


def prepare(i, block, probes, near_col, coeff_low, coeff_high, far_low, far_high):
    for l in range(4):
        for h in range(2):
            j = 2 * l + h
            half = slice(h * LANES, (h + 1) * LANES)
            probes[4 * i + l, :, half] = block[j * SAMPLES : (j + 1) * SAMPLES]
        slab = block[COORD_ROW + 16 * l : COORD_ROW + 16 * (l + 1)]
        near_col[4 * i + l, :, :LANES] = slab
        near_col[4 * i + l, :, LANES:] = rows(slab[8:], slab[:8])
    slabs = [block[COORD_ROW + 64 + 16 * p : COORD_ROW + 80 + 16 * p] for p in range(2)]
    for k in range(CLUSTERS):
        c, half = k // 2, slice(k % 2 * 64, k % 2 * 64 + 64)
        if k < 6:
            own = block[FAR_ROW + 64 * c : FAR_ROW + 64 * (c + 1)][:, half]
        else:
            own = block[FAR_ROW + 192 : FAR_ROW + 224]
            own = rows(own[:, :64], own[:, 64:])
        empty = jnp.zeros_like(own)
        coeff_low[CLUSTERS * i + k] = lanes(own, empty)
        coeff_high[CLUSTERS * i + k] = lanes(empty, own)
        made = slabs[c // 2].astype(F32)[8 * (c % 2) : 8 * (c % 2) + 8, half]
        empty = jnp.zeros_like(made)
        blank = jnp.zeros((8, LANES), F32)
        far_low[CLUSTERS * i + k] = rows(lanes(made, empty), blank).astype(BF16)
        far_high[CLUSTERS * i + k] = rows(lanes(empty, made), blank).astype(BF16)


def work(plan, here, stage, lists, counts, near_row, far_row, prepared, totals):
    probes, near_col, coeff_low, coeff_high, far_low, far_high = prepared
    near_total, far_even, far_odd = totals
    near_first, far_first = (0, 0) if here else (9, 2 * CLUSTERS + 1)

    def near_terms(place, slots):
        terms = []
        for u in range(slots):
            a, b = lists[0, place + u], lists[1, place + u]
            values = matern_of(dot(near_row[near_first + a], near_col[b]))
            terms.append((a, dot(probes[b], values, NT)))
        return terms

    def near_add(terms):
        for a, term in terms:
            near_total[a] += term

    def far_terms(place):
        terms = []
        for u in range(0, FAR_UNROLL, 2):
            a0, a1 = lists[0, place + u], lists[0, place + u + 1]
            b0, b1 = lists[1, place + u], lists[1, place + u + 1]
            square = dot(far_row[far_first + a0], far_low[b0])
            square += dot(far_row[far_first + a1], far_high[b1])
            both = rows(coeff_low[b0], coeff_high[b1])
            terms.append((a0, a1, dot(matern_of(square), both)))
        return terms

    def far_add(terms):
        for a0, a1, term in terms:
            far_even[a0] += term
            far_odd[a1] += term

    half = NEAR_UNROLL // 2

    def bounds(kind, unroll):
        sizes = [counts[k, kind] for k in ((3, 4) if here else (0, 1, 2))]
        ends = [jnp.minimum(sizes[0] // unroll, HERE_UNITS if here else EARLY_UNITS)]
        if not here:
            ends += [sizes[0] // unroll, (sizes[0] + sizes[1]) // unroll]
        first = ends[stage - 1] if stage else 0
        if stage < len(ends):
            return first, (ends[stage] - first) * unroll
        return first, sum(sizes) - first * unroll

    near_from, near_count = bounds(0, NEAR_UNROLL)
    far_from, far_count = bounds(1, FAR_UNROLL)
    halves = (near_count + half - 1) // half
    near_groups = halves // 2
    far_groups = (far_count + FAR_UNROLL - 1) // FAR_UNROLL
    together = jnp.minimum(near_groups, far_groups)
    near_place = here * plan.near + near_from * NEAR_UNROLL
    far_place = plan.far_first + here * plan.far + far_from * FAR_UNROLL

    def joint_step(g, _):
        near = near_terms(near_place + g * NEAR_UNROLL, NEAR_UNROLL)
        far = far_terms(far_place + g * FAR_UNROLL)
        near_add(near)
        far_add(far)
        return 0

    def near_step(g, _):
        near_add(near_terms(near_place + g * NEAR_UNROLL, NEAR_UNROLL))
        return 0

    def far_step(g, _):
        far_add(far_terms(far_place + g * FAR_UNROLL))
        return 0

    lax.fori_loop(0, together, joint_step, 0)
    lax.fori_loop(together, near_groups, near_step, 0)
    lax.fori_loop(together, far_groups, far_step, 0)

    if stage < (1 if here else 3):
        return

    @pl.when(halves % 2 == 1)
    def _():
        near_add(near_terms(near_place + near_groups * NEAR_UNROLL, half))


def write_parts(outs, near_total, far_even, far_odd):
    for i, out in enumerate(outs):
        for j in range(8):
            half = slice(j % 2 * LANES, (j % 2 + 1) * LANES)
            part = near_total[4 * i + j // 2, :, half]
            out[j * SAMPLES : (j + 1) * SAMPLES] = part.astype(BF16)
        parts = []
        for l in range(CLUSTERS):
            even, odd = far_even[CLUSTERS * i + l], far_odd[CLUSTERS * i + l]
            parts.append(even[:, :64] + odd[:, 64:])
        for j in range(3):
            pair = lanes(*parts[2 * j : 2 * j + 2])
            out[FAR_ROW + 64 * j : FAR_ROW + 64 * (j + 1)] = pair.astype(BF16)
        pair = lanes(parts[6][:32], parts[6][32:])
        out[FAR_ROW + 192 : FAR_ROW + 224] = pair.astype(BF16)


def clear(totals):
    for total in totals:
        total[...] = jnp.zeros_like(total)


def early_kernel(plan, copied, members, lists, counts, near_row, far_row, *refs):
    blocks, refs = refs[: len(members)], refs[len(members) :]
    prepared, totals = refs[:6], refs[6:]
    clear(totals)
    for i, block in zip(members, blocks):
        prepare(i, block, *prepared)
    work(plan, 0, 0, lists, counts, near_row, far_row, prepared, totals)


def carry(before, after, copied):
    if copied:
        for old, new in zip(before, after):
            new[...] = old[...]


def second_kernel(plan, copied, members, lists, counts, near_row, far_row, *refs):
    before, refs = refs[:9], refs[9:]
    prepared, totals, here = refs[:6], refs[6:9], refs[9:]
    carry(before, refs, copied)
    clear(here)
    work(plan, 0, 1, lists, counts, near_row, far_row, prepared, totals)
    work(plan, 1, 0, lists, counts, near_row, far_row, prepared, here)


def mid_kernel(plan, copied, members, lists, counts, near_row, far_row, *refs):
    blocks, before, refs = refs[: len(members)], refs[len(members) :][:9], refs[len(members) + 9 :]
    prepared, totals = refs[:6], refs[6:9]
    carry(before, refs, copied)
    for i, block in zip(members, blocks):
        prepare(i, block, *prepared)
    work(plan, 0, 2, lists, counts, near_row, far_row, prepared, totals)


def late_kernel(plan, copied, members, lists, counts, near_row, far_row, *refs):
    blocks, before, refs = refs[: len(members)], refs[len(members) :][:9], refs[len(members) + 9 :]
    prepared, totals, outs = refs[:6], refs[6:9], refs[9:]
    carry(before, refs, copied)
    for i, block in zip(members, blocks):
        prepare(i, block, *prepared)
    work(plan, 0, 3, lists, counts, near_row, far_row, prepared, totals)
    write_parts(outs, *totals)


def here_kernel(plan, copied, lists, counts, near_row, far_row, *refs):
    prepared, before, refs = refs[:6], refs[7:10], refs[10:]
    totals, outs = refs[:3], refs[3:]
    carry(before, refs, copied)
    work(plan, 1, 1, lists, counts, near_row, far_row, prepared, totals)
    write_parts(outs, *totals)


def final_kernel(count, basis, moves, *refs):
    parts, out = refs[:count], refs[count]

    def total(first, count):
        return sum(part[first : first + count].astype(F32) for part in parts)

    def turned(first):
        tall = total(first, 64).T
        return lanes(tall[:64], tall[64:])

    top = total(FAR_ROW + 192, 32)
    top = rows(top[:, :64], top[:, 64:]).T
    middle = turned(FAR_ROW + 128) + dot_wide(top, moves[:, 256:384])
    for j in range(2):
        pair = turned(FAR_ROW + 64 * j) + dot_wide(
            middle[:, j * RANK : (j + 1) * RANK], moves[:, j * 128 : (j + 1) * 128]
        )
        for k in range(2):
            l = 2 * j + k
            expanded = dot_wide(
                pair[:, k * RANK : (k + 1) * RANK], basis[:, l * LEAF : (l + 1) * LEAF]
            )
            for h in range(2):
                place = (2 * l + h) * LANES
                near = total((2 * l + h) * SAMPLES, SAMPLES)
                made = near + expanded[:, h * LANES : (h + 1) * LANES]
                out[:, place : place + LANES] = made.astype(BF16)


def exchange(x, axis, offset):
    size = lax.axis_size(axis)
    return lax.ppermute(x, axis, [(i, i ^ offset) for i in range(size)])


def local(
    probes, points, skeleton, leaf_basis, transfer, near_list, near_count, far_list, far_count
):
    n_row = lax.axis_size("row")
    n_col = lax.axis_size("col")
    n_y = n_row // 4
    probes, basis, moves = probes.T, leaf_basis.T, transfer.T
    inputs = (probes, basis, moves, points, skeleton)
    small = pltpu.CompilerParams(vmem_limit_bytes=8 << 20)
    packed, coords = pl.pallas_call(
        pack_kernel,
        out_shape=[
            jax.ShapeDtypeStruct((PACKED_ROWS, LANES), BF16),
            jax.ShapeDtypeStruct((COORD_ROWS, LANES), BF16),
        ],
        in_specs=[VMEM] * 5,
        out_specs=[VMEM] * 2,
        name="pack",
    )(*inputs)

    plan = Plan(near_list.shape[-1], far_list.shape[-1])
    width = max(LANES, near_list.shape[-1], far_list.shape[-1])

    def placed(x, row):
        return jnp.pad(x, ((row, 8 - row - x.shape[0]), (0, width - x.shape[1])))

    slots = placed(near_list[0, 0], 0) + placed(far_list[0, 0], 2)
    slots = slots + placed(near_count, 4) + placed(far_count, 5)

    def along_z(x, planes, flip):
        pairs = [(z * n_y + y, (z ^ flip) * n_y + y) for z in planes for y in range(n_y)]
        return lax.ppermute(x, "row", pairs)

    own_y = exchange(packed, "row", 1)
    second = along_z(packed, (0, 1, 2, 3), 2)
    neighbour = along_z(packed, (0, 1, 2, 3), 1)
    lists, counts, both = pl.pallas_call(
        functools.partial(plan_kernel, n_col, n_y, plan),
        out_shape=[
            jax.ShapeDtypeStruct((2, plan.size), jnp.int32),
            jax.ShapeDtypeStruct((8, LANES), jnp.int32),
            jax.ShapeDtypeStruct((2 * COORD_ROWS, LANES), BF16),
        ],
        in_specs=[VMEM] * 3,
        out_specs=[VMEM] * 3,
        compiler_params=small,
        cost_estimate=pl.CostEstimate(flops=1 << 30, bytes_accessed=1 << 12, transcendentals=0),
        name="plan",
    )(slots, coords, exchange(coords, "col", 1))

    row_coords = [both] + [exchange(both, "col", k) for k in range(2, n_col, 2)]
    neighbour = tie(neighbour, lists)
    neighbour_y = exchange(neighbour, "row", 1)
    second = tie(second, own_y, neighbour, lists)
    def with_y(block, first=None):
        blocks = [block, exchange(block, "row", 1) if first is None else first]
        return blocks + [exchange(block, "row", y) for y in range(2, n_y)]

    blocks = with_y(packed, own_y) + with_y(neighbour, neighbour_y) + with_y(second)

    row_features = pl.pallas_call(
        functools.partial(row_kernel, n_col),
        out_shape=[
            jax.ShapeDtypeStruct((4 * n_col + 2, LEAF, FEATURES), BF16),
            jax.ShapeDtypeStruct((CLUSTERS * n_col + 2, RANK, FEATURES), BF16),
        ],
        in_specs=[VMEM] * (n_col // 2) + [ANY],
        out_specs=[VMEM] * 2,
        compiler_params=small,
        name="row_side",
    )(*row_coords, second)

    def sums(targets):
        near = (4 * targets + 1, SAMPLES, LEAF)
        far = (CLUSTERS * targets + 1, RANK, LANES)
        return [near, far, far]

    part = jax.ShapeDtypeStruct((COORD_ROW, LANES), BF16)
    held = [
        jax.ShapeDtypeStruct(shape, BF16)
        for shape in [
            (4 * n_row, SAMPLES, LEAF),
            (4 * n_row, FEATURES, LEAF),
            (CLUSTERS * n_row, RANK, LANES),
            (CLUSTERS * n_row, RANK, LANES),
            (CLUSTERS * n_row, FEATURES, LANES),
            (CLUSTERS * n_row, FEATURES, LANES),
        ]
    ]
    held += [jax.ShapeDtypeStruct(shape, F32) for shape in sums(n_col - 2)]
    params = pltpu.CompilerParams(vmem_limit_bytes=32 << 20)
    cost = pl.CostEstimate(flops=1 << 33, bytes_accessed=1 << 20, transcendentals=0)
    local_sums = [jax.ShapeDtypeStruct(shape, F32) for shape in sums(2)]
    copied = sum(math.prod(x.shape) * x.dtype.itemsize for x in held) > 8 << 20

    def stage(kernel, members, out_shape, name):
        first = 4 + len(members)
        return pl.pallas_call(
            functools.partial(kernel, plan, copied, members),
            out_shape=out_shape,
            in_specs=[SMEM] * 2 + [VMEM] * (2 + len(members) + len(handed)),
            out_specs=[VMEM] * len(out_shape),
            input_output_aliases={first + k: k for k in range(len(handed))},
            compiler_params=params,
            cost_estimate=cost,
            name=name,
        )(lists, counts, *row_features, *[blocks[j] for j in members], *handed)

    handed = []
    handed = stage(early_kernel, list(range(2 * n_y + 1)), held, "early")
    third = tie(along_z(second, (0, 1, 2, 3), 1), handed[6])
    blocks += with_y(third)
    both_sums = stage(second_kernel, [], held + local_sums, "second")
    handed, here_totals = both_sums[: len(held)], both_sums[len(held) :]
    handed = stage(mid_kernel, list(range(2 * n_y + 1, 3 * n_y + 1)), held, "mid")
    handed = stage(late_kernel, list(range(3 * n_y + 1, n_row)), held + [part] * (n_col - 2), "late")
    prepared, parts = handed[:6], handed[len(held) :]
    mine, other = parts[0::2], [exchange(part, "col", 1) for part in parts[1::2]]
    joined = pl.pallas_call(
        functools.partial(join_kernel, len(mine)),
        out_shape=[part] * len(mine),
        in_specs=[VMEM] * (2 * len(mine)),
        out_specs=[VMEM] * len(mine),
        compiler_params=params,
        name="join",
    )(*mine, *other)
    arrived = [exchange(joined[k], "col", 2 * k + 2) for k in range(len(mine))]
    here = pl.pallas_call(
        functools.partial(here_kernel, plan, copied),
        out_shape=local_sums + [part] * 2,
        in_specs=[SMEM] * 2 + [VMEM] * 8 + [ANY] + [VMEM] * 3,
        out_specs=[VMEM] * 5,
        input_output_aliases={11 + k: k for k in range(3)},
        compiler_params=params,
        cost_estimate=cost,
        name="here",
    )(lists, counts, *row_features, *prepared, joined[0], *here_totals)[3:]
    arrived = [tie(x, cost=cost) for x in arrived]
    arrived += [here[0], exchange(here[1], "col", 1)]
    sample = pl.pallas_call(
        functools.partial(final_kernel, len(arrived)),
        out_shape=jax.ShapeDtypeStruct((SAMPLES, OWN), BF16),
        in_specs=[VMEM] * (2 + len(arrived)),
        out_specs=VMEM,
        compiler_params=pltpu.CompilerParams(vmem_limit_bytes=16 << 20),
        name="final",
    )(basis, moves, *arrived)
    return sample.T


def solution(mesh):
    placed = (
        P(("row", "col"), None),
        P(None, ("row", "col")),
        P(None, ("row", "col")),
        P(("row", "col"), None),
        P(("row", "col"), None),
        P("row", "col", None, None),
        P("row", "col"),
        P("row", "col", None, None),
        P("row", "col"),
    )
    return jax.shard_map(
        local, mesh=mesh, in_specs=placed, out_specs=P(("row", "col"), None), check_vma=False
    )
```

```python
import functools
import math

import jax
import jax.numpy as jnp
from jax import lax
from jax.experimental import pallas as pl
from jax.experimental.pallas import tpu as pltpu
from jax.sharding import PartitionSpec as P

LEAF = 256
RANK = 64
SAMPLES = 64
OWN = 4 * LEAF
CLUSTERS = 7
LANES = 128
F32 = jnp.float32
BF16 = jnp.bfloat16
FAR_ROW = OWN // LANES * SAMPLES
COORD_ROW = FAR_ROW + CLUSTERS * SAMPLES // 2
COORD_ROWS = 96
PACKED_ROWS = COORD_ROW + COORD_ROWS
FEATURES = 16
CLASSES = 2
NEAR_UNROLL = 8
FAR_UNROLL = 16
RATE = math.sqrt(3.0) / 0.15
EARLY_UNITS = 1
HERE_UNITS = 1

ANY = pl.BlockSpec(memory_space=pl.ANY)
VMEM = pl.BlockSpec(memory_space=pltpu.VMEM)
SMEM = pl.BlockSpec(memory_space=pltpu.SMEM)
NN = (((1,), (0,)), ((), ()))
NT = (((1,), (1,)), ((), ()))


def dot(a, b, dims=NN):
    return lax.dot_general(a, b, dims, preferred_element_type=F32)


def dot_wide(a, b):
    high = a.astype(BF16)
    low = (a - high.astype(F32)).astype(BF16)
    return dot(high, b) + dot(low, b)


def lanes(a, b):
    return jnp.concatenate([a, b], axis=1)


def rows(*parts):
    return jnp.concatenate(parts, axis=0)


def features(points):
    norm = points * points
    norm = norm[0:1] + norm[1:2] + norm[2:3]
    high = norm.astype(BF16).astype(F32)
    rest = norm - high
    middle = rest.astype(BF16).astype(F32)
    ones = jnp.ones_like(norm)
    return rows(points, high, middle, rest - middle, ones, ones)


def row_side(made):
    ones = made[6:7]
    return rows(-2.0 * made[0:3], ones, ones, ones, made[3:4], made[4:5])


def matern_of(square):
    square = jnp.maximum(square, 1e-14)
    x = (square * lax.rsqrt(square)) * -RATE
    return ((1.0 - x) * jnp.exp(x)).astype(BF16)


def pack_kernel(probes, basis, moves, points, skeleton, packed, coords):
    near = features(points[...].astype(F32))
    far = features(lanes(skeleton[...].astype(F32), jnp.zeros((3, 64), F32)))
    chunks = [near[:, j * LANES : (j + 1) * LANES] for j in range(8)]
    chunks += [far[:, j * LANES : (j + 1) * LANES] for j in range(4)]
    made = rows(*chunks).astype(BF16)
    packed[COORD_ROW:] = made
    coords[...] = made
    leaves = []
    for l in range(4):
        part = slice(l * LEAF, (l + 1) * LEAF)
        leaves.append(dot(basis[:, part], probes[:, part], NT).astype(BF16))
    middle = [
        dot(moves[:, j * 128 : (j + 1) * 128], rows(*leaves[2 * j : 2 * j + 2])).astype(BF16)
        for j in range(2)
    ]
    top = dot(moves[:, 256:384], rows(*middle)).astype(BF16)
    for j in range(8):
        packed[j * SAMPLES : (j + 1) * SAMPLES] = probes[:, j * LANES : (j + 1) * LANES]
    packed[FAR_ROW : FAR_ROW + 64] = lanes(leaves[0], leaves[1])
    packed[FAR_ROW + 64 : FAR_ROW + 128] = lanes(leaves[2], leaves[3])
    packed[FAR_ROW + 128 : FAR_ROW + 192] = lanes(middle[0], middle[1])
    packed[FAR_ROW + 192 : FAR_ROW + 224] = lanes(top[:32], top[32:])


class Plan:
    def __init__(self, near_most, far_most):
        self.near = near_most + NEAR_UNROLL
        self.far = far_most + FAR_UNROLL
        self.far_first = -(-CLASSES * self.near // LANES) * LANES
        self.size = self.far_first + -(-CLASSES * self.far // LANES) * LANES


def iota(shape, axis):
    return lax.broadcasted_iota(jnp.int32, shape, axis)


def tie_kernel(*refs):
    del refs


def tie(x, *others, cost=None):
    return pl.pallas_call(
        tie_kernel,
        out_shape=jax.ShapeDtypeStruct(x.shape, x.dtype),
        in_specs=[ANY] * (1 + len(others)),
        out_specs=ANY,
        input_output_aliases={0: 0},
        compiler_params=pltpu.CompilerParams(vmem_limit_bytes=1 << 20),
        cost_estimate=cost,
        name="tie",
    )(x, *others)


def join_kernel(count, *refs):
    for mine, other, out in zip(refs[:count], refs[count : 2 * count], refs[2 * count :]):
        out[...] = (mine[...].astype(F32) + other[...].astype(F32)).astype(BF16)


def sort_slots(a_device, a_rest, b_device, b_rest, count, per_device, n_col, n_y, most, width):
    slots = a_device.shape[1]
    target = a_device ^ lax.axis_index("col")
    source = b_device ^ lax.axis_index("row")
    remote = target >= 2
    stage = jnp.where(source > 3 * n_y, 2, jnp.where(source > 2 * n_y, 1, 0))
    group = jnp.where(remote, stage, jnp.where(stage == 0, 3, 4))
    alive = iota((1, slots), 1) < count
    group = jnp.where(alive, group, 7)
    row = (target - jnp.where(remote, 2, 0)) * per_device + a_rest
    column = source * per_device + b_rest
    member = jnp.where(iota((8, slots), 0) == group, 1.0, 0.0)
    before = jnp.where(iota((slots, slots), 0) < iota((slots, slots), 1), 1.0, 0.0)
    ahead = dot(member.astype(BF16), before.astype(BF16))
    ahead = jnp.sum(member * ahead, axis=0, keepdims=True)
    sizes = jnp.sum(member, axis=1, keepdims=True)
    ahead += jnp.where(group == 4, sizes[3:4], 0.0)
    ahead += jnp.where((group == 1) | (group == 2), sizes[0:1], 0.0)
    ahead += jnp.where(group == 2, sizes[1:2], 0.0)
    place = jnp.where(alive, jnp.where(remote, 0, most) + ahead.astype(jnp.int32), -1)
    chosen = jnp.where(iota((width, slots), 0) == place, 1.0, 0.0).astype(BF16)
    ones = jnp.ones((6, slots), F32)
    values = rows(row.astype(F32), column.astype(F32), ones).astype(BF16)
    found = dot(values, chosen, NT)
    here = iota((1, width), 1) >= most
    blank = jnp.where(here, 2.0 * per_device, (n_col - 2.0) * per_device)
    made = rows(found[0:1] + blank * (1.0 - found[2:3]), found[1:2])
    return made.astype(jnp.int32), sizes.astype(jnp.int32)


def plan_kernel(n_col, n_y, plan, slots, coords, mate, out, counts, both):
    both[:COORD_ROWS] = coords[...]
    both[COORD_ROWS:] = mate[...]
    near_most, far_most = plan.near - NEAR_UNROLL, plan.far - FAR_UNROLL
    a, b = slots[0:1, :near_most], slots[1:2, :near_most]
    near, near_counts = sort_slots(
        lax.shift_right_logical(a, 2), a & 3, lax.shift_right_logical(b, 2), b & 3,
        slots[4:5, 0:1], 4, n_col, n_y, plan.near, plan.far_first,
    )
    a, b = slots[2:3, :far_most], slots[3:4, :far_most]
    a_device = lax.shift_right_logical(a * 9363, 16)
    b_device = lax.shift_right_logical(b * 9363, 16)
    far, far_counts = sort_slots(
        a_device, a - a_device * CLUSTERS, b_device, b - b_device * CLUSTERS,
        slots[5:6, 0:1], CLUSTERS, n_col, n_y, plan.far, plan.size - plan.far_first,
    )
    out[:, : plan.far_first] = near
    out[:, plan.far_first :] = far
    counts[...] = jnp.where(iota((8, LANES), 1) == 0, near_counts, far_counts)


def row_kernel(n_col, *refs):
    chips, near_row, far_row = refs[:-3], refs[-2], refs[-1]
    empty = jnp.zeros((8, LANES), F32)
    for i in range(n_col):
        first = i % 2 * COORD_ROWS
        slabs = [chips[i // 2][first + 16 * s : first + 16 * s + 16].astype(F32) for s in range(6)]
        near, far = (4 * i, CLUSTERS * i) if i < 2 else (4 * i + 1, CLUSTERS * i + 1)
        for l in range(4):
            for h in range(2):
                made = row_side(slabs[l][8 * h : 8 * h + 8])
                near_row[near + l, h * LANES : (h + 1) * LANES] = rows(made, empty).T.astype(BF16)
        for c in range(4):
            slab = slabs[4 + c // 2]
            made = row_side(slab[8 * (c % 2) : 8 * (c % 2) + 8])
            blank = rows(empty, empty)
            for v, parts in enumerate(((made, empty, blank), (blank, made, empty))):
                tall = rows(*parts).T.astype(BF16)
                far_row[v, far + 2 * c] = tall[:64]
                if c < 3:
                    far_row[v, far + 2 * c + 1] = tall[64:]
    for blank in (8, 4 * n_col + 1):
        near_row[blank] = jnp.zeros(near_row.shape[1:], BF16)
    for blank in (2 * CLUSTERS, CLUSTERS * n_col + 1):
        for v in range(2):
            far_row[v, blank] = jnp.zeros(far_row.shape[2:], BF16)


def prepare(i, block, probes, near_col, coeff_low, coeff_high, far_low, far_high):
    for l in range(4):
        for h in range(2):
            j = 2 * l + h
            half = slice(h * LANES, (h + 1) * LANES)
            probes[4 * i + l, :, half] = block[j * SAMPLES : (j + 1) * SAMPLES]
        slab = block[COORD_ROW + 16 * l : COORD_ROW + 16 * (l + 1)]
        near_col[4 * i + l, :, :LANES] = slab
        near_col[4 * i + l, :, LANES:] = rows(slab[8:], slab[:8])
    slabs = [block[COORD_ROW + 64 + 16 * p : COORD_ROW + 80 + 16 * p] for p in range(2)]
    for k in range(CLUSTERS):
        c, half = k // 2, slice(k % 2 * 64, k % 2 * 64 + 64)
        if k < 6:
            own = block[FAR_ROW + 64 * c : FAR_ROW + 64 * (c + 1)][:, half]
        else:
            own = block[FAR_ROW + 192 : FAR_ROW + 224]
            own = rows(own[:, :64], own[:, 64:])
        empty = jnp.zeros_like(own)
        coeff_low[CLUSTERS * i + k] = lanes(own, empty)
        coeff_high[CLUSTERS * i + k] = lanes(empty, own)
        made = slabs[c // 2].astype(F32)[8 * (c % 2) : 8 * (c % 2) + 8, half]
        empty = jnp.zeros_like(made)
        blank = jnp.zeros((8, LANES), F32)
        far_low[CLUSTERS * i + k] = rows(lanes(made, empty), blank).astype(BF16)
        far_high[CLUSTERS * i + k] = rows(lanes(empty, made), blank).astype(BF16)


def work(plan, here, stage, lists, counts, near_row, far_row, prepared, totals):
    probes, near_col, coeff_low, coeff_high, far_low, far_high = prepared
    near_total, far_even, far_odd = totals
    near_first, far_first = (0, 0) if here else (9, 2 * CLUSTERS + 1)

    def near_terms(place, slots):
        terms = []
        for u in range(slots):
            a, b = lists[0, place + u], lists[1, place + u]
            values = matern_of(dot(near_row[near_first + a], near_col[b]))
            terms.append((a, dot(probes[b], values, NT)))
        return terms

    def near_add(terms):
        for a, term in terms:
            near_total[a] += term

    def far_terms(place):
        terms = []
        for u in range(0, FAR_UNROLL, 2):
            a0, a1 = lists[0, place + u], lists[0, place + u + 1]
            b0, b1 = lists[1, place + u], lists[1, place + u + 1]
            left = far_row[0, far_first + a0] + far_row[1, far_first + a1]
            square = dot(left, rows(far_low[b0], far_high[b1]))
            both = rows(coeff_low[b0], coeff_high[b1])
            terms.append((a0, a1, dot(matern_of(square), both)))
        return terms

    def far_add(terms):
        for a0, a1, term in terms:
            far_even[a0] += term
            far_odd[a1] += term

    half = NEAR_UNROLL // 2

    def bounds(kind, unroll):
        sizes = [counts[k, kind] for k in ((3, 4) if here else (0, 1, 2))]
        ends = [jnp.minimum(sizes[0] // unroll, HERE_UNITS if here else EARLY_UNITS)]
        if not here:
            ends += [sizes[0] // unroll, (sizes[0] + sizes[1]) // unroll]
        first = ends[stage - 1] if stage else 0
        if stage < len(ends):
            return first, (ends[stage] - first) * unroll
        return first, sum(sizes) - first * unroll

    near_from, near_count = bounds(0, NEAR_UNROLL)
    far_from, far_count = bounds(1, FAR_UNROLL)
    halves = (near_count + half - 1) // half
    near_groups = halves // 2
    far_groups = (far_count + FAR_UNROLL - 1) // FAR_UNROLL
    together = jnp.minimum(near_groups, far_groups)
    near_place = here * plan.near + near_from * NEAR_UNROLL
    far_place = plan.far_first + here * plan.far + far_from * FAR_UNROLL

    def joint_step(g, _):
        near = near_terms(near_place + g * NEAR_UNROLL, NEAR_UNROLL)
        far = far_terms(far_place + g * FAR_UNROLL)
        near_add(near)
        far_add(far)
        return 0

    def near_step(g, _):
        near_add(near_terms(near_place + g * NEAR_UNROLL, NEAR_UNROLL))
        return 0

    def far_step(g, _):
        far_add(far_terms(far_place + g * FAR_UNROLL))
        return 0

    lax.fori_loop(0, together, joint_step, 0)
    lax.fori_loop(together, near_groups, near_step, 0)
    lax.fori_loop(together, far_groups, far_step, 0)

    if stage < (1 if here else 3):
        return

    @pl.when(halves % 2 == 1)
    def _():
        near_add(near_terms(near_place + near_groups * NEAR_UNROLL, half))


def write_parts(outs, near_total, far_even, far_odd):
    for i, out in enumerate(outs):
        for j in range(8):
            half = slice(j % 2 * LANES, (j % 2 + 1) * LANES)
            part = near_total[4 * i + j // 2, :, half]
            out[j * SAMPLES : (j + 1) * SAMPLES] = part.astype(BF16)
        parts = []
        for l in range(CLUSTERS):
            even, odd = far_even[CLUSTERS * i + l], far_odd[CLUSTERS * i + l]
            parts.append(even[:, :64] + odd[:, 64:])
        for j in range(3):
            pair = lanes(*parts[2 * j : 2 * j + 2])
            out[FAR_ROW + 64 * j : FAR_ROW + 64 * (j + 1)] = pair.astype(BF16)
        pair = lanes(parts[6][:32], parts[6][32:])
        out[FAR_ROW + 192 : FAR_ROW + 224] = pair.astype(BF16)


def clear(totals):
    for total in totals:
        total[...] = jnp.zeros_like(total)


def early_kernel(plan, copied, members, lists, counts, near_row, far_row, *refs):
    blocks, refs = refs[: len(members)], refs[len(members) :]
    prepared, totals = refs[:6], refs[6:]
    clear(totals)
    for i, block in zip(members, blocks):
        prepare(i, block, *prepared)
    work(plan, 0, 0, lists, counts, near_row, far_row, prepared, totals)


def carry(before, after, copied):
    if copied:
        for old, new in zip(before, after):
            new[...] = old[...]


def second_kernel(plan, copied, members, lists, counts, near_row, far_row, *refs):
    before, refs = refs[:9], refs[9:]
    prepared, totals, here = refs[:6], refs[6:9], refs[9:]
    carry(before, refs, copied)
    clear(here)
    work(plan, 0, 1, lists, counts, near_row, far_row, prepared, totals)
    work(plan, 1, 0, lists, counts, near_row, far_row, prepared, here)


def mid_kernel(plan, copied, members, lists, counts, near_row, far_row, *refs):
    blocks, before, refs = refs[: len(members)], refs[len(members) :][:9], refs[len(members) + 9 :]
    prepared, totals = refs[:6], refs[6:9]
    carry(before, refs, copied)
    for i, block in zip(members, blocks):
        prepare(i, block, *prepared)
    work(plan, 0, 2, lists, counts, near_row, far_row, prepared, totals)


def late_kernel(plan, copied, members, lists, counts, near_row, far_row, *refs):
    blocks, before, refs = refs[: len(members)], refs[len(members) :][:9], refs[len(members) + 9 :]
    prepared, totals, outs = refs[:6], refs[6:9], refs[9:]
    carry(before, refs, copied)
    for i, block in zip(members, blocks):
        prepare(i, block, *prepared)
    work(plan, 0, 3, lists, counts, near_row, far_row, prepared, totals)
    write_parts(outs, *totals)


def here_kernel(plan, copied, lists, counts, near_row, far_row, *refs):
    prepared, before, refs = refs[:6], refs[7:10], refs[10:]
    totals, outs = refs[:3], refs[3:]
    carry(before, refs, copied)
    work(plan, 1, 1, lists, counts, near_row, far_row, prepared, totals)
    write_parts(outs, *totals)


def final_kernel(count, basis, moves, *refs):
    parts, out = refs[:count], refs[count]

    def total(first, count):
        return sum(part[first : first + count].astype(F32) for part in parts)

    def turned(first):
        tall = total(first, 64).T
        return lanes(tall[:64], tall[64:])

    top = total(FAR_ROW + 192, 32)
    top = rows(top[:, :64], top[:, 64:]).T
    middle = turned(FAR_ROW + 128) + dot_wide(top, moves[:, 256:384])
    for j in range(2):
        pair = turned(FAR_ROW + 64 * j) + dot_wide(
            middle[:, j * RANK : (j + 1) * RANK], moves[:, j * 128 : (j + 1) * 128]
        )
        for k in range(2):
            l = 2 * j + k
            leaf = pair[:, k * RANK : (k + 1) * RANK].astype(BF16)
            expanded = dot(leaf, basis[:, l * LEAF : (l + 1) * LEAF])
            for h in range(2):
                place = (2 * l + h) * LANES
                near = total((2 * l + h) * SAMPLES, SAMPLES)
                made = near + expanded[:, h * LANES : (h + 1) * LANES]
                out[:, place : place + LANES] = made.astype(BF16)


def exchange(x, axis, offset):
    size = lax.axis_size(axis)
    return lax.ppermute(x, axis, [(i, i ^ offset) for i in range(size)])


def local(
    probes, points, skeleton, leaf_basis, transfer, near_list, near_count, far_list, far_count
):
    n_row = lax.axis_size("row")
    n_col = lax.axis_size("col")
    n_y = n_row // 4
    probes, basis, moves = probes.T, leaf_basis.T, transfer.T
    inputs = (probes, basis, moves, points, skeleton)
    small = pltpu.CompilerParams(vmem_limit_bytes=8 << 20)
    packed, coords = pl.pallas_call(
        pack_kernel,
        out_shape=[
            jax.ShapeDtypeStruct((PACKED_ROWS, LANES), BF16),
            jax.ShapeDtypeStruct((COORD_ROWS, LANES), BF16),
        ],
        in_specs=[VMEM] * 5,
        out_specs=[VMEM] * 2,
        name="pack",
    )(*inputs)

    plan = Plan(near_list.shape[-1], far_list.shape[-1])
    width = max(LANES, near_list.shape[-1], far_list.shape[-1])

    def placed(x, row):
        return jnp.pad(x, ((row, 8 - row - x.shape[0]), (0, width - x.shape[1])))

    slots = placed(near_list[0, 0], 0) + placed(far_list[0, 0], 2)
    slots = slots + placed(near_count, 4) + placed(far_count, 5)

    def along_z(x, planes, flip):
        pairs = [(z * n_y + y, (z ^ flip) * n_y + y) for z in planes for y in range(n_y)]
        return lax.ppermute(x, "row", pairs)

    own_y = exchange(packed, "row", 1)
    second = along_z(packed, (0, 1, 2, 3), 2)
    neighbour = along_z(packed, (0, 1, 2, 3), 1)
    lists, counts, both = pl.pallas_call(
        functools.partial(plan_kernel, n_col, n_y, plan),
        out_shape=[
            jax.ShapeDtypeStruct((2, plan.size), jnp.int32),
            jax.ShapeDtypeStruct((8, LANES), jnp.int32),
            jax.ShapeDtypeStruct((2 * COORD_ROWS, LANES), BF16),
        ],
        in_specs=[VMEM] * 3,
        out_specs=[VMEM] * 3,
        compiler_params=small,
        cost_estimate=pl.CostEstimate(flops=1 << 30, bytes_accessed=1 << 12, transcendentals=0),
        name="plan",
    )(slots, coords, exchange(coords, "col", 1))

    row_coords = [both] + [exchange(both, "col", k) for k in range(2, n_col, 2)]
    neighbour = tie(neighbour, lists)
    neighbour_y = exchange(neighbour, "row", 1)
    second = tie(second, own_y, neighbour, lists)
    def with_y(block, first=None):
        blocks = [block, exchange(block, "row", 1) if first is None else first]
        return blocks + [exchange(block, "row", y) for y in range(2, n_y)]

    blocks = with_y(packed, own_y) + with_y(neighbour, neighbour_y) + with_y(second)

    row_features = pl.pallas_call(
        functools.partial(row_kernel, n_col),
        out_shape=[
            jax.ShapeDtypeStruct((4 * n_col + 2, LEAF, FEATURES), BF16),
            jax.ShapeDtypeStruct((2, CLUSTERS * n_col + 2, RANK, 2 * FEATURES), BF16),
        ],
        in_specs=[VMEM] * (n_col // 2) + [ANY],
        out_specs=[VMEM] * 2,
        compiler_params=small,
        name="row_side",
    )(*row_coords, second)

    def sums(targets):
        near = (4 * targets + 1, SAMPLES, LEAF)
        far = (CLUSTERS * targets + 1, RANK, LANES)
        return [near, far, far]

    part = jax.ShapeDtypeStruct((COORD_ROW, LANES), BF16)
    held = [
        jax.ShapeDtypeStruct(shape, BF16)
        for shape in [
            (4 * n_row, SAMPLES, LEAF),
            (4 * n_row, FEATURES, LEAF),
            (CLUSTERS * n_row, RANK, LANES),
            (CLUSTERS * n_row, RANK, LANES),
            (CLUSTERS * n_row, FEATURES, LANES),
            (CLUSTERS * n_row, FEATURES, LANES),
        ]
    ]
    held += [jax.ShapeDtypeStruct(shape, F32) for shape in sums(n_col - 2)]
    params = pltpu.CompilerParams(vmem_limit_bytes=32 << 20)
    cost = pl.CostEstimate(flops=1 << 33, bytes_accessed=1 << 20, transcendentals=0)
    local_sums = [jax.ShapeDtypeStruct(shape, F32) for shape in sums(2)]
    copied = sum(math.prod(x.shape) * x.dtype.itemsize for x in held) > 8 << 20

    def stage(kernel, members, out_shape, name):
        first = 4 + len(members)
        return pl.pallas_call(
            functools.partial(kernel, plan, copied, members),
            out_shape=out_shape,
            in_specs=[SMEM] * 2 + [VMEM] * (2 + len(members) + len(handed)),
            out_specs=[VMEM] * len(out_shape),
            input_output_aliases={first + k: k for k in range(len(handed))},
            compiler_params=params,
            cost_estimate=cost,
            name=name,
        )(lists, counts, *row_features, *[blocks[j] for j in members], *handed)

    handed = []
    handed = stage(early_kernel, list(range(2 * n_y + 1)), held, "early")
    third = tie(along_z(second, (0, 1, 2, 3), 1), handed[6])
    blocks += with_y(third)
    both_sums = stage(second_kernel, [], held + local_sums, "second")
    handed, here_totals = both_sums[: len(held)], both_sums[len(held) :]
    handed = stage(mid_kernel, list(range(2 * n_y + 1, 3 * n_y + 1)), held, "mid")
    handed = stage(late_kernel, list(range(3 * n_y + 1, n_row)), held + [part] * (n_col - 2), "late")
    prepared, parts = handed[:6], handed[len(held) :]
    mine, other = parts[0::2], [exchange(part, "col", 1) for part in parts[1::2]]
    joined = pl.pallas_call(
        functools.partial(join_kernel, len(mine)),
        out_shape=[part] * len(mine),
        in_specs=[VMEM] * (2 * len(mine)),
        out_specs=[VMEM] * len(mine),
        compiler_params=params,
        name="join",
    )(*mine, *other)
    arrived = [exchange(joined[k], "col", 2 * k + 2) for k in range(len(mine))]
    here = pl.pallas_call(
        functools.partial(here_kernel, plan, copied),
        out_shape=local_sums + [part] * 2,
        in_specs=[SMEM] * 2 + [VMEM] * 8 + [ANY] + [VMEM] * 3,
        out_specs=[VMEM] * 5,
        input_output_aliases={11 + k: k for k in range(3)},
        compiler_params=params,
        cost_estimate=cost,
        name="here",
    )(lists, counts, *row_features, *prepared, joined[0], *here_totals)[3:]
    arrived = [tie(x, cost=cost) for x in arrived]
    arrived += [here[0], exchange(here[1], "col", 1)]
    sample = pl.pallas_call(
        functools.partial(final_kernel, len(arrived)),
        out_shape=jax.ShapeDtypeStruct((SAMPLES, OWN), BF16),
        in_specs=[VMEM] * (2 + len(arrived)),
        out_specs=VMEM,
        compiler_params=pltpu.CompilerParams(vmem_limit_bytes=16 << 20),
        name="final",
    )(basis, moves, *arrived)
    return sample.T


def solution(mesh):
    placed = (
        P(("row", "col"), None),
        P(None, ("row", "col")),
        P(None, ("row", "col")),
        P(("row", "col"), None),
        P(("row", "col"), None),
        P("row", "col", None, None),
        P("row", "col"),
        P("row", "col", None, None),
        P("row", "col"),
    )
    return jax.shard_map(
        local, mesh=mesh, in_specs=placed, out_specs=P(("row", "col"), None), check_vma=False
    )
```

```python
import functools
import math

import jax
import jax.numpy as jnp
from jax import lax
from jax.experimental import pallas as pl
from jax.experimental.pallas import tpu as pltpu
from jax.sharding import PartitionSpec as P

LEAF = 256
RANK = 64
SAMPLES = 64
OWN = 4 * LEAF
CLUSTERS = 7
LANES = 128
F32 = jnp.float32
BF16 = jnp.bfloat16
FAR_ROW = OWN // LANES * SAMPLES
COORD_ROW = FAR_ROW + CLUSTERS * SAMPLES // 2
COORD_ROWS = 96
PACKED_ROWS = COORD_ROW + COORD_ROWS
FEATURES = 16
CLASSES = 2
NEAR_UNROLL = 8
FAR_UNROLL = 16
RATE = math.sqrt(3.0) / 0.15
EARLY_UNITS = 1
HERE_UNITS = 1

ANY = pl.BlockSpec(memory_space=pl.ANY)
VMEM = pl.BlockSpec(memory_space=pltpu.VMEM)
SMEM = pl.BlockSpec(memory_space=pltpu.SMEM)
NN = (((1,), (0,)), ((), ()))
NT = (((1,), (1,)), ((), ()))


def dot(a, b, dims=NN):
    return lax.dot_general(a, b, dims, preferred_element_type=F32)


def dot_wide(a, b):
    high = a.astype(BF16)
    low = (a - high.astype(F32)).astype(BF16)
    return dot(high, b) + dot(low, b)


def lanes(a, b):
    return jnp.concatenate([a, b], axis=1)


def rows(*parts):
    return jnp.concatenate(parts, axis=0)


def features(points):
    norm = points * points
    norm = norm[0:1] + norm[1:2] + norm[2:3]
    high = norm.astype(BF16).astype(F32)
    rest = norm - high
    middle = rest.astype(BF16).astype(F32)
    ones = jnp.ones_like(norm)
    return rows(points, high, middle, rest - middle, ones, ones)


def row_side(made):
    ones = made[6:7]
    return rows(-2.0 * made[0:3], ones, ones, ones, made[3:4], made[4:5])


def matern_of(square):
    square = jnp.maximum(square, 1e-14)
    x = (square * lax.rsqrt(square)) * -RATE
    return ((1.0 - x) * jnp.exp(x)).astype(BF16)


def pack_kernel(probes, basis, moves, points, skeleton, packed, coords):
    near = features(points[...].astype(F32))
    far = features(lanes(skeleton[...].astype(F32), jnp.zeros((3, 64), F32)))
    chunks = [near[:, j * LANES : (j + 1) * LANES] for j in range(8)]
    chunks += [far[:, j * LANES : (j + 1) * LANES] for j in range(4)]
    made = rows(*chunks).astype(BF16)
    packed[COORD_ROW:] = made
    coords[...] = made
    leaves = []
    for l in range(4):
        part = slice(l * LEAF, (l + 1) * LEAF)
        leaves.append(dot(basis[:, part], probes[:, part], NT).astype(BF16))
    middle = [
        dot(moves[:, j * 128 : (j + 1) * 128], rows(*leaves[2 * j : 2 * j + 2])).astype(BF16)
        for j in range(2)
    ]
    top = dot(moves[:, 256:384], rows(*middle)).astype(BF16)
    for j in range(8):
        packed[j * SAMPLES : (j + 1) * SAMPLES] = probes[:, j * LANES : (j + 1) * LANES]
    packed[FAR_ROW : FAR_ROW + 64] = lanes(leaves[0], leaves[1])
    packed[FAR_ROW + 64 : FAR_ROW + 128] = lanes(leaves[2], leaves[3])
    packed[FAR_ROW + 128 : FAR_ROW + 192] = lanes(middle[0], middle[1])
    packed[FAR_ROW + 192 : FAR_ROW + 224] = lanes(top[:32], top[32:])


class Plan:
    def __init__(self, near_most, far_most):
        self.near = near_most + NEAR_UNROLL
        self.far = far_most + FAR_UNROLL
        self.far_first = -(-CLASSES * self.near // LANES) * LANES
        self.size = self.far_first + -(-CLASSES * self.far // LANES) * LANES


def iota(shape, axis):
    return lax.broadcasted_iota(jnp.int32, shape, axis)


def tie_kernel(*refs):
    del refs


def tie(x, *others, cost=None):
    return pl.pallas_call(
        tie_kernel,
        out_shape=jax.ShapeDtypeStruct(x.shape, x.dtype),
        in_specs=[ANY] * (1 + len(others)),
        out_specs=ANY,
        input_output_aliases={0: 0},
        compiler_params=pltpu.CompilerParams(vmem_limit_bytes=1 << 20),
        cost_estimate=cost,
        name="tie",
    )(x, *others)


def join_kernel(count, *refs):
    for mine, other, out in zip(refs[:count], refs[count : 2 * count], refs[2 * count :]):
        out[...] = (mine[...].astype(F32) + other[...].astype(F32)).astype(BF16)


def sort_slots(a_device, a_rest, b_device, b_rest, count, per_device, n_col, n_y, most, width):
    slots = a_device.shape[1]
    target = a_device ^ lax.axis_index("col")
    source = b_device ^ lax.axis_index("row")
    remote = target >= 2
    stage = jnp.where(source > 3 * n_y, 2, jnp.where(source > 2 * n_y, 1, 0))
    group = jnp.where(remote, stage, jnp.where(stage == 0, 3, 4))
    alive = iota((1, slots), 1) < count
    group = jnp.where(alive, group, 7)
    row = (target - jnp.where(remote, 2, 0)) * per_device + a_rest
    column = source * per_device + b_rest
    member = jnp.where(iota((8, slots), 0) == group, 1.0, 0.0)
    before = jnp.where(iota((slots, slots), 0) < iota((slots, slots), 1), 1.0, 0.0)
    ahead = dot(member.astype(BF16), before.astype(BF16))
    ahead = jnp.sum(member * ahead, axis=0, keepdims=True)
    sizes = jnp.sum(member, axis=1, keepdims=True)
    ahead += jnp.where(group == 4, sizes[3:4], 0.0)
    ahead += jnp.where((group == 1) | (group == 2), sizes[0:1], 0.0)
    ahead += jnp.where(group == 2, sizes[1:2], 0.0)
    place = jnp.where(alive, jnp.where(remote, 0, most) + ahead.astype(jnp.int32), -1)
    chosen = jnp.where(iota((width, slots), 0) == place, 1.0, 0.0).astype(BF16)
    ones = jnp.ones((6, slots), F32)
    values = rows(row.astype(F32), column.astype(F32), ones).astype(BF16)
    found = dot(values, chosen, NT)
    here = iota((1, width), 1) >= most
    blank = jnp.where(here, 2.0 * per_device, (n_col - 2.0) * per_device)
    made = rows(found[0:1] + blank * (1.0 - found[2:3]), found[1:2])
    return made.astype(jnp.int32), sizes.astype(jnp.int32)


def plan_kernel(n_col, n_y, plan, slots, coords, mate, out, counts, both):
    both[:COORD_ROWS] = coords[...]
    both[COORD_ROWS:] = mate[...]
    near_most, far_most = plan.near - NEAR_UNROLL, plan.far - FAR_UNROLL
    a, b = slots[0:1, :near_most], slots[1:2, :near_most]
    near, near_counts = sort_slots(
        lax.shift_right_logical(a, 2), a & 3, lax.shift_right_logical(b, 2), b & 3,
        slots[4:5, 0:1], 4, n_col, n_y, plan.near, plan.far_first,
    )
    a, b = slots[2:3, :far_most], slots[3:4, :far_most]
    a_device = lax.shift_right_logical(a * 9363, 16)
    b_device = lax.shift_right_logical(b * 9363, 16)
    far, far_counts = sort_slots(
        a_device, a - a_device * CLUSTERS, b_device, b - b_device * CLUSTERS,
        slots[5:6, 0:1], CLUSTERS, n_col, n_y, plan.far, plan.size - plan.far_first,
    )
    out[:, : plan.far_first] = near
    out[:, plan.far_first :] = far
    counts[...] = jnp.where(iota((8, LANES), 1) == 0, near_counts, far_counts)


def row_kernel(n_col, *refs):
    chips, near_row, far_row = refs[:-3], refs[-2], refs[-1]
    empty = jnp.zeros((8, LANES), F32)
    for i in range(n_col):
        first = i % 2 * COORD_ROWS
        slabs = [chips[i // 2][first + 16 * s : first + 16 * s + 16].astype(F32) for s in range(6)]
        near, far = (4 * i, CLUSTERS * i) if i < 2 else (4 * i + 1, CLUSTERS * i + 1)
        for l in range(4):
            for h in range(2):
                made = row_side(slabs[l][8 * h : 8 * h + 8])
                near_row[near + l, h * LANES : (h + 1) * LANES] = rows(made, empty).T.astype(BF16)
        for c in range(4):
            slab = slabs[4 + c // 2]
            made = row_side(slab[8 * (c % 2) : 8 * (c % 2) + 8])
            tall = rows(made, empty).T.astype(BF16)
            far_row[far + 2 * c] = tall[:64]
            if c < 3:
                far_row[far + 2 * c + 1] = tall[64:]
    for blank in (8, 4 * n_col + 1):
        near_row[blank] = jnp.zeros(near_row.shape[1:], BF16)
    for blank in (2 * CLUSTERS, CLUSTERS * n_col + 1):
        far_row[blank] = jnp.zeros(far_row.shape[1:], BF16)


def prepare(i, block, probes, near_col, coeff_low, coeff_high, far_low, far_high):
    for l in range(4):
        for h in range(2):
            j = 2 * l + h
            half = slice(h * LANES, (h + 1) * LANES)
            probes[4 * i + l, :, half] = block[j * SAMPLES : (j + 1) * SAMPLES]
        slab = block[COORD_ROW + 16 * l : COORD_ROW + 16 * (l + 1)]
        near_col[4 * i + l, :, :LANES] = slab
        near_col[4 * i + l, :, LANES:] = rows(slab[8:], slab[:8])
    slabs = [block[COORD_ROW + 64 + 16 * p : COORD_ROW + 80 + 16 * p] for p in range(2)]
    for k in range(CLUSTERS):
        c, half = k // 2, slice(k % 2 * 64, k % 2 * 64 + 64)
        if k < 6:
            own = block[FAR_ROW + 64 * c : FAR_ROW + 64 * (c + 1)][:, half]
        else:
            own = block[FAR_ROW + 192 : FAR_ROW + 224]
            own = rows(own[:, :64], own[:, 64:])
        empty = jnp.zeros_like(own)
        coeff_low[CLUSTERS * i + k] = lanes(own, empty)
        coeff_high[CLUSTERS * i + k] = lanes(empty, own)
        made = slabs[c // 2].astype(F32)[8 * (c % 2) : 8 * (c % 2) + 8, half]
        empty = jnp.zeros_like(made)
        blank = jnp.zeros((8, LANES), F32)
        far_low[CLUSTERS * i + k] = rows(lanes(made, empty), blank).astype(BF16)
        far_high[CLUSTERS * i + k] = rows(lanes(empty, made), blank).astype(BF16)


def work(plan, here, stage, lists, counts, near_row, far_row, prepared, totals):
    probes, near_col, coeff_low, coeff_high, far_low, far_high = prepared
    near_total, far_even, far_odd = totals
    near_first, far_first = (0, 0) if here else (9, 2 * CLUSTERS + 1)

    def near_slot(place):
        a, b = lists[0, place], lists[1, place]
        values = matern_of(dot(near_row[near_first + a], near_col[b]))
        near_total[a] += dot(probes[b], values, NT)

    def far_pair(place):
        a0, a1 = lists[0, place], lists[0, place + 1]
        b0, b1 = lists[1, place], lists[1, place + 1]
        square = dot(far_row[far_first + a0], far_low[b0])
        square += dot(far_row[far_first + a1], far_high[b1])
        term = dot(matern_of(square), rows(coeff_low[b0], coeff_high[b1]))
        far_even[a0] += term
        far_odd[a1] += term

    half = NEAR_UNROLL // 2

    def bounds(kind, unroll):
        sizes = [counts[k, kind] for k in ((3, 4) if here else (0, 1, 2))]
        ends = [jnp.minimum(sizes[0] // unroll, HERE_UNITS if here else EARLY_UNITS)]
        if not here:
            ends += [sizes[0] // unroll, (sizes[0] + sizes[1]) // unroll]
        first = ends[stage - 1] if stage else 0
        if stage < len(ends):
            return first, (ends[stage] - first) * unroll
        return first, sum(sizes) - first * unroll

    near_from, near_count = bounds(0, NEAR_UNROLL)
    far_from, far_count = bounds(1, FAR_UNROLL)
    halves = (near_count + half - 1) // half
    near_groups = halves // 2
    far_groups = (far_count + FAR_UNROLL - 1) // FAR_UNROLL
    together = jnp.minimum(near_groups, far_groups)
    near_place = here * plan.near + near_from * NEAR_UNROLL
    far_place = plan.far_first + here * plan.far + far_from * FAR_UNROLL

    def joint_step(g, _):
        for u in range(NEAR_UNROLL):
            near_slot(near_place + g * NEAR_UNROLL + u)
            far_pair(far_place + g * FAR_UNROLL + 2 * u)
        return 0

    def near_step(g, _):
        for u in range(NEAR_UNROLL):
            near_slot(near_place + g * NEAR_UNROLL + u)
        return 0

    def far_step(g, _):
        for u in range(0, FAR_UNROLL, 2):
            far_pair(far_place + g * FAR_UNROLL + u)
        return 0

    lax.fori_loop(0, together, joint_step, 0)
    lax.fori_loop(together, near_groups, near_step, 0)
    lax.fori_loop(together, far_groups, far_step, 0)

    if stage < (1 if here else 3):
        return

    @pl.when(halves % 2 == 1)
    def _():
        for u in range(half):
            near_slot(near_place + near_groups * NEAR_UNROLL + u)


def write_parts(outs, near_total, far_even, far_odd):
    for i, out in enumerate(outs):
        for j in range(8):
            half = slice(j % 2 * LANES, (j % 2 + 1) * LANES)
            part = near_total[4 * i + j // 2, :, half]
            out[j * SAMPLES : (j + 1) * SAMPLES] = part.astype(BF16)
        parts = []
        for l in range(CLUSTERS):
            even, odd = far_even[CLUSTERS * i + l], far_odd[CLUSTERS * i + l]
            parts.append(even[:, :64] + odd[:, 64:])
        for j in range(3):
            pair = lanes(*parts[2 * j : 2 * j + 2])
            out[FAR_ROW + 64 * j : FAR_ROW + 64 * (j + 1)] = pair.astype(BF16)
        pair = lanes(parts[6][:32], parts[6][32:])
        out[FAR_ROW + 192 : FAR_ROW + 224] = pair.astype(BF16)


def clear(totals):
    for total in totals:
        total[...] = jnp.zeros_like(total)


def early_kernel(plan, copied, members, lists, counts, near_row, far_row, *refs):
    blocks, refs = refs[: len(members)], refs[len(members) :]
    prepared, totals = refs[:6], refs[6:]
    clear(totals)
    for i, block in zip(members, blocks):
        prepare(i, block, *prepared)
    work(plan, 0, 0, lists, counts, near_row, far_row, prepared, totals)


def carry(before, after, copied):
    if copied:
        for old, new in zip(before, after):
            new[...] = old[...]


def second_kernel(plan, copied, members, lists, counts, near_row, far_row, *refs):
    before, refs = refs[:9], refs[9:]
    prepared, totals, here = refs[:6], refs[6:9], refs[9:]
    carry(before, refs, copied)
    clear(here)
    work(plan, 0, 1, lists, counts, near_row, far_row, prepared, totals)
    work(plan, 1, 0, lists, counts, near_row, far_row, prepared, here)


def mid_kernel(plan, copied, members, lists, counts, near_row, far_row, *refs):
    blocks, before, refs = refs[: len(members)], refs[len(members) :][:9], refs[len(members) + 9 :]
    prepared, totals = refs[:6], refs[6:9]
    carry(before, refs, copied)
    for i, block in zip(members, blocks):
        prepare(i, block, *prepared)
    work(plan, 0, 2, lists, counts, near_row, far_row, prepared, totals)


def late_kernel(plan, copied, members, lists, counts, near_row, far_row, *refs):
    blocks, before, refs = refs[: len(members)], refs[len(members) :][:9], refs[len(members) + 9 :]
    prepared, totals, outs = refs[:6], refs[6:9], refs[9:]
    carry(before, refs, copied)
    for i, block in zip(members, blocks):
        prepare(i, block, *prepared)
    work(plan, 0, 3, lists, counts, near_row, far_row, prepared, totals)
    write_parts(outs, *totals)


def here_kernel(plan, copied, lists, counts, near_row, far_row, *refs):
    prepared, before, refs = refs[:6], refs[7:10], refs[10:]
    totals, outs = refs[:3], refs[3:]
    carry(before, refs, copied)
    work(plan, 1, 1, lists, counts, near_row, far_row, prepared, totals)
    write_parts(outs, *totals)


def final_kernel(count, basis, moves, *refs):
    parts, out = refs[:count], refs[count]

    def total(first, count):
        return sum(part[first : first + count].astype(F32) for part in parts)

    def turned(first):
        tall = total(first, 64).T
        return lanes(tall[:64], tall[64:])

    top = total(FAR_ROW + 192, 32)
    top = rows(top[:, :64], top[:, 64:]).T
    middle = turned(FAR_ROW + 128) + dot_wide(top, moves[:, 256:384])
    for j in range(2):
        pair = turned(FAR_ROW + 64 * j) + dot_wide(
            middle[:, j * RANK : (j + 1) * RANK], moves[:, j * 128 : (j + 1) * 128]
        )
        for k in range(2):
            l = 2 * j + k
            expanded = dot_wide(
                pair[:, k * RANK : (k + 1) * RANK], basis[:, l * LEAF : (l + 1) * LEAF]
            )
            for h in range(2):
                place = (2 * l + h) * LANES
                near = total((2 * l + h) * SAMPLES, SAMPLES)
                made = near + expanded[:, h * LANES : (h + 1) * LANES]
                out[:, place : place + LANES] = made.astype(BF16)


def exchange(x, axis, offset):
    size = lax.axis_size(axis)
    return lax.ppermute(x, axis, [(i, i ^ offset) for i in range(size)])


def local(
    probes, points, skeleton, leaf_basis, transfer, near_list, near_count, far_list, far_count
):
    n_row = lax.axis_size("row")
    n_col = lax.axis_size("col")
    n_y = n_row // 4
    probes, basis, moves = probes.T, leaf_basis.T, transfer.T
    inputs = (probes, basis, moves, points, skeleton)
    small = pltpu.CompilerParams(vmem_limit_bytes=8 << 20)
    packed, coords = pl.pallas_call(
        pack_kernel,
        out_shape=[
            jax.ShapeDtypeStruct((PACKED_ROWS, LANES), BF16),
            jax.ShapeDtypeStruct((COORD_ROWS, LANES), BF16),
        ],
        in_specs=[VMEM] * 5,
        out_specs=[VMEM] * 2,
        name="pack",
    )(*inputs)

    plan = Plan(near_list.shape[-1], far_list.shape[-1])
    width = max(LANES, near_list.shape[-1], far_list.shape[-1])

    def placed(x, row):
        return jnp.pad(x, ((row, 8 - row - x.shape[0]), (0, width - x.shape[1])))

    slots = placed(near_list[0, 0], 0) + placed(far_list[0, 0], 2)
    slots = slots + placed(near_count, 4) + placed(far_count, 5)

    def along_z(x, planes, flip):
        pairs = [(z * n_y + y, (z ^ flip) * n_y + y) for z in planes for y in range(n_y)]
        return lax.ppermute(x, "row", pairs)

    own_y = exchange(packed, "row", 1)
    second = along_z(packed, (0, 1, 2, 3), 2)
    neighbour = along_z(packed, (0, 1, 2, 3), 1)
    lists, counts, both = pl.pallas_call(
        functools.partial(plan_kernel, n_col, n_y, plan),
        out_shape=[
            jax.ShapeDtypeStruct((2, plan.size), jnp.int32),
            jax.ShapeDtypeStruct((8, LANES), jnp.int32),
            jax.ShapeDtypeStruct((2 * COORD_ROWS, LANES), BF16),
        ],
        in_specs=[VMEM] * 3,
        out_specs=[VMEM] * 3,
        compiler_params=small,
        cost_estimate=pl.CostEstimate(flops=1 << 30, bytes_accessed=1 << 12, transcendentals=0),
        name="plan",
    )(slots, coords, exchange(coords, "col", 1))

    row_coords = [both] + [exchange(both, "col", k) for k in range(2, n_col, 2)]
    neighbour = tie(neighbour, lists)
    neighbour_y = exchange(neighbour, "row", 1)
    second = tie(second, own_y, neighbour, lists)
    def with_y(block, first=None):
        blocks = [block, exchange(block, "row", 1) if first is None else first]
        return blocks + [exchange(block, "row", y) for y in range(2, n_y)]

    blocks = with_y(packed, own_y) + with_y(neighbour, neighbour_y) + with_y(second)

    row_features = pl.pallas_call(
        functools.partial(row_kernel, n_col),
        out_shape=[
            jax.ShapeDtypeStruct((4 * n_col + 2, LEAF, FEATURES), BF16),
            jax.ShapeDtypeStruct((CLUSTERS * n_col + 2, RANK, FEATURES), BF16),
        ],
        in_specs=[VMEM] * (n_col // 2) + [ANY],
        out_specs=[VMEM] * 2,
        compiler_params=small,
        name="row_side",
    )(*row_coords, second)

    def sums(targets):
        near = (4 * targets + 1, SAMPLES, LEAF)
        far = (CLUSTERS * targets + 1, RANK, LANES)
        return [near, far, far]

    part = jax.ShapeDtypeStruct((COORD_ROW, LANES), BF16)
    held = [
        jax.ShapeDtypeStruct(shape, BF16)
        for shape in [
            (4 * n_row, SAMPLES, LEAF),
            (4 * n_row, FEATURES, LEAF),
            (CLUSTERS * n_row, RANK, LANES),
            (CLUSTERS * n_row, RANK, LANES),
            (CLUSTERS * n_row, FEATURES, LANES),
            (CLUSTERS * n_row, FEATURES, LANES),
        ]
    ]
    held += [jax.ShapeDtypeStruct(shape, F32) for shape in sums(n_col - 2)]
    params = pltpu.CompilerParams(vmem_limit_bytes=32 << 20)
    cost = pl.CostEstimate(flops=1 << 33, bytes_accessed=1 << 20, transcendentals=0)
    local_sums = [jax.ShapeDtypeStruct(shape, F32) for shape in sums(2)]
    copied = sum(math.prod(x.shape) * x.dtype.itemsize for x in held) > 8 << 20

    def stage(kernel, members, out_shape, name):
        first = 4 + len(members)
        return pl.pallas_call(
            functools.partial(kernel, plan, copied, members),
            out_shape=out_shape,
            in_specs=[SMEM] * 2 + [VMEM] * (2 + len(members) + len(handed)),
            out_specs=[VMEM] * len(out_shape),
            input_output_aliases={first + k: k for k in range(len(handed))},
            compiler_params=params,
            cost_estimate=cost,
            name=name,
        )(lists, counts, *row_features, *[blocks[j] for j in members], *handed)

    handed = []
    handed = stage(early_kernel, list(range(2 * n_y + 1)), held, "early")
    third = tie(along_z(second, (0, 1, 2, 3), 1), handed[6])
    blocks += with_y(third)
    both_sums = stage(second_kernel, [], held + local_sums, "second")
    handed, here_totals = both_sums[: len(held)], both_sums[len(held) :]
    handed = stage(mid_kernel, list(range(2 * n_y + 1, 3 * n_y + 1)), held, "mid")
    handed = stage(late_kernel, list(range(3 * n_y + 1, n_row)), held + [part] * (n_col - 2), "late")
    prepared, parts = handed[:6], handed[len(held) :]
    mine, other = parts[0::2], [exchange(part, "col", 1) for part in parts[1::2]]
    joined = pl.pallas_call(
        functools.partial(join_kernel, len(mine)),
        out_shape=[part] * len(mine),
        in_specs=[VMEM] * (2 * len(mine)),
        out_specs=[VMEM] * len(mine),
        compiler_params=params,
        name="join",
    )(*mine, *other)
    arrived = [exchange(joined[k], "col", 2 * k + 2) for k in range(len(mine))]
    here = pl.pallas_call(
        functools.partial(here_kernel, plan, copied),
        out_shape=local_sums + [part] * 2,
        in_specs=[SMEM] * 2 + [VMEM] * 8 + [ANY] + [VMEM] * 3,
        out_specs=[VMEM] * 5,
        input_output_aliases={11 + k: k for k in range(3)},
        compiler_params=params,
        cost_estimate=cost,
        name="here",
    )(lists, counts, *row_features, *prepared, joined[0], *here_totals)[3:]
    arrived = [tie(x, cost=cost) for x in arrived]
    arrived += [here[0], exchange(here[1], "col", 1)]
    sample = pl.pallas_call(
        functools.partial(final_kernel, len(arrived)),
        out_shape=jax.ShapeDtypeStruct((SAMPLES, OWN), BF16),
        in_specs=[VMEM] * (2 + len(arrived)),
        out_specs=VMEM,
        compiler_params=pltpu.CompilerParams(vmem_limit_bytes=16 << 20),
        name="final",
    )(basis, moves, *arrived)
    return sample.T


def solution(mesh):
    placed = (
        P(("row", "col"), None),
        P(None, ("row", "col")),
        P(None, ("row", "col")),
        P(("row", "col"), None),
        P(("row", "col"), None),
        P("row", "col", None, None),
        P("row", "col"),
        P("row", "col", None, None),
        P("row", "col"),
    )
    return jax.shard_map(
        local, mesh=mesh, in_specs=placed, out_specs=P(("row", "col"), None), check_vma=False
    )
```

```python
import functools
import math

import jax
import jax.numpy as jnp
from jax import lax
from jax.experimental import pallas as pl
from jax.experimental.pallas import tpu as pltpu
from jax.sharding import PartitionSpec as P

LEAF = 256
RANK = 64
SAMPLES = 64
OWN = 4 * LEAF
CLUSTERS = 7
LANES = 128
F32 = jnp.float32
BF16 = jnp.bfloat16
FAR_ROW = OWN // LANES * SAMPLES
COORD_ROW = FAR_ROW + CLUSTERS * SAMPLES // 2
COORD_ROWS = 96
PACKED_ROWS = COORD_ROW + COORD_ROWS
FEATURES = 16
CLASSES = 2
NEAR_UNROLL = 8
FAR_UNROLL = 16
RATE = math.sqrt(3.0) / 0.15
EARLY_UNITS = 1
HERE_UNITS = 1

ANY = pl.BlockSpec(memory_space=pl.ANY)
VMEM = pl.BlockSpec(memory_space=pltpu.VMEM)
SMEM = pl.BlockSpec(memory_space=pltpu.SMEM)
NN = (((1,), (0,)), ((), ()))
NT = (((1,), (1,)), ((), ()))


def dot(a, b, dims=NN):
    return lax.dot_general(a, b, dims, preferred_element_type=F32)


def dot_wide(a, b):
    high = a.astype(BF16)
    low = (a - high.astype(F32)).astype(BF16)
    return dot(high, b) + dot(low, b)


def lanes(a, b):
    return jnp.concatenate([a, b], axis=1)


def rows(*parts):
    return jnp.concatenate(parts, axis=0)


def features(points):
    norm = points * points
    norm = norm[0:1] + norm[1:2] + norm[2:3]
    high = norm.astype(BF16).astype(F32)
    rest = norm - high
    middle = rest.astype(BF16).astype(F32)
    ones = jnp.ones_like(norm)
    return rows(points, high, middle, rest - middle, ones, ones)


def row_side(made):
    ones = made[6:7]
    return rows(-2.0 * made[0:3], ones, ones, ones, made[3:4], made[4:5])


def matern_of(square):
    square = jnp.maximum(square, 1e-14)
    x = (square * lax.rsqrt(square)) * -RATE
    return ((1.0 - x) * jnp.exp(x)).astype(BF16)


def pack_kernel(probes, basis, moves, points, skeleton, packed, coords):
    near = features(points[...].astype(F32))
    far = features(lanes(skeleton[...].astype(F32), jnp.zeros((3, 64), F32)))
    chunks = [near[:, j * LANES : (j + 1) * LANES] for j in range(8)]
    chunks += [far[:, j * LANES : (j + 1) * LANES] for j in range(4)]
    made = rows(*chunks).astype(BF16)
    packed[COORD_ROW:] = made
    coords[...] = made
    leaves = []
    for l in range(4):
        part = slice(l * LEAF, (l + 1) * LEAF)
        leaves.append(dot(basis[:, part], probes[:, part], NT).astype(BF16))
    middle = [
        dot(moves[:, j * 128 : (j + 1) * 128], rows(*leaves[2 * j : 2 * j + 2])).astype(BF16)
        for j in range(2)
    ]
    top = dot(moves[:, 256:384], rows(*middle)).astype(BF16)
    for j in range(8):
        packed[j * SAMPLES : (j + 1) * SAMPLES] = probes[:, j * LANES : (j + 1) * LANES]
    packed[FAR_ROW : FAR_ROW + 64] = lanes(leaves[0], leaves[1])
    packed[FAR_ROW + 64 : FAR_ROW + 128] = lanes(leaves[2], leaves[3])
    packed[FAR_ROW + 128 : FAR_ROW + 192] = lanes(middle[0], middle[1])
    packed[FAR_ROW + 192 : FAR_ROW + 224] = lanes(top[:32], top[32:])


class Plan:
    def __init__(self, near_most, far_most):
        self.near = near_most + NEAR_UNROLL
        self.far = far_most + FAR_UNROLL
        self.far_first = -(-CLASSES * self.near // LANES) * LANES
        self.size = self.far_first + -(-CLASSES * self.far // LANES) * LANES


def iota(shape, axis):
    return lax.broadcasted_iota(jnp.int32, shape, axis)


def tie_kernel(*refs):
    del refs


def tie(x, *others, cost=None):
    return pl.pallas_call(
        tie_kernel,
        out_shape=jax.ShapeDtypeStruct(x.shape, x.dtype),
        in_specs=[ANY] * (1 + len(others)),
        out_specs=ANY,
        input_output_aliases={0: 0},
        compiler_params=pltpu.CompilerParams(vmem_limit_bytes=1 << 20),
        cost_estimate=cost,
        name="tie",
    )(x, *others)


def join_kernel(count, *refs):
    for mine, other, out in zip(refs[:count], refs[count : 2 * count], refs[2 * count :]):
        out[...] = (mine[...].astype(F32) + other[...].astype(F32)).astype(BF16)


def sort_slots(a_device, a_rest, b_device, b_rest, count, per_device, n_col, n_y, most, width):
    slots = a_device.shape[1]
    target = a_device ^ lax.axis_index("col")
    source = b_device ^ lax.axis_index("row")
    remote = target >= 2
    stage = jnp.where(source > 3 * n_y, 2, jnp.where(source > 2 * n_y, 1, 0))
    group = jnp.where(remote, stage, jnp.where(stage == 0, 3, 4))
    alive = iota((1, slots), 1) < count
    group = jnp.where(alive, group, 7)
    row = (target - jnp.where(remote, 2, 0)) * per_device + a_rest
    column = source * per_device + b_rest
    member = jnp.where(iota((8, slots), 0) == group, 1.0, 0.0)
    before = jnp.where(iota((slots, slots), 0) < iota((slots, slots), 1), 1.0, 0.0)
    ahead = dot(member.astype(BF16), before.astype(BF16))
    ahead = jnp.sum(member * ahead, axis=0, keepdims=True)
    sizes = jnp.sum(member, axis=1, keepdims=True)
    ahead += jnp.where(group == 4, sizes[3:4], 0.0)
    ahead += jnp.where((group == 1) | (group == 2), sizes[0:1], 0.0)
    ahead += jnp.where(group == 2, sizes[1:2], 0.0)
    place = jnp.where(alive, jnp.where(remote, 0, most) + ahead.astype(jnp.int32), -1)
    chosen = jnp.where(iota((width, slots), 0) == place, 1.0, 0.0).astype(BF16)
    ones = jnp.ones((6, slots), F32)
    values = rows(row.astype(F32), column.astype(F32), ones).astype(BF16)
    found = dot(values, chosen, NT)
    here = iota((1, width), 1) >= most
    blank = jnp.where(here, 2.0 * per_device, (n_col - 2.0) * per_device)
    made = rows(found[0:1] + blank * (1.0 - found[2:3]), found[1:2])
    return made.astype(jnp.int32), sizes.astype(jnp.int32)


def plan_kernel(n_col, n_y, plan, slots, coords, mate, out, counts, both):
    both[:COORD_ROWS] = coords[...]
    both[COORD_ROWS:] = mate[...]
    near_most, far_most = plan.near - NEAR_UNROLL, plan.far - FAR_UNROLL
    a, b = slots[0:1, :near_most], slots[1:2, :near_most]
    near, near_counts = sort_slots(
        lax.shift_right_logical(a, 2), a & 3, lax.shift_right_logical(b, 2), b & 3,
        slots[4:5, 0:1], 4, n_col, n_y, plan.near, plan.far_first,
    )
    a, b = slots[2:3, :far_most], slots[3:4, :far_most]
    a_device = lax.shift_right_logical(a * 9363, 16)
    b_device = lax.shift_right_logical(b * 9363, 16)
    far, far_counts = sort_slots(
        a_device, a - a_device * CLUSTERS, b_device, b - b_device * CLUSTERS,
        slots[5:6, 0:1], CLUSTERS, n_col, n_y, plan.far, plan.size - plan.far_first,
    )
    out[:, : plan.far_first] = near
    out[:, plan.far_first :] = far
    counts[...] = jnp.where(iota((8, LANES), 1) == 0, near_counts, far_counts)


def row_kernel(n_col, *refs):
    chips, near_row, far_row = refs[:-3], refs[-2], refs[-1]
    empty = jnp.zeros((8, LANES), F32)
    for i in range(n_col):
        first = i % 2 * COORD_ROWS
        slabs = [chips[i // 2][first + 16 * s : first + 16 * s + 16].astype(F32) for s in range(6)]
        near, far = (4 * i, CLUSTERS * i) if i < 2 else (4 * i + 1, CLUSTERS * i + 1)
        for l in range(4):
            for h in range(2):
                made = row_side(slabs[l][8 * h : 8 * h + 8])
                near_row[near + l, h * LANES : (h + 1) * LANES] = rows(made, empty).T.astype(BF16)
        for c in range(4):
            slab = slabs[4 + c // 2]
            made = row_side(slab[8 * (c % 2) : 8 * (c % 2) + 8])
            tall = rows(made, empty).T.astype(BF16)
            far_row[far + 2 * c] = tall[:64]
            if c < 3:
                far_row[far + 2 * c + 1] = tall[64:]
    for blank in (8, 4 * n_col + 1):
        near_row[blank] = jnp.zeros(near_row.shape[1:], BF16)
    for blank in (2 * CLUSTERS, CLUSTERS * n_col + 1):
        far_row[blank] = jnp.zeros(far_row.shape[1:], BF16)


def prepare(i, block, probes, near_col, coeff_low, coeff_high, far_low, far_high):
    for l in range(4):
        for h in range(2):
            j = 2 * l + h
            half = slice(h * LANES, (h + 1) * LANES)
            probes[4 * i + l, :, half] = block[j * SAMPLES : (j + 1) * SAMPLES]
        slab = block[COORD_ROW + 16 * l : COORD_ROW + 16 * (l + 1)]
        near_col[4 * i + l, :, :LANES] = slab
        near_col[4 * i + l, :, LANES:] = rows(slab[8:], slab[:8])
    slabs = [block[COORD_ROW + 64 + 16 * p : COORD_ROW + 80 + 16 * p] for p in range(2)]
    for k in range(CLUSTERS):
        c, half = k // 2, slice(k % 2 * 64, k % 2 * 64 + 64)
        if k < 6:
            own = block[FAR_ROW + 64 * c : FAR_ROW + 64 * (c + 1)][:, half]
        else:
            own = block[FAR_ROW + 192 : FAR_ROW + 224]
            own = rows(own[:, :64], own[:, 64:])
        empty = jnp.zeros_like(own)
        coeff_low[CLUSTERS * i + k] = lanes(own, empty)
        coeff_high[CLUSTERS * i + k] = lanes(empty, own)
        made = slabs[c // 2].astype(F32)[8 * (c % 2) : 8 * (c % 2) + 8, half]
        empty = jnp.zeros_like(made)
        blank = jnp.zeros((8, LANES), F32)
        far_low[CLUSTERS * i + k] = rows(lanes(made, empty), blank).astype(BF16)
        far_high[CLUSTERS * i + k] = rows(lanes(empty, made), blank).astype(BF16)


def work(plan, here, stage, lists, counts, near_row, far_row, prepared, totals):
    probes, near_col, coeff_low, coeff_high, far_low, far_high = prepared
    near_total, far_even, far_odd = totals
    near_first, far_first = (0, 0) if here else (9, 2 * CLUSTERS + 1)

    def near_slot(place):
        a, b = lists[0, place], lists[1, place]
        values = matern_of(dot(near_row[near_first + a], near_col[b]))
        near_total[a] += dot(probes[b], values, NT)

    def far_pair(place):
        a0, a1 = lists[0, place], lists[0, place + 1]
        b0, b1 = lists[1, place], lists[1, place + 1]
        square = dot(far_row[far_first + a0], far_low[b0])
        square += dot(far_row[far_first + a1], far_high[b1])
        term = dot(matern_of(square), rows(coeff_low[b0], coeff_high[b1]))
        far_even[a0] += term
        far_odd[a1] += term

    half = NEAR_UNROLL // 2

    def bounds(kind, unroll):
        sizes = [counts[k, kind] for k in ((3, 4) if here else (0, 1, 2))]
        ends = [jnp.minimum(sizes[0] // unroll, HERE_UNITS if here else EARLY_UNITS)]
        if not here:
            ends += [sizes[0] // unroll, (sizes[0] + sizes[1]) // unroll]
        first = ends[stage - 1] if stage else 0
        if stage < len(ends):
            return first, (ends[stage] - first) * unroll
        return first, sum(sizes) - first * unroll

    near_from, near_count = bounds(0, NEAR_UNROLL)
    far_from, far_count = bounds(1, FAR_UNROLL)
    halves = (near_count + half - 1) // half
    near_groups = halves // 2
    far_half = FAR_UNROLL // 2
    far_halves = (far_count + far_half - 1) // far_half
    far_groups = far_halves // 2
    together = jnp.minimum(near_groups, far_groups)
    near_place = here * plan.near + near_from * NEAR_UNROLL
    far_place = plan.far_first + here * plan.far + far_from * FAR_UNROLL

    def joint_step(g, _):
        for u in range(NEAR_UNROLL):
            near_slot(near_place + g * NEAR_UNROLL + u)
            far_pair(far_place + g * FAR_UNROLL + 2 * u)
        return 0

    def near_step(g, _):
        for u in range(NEAR_UNROLL):
            near_slot(near_place + g * NEAR_UNROLL + u)
        return 0

    def far_step(g, _):
        for u in range(0, FAR_UNROLL, 2):
            far_pair(far_place + g * FAR_UNROLL + u)
        return 0

    lax.fori_loop(0, together, joint_step, 0)
    lax.fori_loop(together, near_groups, near_step, 0)
    lax.fori_loop(together, far_groups, far_step, 0)

    if stage < (1 if here else 3):
        return

    @pl.when(halves % 2 == 1)
    def _():
        for u in range(half):
            near_slot(near_place + near_groups * NEAR_UNROLL + u)

    @pl.when(far_halves % 2 == 1)
    def _():
        for u in range(0, far_half, 2):
            far_pair(far_place + far_groups * FAR_UNROLL + u)


def write_parts(outs, near_total, far_even, far_odd):
    for i, out in enumerate(outs):
        for j in range(8):
            half = slice(j % 2 * LANES, (j % 2 + 1) * LANES)
            part = near_total[4 * i + j // 2, :, half]
            out[j * SAMPLES : (j + 1) * SAMPLES] = part.astype(BF16)
        parts = []
        for l in range(CLUSTERS):
            even, odd = far_even[CLUSTERS * i + l], far_odd[CLUSTERS * i + l]
            parts.append(even[:, :64] + odd[:, 64:])
        for j in range(3):
            pair = lanes(*parts[2 * j : 2 * j + 2])
            out[FAR_ROW + 64 * j : FAR_ROW + 64 * (j + 1)] = pair.astype(BF16)
        pair = lanes(parts[6][:32], parts[6][32:])
        out[FAR_ROW + 192 : FAR_ROW + 224] = pair.astype(BF16)


def clear(totals):
    for total in totals:
        total[...] = jnp.zeros_like(total)


def early_kernel(plan, copied, members, lists, counts, near_row, far_row, *refs):
    blocks, refs = refs[: len(members)], refs[len(members) :]
    prepared, totals = refs[:6], refs[6:]
    clear(totals)
    for i, block in zip(members, blocks):
        prepare(i, block, *prepared)
    work(plan, 0, 0, lists, counts, near_row, far_row, prepared, totals)


def carry(before, after, copied):
    if copied:
        for old, new in zip(before, after):
            new[...] = old[...]


def second_kernel(plan, copied, members, lists, counts, near_row, far_row, *refs):
    before, refs = refs[:9], refs[9:]
    prepared, totals, here = refs[:6], refs[6:9], refs[9:]
    carry(before, refs, copied)
    clear(here)
    work(plan, 0, 1, lists, counts, near_row, far_row, prepared, totals)
    work(plan, 1, 0, lists, counts, near_row, far_row, prepared, here)


def mid_kernel(plan, copied, members, lists, counts, near_row, far_row, *refs):
    blocks, before, refs = refs[: len(members)], refs[len(members) :][:9], refs[len(members) + 9 :]
    prepared, totals = refs[:6], refs[6:9]
    carry(before, refs, copied)
    for i, block in zip(members, blocks):
        prepare(i, block, *prepared)
    work(plan, 0, 2, lists, counts, near_row, far_row, prepared, totals)


def late_kernel(plan, copied, members, lists, counts, near_row, far_row, *refs):
    blocks, before, refs = refs[: len(members)], refs[len(members) :][:9], refs[len(members) + 9 :]
    prepared, totals, outs = refs[:6], refs[6:9], refs[9:]
    carry(before, refs, copied)
    for i, block in zip(members, blocks):
        prepare(i, block, *prepared)
    work(plan, 0, 3, lists, counts, near_row, far_row, prepared, totals)
    write_parts(outs, *totals)


def here_kernel(plan, copied, lists, counts, near_row, far_row, *refs):
    prepared, before, refs = refs[:6], refs[7:10], refs[10:]
    totals, outs = refs[:3], refs[3:]
    carry(before, refs, copied)
    work(plan, 1, 1, lists, counts, near_row, far_row, prepared, totals)
    write_parts(outs, *totals)


def final_kernel(count, basis, moves, *refs):
    parts, out = refs[:count], refs[count]

    def total(first, count):
        return sum(part[first : first + count].astype(F32) for part in parts)

    def turned(first):
        tall = total(first, 64).T
        return lanes(tall[:64], tall[64:])

    top = total(FAR_ROW + 192, 32)
    top = rows(top[:, :64], top[:, 64:]).T
    middle = turned(FAR_ROW + 128) + dot_wide(top, moves[:, 256:384])
    for j in range(2):
        pair = turned(FAR_ROW + 64 * j) + dot_wide(
            middle[:, j * RANK : (j + 1) * RANK], moves[:, j * 128 : (j + 1) * 128]
        )
        for k in range(2):
            l = 2 * j + k
            expanded = dot_wide(
                pair[:, k * RANK : (k + 1) * RANK], basis[:, l * LEAF : (l + 1) * LEAF]
            )
            for h in range(2):
                place = (2 * l + h) * LANES
                near = total((2 * l + h) * SAMPLES, SAMPLES)
                made = near + expanded[:, h * LANES : (h + 1) * LANES]
                out[:, place : place + LANES] = made.astype(BF16)


def exchange(x, axis, offset):
    size = lax.axis_size(axis)
    return lax.ppermute(x, axis, [(i, i ^ offset) for i in range(size)])


def local(
    probes, points, skeleton, leaf_basis, transfer, near_list, near_count, far_list, far_count
):
    n_row = lax.axis_size("row")
    n_col = lax.axis_size("col")
    n_y = n_row // 4
    probes, basis, moves = probes.T, leaf_basis.T, transfer.T
    inputs = (probes, basis, moves, points, skeleton)
    small = pltpu.CompilerParams(vmem_limit_bytes=8 << 20)
    packed, coords = pl.pallas_call(
        pack_kernel,
        out_shape=[
            jax.ShapeDtypeStruct((PACKED_ROWS, LANES), BF16),
            jax.ShapeDtypeStruct((COORD_ROWS, LANES), BF16),
        ],
        in_specs=[VMEM] * 5,
        out_specs=[VMEM] * 2,
        name="pack",
    )(*inputs)

    plan = Plan(near_list.shape[-1], far_list.shape[-1])
    width = max(LANES, near_list.shape[-1], far_list.shape[-1])

    def placed(x, row):
        return jnp.pad(x, ((row, 8 - row - x.shape[0]), (0, width - x.shape[1])))

    slots = placed(near_list[0, 0], 0) + placed(far_list[0, 0], 2)
    slots = slots + placed(near_count, 4) + placed(far_count, 5)

    def along_z(x, planes, flip):
        pairs = [(z * n_y + y, (z ^ flip) * n_y + y) for z in planes for y in range(n_y)]
        return lax.ppermute(x, "row", pairs)

    own_y = exchange(packed, "row", 1)
    second = along_z(packed, (0, 1, 2, 3), 2)
    neighbour = along_z(packed, (0, 1, 2, 3), 1)
    lists, counts, both = pl.pallas_call(
        functools.partial(plan_kernel, n_col, n_y, plan),
        out_shape=[
            jax.ShapeDtypeStruct((2, plan.size), jnp.int32),
            jax.ShapeDtypeStruct((8, LANES), jnp.int32),
            jax.ShapeDtypeStruct((2 * COORD_ROWS, LANES), BF16),
        ],
        in_specs=[VMEM] * 3,
        out_specs=[VMEM] * 3,
        compiler_params=small,
        cost_estimate=pl.CostEstimate(flops=1 << 30, bytes_accessed=1 << 12, transcendentals=0),
        name="plan",
    )(slots, coords, exchange(coords, "col", 1))

    row_coords = [both] + [exchange(both, "col", k) for k in range(2, n_col, 2)]
    neighbour = tie(neighbour, lists)
    neighbour_y = exchange(neighbour, "row", 1)
    second = tie(second, own_y, neighbour, lists)
    def with_y(block, first=None):
        blocks = [block, exchange(block, "row", 1) if first is None else first]
        return blocks + [exchange(block, "row", y) for y in range(2, n_y)]

    blocks = with_y(packed, own_y) + with_y(neighbour, neighbour_y) + with_y(second)

    row_features = pl.pallas_call(
        functools.partial(row_kernel, n_col),
        out_shape=[
            jax.ShapeDtypeStruct((4 * n_col + 2, LEAF, FEATURES), BF16),
            jax.ShapeDtypeStruct((CLUSTERS * n_col + 2, RANK, FEATURES), BF16),
        ],
        in_specs=[VMEM] * (n_col // 2) + [ANY],
        out_specs=[VMEM] * 2,
        compiler_params=small,
        name="row_side",
    )(*row_coords, second)

    def sums(targets):
        near = (4 * targets + 1, SAMPLES, LEAF)
        far = (CLUSTERS * targets + 1, RANK, LANES)
        return [near, far, far]

    part = jax.ShapeDtypeStruct((COORD_ROW, LANES), BF16)
    held = [
        jax.ShapeDtypeStruct(shape, BF16)
        for shape in [
            (4 * n_row, SAMPLES, LEAF),
            (4 * n_row, FEATURES, LEAF),
            (CLUSTERS * n_row, RANK, LANES),
            (CLUSTERS * n_row, RANK, LANES),
            (CLUSTERS * n_row, FEATURES, LANES),
            (CLUSTERS * n_row, FEATURES, LANES),
        ]
    ]
    held += [jax.ShapeDtypeStruct(shape, F32) for shape in sums(n_col - 2)]
    params = pltpu.CompilerParams(vmem_limit_bytes=32 << 20)
    cost = pl.CostEstimate(flops=1 << 33, bytes_accessed=1 << 20, transcendentals=0)
    local_sums = [jax.ShapeDtypeStruct(shape, F32) for shape in sums(2)]
    copied = sum(math.prod(x.shape) * x.dtype.itemsize for x in held) > 8 << 20

    def stage(kernel, members, out_shape, name):
        first = 4 + len(members)
        return pl.pallas_call(
            functools.partial(kernel, plan, copied, members),
            out_shape=out_shape,
            in_specs=[SMEM] * 2 + [VMEM] * (2 + len(members) + len(handed)),
            out_specs=[VMEM] * len(out_shape),
            input_output_aliases={first + k: k for k in range(len(handed))},
            compiler_params=params,
            cost_estimate=cost,
            name=name,
        )(lists, counts, *row_features, *[blocks[j] for j in members], *handed)

    handed = []
    handed = stage(early_kernel, list(range(2 * n_y + 1)), held, "early")
    third = tie(along_z(second, (0, 1, 2, 3), 1), handed[6])
    blocks += with_y(third)
    both_sums = stage(second_kernel, [], held + local_sums, "second")
    handed, here_totals = both_sums[: len(held)], both_sums[len(held) :]
    handed = stage(mid_kernel, list(range(2 * n_y + 1, 3 * n_y + 1)), held, "mid")
    handed = stage(late_kernel, list(range(3 * n_y + 1, n_row)), held + [part] * (n_col - 2), "late")
    prepared, parts = handed[:6], handed[len(held) :]
    mine, other = parts[0::2], [exchange(part, "col", 1) for part in parts[1::2]]
    joined = pl.pallas_call(
        functools.partial(join_kernel, len(mine)),
        out_shape=[part] * len(mine),
        in_specs=[VMEM] * (2 * len(mine)),
        out_specs=[VMEM] * len(mine),
        compiler_params=params,
        name="join",
    )(*mine, *other)
    arrived = [exchange(joined[k], "col", 2 * k + 2) for k in range(len(mine))]
    here = pl.pallas_call(
        functools.partial(here_kernel, plan, copied),
        out_shape=local_sums + [part] * 2,
        in_specs=[SMEM] * 2 + [VMEM] * 8 + [ANY] + [VMEM] * 3,
        out_specs=[VMEM] * 5,
        input_output_aliases={11 + k: k for k in range(3)},
        compiler_params=params,
        cost_estimate=cost,
        name="here",
    )(lists, counts, *row_features, *prepared, joined[0], *here_totals)[3:]
    arrived = [tie(x, cost=cost) for x in arrived]
    arrived += [here[0], exchange(here[1], "col", 1)]
    sample = pl.pallas_call(
        functools.partial(final_kernel, len(arrived)),
        out_shape=jax.ShapeDtypeStruct((SAMPLES, OWN), BF16),
        in_specs=[VMEM] * (2 + len(arrived)),
        out_specs=VMEM,
        compiler_params=pltpu.CompilerParams(vmem_limit_bytes=16 << 20),
        name="final",
    )(basis, moves, *arrived)
    return sample.T


def solution(mesh):
    placed = (
        P(("row", "col"), None),
        P(None, ("row", "col")),
        P(None, ("row", "col")),
        P(("row", "col"), None),
        P(("row", "col"), None),
        P("row", "col", None, None),
        P("row", "col"),
        P("row", "col", None, None),
        P("row", "col"),
    )
    return jax.shard_map(
        local, mesh=mesh, in_specs=placed, out_specs=P(("row", "col"), None), check_vma=False
    )
```
